32 devices in a mesh: seq: 8 (over y, x, core), head: 4 (over z).
Axes of the slice: x: 2, y: 2, z: 4, core: 2. Of those that a mesh axis runs over, the one named last changes fastest.
Arguments:
- tokens: bfloat16 [4, 4096, 1536], P(None, 'seq'), may hold values from -6 to 6
- norm_gain: float32 [1536], replicated, may hold values from 0.25 to 1.75
- gate_weight: bfloat16 [1536, 3072], P(None, 'head'), may hold values from -0.15625 to 0.15625
- value_weight: bfloat16 [1536, 3072], P(None, 'head'), may hold values from -0.15625 to 0.15625
- state_weight: bfloat16 [1536, 256], replicated, may hold values from -0.15625 to 0.15625
- step_weight: bfloat16 [1536, 48], P(None, 'head'), may hold values from -0.15625 to 0.15625
- value_kernel: float32 [4, 3072], P(None, 'head'), may hold values from -3 to 3
- value_offset: float32 [3072], P('head'), may hold values from -3 to 3
- state_kernel: float32 [4, 256], replicated, may hold values from -3 to 3
- state_offset: float32 [256], replicated, may hold values from -3 to 3
- step_bias: float32 [48], P('head'), may hold values from -3.5 to -2
- log_rate: float32 [48], P('head'), may hold values from -16 to 0, as said below
- skip_gain: float32 [48], P('head'), may hold values from 0.5 to 2
- mixer_gain: float32 [3072], P('head'), may hold values from 0.25 to 1.75
- out_weight: bfloat16 [3072, 1536], P('head'), may hold values from -0.109375 to 0.109375
- cotangent: bfloat16 [4, 4096, 1536], P(None, 'seq'), may hold values from -6 to 6
Outputs:
- result: bfloat16 [4, 4096, 1536], P(None, 'seq')
- tokens_grad: float32 [4, 4096, 1536], P(None, 'seq')
- norm_gain_grad: float32 [1536], replicated
- gate_weight_grad: float32 [1536, 3072], P(None, 'head')
- value_weight_grad: float32 [1536, 3072], P(None, 'head')
- state_weight_grad: float32 [1536, 256], replicated
- step_weight_grad: float32 [1536, 48], P(None, 'head')
- value_filter_gradient: float32 [4, 3072], P(None, 'head')
- value_offset_grad: float32 [3072], P('head')
- state_kernel_grad: float32 [4, 256], replicated
- state_offset_grad: float32 [256], replicated
- step_bias_grad: float32 [48], P('head')
- log_rate_grad: float32 [48], P('head')
- skip_gain_grad: float32 [48], P('head')
- mixer_gain_grad: float32 [3072], P('head')
- out_weight_grad: float32 [3072, 1536], P('head')
The draws below stay inside these ranges and needn't reach their ends.
Inputs may be any that keep to these rules, and one draw needn't show every extreme that they name: `log_rate`: one value a head.
All inputs are finite; a program needn't handle non-finite values.
Results may differ from the reference program's by a relative error of at most 0.025.
The reference program's roundings to bfloat16 on the way count: a program that leaves them out, or rounds other values in their place, can miss the bound.
Values may be sent and summed in bfloat16 or wider, within the bound.
A program may use at most 320 MiB of HBM per device.

```python
import math
import jax
import jax.numpy as jnp
from jax import lax

D = 1536
HEADS = 48
HEAD_DIM = 64
NSTATE = 128
INNER = 3072
KCONV = 4
GROUP = 256
SEQS = 4
LENGTH = 4096


def draw_log_rate(key, part):
    key = jax.random.fold_in(key, 17)
    pick_key, slow_key, fast_key = jax.random.split(key, 3)
    slow_portion = 4
    slow_heads = jax.random.randint(pick_key, (HEADS,), 0, 8) < slow_portion
    slow_value = math.log(0.5 / (LENGTH * 0.06)) + jax.random.uniform(slow_key, (HEADS,), jnp.float32, -0.3, 0.3)
    fast_value = jax.random.uniform(fast_key, (HEADS,), jnp.float32, math.log(0.3), 0.0)
    return jnp.where(slow_heads, slow_value, fast_value).astype(jnp.float32)


def levels(key, shape, cuts, low, high):
    level, own = 1.0, jax.random.fold_in(key, 6)
    for dim, blocks in cuts:
        draws = jnp.exp(jax.random.uniform(jax.random.fold_in(own, dim), (blocks,), jnp.float32, low / len(cuts), high / len(cuts)))
        level = level * jnp.repeat(draws, shape[dim] // blocks).reshape([-1 if axis == dim else 1 for axis in range(len(shape))])
    return level


def gaussian(rng, dims, scale, reach, cuts=(), held_as=jnp.bfloat16):
    drawn = jax.random.normal(rng, dims, jnp.float32) * scale
    if len(cuts) > 0:
        drawn = levels(rng, dims, cuts, -0.22, 0.18) * drawn
    return jnp.clip(drawn, min=-reach, max=reach).astype(held_as)


def setup_inputs(seed: int = 0) -> dict:
    splits = jax.random.split(jax.random.key(seed), 17)
    tokens = gaussian(splits[0], (SEQS, LENGTH, D), 1.0, 6.0, ((1, 8),))
    norm_gain = jnp.clip(1.0 + 0.15 * jax.random.normal(splits[1], (D,), jnp.float32), 0.25, 1.75)
    gate_weight = gaussian(splits[2], (D, INNER), D ** -0.5, 0.15625, ((1, 4),))
    value_weight = gaussian(splits[3], (D, INNER), D ** -0.5, 0.15625, ((1, 4),))
    state_weight = gaussian(splits[4], (D, 2 * NSTATE), D ** -0.5, 0.15625)
    step_weight = gaussian(splits[5], (D, HEADS), D ** -0.5, 0.15625, ((1, 4),))
    value_kernel = gaussian(splits[6], (KCONV, INNER), KCONV ** -0.5, 3.0, ((1, 4),), jnp.float32)
    value_offset = gaussian(splits[7], (INNER,), 0.3, 3.0, ((0, 4),), jnp.float32)
    state_kernel = gaussian(splits[8], (KCONV, 2 * NSTATE), KCONV ** -0.5, 3.0, (), jnp.float32)
    state_offset = gaussian(splits[9], (2 * NSTATE,), 0.3, 3.0, (), jnp.float32)
    step_bias = jnp.clip(-3.5 + 1.5 * jax.random.uniform(splits[10], (HEADS,), jnp.float32) ** levels(splits[10], (HEADS,), ((0, 4),), -0.2, 0.2), -3.5, -2.0)
    log_rate = draw_log_rate(jax.random.fold_in(splits[16], 71), 0)
    skip_gain = jnp.clip(0.5 + 1.5 * jax.random.uniform(splits[12], (HEADS,), jnp.float32) ** levels(splits[12], (HEADS,), ((0, 4),), -0.2, 0.2), 0.5, 2.0)
    mixer_gain = jnp.clip(1.0 + 0.15 * jax.random.normal(splits[13], (INNER,), jnp.float32), 0.25, 1.75)
    out_weight = gaussian(splits[14], (INNER, D), INNER ** -0.5, 0.109375, ((0, 4),))
    cotangent = gaussian(splits[15], (SEQS, LENGTH, D), 1.0, 6.0, ((1, 8),))
    return {"tokens": tokens, "norm_gain": norm_gain, "gate_weight": gate_weight, "value_weight": value_weight, "state_weight": state_weight, "step_weight": step_weight, "value_kernel": value_kernel, "value_offset": value_offset, "state_kernel": state_kernel, "state_offset": state_offset, "step_bias": step_bias, "log_rate": log_rate, "skip_gain": skip_gain, "mixer_gain": mixer_gain, "out_weight": out_weight, "cotangent": cotangent}


epsilon = 1e-05
highest_precision = lax.Precision.HIGHEST

@jax.custom_vjp
def low(v):
    return lax.optimization_barrier(v.astype(jnp.bfloat16)).astype(jnp.float32)

@jax.custom_vjp
def low_back(v):
    return v

def low_keep(v):
    return (low(v), None)

def low_pass(kept, grad):
    return (grad,)

def back_keep(v):
    return (v, None)

def back_low(kept, grad):
    return (low(grad),)
low.defvjp(low_keep, low_pass)
low_back.defvjp(back_keep, back_low)

def project(value_rows, weight_matrix):
    return jnp.einsum('wpi,ix->wpx', value_rows, weight_matrix, precision=highest_precision)

def causal_conv(value_rows, kernel, offset):
    taps = kernel.shape[0]
    length = value_rows.shape[1]
    padded = jnp.pad(value_rows, ((0, 0), (taps - 1, 0), (0, 0)))
    total = offset + kernel[0] * padded[:, 0:length]
    for tap in range(1, taps):
        total = total + kernel[tap] * padded[:, tap:tap + length]
    return total

def sequence_block(tokens, params):
    norm_gain, gate_weight, value_weight, state_weight, step_weight, value_kernel, value_offset, state_kernel, state_offset, step_bias, log_rate, skip_gain, mixer_gain, out_weight = params
    seqs, length, width = tokens.shape
    inv_rms = lax.rsqrt(lax.optimization_barrier(jnp.mean(tokens * tokens, axis=-1, keepdims=True)) + epsilon)
    normed = low(tokens * inv_rms * norm_gain)
    gate = low_back(project(normed, gate_weight))
    x_part = low_back(low(project(normed, value_weight)))
    bc_part = low_back(low(project(normed, state_weight)))
    step_raw = low_back(project(normed, step_weight))
    x_conv = causal_conv(x_part, value_kernel, value_offset)
    bc_conv = causal_conv(bc_part, state_kernel, state_offset)
    x_act = low(jax.nn.silu(x_conv))
    bc_act = low(jax.nn.silu(bc_conv))
    step = jax.nn.softplus(step_raw + step_bias)
    rate = -jnp.exp(log_rate)
    blocks = length // GROUP
    x_heads = jnp.moveaxis(x_act.reshape(seqs, blocks, GROUP, HEADS, HEAD_DIM), 1, 0)
    b_mat = jnp.moveaxis(bc_act[..., :NSTATE].reshape(seqs, blocks, GROUP, NSTATE), 1, 0)
    c_mat = jnp.moveaxis(bc_act[..., NSTATE:].reshape(seqs, blocks, GROUP, NSTATE), 1, 0)
    step_heads = jnp.moveaxis(jnp.transpose(step.reshape(seqs, blocks, GROUP, HEADS), (0, 1, 3, 2)), 1, 0)
    lower = jnp.arange(GROUP)[:, None] >= jnp.arange(GROUP)[None, :]

    def block_step(state, pieces):
        x_blk, b_blk, c_blk, step_block_rows = pieces
        cum = jnp.cumsum(step_block_rows * rate[:, None], axis=-1)
        decay = jnp.exp(jnp.where(lower, cum[..., :, None] - cum[..., None, :], -jnp.inf))
        cross = low_back(jnp.einsum('stn,sun->stu', c_blk, b_blk, precision=highest_precision))
        mix = low(cross[:, None] * decay * step_block_rows[..., None, :])
        within = jnp.einsum('shtu,suhp->sthp', mix, x_blk, precision=highest_precision)
        growth = jnp.exp(cum)
        c_scaled = low(c_blk[:, None] * growth[..., None])
        across = jnp.einsum('shtn,shpn->sthp', c_scaled, low(state), precision=highest_precision)
        ssd = low_back(within + across)
        last = cum[..., -1]
        weight_u = jnp.exp(last[..., None] - cum) * step_block_rows
        weighted = low(x_blk * jnp.transpose(weight_u, (0, 2, 1))[..., None])
        contrib = low_back(jnp.einsum('suhp,sun->shpn', weighted, b_blk, precision=highest_precision))
        state = jnp.exp(last)[..., None, None] * state + contrib
        return (state, ssd)
    begin = jnp.zeros((seqs, HEADS, HEAD_DIM, NSTATE), jnp.float32)
    ignored, ssd_blocks = lax.scan(jax.checkpoint(block_step), begin, (x_heads, b_mat, c_mat, step_heads))
    ssd = jnp.moveaxis(ssd_blocks, 0, 1).reshape(seqs, length, INNER)
    mixed = ssd + jnp.repeat(skip_gain, HEAD_DIM) * x_act
    gated = mixed * jax.nn.silu(gate)
    mixer_rms = lax.rsqrt(lax.optimization_barrier(jnp.mean(gated * gated, axis=-1, keepdims=True)) + epsilon)
    gnormed = low(gated * mixer_rms * mixer_gain)
    return tokens + project(gnormed, out_weight)

def forward(tokens, norm_gain, gate_weight, value_weight, state_weight, step_weight, value_kernel, value_offset, state_kernel, state_offset, step_bias, log_rate, skip_gain, mixer_gain, out_weight):
    params = (norm_gain, gate_weight, value_weight, state_weight, step_weight, value_kernel, value_offset, state_kernel, state_offset, step_bias, log_rate, skip_gain, mixer_gain, out_weight)

    def one_sequence(carry, sequence):
        return (carry, jax.checkpoint(sequence_block)(sequence[None], params)[0])
    ignored, outputs = lax.scan(one_sequence, jnp.zeros((), jnp.float32), tokens)
    return outputs

def reference(tokens, norm_gain, gate_weight, value_weight, state_weight, step_weight, value_kernel, value_offset, state_kernel, state_offset, step_bias, log_rate, skip_gain, mixer_gain, out_weight, cotangent):
    inputs = (tokens.astype(jnp.float32), norm_gain.astype(jnp.float32), gate_weight.astype(jnp.float32), value_weight.astype(jnp.float32), state_weight.astype(jnp.float32), step_weight.astype(jnp.float32), value_kernel.astype(jnp.float32), value_offset.astype(jnp.float32), state_kernel.astype(jnp.float32), state_offset.astype(jnp.float32), step_bias.astype(jnp.float32), log_rate.astype(jnp.float32), skip_gain.astype(jnp.float32), mixer_gain.astype(jnp.float32), out_weight.astype(jnp.float32))
    result, pullback = jax.vjp(forward, *inputs)
    grads = pullback(cotangent.astype(jnp.float32))
    return (result.astype(jnp.bfloat16), grads[0], grads[1], grads[2], grads[3], grads[4], grads[5], grads[6], grads[7], grads[8], grads[9], grads[10], grads[11], grads[12], grads[13], grads[14])
```

```python
import functools

import jax
import jax.numpy as jnp
from jax import lax
from jax.experimental import pallas as pl
from jax.experimental.pallas import tpu as pltpu
from jax.sharding import PartitionSpec as P

EPS = 1e-05
T = 128
HALO = 16
LANES = 128
F32 = jnp.float32
BF16 = jnp.bfloat16


def mm(a, b):
    return lax.dot_general(a, b, (((1,), (0,)), ((), ())), preferred_element_type=F32)


def mm_t(a, b):
    return lax.dot_general(a, b, (((1,), (1,)), ((), ())), preferred_element_type=F32)


def t_mm(a, b):
    return lax.dot_general(a, b, (((0,), (0,)), ((), ())), preferred_element_type=F32)


def split(v, parts):
    pieces = []
    for _ in range(parts):
        piece = v.astype(BF16)
        pieces.append(piece)
        v = v - piece.astype(F32)
    return pieces


def expand(v, wide):
    return mm(jnp.concatenate(split(v, 2), axis=1), wide)


def expand_row(v, wide):
    return expand(jnp.broadcast_to(v, (16, LANES)), wide)[0:1]


def head_sum(v, wide):
    hi, lo = split(v, 2)
    return mm_t(hi, wide[:LANES]) + mm_t(lo, wide[:LANES])


def exact_tri(tri, v):
    a, b, c = split(v, 3)
    return mm(tri, a) + (mm(tri, b) + mm(tri, c))


def sigmoid(v):
    return 0.5 * jnp.tanh(0.5 * v) + 0.5


def softplus(v):
    return jnp.maximum(v, 0.0) + jnp.log(1.0 + jnp.exp(-jnp.abs(v)))


def lower():
    row = lax.broadcasted_iota(jnp.int32, (T, T), 0)
    col = lax.broadcasted_iota(jnp.int32, (T, T), 1)
    return row >= col


def half_mask(rows):
    return lax.broadcasted_iota(jnp.int32, (rows, LANES), 1) < LANES // 2


def pair_rows(v):
    left = half_mask(v.shape[0])
    zero = jnp.zeros_like(v)
    return jnp.concatenate([jnp.where(left, v, zero), jnp.where(left, zero, v)], axis=0)


def rows_of(b):
    return pl.ds(pl.multiple_of(b * T, T), T)


def front(
    tok, halo, ngain, gate_w, value_w, state_w, step_w, vk, vo, sk, so, sbias, rate, wide, tri,
    normed_o, gate_o, xext_o, bcext_o, sraw_o, xact_o, bcact_o, step_o, cum_o, lstart_o, lstate_o, pre_o,
    nx, xe, be, st, run,
):
    length = tok.shape[1]
    blocks = length // T
    n = bcact_o.shape[2] // 2

    def norm(v):
        v = v.astype(F32)
        inv = lax.rsqrt(jnp.mean(v * v, axis=1, keepdims=True) + EPS)
        return (v * inv * ngain[...]).astype(BF16)

    nx[0:HALO] = norm(halo[0])

    def norm_rows(b, _):
        r = rows_of(b)
        v = norm(tok[0, r, :])
        nx[pl.ds(pl.multiple_of(HALO + b * T, HALO), T), :] = v
        normed_o[0, r, :] = v
        return 0

    lax.fori_loop(0, blocks, norm_rows, 0)
    x = mm(nx[...], value_w[...]).astype(BF16)
    xext_o[0] = x
    xe[...] = x.astype(F32)
    bc = mm(nx[...], state_w[...]).astype(BF16)
    bcext_o[0] = bc
    be[...] = bc.astype(F32)
    gate_o[0] = mm(nx[HALO:], gate_w[...])
    sraw_o[0] = mm(nx[HALO:], step_w[...])
    st[...] = jnp.zeros_like(st)
    run[...] = jnp.zeros_like(run)
    pre_o[0] = jnp.zeros_like(pre_o[0])
    for b in range(blocks):
        r0 = b * T
        r = slice(r0, r0 + T)
        taps = vk.shape[0]
        base = HALO - taps + 1
        xc = vo[...] + vk[0:1] * xe[r0 + base : r0 + base + T]
        bcc = so[...] + sk[0:1] * be[r0 + base : r0 + base + T]
        for k in range(1, taps):
            xc = xc + vk[k : k + 1] * xe[r0 + base + k : r0 + base + k + T]
            bcc = bcc + sk[k : k + 1] * be[r0 + base + k : r0 + base + k + T]
        xa = (xc * sigmoid(xc)).astype(BF16)
        bca = (bcc * sigmoid(bcc)).astype(BF16)
        xact_o[0, r, :] = xa
        bcact_o[0, r, :] = bca
        step = softplus(sraw_o[0, r, :] + sbias[...])
        cum = exact_tri(tri[...], step * rate[...])
        step_o[0, r, :] = step
        cum_o[0, r, :] = cum
        last = cum[T - 1 : T]
        weight = jnp.exp(last - cum) * step
        weighted = (xa.astype(F32) * expand(weight, wide[...])).astype(BF16)
        contrib = t_mm(bca[:, :n], weighted)
        lstart_o[0, b] = st[...].astype(BF16)
        st[...] = expand_row(jnp.exp(last), wide[...]) * st[...] + contrib
        run[0:1] = run[0:1] + last
        pre_o[0, b + 1 : b + 2] = run[0:1]
    lstate_o[0, 0:n] = st[...].astype(BF16)
    hi, mid, lo = split(expand_row(run[0:1], wide[...]), 3)
    at = lax.broadcasted_iota(jnp.int32, (HALO, hi.shape[1]), 0)
    hi, mid, lo = [jnp.broadcast_to(v.astype(F32), at.shape) for v in (hi, mid, lo)]
    tail = jnp.where(at == 0, hi, jnp.where(at == 1, mid, jnp.where(at == 2, lo, 0.0)))
    lstate_o[0, n : n + HALO] = tail.astype(BF16)


def scan_out(
    xact, bcact, step_i, cum_i, gate, lstart, entry, pre, cot, out_w, mgain, skip, wide,
    ssd_o, gn_o, y_o, sums_o,
    gm,
):
    length = xact.shape[1]
    blocks = length // T
    n = bcact.shape[2] // 2
    inner = xact.shape[2]
    gn_o[0] = mm_t(cot[0], out_w[...])

    def block(b, _):
        r = rows_of(b)
        xa = xact[0, r, :]
        bca = bcact[0, r, :]
        bm, cm = bca[:, :n], bca[:, n:]
        cum = cum_i[0, r, :]
        cum_t = cum.T
        cross = jnp.where(lower(), mm_t(cm, bm), 0.0)
        start = expand_row(jnp.exp(pre[0, pl.ds(b, 1), :]), wide[...]) * entry[0] + lstart[0, b].astype(F32)
        across = expand(jnp.exp(cum), wide[...]) * mm(cm, start.astype(BF16))
        xs = (xa.astype(F32) * expand(step_i[0, r, :], wide[...])).astype(BF16)
        for p in range(inner // LANES):
            mix = []
            for h in (2 * p, 2 * p + 1):
                decay = jnp.exp(jnp.minimum(cum[:, h : h + 1] - cum_t[h : h + 1, :], 0.0))
                mix.append((cross * decay).astype(BF16))
            lanes = slice(p * LANES, (p + 1) * LANES)
            within = mm(jnp.concatenate(mix, axis=1), pair_rows(xs[:, lanes]))
            ssd_o[0, r, lanes] = within + across[:, lanes]
        mixed = ssd_o[0, r, :] + skip[...] * xa.astype(F32)
        g = gate[0, r, :]
        gated = mixed * (g * sigmoid(g))
        gg = gated * mgain[...]
        gm[r, :] = gg.astype(BF16)
        squares = jnp.sum(gated * gated, axis=1, keepdims=True)
        dots = jnp.sum(gg * gn_o[0, r, :], axis=1, keepdims=True)
        lane = lax.broadcasted_iota(jnp.int32, (T, LANES), 1)
        both = jnp.where(lane == 0, squares, jnp.where(lane == 1, dots, 0.0))
        sums_o[0, :, r] = both.T[0:8]
        return 0

    lax.fori_loop(0, blocks, block, 0)
    y_o[0] = mm(gm[...], out_w[...]).astype(BF16)


def back_one(
    xact, bcact, step_i, cum_i, gate, ssd, gn, sums, lstart, entry, pre, mgain, skip, wide,
    gnormed_o, gate_grad_o, xg_o, cumg_o, stepg_o, bcg_o, lend_o, lgrad_o, mgg_o, skg_o,
    z, acc,
    *, inner_all,
):
    length = xact.shape[1]
    blocks = length // T
    n = bcact.shape[2] // 2
    inner = xact.shape[2]

    @pl.when(pl.program_id(0) == 0)
    def _():
        mgg_o[...] = jnp.zeros_like(mgg_o)
        skg_o[...] = jnp.zeros_like(skg_o)

    acc[...] = jnp.zeros_like(acc)

    def block(i, _):
        b = blocks - 1 - i
        r = rows_of(b)
        low_x = xact[0, r, :]
        xa = low_x.astype(F32)
        bca = bcact[0, r, :]
        bm, cm = bca[:, :n], bca[:, n:]
        cum = cum_i[0, r, :]
        cum_t = cum.T
        sums_b = sums[0, :, r]
        columns = jnp.concatenate([sums_b, jnp.zeros((LANES - 8, T), F32)], axis=0).T
        rms = lax.rsqrt(columns[:, 0:1] / inner_all + EPS)
        coef = rms * rms * rms * (columns[:, 1:2] / inner_all)
        ssd_b = ssd[0, r, :]
        mixed = ssd_b + skip[...] * xa
        g = gate[0, r, :]
        sg = sigmoid(g)
        gated = mixed * (g * sg)
        grad_norm = gn[0, r, :]
        normalised = gated * rms
        gnormed_o[0, r, :] = (normalised * mgain[...]).astype(BF16)
        mgg_o[0:1] += jnp.sum(grad_norm * normalised, axis=0, keepdims=True)
        grad_gated = rms * (grad_norm * mgain[...]) - gated * coef
        gate_grad_o[0, r, :] = (grad_gated * mixed * (sg * (1.0 + g * (1.0 - sg)))).astype(BF16)
        grad_mixed = grad_gated * (g * sg)
        skg_o[0:1] += jnp.sum(grad_mixed * xa, axis=0, keepdims=True)
        dy = grad_mixed.astype(BF16)
        start = expand_row(jnp.exp(pre[0, pl.ds(b, 1), :]), wide[...]) * entry[0] + lstart[0, b].astype(F32)
        gdy = (expand(jnp.exp(cum), wide[...]) * dy.astype(F32)).astype(BF16)
        c_grad = mm_t(gdy, start.astype(BF16))
        lend_o[0, b] = acc[...].astype(BF16)
        acc[...] = expand_row(jnp.exp(cum[T - 1 : T]), wide[...]) * acc[...] + t_mm(cm, gdy)
        step_wide = expand(step_i[0, r, :], wide[...])
        xs = (xa * step_wide).astype(BF16)
        cross = jnp.where(lower(), mm_t(cm, bm), 0.0)
        cross_part = jnp.zeros((T, T), F32)
        for p in range(inner // LANES):
            lanes = slice(p * LANES, (p + 1) * LANES)
            dy_two = pair_rows(dy[:, lanes])
            mix_grad = mm_t(dy_two, xs[:, lanes])
            mix = []
            for j in (0, 1):
                h = 2 * p + j
                decay = jnp.exp(jnp.minimum(cum[:, h : h + 1] - cum_t[h : h + 1, :], 0.0))
                mix.append((cross * decay).astype(BF16))
                cross_part = cross_part + mix_grad[j * T : (j + 1) * T] * decay
            z[:, lanes] = t_mm(jnp.concatenate(mix, axis=0), dy_two)
        cross_low = jnp.where(lower(), cross_part, 0.0).astype(BF16)
        bcg_o[0, r, 0:n] = t_mm(cross_low, cm)
        bcg_o[0, r, n : 2 * n] = c_grad + mm(cross_low, bm)
        zz = z[...]
        xg_o[0, r, :] = step_wide * zz + skip[...] * grad_mixed
        cumg_o[0, r, :] = head_sum(dy.astype(F32) * ssd_b - xs.astype(F32) * zz, wide[...])
        stepg_o[0, r, :] = head_sum(xa * zz, wide[...])
        return 0

    lax.fori_loop(0, blocks, block, 0)
    lgrad_o[0] = acc[...].astype(BF16)


def back_two(
    xact, bcact, xext, bcext, step_i, cum_i, sraw, xg, cumg, stepg, bcg, lstart, entry, lend, after, pre,
    vk, vo, sk, so, sbias, rate, wide, tri,
    xpg_o, xhalo_o, bpg_o, bhalo_o, raw_o, vkg_o, skg_o, heads_o,
    xe, be, xcg, bcg_s,
):
    length = xact.shape[1]
    blocks = length // T
    n = bcact.shape[2] // 2
    taps = vk.shape[0]
    base = HALO - taps + 1

    @pl.when(pl.program_id(0) == 0)
    def _():
        vkg_o[...] = jnp.zeros_like(vkg_o)
        skg_o[...] = jnp.zeros_like(skg_o)
        heads_o[...] = jnp.zeros_like(heads_o)

    xe[...] = xext[0].astype(F32)
    be[...] = bcext[0].astype(F32)
    for ref in (xcg, bcg_s):
        ref[0:HALO] = jnp.zeros((HALO, ref.shape[1]), F32)
        ref[HALO + length :] = jnp.zeros((HALO, ref.shape[1]), F32)

    def conv_rows(ext, kernel, offset, r0):
        total = offset[...] + kernel[0:1] * ext[r0 + base : r0 + base + T]
        for k in range(1, taps):
            total = total + kernel[k : k + 1] * ext[r0 + base + k : r0 + base + k + T]
        sg = sigmoid(total)
        return sg * (1.0 + total * (1.0 - sg))

    def filter_grad(grad, ext, out, r0):
        for k in range(taps):
            out[k : k + 1] += jnp.sum(grad * ext[r0 + base + k : r0 + base + k + T], axis=0, keepdims=True)
        out[taps : taps + 1] += jnp.sum(grad, axis=0, keepdims=True)

    for b in range(blocks):
        r0 = b * T
        r = slice(r0, r0 + T)
        xa = xact[0, r, :].astype(F32)
        bm = bcact[0, r, 0:n]
        cum = cum_i[0, r, :]
        step = step_i[0, r, :]
        last = cum[T - 1 : T]
        start = expand_row(jnp.exp(pre[0, b : b + 1]), wide[...]) * entry[0] + lstart[0, b].astype(F32)
        suffix = jnp.exp(pre[0, blocks : blocks + 1] - pre[0, b + 1 : b + 2])
        end = expand_row(suffix, wide[...]) * after[0] + lend[0, b].astype(F32)
        end_low = end.astype(BF16)
        weighted_grad = mm(bm, end_low)
        reach = jnp.exp(last - cum)
        weight = reach * step
        weight_wide = expand(weight, wide[...])
        weighted = (xa * weight_wide).astype(BF16)
        bcg_b = bcg[0, r, :]
        b_total = bcg_b[:, 0:n] + mm_t(weighted, end_low)
        bc_total = jnp.concatenate([b_total, bcg_b[:, n:]], axis=1)
        w_grad = head_sum(weighted_grad * xa, wide[...])
        part = w_grad * weight
        product = jnp.broadcast_to(jnp.sum(end * start, axis=0, keepdims=True), (16, end.shape[1]))
        fade_grad = jnp.exp(last) * head_sum(product, wide[...])[0:1]
        at_last = lax.broadcasted_iota(jnp.int32, (T, LANES), 0) == T - 1
        extra = fade_grad + jnp.sum(part, axis=0, keepdims=True)
        cum_grad = cumg[0, r, :] - part + jnp.where(at_last, extra, 0.0)
        a, bb, c = split(cum_grad, 3)
        rise = t_mm(tri[...], a) + (t_mm(tri[...], bb) + t_mm(tri[...], c))
        step_grad = stepg[0, r, :] + w_grad * reach + rise * rate[...]
        raw = step_grad * sigmoid(sraw[0, r, :] + sbias[...])
        raw_o[0, r, :] = raw.astype(BF16)
        heads_o[0:1] += jnp.sum(raw, axis=0, keepdims=True)
        heads_o[1:2] += jnp.sum(rise * step, axis=0, keepdims=True)
        grad = (xg[0, r, :] + weighted_grad * weight_wide) * conv_rows(xe, vk, vo, r0)
        filter_grad(grad, xe, vkg_o, r0)
        xcg[HALO + r0 : HALO + r0 + T] = grad
        grad = bc_total * conv_rows(be, sk, so, r0)
        filter_grad(grad, be, skg_o, r0)
        bcg_s[HALO + r0 : HALO + r0 + T] = grad

    def conv_back(ref, kernel, r0, rows):
        total = kernel[0:1] * ref[r0 + taps - 1 : r0 + taps - 1 + rows]
        for k in range(1, taps):
            total = total + kernel[k : k + 1] * ref[r0 + taps - 1 - k : r0 + taps - 1 - k + rows]
        return total.astype(BF16)

    xhalo_o[0] = conv_back(xcg, vk, 0, HALO)
    bhalo_o[0] = conv_back(bcg_s, sk, 0, HALO)
    for b in range(blocks):
        r0 = b * T
        xpg_o[0, r0 : r0 + T] = conv_back(xcg, vk, HALO + r0, T)
        bpg_o[0, r0 : r0 + T] = conv_back(bcg_s, sk, HALO + r0, T)


def per_seq(shape):
    rest = shape[1:]
    return pl.BlockSpec((1,) + tuple(rest), lambda s: (s,) + (0,) * len(rest))


def whole(shape):
    return pl.BlockSpec(tuple(shape), lambda s: (0,) * len(shape))


def call(body, seqs, ins, outs, scratch, flops):
    in_specs = [per_seq(a.shape) if a.ndim >= 3 else whole(a.shape) for a in ins]
    out_specs = [per_seq(s) if cut else whole(s) for s, _, cut in outs]
    moved = sum(a.size * a.dtype.itemsize for a in ins)
    for s, d, _ in outs:
        size = jnp.dtype(d).itemsize
        for k in s:
            size *= k
        moved += size
    return pl.pallas_call(
        body,
        grid=(seqs,),
        in_specs=in_specs,
        out_specs=out_specs,
        out_shape=[jax.ShapeDtypeStruct(s, d) for s, d, _ in outs],
        scratch_shapes=scratch,
        compiler_params=pltpu.CompilerParams(
            dimension_semantics=("arbitrary",), vmem_limit_bytes=56 * 1024 * 1024
        ),
        cost_estimate=pl.CostEstimate(flops=flops, bytes_accessed=moved, transcendentals=0),
    )(*ins)


def shards(
    tokens, norm_gain, gate_weight, value_weight, state_weight, step_weight, value_kernel, value_offset,
    state_kernel, state_offset, step_bias, log_rate, skip_gain, mixer_gain, out_weight, cotangent,
):
    seqs, length, width = tokens.shape
    flat = seqs * length
    inner = gate_weight.shape[1]
    heads = step_weight.shape[1]
    head_size = inner // heads
    n2 = state_weight.shape[1]
    n = n2 // 2
    taps = value_kernel.shape[0]
    blocks = length // T
    devices, me = lax.axis_size("seq"), lax.axis_index("seq")
    inner_all = inner * lax.axis_size("head")

    halo = lax.ppermute(tokens[:, length - HALO :], "seq", [(i, i + 1) for i in range(devices - 1)])
    pad = LANES - heads
    rate_row = -jnp.exp(log_rate)
    rate = jnp.pad(rate_row, (0, pad))[None]
    bias = jnp.pad(step_bias, (0, pad))[None]
    step_w = jnp.pad(step_weight, ((0, 0), (0, pad)))
    skip = jnp.repeat(skip_gain, head_size)[None]
    gain = mixer_gain[None]
    one = (jnp.arange(inner)[None, :] // head_size == jnp.arange(LANES)[:, None]).astype(BF16)
    wide = jnp.concatenate([one, one], axis=0)
    tri = (jnp.arange(T)[:, None] >= jnp.arange(T)[None, :]).astype(BF16)
    vo, so = value_offset[None], state_offset[None]

    def big(cols, dtype, rows=length):
        return ((seqs, rows, cols), dtype, True)

    vmem = pltpu.VMEM
    ext = length + HALO
    (normed, gate, xext, bcext, sraw, xact, bcact, step, cum, lstart, lstate, pre) = call(
        front, seqs,
        [tokens, halo, norm_gain[None], gate_weight, value_weight, state_weight, step_w,
         value_kernel, vo, state_kernel, so, bias, rate, wide, tri],
        [big(width, BF16), big(inner, F32), big(inner, BF16, ext), big(n2, BF16, ext), big(LANES, F32),
         big(inner, BF16), big(n2, BF16), big(LANES, F32), big(LANES, F32),
         ((seqs, blocks, n, inner), BF16, True), big(inner, BF16, n + HALO), big(LANES, F32, 8)],
        [vmem((ext, width), BF16), vmem((ext, inner), F32), vmem((ext, n2), F32), vmem((n, inner), F32),
         vmem((8, LANES), F32)],
        2 * flat * width * (2 * inner + n2 + LANES),
    )
    states = lax.all_gather(lstate, "seq")
    log_fade = jnp.sum(states[:, :, n : n + 3].astype(F32), axis=2)
    index = jnp.arange(devices)
    prefix = jnp.cumsum(log_fade, axis=0)
    zero = jnp.zeros_like(prefix[:1])
    before = jnp.concatenate([zero, prefix[:-1]], axis=0)
    my_before = lax.dynamic_index_in_dim(before, me, 0)
    my_prefix = lax.dynamic_index_in_dim(prefix, me, 0)
    earlier = (index < me)[:, None, None]
    later = (index > me)[:, None, None]
    from_left = jnp.where(earlier, jnp.exp(jnp.where(earlier, my_before - prefix, 0.0)), 0.0)
    from_right = jnp.where(later, jnp.exp(jnp.where(later, before - my_prefix, 0.0)), 0.0)
    entry = jnp.sum(from_left[:, :, None] * states[:, :, :n].astype(F32), axis=0)

    ssd, gn, y, sums = call(
        scan_out, seqs,
        [xact, bcact, step, cum, gate, lstart, entry, pre, cotangent, out_weight, gain, skip, wide],
        [big(inner, F32), big(inner, F32), big(width, BF16), ((seqs, 8, length), F32, True)],
        [vmem((length, inner), BF16)],
        4 * flat * width * inner,
    )
    y = lax.psum(y, "head")
    sums = lax.psum(sums, "head")
    gnormed, gate_grad, xg, cumg, stepg, bcg, lend, lgrad, mgg, skg = call(
        functools.partial(back_one, inner_all=inner_all), seqs,
        [xact, bcact, step, cum, gate, ssd, gn, sums, lstart, entry, pre, gain, skip, wide],
        [big(inner, BF16), big(inner, BF16), big(inner, F32), big(LANES, F32), big(LANES, F32), big(n2, F32),
         ((seqs, blocks, n, inner), BF16, True), big(inner, BF16, n),
         ((8, inner), F32, False), ((8, inner), F32, False)],
        [vmem((T, inner), F32), vmem((n, inner), F32)],
        2 * flat * T * inner * 8,
    )
    grads = lax.all_gather(lgrad, "seq")
    after = jnp.sum(from_right[:, :, None] * grads.astype(F32), axis=0)
    xpg, xhalo, bpg, bhalo, raw, vkg, skgr, head_rows = call(
        back_two, seqs,
        [xact, bcact, xext, bcext, step, cum, sraw, xg, cumg, stepg, bcg, lstart, entry, lend, after, pre,
         value_kernel, vo, state_kernel, so, bias, rate, wide, tri],
        [big(inner, BF16), big(inner, BF16, HALO), big(n2, BF16), big(n2, BF16, HALO), big(LANES, BF16),
         ((8, inner), F32, False), ((8, n2), F32, False), ((8, LANES), F32, False)],
        [vmem((ext, inner), F32), vmem((ext, n2), F32), vmem((ext + HALO, inner), F32),
         vmem((ext + HALO, n2), F32)],
        2 * flat * T * inner * 4,
    )
    back = [(i + 1, i) for i in range(devices - 1)]
    xhalo, bhalo = lax.ppermute((xhalo, bhalo), "seq", back)
    xpg = xpg.at[:, length - HALO :].add(xhalo)
    bpg = bpg.at[:, length - HALO :].add(bhalo)

    def flatten(v):
        return v.reshape(flat, v.shape[-1])

    normed_f, xpg_f, bpg_f, raw_f, gg_f = [flatten(v) for v in (normed, xpg, bpg, raw, gate_grad)]
    out_weight_grad = t_mm(flatten(gnormed), flatten(cotangent)).astype(BF16)
    gate_weight_grad = t_mm(normed_f, gg_f).astype(BF16)
    value_weight_grad = t_mm(normed_f, xpg_f).astype(BF16)
    state_weight_grad = t_mm(normed_f, bpg_f).astype(BF16)
    step_weight_grad = t_mm(normed_f, raw_f)[:, :heads].astype(BF16)
    normed_grad = (
        mm_t(gg_f, gate_weight) + mm_t(xpg_f, value_weight) + mm_t(bpg_f, state_weight) + mm_t(raw_f, step_w)
    ).astype(BF16)
    normed_grad = lax.psum(normed_grad, "head").astype(F32).reshape(seqs, length, width)

    resid = tokens.astype(F32)
    inv_rms = lax.rsqrt(jnp.mean(resid * resid, axis=-1, keepdims=True) + EPS)
    mixer_rms = lax.rsqrt(sums[:, 0] / inner_all + EPS)[..., None]
    result = (resid + y.astype(F32) * mixer_rms).astype(BF16)
    norm_gain_grad = jnp.sum(normed_grad * resid * inv_rms, axis=(0, 1))
    scaled_in = normed_grad * norm_gain
    tokens_grad = (
        cotangent.astype(F32)
        + inv_rms * scaled_in
        - resid * inv_rms**3 * (jnp.sum(scaled_in * resid, axis=-1, keepdims=True) / width)
    )
    skip_gain_grad = jnp.sum(skg[0].reshape(heads, head_size), axis=1)
    step_bias_grad = head_rows[0, :heads]
    log_rate_grad = head_rows[1, :heads] * rate_row
    own = lax.psum(
        (norm_gain_grad, vkg[: taps + 1], step_bias_grad, log_rate_grad, skip_gain_grad, mgg[0]), "seq"
    )
    norm_gain_grad, vkg, step_bias_grad, log_rate_grad, skip_gain_grad, mixer_gain_grad = own
    skgr = lax.psum(skgr[: taps + 1], ("seq", "head"))
    weights = lax.psum((gate_weight_grad, value_weight_grad, step_weight_grad, out_weight_grad), "seq")
    gate_weight_grad, value_weight_grad, step_weight_grad, out_weight_grad = [v.astype(F32) for v in weights]
    state_weight_grad = lax.psum(state_weight_grad, ("seq", "head")).astype(F32)
    return (
        result, tokens_grad, norm_gain_grad, gate_weight_grad, value_weight_grad, state_weight_grad,
        step_weight_grad, vkg[:taps], vkg[taps], skgr[:taps], skgr[taps], step_bias_grad, log_rate_grad,
        skip_gain_grad, mixer_gain_grad, out_weight_grad,
    )


def solution(mesh):
    rows, cols, vec = P(None, "seq", None), P(None, "head"), P("head")
    in_specs = (rows, P(), cols, cols, P(), cols, cols, vec, P(), P(), vec, vec, vec, vec, P("head", None), rows)
    out_specs = (rows, rows, P(), cols, cols, P(), cols, cols, vec, P(), P(), vec, vec, vec, vec, P("head", None))
    return jax.shard_map(shards, mesh=mesh, in_specs=in_specs, out_specs=out_specs, check_vma=False)
```

```python
import functools

import jax
import jax.numpy as jnp
from jax import lax
from jax.experimental import pallas as pl
from jax.experimental.pallas import tpu as pltpu
from jax.sharding import PartitionSpec as P

EPS = 1e-05
T = 256
SUB = 128
HALO = 16
LANES = 128
F32 = jnp.float32
BF16 = jnp.bfloat16


def mm(a, b):
    return lax.dot_general(a, b, (((1,), (0,)), ((), ())), preferred_element_type=F32)


def mm_t(a, b):
    return lax.dot_general(a, b, (((1,), (1,)), ((), ())), preferred_element_type=F32)


def t_mm(a, b):
    return lax.dot_general(a, b, (((0,), (0,)), ((), ())), preferred_element_type=F32)


def split(v, parts):
    pieces = []
    for _ in range(parts):
        piece = v.astype(BF16)
        pieces.append(piece)
        v = v - piece.astype(F32)
    return pieces


def expand(v, wide):
    return mm(jnp.concatenate(split(v, 2), axis=1), wide)


def expand_row(v, wide):
    return expand(jnp.broadcast_to(v, (16, LANES)), wide)[0:1]


def head_sum(v, wide):
    hi, lo = split(v, 2)
    return mm_t(hi, wide[:LANES]) + mm_t(lo, wide[:LANES])


def exact_tri(tri, v):
    a, b, c = split(v, 3)
    return mm(tri, a) + (mm(tri, b) + mm(tri, c))


def sigmoid(v):
    return 0.5 * jnp.tanh(0.5 * v) + 0.5


def softplus(v):
    return jnp.maximum(v, 0.0) + jnp.log1p(jnp.exp(-jnp.abs(v)))


def lower():
    row = lax.broadcasted_iota(jnp.int32, (SUB, SUB), 0)
    col = lax.broadcasted_iota(jnp.int32, (SUB, SUB), 1)
    return row >= col


def tile(i):
    return slice(i * SUB, (i + 1) * SUB)


def tiles():
    return [(i, j) for i in range(T // SUB) for j in range(i + 1)]


def cross_tiles(cm, bm):
    found = {}
    for i, j in tiles():
        value = mm_t(cm[tile(i)], bm[tile(j)])
        found[i, j] = jnp.where(lower(), value, 0.0) if i == j else value
    return found


def decay_tile(cum, cum_t, h, i, j):
    gap = cum[tile(i), h : h + 1] - cum_t[h : h + 1, tile(j)]
    return jnp.exp(jnp.minimum(gap, 0.0) if i == j else gap)


def half_mask(rows):
    return lax.broadcasted_iota(jnp.int32, (rows, LANES), 1) < LANES // 2


def pair_rows(v):
    left = half_mask(v.shape[0])
    zero = jnp.zeros_like(v)
    return jnp.concatenate([jnp.where(left, v, zero), jnp.where(left, zero, v)], axis=0)


def rows_of(b):
    return pl.ds(pl.multiple_of(b * T, T), T)


MESH = pl.DeviceIdType.MESH


class Exchange:
    def __init__(self, rounds, backward, total, before, logs, out, back, send, recv):
        self.rounds, self.backward = rounds, backward
        self.total, self.before, self.logs = total, before, logs
        self.out, self.back, self.send, self.recv = out, back, send, recv
        self.me = lax.axis_index("seq")

    def partner(self, r):
        bit = 1 << r
        return self.me + bit - 2 * bit * (lax.div(self.me, bit) % 2)

    def greet(self):
        barrier = pltpu.get_barrier_semaphore()
        for r in range(self.rounds):
            pl.semaphore_signal(barrier, inc=1, device_id={"seq": self.partner(r)}, device_id_type=MESH)
        pl.semaphore_wait(barrier, self.rounds)

    def copy(self, r, s):
        return pltpu.make_async_remote_copy(
            src_ref=self.out.at[r, s], dst_ref=self.back.at[r, s],
            send_sem=self.send.at[r, s], recv_sem=self.recv.at[r, s],
            device_id={"seq": self.partner(r)}, device_id_type=MESH,
        )

    def begin(self, s, state, log):
        self.total[s] = state
        self.before[s] = jnp.zeros_like(state)
        self.logs[s] = jnp.zeros(self.logs.shape[1:], F32)
        self.logs[s, 0:1] = log

    def push(self, r, s):
        n = self.total.shape[1]
        self.out[r, s, 0:n] = self.total[s].astype(BF16)
        hi, mid, lo = [v.astype(F32) for v in split(self.logs[s, 0:1], 3)]
        at = lax.broadcasted_iota(jnp.int32, (HALO, hi.shape[1]), 0)
        tail = jnp.where(at == 0, hi, jnp.where(at == 1, mid, jnp.where(at == 2, lo, 0.0)))
        self.out[r, s, n : n + HALO] = tail.astype(BF16)
        self.copy(r, s).start()

    def take(self, r, s):
        n = self.total.shape[1]
        copy = self.copy(r, s)
        copy.wait_recv()
        copy.wait_send()
        state = self.back[r, s, 0:n].astype(F32)
        tail = self.back[r, s, n : n + HALO].astype(F32)
        log = tail[0:1] + tail[1:2] + tail[2:3]
        upper = lax.div(self.me, 1 << r) % 2 == 1
        near = jnp.logical_not(upper) if self.backward else upper
        mine, theirs = self.logs[s, 0:1], self.logs[s, 1:2]
        self.before[s] = self.before[s] + jnp.where(near, jnp.exp(theirs), 0.0) * state
        self.logs[s, 1:2] = theirs + jnp.where(near, log, 0.0)
        own = jnp.where(near, 1.0, jnp.exp(log))
        other = jnp.where(near, jnp.exp(mine), 1.0)
        self.total[s] = own * self.total[s] + other * state
        self.logs[s, 0:1] = mine + log

    def advance(self, i, seqs):
        @pl.when(i < seqs)
        def _():
            self.push(0, i)

        for r in range(self.rounds):
            s = i - 1 - r

            @pl.when((s >= 0) & (s < seqs))
            def _():
                self.take(r, s)
                if r + 1 < self.rounds:
                    self.push(r + 1, s)

    @staticmethod
    def scratch(rounds, seqs, n, inner):
        return [
            pltpu.VMEM((seqs, n, inner), F32), pltpu.VMEM((seqs, n, inner), F32), pltpu.VMEM((seqs, 8, inner), F32),
            pltpu.VMEM((rounds, seqs, n + HALO, inner), BF16), pltpu.VMEM((rounds, seqs, n + HALO, inner), BF16),
            pltpu.SemaphoreType.DMA((rounds, seqs)), pltpu.SemaphoreType.DMA((rounds, seqs)),
        ]


def front(
    tok, halo, ngain, gate_w, value_w, state_w, step_w, vk, vo, sk, so, sbias, rate, wide, tri,
    normed_o, gate_o, xext_o, bcext_o, sraw_o, xact_o, bcact_o, step_o, cum_o, lstart_o, pre_o, entry_o,
    nx, xe, be, st, run, total, before, logs, out, back, send, recv,
    *, seqs, rounds,
):
    i = pl.program_id(0)
    scan = Exchange(rounds, False, total, before, logs, out, back, send, recv)

    @pl.when(i == 0)
    def _():
        scan.greet()

    @pl.when(i < seqs)
    def _():
        front_rows(
            tok, halo, ngain, gate_w, value_w, state_w, step_w, vk, vo, sk, so, sbias, rate, wide, tri,
            normed_o, gate_o, xext_o, bcext_o, sraw_o, xact_o, bcact_o, step_o, cum_o, lstart_o, pre_o,
            nx, xe, be, st, run,
        )
        scan.begin(i, st[...], expand_row(run[0:1], wide[...]))

    scan.advance(i, seqs)

    @pl.when(i == seqs + rounds - 1)
    def _():
        entry_o[...] = before[...]


def front_rows(
    tok, halo, ngain, gate_w, value_w, state_w, step_w, vk, vo, sk, so, sbias, rate, wide, tri,
    normed_o, gate_o, xext_o, bcext_o, sraw_o, xact_o, bcact_o, step_o, cum_o, lstart_o, pre_o,
    nx, xe, be, st, run,
):
    length = tok.shape[1]
    blocks = length // T
    n = bcact_o.shape[2] // 2

    def norm(v):
        v = v.astype(F32)
        inv = lax.rsqrt(jnp.mean(v * v, axis=1, keepdims=True) + EPS)
        return (v * inv * ngain[...]).astype(BF16)

    nx[0:HALO] = norm(halo[0])

    def norm_rows(b, _):
        r = rows_of(b)
        v = norm(tok[0, r, :])
        nx[pl.ds(pl.multiple_of(HALO + b * T, HALO), T), :] = v
        normed_o[0, r, :] = v
        return 0

    lax.fori_loop(0, blocks, norm_rows, 0)
    x = mm(nx[...], value_w[...]).astype(BF16)
    xext_o[0] = x
    xe[...] = x.astype(F32)
    bc = mm(nx[...], state_w[...]).astype(BF16)
    bcext_o[0] = bc
    be[...] = bc.astype(F32)
    gate_o[0] = mm(nx[HALO:], gate_w[...])
    sraw_o[0] = mm(nx[HALO:], step_w[...])
    st[...] = jnp.zeros_like(st)
    run[...] = jnp.zeros_like(run)
    pre_o[0] = jnp.zeros_like(pre_o[0])
    for b in range(blocks):
        r0 = b * T
        r = slice(r0, r0 + T)
        taps = vk.shape[0]
        base = HALO - taps + 1
        xc = vo[...] + vk[0:1] * xe[r0 + base : r0 + base + T]
        bcc = so[...] + sk[0:1] * be[r0 + base : r0 + base + T]
        for k in range(1, taps):
            xc = xc + vk[k : k + 1] * xe[r0 + base + k : r0 + base + k + T]
            bcc = bcc + sk[k : k + 1] * be[r0 + base + k : r0 + base + k + T]
        xa = (xc * sigmoid(xc)).astype(BF16)
        bca = (bcc * sigmoid(bcc)).astype(BF16)
        xact_o[0, r, :] = xa
        bcact_o[0, r, :] = bca
        step = softplus(sraw_o[0, r, :] + sbias[...])
        cum = exact_tri(tri[...], step * rate[...])
        step_o[0, r, :] = step
        cum_o[0, r, :] = cum
        last = cum[T - 1 : T]
        weight = jnp.exp(last - cum) * step
        weighted = (xa.astype(F32) * expand(weight, wide[...])).astype(BF16)
        contrib = t_mm(bca[:, :n], weighted)
        lstart_o[0, b] = st[...]
        st[...] = expand_row(jnp.exp(last), wide[...]) * st[...] + contrib
        run[0:1] = run[0:1] + last
        pre_o[0, b + 1 : b + 2] = run[0:1]


def scan_out(
    xact, bcact, step_i, cum_i, gate, lstart, entry, pre, cot, out_w, mgain, skip, wide,
    ssd_o, gn_o, y_o, sums_o,
    gm,
):
    length = xact.shape[1]
    blocks = length // T
    n = bcact.shape[2] // 2
    inner = xact.shape[2]
    gn_o[0] = mm_t(cot[0], out_w[...])

    def block(b, _):
        r = rows_of(b)
        xa = xact[0, r, :]
        bca = bcact[0, r, :]
        bm, cm = bca[:, :n], bca[:, n:]
        cum = cum_i[0, r, :]
        cum_t = cum.T
        cross = cross_tiles(cm, bm)
        start = expand_row(jnp.exp(pre[0, pl.ds(b, 1), :]), wide[...]) * entry[0] + lstart[0, b]
        start = start.astype(BF16)
        grown = jnp.exp(cum)
        cm = cm.astype(F32)
        xs = (xa.astype(F32) * expand(step_i[0, r, :], wide[...])).astype(BF16)
        for p in range(inner // LANES):
            lanes = slice(p * LANES, (p + 1) * LANES)
            two = (2 * p, 2 * p + 1)
            start_two = pair_rows(start[:, lanes])
            xs_two = [pair_rows(xs[tile(j), lanes]) for j in range(T // SUB)]
            for i in range(T // SUB):
                left = [(cm[tile(i)] * grown[tile(i), h : h + 1]).astype(BF16) for h in two]
                right = [start_two]
                for j in range(i + 1):
                    left += [(cross[i, j] * decay_tile(cum, cum_t, h, i, j)).astype(BF16) for h in two]
                    right.append(xs_two[j])
                rows = pl.ds(pl.multiple_of(b * T + i * SUB, SUB), SUB)
                ssd_o[0, rows, lanes] = mm(jnp.concatenate(left, axis=1), jnp.concatenate(right, axis=0))
        mixed = ssd_o[0, r, :] + skip[...] * xa.astype(F32)
        g = gate[0, r, :]
        gated = mixed * (g * sigmoid(g))
        gg = gated * mgain[...]
        gm[r, :] = gg.astype(BF16)
        squares = jnp.sum(gated * gated, axis=1, keepdims=True)
        dots = jnp.sum(gg * gn_o[0, r, :], axis=1, keepdims=True)
        lane = lax.broadcasted_iota(jnp.int32, (T, LANES), 1)
        both = jnp.where(lane == 0, squares, jnp.where(lane == 1, dots, 0.0))
        sums_o[0, :, r] = both.T[0:8]
        return 0

    lax.fori_loop(0, blocks, block, 0)
    y_o[0] = mm(gm[...], out_w[...]).astype(BF16)


def back_one(
    xact, bcact, step_i, cum_i, gate, ssd, gn, sums, lstart, entry, pre, mgain, skip, wide,
    gnormed_o, gate_grad_o, xg_o, cumg_o, stepg_o, bcg_o, lend_o, rms_o, mgg_o, skg_o, after_o,
    z, acc, dys, use, total, before, logs, out, back, send, recv,
    *, inner_all, seqs, rounds,
):
    i = pl.program_id(0)
    scan = Exchange(rounds, True, total, before, logs, out, back, send, recv)

    @pl.when(i == 0)
    def _():
        scan.greet()
        mgg_o[...] = jnp.zeros_like(mgg_o)
        skg_o[...] = jnp.zeros_like(skg_o)

    @pl.when(i < seqs)
    def _():
        back_one_rows(
            xact, bcact, step_i, cum_i, gate, ssd, gn, sums, lstart, entry, pre, mgain, skip, wide,
            gnormed_o, gate_grad_o, xg_o, cumg_o, stepg_o, bcg_o, lend_o, rms_o, mgg_o, skg_o,
            z, acc, dys, use, inner_all,
        )
        blocks = xact.shape[1] // T
        scan.begin(i, acc[...], expand_row(pre[0, blocks : blocks + 1], wide[...]))

    scan.advance(i, seqs)

    @pl.when(i == seqs + rounds - 1)
    def _():
        after_o[...] = before[...]


def back_one_rows(
    xact, bcact, step_i, cum_i, gate, ssd, gn, sums, lstart, entry, pre, mgain, skip, wide,
    gnormed_o, gate_grad_o, xg_o, cumg_o, stepg_o, bcg_o, lend_o, rms_o, mgg_o, skg_o,
    z, acc, dys, use, inner_all,
):
    length = xact.shape[1]
    blocks = length // T
    n = bcact.shape[2] // 2
    inner = xact.shape[2]
    acc[...] = jnp.zeros_like(acc)

    def block(i, _):
        b = blocks - 1 - i
        r = rows_of(b)
        sums_b = sums[0, :, r]
        columns = jnp.concatenate([sums_b, jnp.zeros((LANES - 8, T), F32)], axis=0).T
        for i in range(T // SUB):
            ri = pl.ds(pl.multiple_of(b * T + i * SUB, SUB), SUB)
            xa = xact[0, ri, :].astype(F32)
            rms = lax.rsqrt(columns[tile(i), 0:1] / inner_all + EPS)
            rms_o[0, ri, :] = jnp.broadcast_to(rms, (SUB, LANES))
            coef = rms * rms * rms * (columns[tile(i), 1:2] / inner_all)
            mixed = ssd[0, ri, :] + skip[...] * xa
            g = gate[0, ri, :]
            sg = sigmoid(g)
            gated = mixed * (g * sg)
            grad_norm = gn[0, ri, :]
            normalised = gated * rms
            gnormed_o[0, ri, :] = (normalised * mgain[...]).astype(BF16)
            mgg_o[0:1] += jnp.sum(grad_norm * normalised, axis=0, keepdims=True)
            grad_gated = rms * (grad_norm * mgain[...]) - gated * coef
            gate_grad_o[0, ri, :] = (grad_gated * mixed * (sg * (1.0 + g * (1.0 - sg)))).astype(BF16)
            grad_mixed = grad_gated * (g * sg)
            skg_o[0:1] += jnp.sum(grad_mixed * xa, axis=0, keepdims=True)
            xg_o[0, ri, :] = skip[...] * grad_mixed
            dys[tile(i)] = grad_mixed.astype(BF16)
        dy = dys[...]
        xa = xact[0, r, :].astype(F32)
        bca = bcact[0, r, :]
        bm, cm = bca[:, :n], bca[:, n:]
        cm32 = cm.astype(F32)
        cum = cum_i[0, r, :]
        cum_t = cum.T
        grown = jnp.exp(cum)
        start = expand_row(jnp.exp(pre[0, pl.ds(b, 1), :]), wide[...]) * entry[0] + lstart[0, b]
        start = start.astype(BF16)
        gdy_hi, gdy_lo = split(expand(grown, wide[...]) * dy.astype(F32), 2)
        c_grad = mm_t(gdy_hi, start) + mm_t(gdy_lo, start)
        step_wide = expand(step_i[0, r, :], wide[...])
        xs = (xa * step_wide).astype(BF16)
        cross = cross_tiles(cm, bm)
        cross_part = {ij: jnp.zeros((SUB, SUB), F32) for ij in tiles()}
        for p in range(inner // LANES):
            lanes = slice(p * LANES, (p + 1) * LANES)
            two = (2 * p, 2 * p + 1)
            scaled = [(cm32 * grown[:, h : h + 1]).astype(BF16) for h in two]
            used = None
            zs = [None] * (T // SUB)
            for i in range(T // SUB):
                dy_two = pair_rows(dy[tile(i), lanes])
                term = t_mm(jnp.concatenate([v[tile(i)] for v in scaled], axis=0), dy_two)
                used = term if used is None else used + term
                for j in range(i + 1):
                    mix_grad = mm_t(dy_two, xs[tile(j), lanes])
                    mix = []
                    for k, h in enumerate(two):
                        decay = decay_tile(cum, cum_t, h, i, j)
                        mix.append((cross[i, j] * decay).astype(BF16))
                        cross_part[i, j] = cross_part[i, j] + mix_grad[tile(k)] * decay
                    term = t_mm(jnp.concatenate(mix, axis=0), dy_two)
                    zs[j] = term if zs[j] is None else zs[j] + term
            use[:, lanes] = used
            for j in range(T // SUB):
                z[tile(j), lanes] = zs[j]
        lend_o[0, b] = acc[...]
        acc[...] = expand_row(grown[T - 1 : T], wide[...]) * acc[...] + use[...]
        rows = []
        for i in range(T // SUB):
            row = [jnp.where(lower(), cross_part[i, j], 0.0) if i == j else cross_part[i, j] for j in range(i + 1)]
            row += [jnp.zeros((SUB, SUB), F32)] * (T // SUB - 1 - i)
            rows.append(jnp.concatenate(row, axis=1))
        cross_low = jnp.concatenate(rows, axis=0).astype(BF16)
        bcg_o[0, r, 0:n] = t_mm(cross_low, cm)
        bcg_o[0, r, n : 2 * n] = c_grad + mm(cross_low, bm)
        zz = z[...]
        xg_o[0, r, :] = xg_o[0, r, :] + step_wide * zz
        cumg_o[0, r, :] = head_sum(dy.astype(F32) * ssd[0, r, :] - xs.astype(F32) * zz, wide[...])
        stepg_o[0, r, :] = head_sum(xa * zz, wide[...])
        return 0

    lax.fori_loop(0, blocks, block, 0)


def back_two(
    xact, bcact, xext, bcext, step_i, cum_i, sraw, xg, cumg, stepg, bcg, lstart, entry, lend, after, pre,
    vk, vo, sk, so, sbias, rate, wide, tri,
    xpg_o, xhalo_o, bpg_o, bhalo_o, raw_o, vkg_o, skg_o, heads_o,
    xe, be, xcg, bcg_s,
):
    length = xact.shape[1]
    blocks = length // T
    n = bcact.shape[2] // 2
    taps = vk.shape[0]
    base = HALO - taps + 1

    @pl.when(pl.program_id(0) == 0)
    def _():
        vkg_o[...] = jnp.zeros_like(vkg_o)
        skg_o[...] = jnp.zeros_like(skg_o)
        heads_o[...] = jnp.zeros_like(heads_o)

    xe[...] = xext[0].astype(F32)
    be[...] = bcext[0].astype(F32)
    for ref in (xcg, bcg_s):
        ref[0:HALO] = jnp.zeros((HALO, ref.shape[1]), F32)
        ref[HALO + length :] = jnp.zeros((HALO, ref.shape[1]), F32)

    def conv_rows(ext, kernel, offset, r0):
        total = offset[...] + kernel[0:1] * ext[r0 + base : r0 + base + T]
        for k in range(1, taps):
            total = total + kernel[k : k + 1] * ext[r0 + base + k : r0 + base + k + T]
        sg = sigmoid(total)
        return sg * (1.0 + total * (1.0 - sg))

    def filter_grad(grad, ext, out, r0):
        for k in range(taps):
            out[k : k + 1] += jnp.sum(grad * ext[r0 + base + k : r0 + base + k + T], axis=0, keepdims=True)
        out[taps : taps + 1] += jnp.sum(grad, axis=0, keepdims=True)

    for b in range(blocks):
        r0 = b * T
        r = slice(r0, r0 + T)
        xa = xact[0, r, :].astype(F32)
        bm = bcact[0, r, 0:n]
        cum = cum_i[0, r, :]
        step = step_i[0, r, :]
        last = cum[T - 1 : T]
        start = expand_row(jnp.exp(pre[0, b : b + 1]), wide[...]) * entry[0] + lstart[0, b]
        suffix = jnp.exp(pre[0, blocks : blocks + 1] - pre[0, b + 1 : b + 2])
        end = expand_row(suffix, wide[...]) * after[0] + lend[0, b]
        end_low = end.astype(BF16)
        weighted_grad = mm(bm, end_low)
        reach = jnp.exp(last - cum)
        weight = reach * step
        weight_wide = expand(weight, wide[...])
        weighted = (xa * weight_wide).astype(BF16)
        bcg_b = bcg[0, r, :]
        b_total = bcg_b[:, 0:n] + mm_t(weighted, end_low)
        bc_total = jnp.concatenate([b_total, bcg_b[:, n:]], axis=1)
        w_grad = head_sum(weighted_grad * xa, wide[...])
        part = w_grad * weight
        product = jnp.broadcast_to(jnp.sum(end * start, axis=0, keepdims=True), (16, end.shape[1]))
        fade_grad = jnp.exp(last) * head_sum(product, wide[...])[0:1]
        at_last = lax.broadcasted_iota(jnp.int32, (T, LANES), 0) == T - 1
        extra = fade_grad + jnp.sum(part, axis=0, keepdims=True)
        cum_grad = cumg[0, r, :] - part + jnp.where(at_last, extra, 0.0)
        a, bb, c = split(cum_grad, 3)
        rise = t_mm(tri[...], a) + (t_mm(tri[...], bb) + t_mm(tri[...], c))
        step_grad = stepg[0, r, :] + w_grad * reach + rise * rate[...]
        raw = step_grad * sigmoid(sraw[0, r, :] + sbias[...])
        raw_o[0, r, :] = raw.astype(BF16)
        heads_o[0:1] += jnp.sum(raw, axis=0, keepdims=True)
        heads_o[1:2] += jnp.sum(rise * step, axis=0, keepdims=True)
        grad = (xg[0, r, :] + weighted_grad * weight_wide) * conv_rows(xe, vk, vo, r0)
        filter_grad(grad, xe, vkg_o, r0)
        xcg[HALO + r0 : HALO + r0 + T] = grad
        grad = bc_total * conv_rows(be, sk, so, r0)
        filter_grad(grad, be, skg_o, r0)
        bcg_s[HALO + r0 : HALO + r0 + T] = grad

    def conv_back(ref, kernel, r0, rows):
        total = kernel[0:1] * ref[r0 + taps - 1 : r0 + taps - 1 + rows]
        for k in range(1, taps):
            total = total + kernel[k : k + 1] * ref[r0 + taps - 1 - k : r0 + taps - 1 - k + rows]
        return total.astype(BF16)

    xhalo_o[0] = conv_back(xcg, vk, 0, HALO)
    bhalo_o[0] = conv_back(bcg_s, sk, 0, HALO)
    for b in range(blocks):
        r0 = b * T
        xpg_o[0, r0 : r0 + T] = conv_back(xcg, vk, HALO + r0, T)
        bpg_o[0, r0 : r0 + T] = conv_back(bcg_s, sk, HALO + r0, T)


def head_sums(mine, out, slots, send, recv):
    z = lax.axis_index("head")
    count = slots.shape[0]
    barrier = pltpu.get_barrier_semaphore()
    for d in range(1, count):
        pl.semaphore_signal(barrier, inc=1, device_id={"head": lax.rem(z + d, count)}, device_id_type=MESH)
    pl.semaphore_wait(barrier, count - 1)
    copies = []
    for d in range(1, count):
        copies.append(pltpu.make_async_remote_copy(
            src_ref=mine, dst_ref=slots.at[z], send_sem=send.at[d], recv_sem=recv.at[d],
            device_id={"head": lax.rem(z + d, count)}, device_id_type=MESH,
        ))
        copies[-1].start()
    slots[z] = mine[...]
    for copy in copies:
        copy.wait_recv()
    total = slots[0]
    for d in range(1, count):
        total = total + slots[d]
    out[...] = total
    for copy in copies:
        copy.wait_send()


class Chain:
    def __init__(self, own, got, far, sems):
        z = lax.axis_index("head")
        self.end = (z == 0) | (z == 3)
        self.side = z + 1 - 2 * (z % 2)
        self.other = 3 - z
        self.own, self.got, self.far = own, got, far
        self.sems = sems

    @staticmethod
    def scratch(n, chunk, width):
        buffer = pltpu.VMEM((n, chunk, width), BF16)
        return [buffer, buffer, buffer] + [pltpu.SemaphoreType.DMA((n,))] * 6

    def copy(self, kind, k, source=None):
        src, dst, to = [(self.own, self.got, self.side), (self.own, self.far, self.other), (self.got, self.got, self.side)][kind]
        return pltpu.make_async_remote_copy(
            src_ref=src.at[k] if source is None else source, dst_ref=dst.at[k],
            send_sem=self.sems[2 * kind].at[k], recv_sem=self.sems[2 * kind + 1].at[k],
            device_id={"head": to}, device_id_type=MESH,
        )

    def inward(self, k, source=None):
        @pl.when(self.end)
        def _():
            self.copy(0, k, source).start()

    def across(self, k, mine=None):
        @pl.when(jnp.logical_not(self.end))
        def _():
            self.copy(0, k).wait_recv()
            value = (self.own[k] if mine is None else mine[...]).astype(F32)
            self.own[k] = (value + self.got[k].astype(F32)).astype(BF16)
            self.copy(1, k).start()

    def outward(self, k):
        @pl.when(jnp.logical_not(self.end))
        def _():
            self.copy(1, k).wait_recv()
            self.got[k] = (self.own[k].astype(F32) + self.far[k].astype(F32)).astype(BF16)
            self.copy(2, k).start()

    def total(self, k):
        @pl.when(self.end)
        def _():
            self.copy(2, k).wait_recv()

        return self.got[k].astype(F32)

    def drain(self, n):
        def one(k, _):
            @pl.when(self.end)
            def _():
                self.copy(0, k).wait_send()

            @pl.when(jnp.logical_not(self.end))
            def _():
                self.copy(1, k).wait_send()
                self.copy(2, k).wait_send()

            return 0

        lax.fori_loop(0, n, one, 0)


class SmallSums:
    def __init__(self, rounds, acc, out, back, zback, done, sems, vec, vback, vsems):
        self.rounds = rounds
        self.acc, self.out, self.back, self.zback, self.done, self.sems = acc, out, back, zback, done, sems
        self.vec, self.vback, self.vsems = vec, vback, vsems
        self.me, self.z = lax.axis_index("seq"), lax.axis_index("head")
        self.stages = 2 * rounds + 2

    @staticmethod
    def scratch(rounds, rows, cols, vec_shape):
        half = pltpu.VMEM((rounds, rows // 2, cols), BF16)
        return [
            pltpu.VMEM((rows, cols), F32), half, half, pltpu.VMEM((4, rows >> rounds, cols), BF16), pltpu.VMEM((rows, cols), BF16),
            pltpu.SemaphoreType.DMA((4 * rounds + 8,)), pltpu.VMEM(vec_shape, F32), pltpu.VMEM((4,) + vec_shape, F32), pltpu.SemaphoreType.DMA((8,)),
        ]

    def partner(self, r):
        bit = 1 << r
        return self.me + bit - 2 * bit * (lax.div(self.me, bit) % 2)

    def start_of(self, r):
        rows = self.acc.shape[0]
        first = 0
        for k in range(r):
            first = first + (lax.div(self.me, 1 << k) % 2) * (rows >> (k + 1))
        return first, rows >> r

    def halving(self, r):
        size = self.acc.shape[0] >> (r + 1)
        return pltpu.make_async_remote_copy(
            src_ref=self.out.at[r, pl.ds(0, size)], dst_ref=self.back.at[r, pl.ds(0, size)],
            send_sem=self.sems.at[r], recv_sem=self.sems.at[self.rounds + r],
            device_id={"seq": self.partner(r)}, device_id_type=MESH,
        )

    def gathering(self, r, mine):
        first, size = self.start_of(r + 1)
        if not mine:
            first = first + size - 2 * size * (lax.div(self.me, 1 << r) % 2)
        at = pl.ds(pl.multiple_of(first, 16), size)
        return pltpu.make_async_remote_copy(
            src_ref=self.done.at[at], dst_ref=self.done.at[at],
            send_sem=self.sems.at[2 * self.rounds + r], recv_sem=self.sems.at[3 * self.rounds + r],
            device_id={"seq": self.partner(r)}, device_id_type=MESH,
        )

    def to_head(self, d, vec):
        src, dst, sems, base = (self.vec, self.vback, self.vsems, 0) if vec else (self.share(), self.zback, self.sems, 4 * self.rounds)
        return pltpu.make_async_remote_copy(
            src_ref=src, dst_ref=dst.at[self.z], send_sem=sems.at[base + d], recv_sem=sems.at[base + 4 + d],
            device_id={"head": lax.rem(self.z + d, 4)}, device_id_type=MESH,
        )

    def share(self):
        first, size = self.start_of(self.rounds)
        return self.done.at[pl.ds(pl.multiple_of(first, 16), size)]

    def push_half(self, r):
        first, size = self.start_of(r)
        half = size // 2
        theirs = first + half - half * (lax.div(self.me, 1 << r) % 2)
        self.out[r, pl.ds(0, half), :] = self.acc[pl.ds(pl.multiple_of(theirs, 16), half), :].astype(BF16)
        self.halving(r).start()

    def stage(self, k):
        rounds = self.rounds
        if k == 0:
            for d in range(1, 4):
                self.to_head(d, True).start()
            self.vback[self.z] = self.vec[...]
        if 0 < k <= rounds:
            r = k - 1
            copy = self.halving(r)
            copy.wait()
            first, size = self.start_of(r + 1)
            at = pl.ds(pl.multiple_of(first, 16), size)
            self.acc[at, :] = self.acc[at, :] + self.back[r, pl.ds(0, size), :].astype(F32)
        if k < rounds:
            self.push_half(k)
        if k == rounds:
            first, size = self.start_of(rounds)
            at = pl.ds(pl.multiple_of(first, 16), size)
            self.done[at, :] = self.acc[at, :].astype(BF16)
            for d in range(1, 4):
                self.to_head(d, False).start()
            self.zback[self.z] = self.done[at, :]
        if k == rounds + 1:
            for d in range(1, 4):
                self.to_head(d, False).wait()
                self.to_head(d, True).wait()
            first, size = self.start_of(rounds)
            at = pl.ds(pl.multiple_of(first, 16), size)
            total = self.zback[0].astype(F32)
            vec = self.vback[0]
            for d in range(1, 4):
                total = total + self.zback[d].astype(F32)
                vec = vec + self.vback[d]
            self.done[at, :] = total.astype(BF16)
            self.vec[...] = vec
            self.gathering(rounds - 1, True).start()
        if k > rounds + 1:
            r = rounds - 1 - (k - rounds - 2)
            self.gathering(r, True).wait_send()
            self.gathering(r, False).wait_recv()
            if r > 0:
                self.gathering(r - 1, True).start()


CHUNK = 64
LAG = 2


def finish(
    y_all, y, gate_grad, xpg, bpg, raw, tok, cot, rms, gate_w, value_w, state_w, step_w, ngain, small, state_grad, state_rows,
    result_o, tokens_grad_o, small_o, state_o,
    own, got, far, sa, sb, sc, sd, se, sf, yown, ygot, yfar, ta, tb, tc, td, te, tf, rows, out, back, send, recv,
    s_acc, s_out, s_back, s_zback, s_done, s_sems, s_vec, s_vback, s_vsems,
    *, n, rounds,
):
    i = pl.program_id(0)
    sums = SmallSums(rounds, s_acc, s_out, s_back, s_zback, s_done, s_sems, s_vec, s_vback, s_vsems)
    chain = Chain(own, got, far, (sa, sb, sc, sd, se, sf))
    ychain = Chain(yown, ygot, yfar, (ta, tb, tc, td, te, tf))
    me = lax.axis_index("seq")

    def partner(r):
        bit = 1 << r
        return me + bit - 2 * bit * (lax.div(me, bit) % 2)

    @pl.when(i == 0)
    def _():
        barrier = pltpu.get_barrier_semaphore()
        for r in range(rounds):
            pl.semaphore_signal(barrier, inc=1, device_id={"seq": partner(r)}, device_id_type=MESH)
        z = lax.axis_index("head")
        for d in range(1, 4):
            pl.semaphore_signal(barrier, inc=1, device_id={"head": lax.rem(z + d, 4)}, device_id_type=MESH)
        pl.semaphore_wait(barrier, rounds + 3)
        s_acc[...] = state_grad[...].astype(F32)
        s_vec[...] = state_rows[...]
        rows[0:8] = small[...]
        rows[8:] = jnp.zeros_like(rows[8:])

    k = i - 2 * LAG

    @pl.when((k >= 0) & (k < n))
    def _():
        chain.outward(k)
        ychain.outward(k)

    k = i - LAG

    @pl.when((k >= 0) & (k < n))
    def _():
        chain.across(k)
        ychain.across(k, y)

    @pl.when(i < n)
    def _():
        ychain.inward(i, y_all.at[pl.ds(pl.multiple_of(i * CHUNK, CHUNK), CHUNK)])
        value = mm_t(gate_grad[...], gate_w[...]) + mm_t(xpg[...], value_w[...])
        own[i] = (value + (mm_t(bpg[...], state_w[...]) + mm_t(raw[...], step_w[...]))).astype(BF16)
        chain.inward(i)

    for stage in range(sums.stages):

        @pl.when(i == 1 + 2 * stage)
        def _():
            sums.stage(stage)

    k = i - 3 * LAG

    @pl.when(k >= 0)
    def _():
        grad = chain.total(k)
        branch = ychain.total(k)
        t = tok[...].astype(F32)
        width = t.shape[1]
        inv = lax.rsqrt(jnp.mean(t * t, axis=1, keepdims=True) + EPS)
        result_o[...] = (t + branch * rms[:, 0:1]).astype(BF16)
        scaled = grad * ngain[...]
        dot = jnp.sum(scaled * t, axis=1, keepdims=True) / width
        tokens_grad_o[...] = cot[...].astype(F32) + inv * scaled - t * (inv * inv * inv * dot)
        gain = jnp.sum(grad * t * inv, axis=0, keepdims=True)
        half = width // 2
        rows[8:9] += gain[:, :half]
        rows[9:10] += gain[:, half:]

    @pl.when(i == n + 3 * LAG - 1)
    def _():
        chain.drain(n)
        ychain.drain(n)
        rows[16:24, 0 : s_vec.shape[1]] = s_vec[...]
        for r in range(rounds):
            copy = pltpu.make_async_remote_copy(
                src_ref=out.at[r], dst_ref=back.at[r], send_sem=send.at[r], recv_sem=recv.at[r],
                device_id={"seq": partner(r)}, device_id_type=MESH,
            )
            out[r] = rows[...]
            copy.start()
            copy.wait()
            rows[...] = rows[...] + back[r]
        state_o[...] = s_done[...]
        small_o[...] = rows[...]


def call(body, steps, seqs, ins, outs, scratch, flops, collective_id=None):
    def cut(shape):
        rest = tuple(shape[1:])
        return pl.BlockSpec((1,) + rest, lambda s: (jnp.minimum(s, seqs - 1),) + (0,) * len(rest))

    def whole(shape):
        return pl.BlockSpec(tuple(shape), lambda s: (0,) * len(shape))

    in_specs = [cut(a.shape) if a.ndim >= 3 else whole(a.shape) for a in ins]
    out_specs = [cut(s) if c else whole(s) for s, _, c in outs]
    moved = sum(a.size * a.dtype.itemsize for a in ins)
    for s, d, _ in outs:
        size = jnp.dtype(d).itemsize
        for k in s:
            size *= k
        moved += size
    return pl.pallas_call(
        body,
        grid=(steps,),
        in_specs=in_specs,
        out_specs=out_specs,
        out_shape=[jax.ShapeDtypeStruct(s, d) for s, d, _ in outs],
        scratch_shapes=scratch,
        compiler_params=pltpu.CompilerParams(
            dimension_semantics=("arbitrary",), vmem_limit_bytes=60 * 1024 * 1024,
            collective_id=collective_id, has_side_effects=collective_id is not None,
        ),
        cost_estimate=pl.CostEstimate(flops=flops, bytes_accessed=moved, transcendentals=0),
    )(*ins)


def shards(
    tokens, norm_gain, gate_weight, value_weight, state_weight, step_weight, value_kernel, value_offset,
    state_kernel, state_offset, step_bias, log_rate, skip_gain, mixer_gain, out_weight, cotangent,
):
    seqs, length, width = tokens.shape
    flat = seqs * length
    inner = gate_weight.shape[1]
    heads = step_weight.shape[1]
    head_size = inner // heads
    n2 = state_weight.shape[1]
    n = n2 // 2
    taps = value_kernel.shape[0]
    blocks = length // T
    devices = lax.axis_size("seq")
    rounds = devices.bit_length() - 1
    assert devices == 1 << rounds
    inner_all = inner * lax.axis_size("head")

    halo = lax.ppermute(tokens[:, length - HALO :], "seq", [(i, i + 1) for i in range(devices - 1)])
    pad = LANES - heads
    rate_row = -jnp.exp(log_rate)
    rate = jnp.pad(rate_row, (0, pad))[None]
    bias = jnp.pad(step_bias, (0, pad))[None]
    step_w = jnp.pad(step_weight, ((0, 0), (0, pad)))
    skip = jnp.repeat(skip_gain, head_size)[None]
    gain = mixer_gain[None]
    one = (jnp.arange(inner)[None, :] // head_size == jnp.arange(LANES)[:, None]).astype(BF16)
    wide = jnp.concatenate([one, one], axis=0)
    tri = (jnp.arange(T)[:, None] >= jnp.arange(T)[None, :]).astype(BF16)
    vo, so = value_offset[None], state_offset[None]

    def big(cols, dtype, rows=length):
        return ((seqs, rows, cols), dtype, True)

    vmem = pltpu.VMEM
    ext = length + HALO
    (normed, gate, xext, bcext, sraw, xact, bcact, step, cum, lstart, pre, entry) = call(
        functools.partial(front, seqs=seqs, rounds=rounds), seqs + rounds, seqs,
        [tokens, halo, norm_gain[None], gate_weight, value_weight, state_weight, step_w,
         value_kernel, vo, state_kernel, so, bias, rate, wide, tri],
        [big(width, BF16), big(inner, F32), big(inner, BF16, ext), big(n2, BF16, ext), big(LANES, F32),
         big(inner, BF16), big(n2, BF16), big(LANES, F32), big(LANES, F32),
         ((seqs, blocks, n, inner), F32, True), big(LANES, F32, 8),
         ((seqs, n, inner), F32, False)],
        [vmem((ext, width), BF16), vmem((ext, inner), F32), vmem((ext, n2), F32), vmem((n, inner), F32),
         vmem((8, LANES), F32)] + Exchange.scratch(rounds, seqs, n, inner),
        2 * flat * width * (2 * inner + n2 + LANES), 1,
    )
    ssd, gn, y, sums = call(
        scan_out, seqs, seqs,
        [xact, bcact, step, cum, gate, lstart, entry, pre, cotangent, out_weight, gain, skip, wide],
        [big(inner, F32), big(inner, F32), big(width, BF16), ((seqs, 8, length), F32, True)],
        [vmem((length, inner), BF16)],
        4 * flat * width * inner,
    )
    group = lax.axis_size("head")
    sums = pl.pallas_call(
        head_sums,
        out_shape=jax.ShapeDtypeStruct(sums.shape, F32),
        in_specs=[pl.BlockSpec(memory_space=pltpu.VMEM)],
        out_specs=pl.BlockSpec(memory_space=pltpu.VMEM),
        scratch_shapes=[vmem((group,) + sums.shape, F32), pltpu.SemaphoreType.DMA((group,)), pltpu.SemaphoreType.DMA((group,))],
        compiler_params=pltpu.CompilerParams(collective_id=2, has_side_effects=True),
    )(sums)
    gnormed, gate_grad, xg, cumg, stepg, bcg, lend, rms, mgg, skg, after = call(
        functools.partial(back_one, inner_all=inner_all, seqs=seqs, rounds=rounds), seqs + rounds, seqs,
        [xact, bcact, step, cum, gate, ssd, gn, sums, lstart, entry, pre, gain, skip, wide],
        [big(inner, BF16), big(inner, BF16), big(inner, F32), big(LANES, F32), big(LANES, F32), big(n2, F32),
         ((seqs, blocks, n, inner), F32, True), big(LANES, F32),
         ((8, inner), F32, False), ((8, inner), F32, False), ((seqs, n, inner), F32, False)],
        [vmem((T, inner), F32), vmem((n, inner), F32), vmem((T, inner), BF16), vmem((n, inner), F32)]
        + Exchange.scratch(rounds, seqs, n, inner),
        2 * flat * T * inner * 8, 3,
    )
    xpg, xhalo, bpg, bhalo, raw, vkg, skgr, head_rows = call(
        back_two, seqs, seqs,
        [xact, bcact, xext, bcext, step, cum, sraw, xg, cumg, stepg, bcg, lstart, entry, lend, after, pre,
         value_kernel, vo, state_kernel, so, bias, rate, wide, tri],
        [big(inner, BF16), big(inner, BF16, HALO), big(n2, BF16), big(n2, BF16, HALO), big(LANES, BF16),
         ((8, inner), F32, False), ((8, n2), F32, False), ((8, LANES), F32, False)],
        [vmem((ext, inner), F32), vmem((ext, n2), F32), vmem((ext + HALO, inner), F32),
         vmem((ext + HALO, n2), F32)],
        2 * flat * T * inner * 4,
    )
    back = [(i + 1, i) for i in range(devices - 1)]
    xhalo, bhalo = lax.ppermute((xhalo, bhalo), "seq", back)
    xpg = xpg.at[:, length - HALO :].add(xhalo)
    bpg = bpg.at[:, length - HALO :].add(bhalo)

    def flatten(v):
        return v.reshape(flat, v.shape[-1])

    normed_f, xpg_f, bpg_f, raw_f, gg_f = [flatten(v) for v in (normed, xpg, bpg, raw, gate_grad)]
    out_weight_grad = t_mm(flatten(gnormed), flatten(cotangent)).astype(BF16)
    gate_weight_grad = t_mm(normed_f, gg_f).astype(BF16)
    value_weight_grad = t_mm(normed_f, xpg_f).astype(BF16)
    state_weight_grad = t_mm(normed_f, bpg_f).astype(BF16)
    step_weight_grad = t_mm(normed_f, raw_f).astype(BF16)
    head_row = jnp.pad(head_rows[:2].reshape(1, 2 * LANES), ((0, 0), (0, inner - 2 * LANES)))
    small = jnp.concatenate([vkg[: taps + 1], mgg[:1], skg[:1], head_row], axis=0)
    n_chunks = flat // CHUNK

    def lagged(cols, lag):
        return pl.BlockSpec((CHUNK, cols), lambda i: (jnp.clip(i - lag, 0, n_chunks - 1), 0))

    def once(v):
        return pl.BlockSpec(v.shape, lambda i: (0,) * v.ndim, pipeline_mode=pl.Buffered(1))

    y_f = flatten(y)
    late = (gate_weight, value_weight, state_weight, step_w, norm_gain[None], small, state_weight_grad, skgr)
    result, tokens_grad, small, state_weight_grad = pl.pallas_call(
        functools.partial(finish, n=n_chunks, rounds=rounds),
        grid=(n_chunks + 3 * LAG,),
        in_specs=[pl.BlockSpec(memory_space=pl.ANY), lagged(width, LAG)]
        + [lagged(v.shape[1], 0) for v in (gg_f, xpg_f, bpg_f, raw_f)]
        + [lagged(width, 3 * LAG), lagged(width, 3 * LAG), lagged(LANES, 3 * LAG)]
        + [once(v) for v in late],
        out_specs=[lagged(width, 3 * LAG), lagged(width, 3 * LAG), pl.BlockSpec((24, inner), lambda i: (0, 0)),
                   once(state_weight_grad)],
        out_shape=[
            jax.ShapeDtypeStruct((flat, width), BF16), jax.ShapeDtypeStruct((flat, width), F32),
            jax.ShapeDtypeStruct((24, inner), F32), jax.ShapeDtypeStruct(state_weight_grad.shape, BF16),
        ],
        scratch_shapes=Chain.scratch(n_chunks, CHUNK, width) + Chain.scratch(n_chunks, CHUNK, width) + [
            vmem((24, inner), F32), vmem((rounds, 24, inner), F32), vmem((rounds, 24, inner), F32),
            pltpu.SemaphoreType.DMA((rounds,)), pltpu.SemaphoreType.DMA((rounds,)),
        ] + SmallSums.scratch(rounds, width, n2, skgr.shape),
        compiler_params=pltpu.CompilerParams(
            dimension_semantics=("arbitrary",), vmem_limit_bytes=62 * 1024 * 1024, collective_id=4, has_side_effects=True
        ),
        cost_estimate=pl.CostEstimate(flops=10**11, bytes_accessed=10**8, transcendentals=0),
    )(y_f, y_f, gg_f, xpg_f, bpg_f, raw_f, flatten(tokens), flatten(cotangent), flatten(rms),
      *late)
    result, tokens_grad = result.reshape(tokens.shape), tokens_grad.reshape(tokens.shape)
    vkg, mixer_gain_grad, skg, head_row = small[: taps + 1], small[taps + 1], small[taps + 2], small[taps + 3]
    norm_gain_grad = small[8:10].reshape(width)
    skgr = small[16:24, :n2]
    skip_gain_grad = jnp.sum(skg.reshape(heads, head_size), axis=1)
    step_bias_grad = head_row[:heads]
    log_rate_grad = head_row[LANES : LANES + heads] * rate_row
    out_weight_grad = lax.psum(out_weight_grad, "seq").astype(F32)
    gate_weight_grad = lax.psum(gate_weight_grad, "seq").astype(F32)
    value_weight_grad = lax.psum(value_weight_grad, "seq").astype(F32)
    step_weight_grad = lax.psum(step_weight_grad, "seq")[:, :heads].astype(F32)
    state_weight_grad = state_weight_grad.astype(F32)
    return (
        result, tokens_grad, norm_gain_grad, gate_weight_grad, value_weight_grad, state_weight_grad,
        step_weight_grad, vkg[:taps], vkg[taps], skgr[:taps], skgr[taps], step_bias_grad, log_rate_grad,
        skip_gain_grad, mixer_gain_grad, out_weight_grad,
    )


def solution(mesh):
    rows, cols, vec = P(None, "seq", None), P(None, "head"), P("head")
    in_specs = (rows, P(), cols, cols, P(), cols, cols, vec, P(), P(), vec, vec, vec, vec, P("head", None), rows)
    out_specs = (rows, rows, P(), cols, cols, P(), cols, cols, vec, P(), P(), vec, vec, vec, vec, P("head", None))
    return jax.shard_map(shards, mesh=mesh, in_specs=in_specs, out_specs=out_specs, check_vma=False)
```

```python
import functools

import jax
import jax.numpy as jnp
from jax import lax
from jax.experimental import pallas as pl
from jax.experimental.pallas import tpu as pltpu
from jax.sharding import PartitionSpec as P

EPS = 1e-05
T = 256
SUB = 128
HALO = 16
LANES = 128
F32 = jnp.float32
BF16 = jnp.bfloat16


def mm(a, b):
    return lax.dot_general(a, b, (((1,), (0,)), ((), ())), preferred_element_type=F32)


def mm_t(a, b):
    return lax.dot_general(a, b, (((1,), (1,)), ((), ())), preferred_element_type=F32)


def t_mm(a, b):
    return lax.dot_general(a, b, (((0,), (0,)), ((), ())), preferred_element_type=F32)


def split(v, parts):
    pieces = []
    for _ in range(parts):
        piece = v.astype(BF16)
        pieces.append(piece)
        v = v - piece.astype(F32)
    return pieces


def expand(v, wide):
    return mm(jnp.concatenate(split(v, 2), axis=1), wide)


def expand_row(v, wide):
    return expand(jnp.broadcast_to(v, (16, LANES)), wide)[0:1]


def head_sum(v, wide):
    hi, lo = split(v, 2)
    return mm_t(hi, wide[:LANES]) + mm_t(lo, wide[:LANES])


def exact_tri(tri, v):
    a, b, c = split(v, 3)
    return mm(tri, a) + (mm(tri, b) + mm(tri, c))


def sigmoid(v):
    return 0.5 * jnp.tanh(0.5 * v) + 0.5


def softplus(v):
    return jnp.maximum(v, 0.0) + jnp.log1p(jnp.exp(-jnp.abs(v)))


def lower():
    row = lax.broadcasted_iota(jnp.int32, (SUB, SUB), 0)
    col = lax.broadcasted_iota(jnp.int32, (SUB, SUB), 1)
    return row >= col


def tile(i):
    return slice(i * SUB, (i + 1) * SUB)


def tiles():
    return [(i, j) for i in range(T // SUB) for j in range(i + 1)]


def cross_tiles(cm, bm):
    found = {}
    for i, j in tiles():
        value = mm_t(cm[tile(i)], bm[tile(j)])
        found[i, j] = jnp.where(lower(), value, 0.0) if i == j else value
    return found


def decay_tile(cum, cum_t, h, i, j):
    gap = cum[tile(i), h : h + 1] - cum_t[h : h + 1, tile(j)]
    return jnp.exp(jnp.minimum(gap, 0.0) if i == j else gap)


def half_mask(rows):
    return lax.broadcasted_iota(jnp.int32, (rows, LANES), 1) < LANES // 2


def pair_rows(v):
    left = half_mask(v.shape[0])
    zero = jnp.zeros_like(v)
    return jnp.concatenate([jnp.where(left, v, zero), jnp.where(left, zero, v)], axis=0)


def rows_of(b):
    return pl.ds(pl.multiple_of(b * T, T), T)


MESH = pl.DeviceIdType.MESH
CHUNK = 64
LAG = 2


def greet_head():
    z = lax.axis_index("head")
    for d in range(1, 4):
        pl.semaphore_signal(
            pltpu.get_barrier_semaphore(), inc=1, device_id={"head": lax.rem(z + d, 4)}, device_id_type=MESH)


class Chain:
    def __init__(self, own, got, far, sems):
        z = lax.axis_index("head")
        self.end = (z == 0) | (z == 3)
        self.side = z + 1 - 2 * (z % 2)
        self.other = 3 - z
        self.own, self.got, self.far = own, got, far
        self.sems = sems

    @staticmethod
    def scratch(n, chunk, width):
        buffer = pltpu.VMEM((n, chunk, width), BF16)
        return [buffer, buffer, buffer] + [pltpu.SemaphoreType.DMA((n,))] * 6

    def copy(self, kind, k):
        src, dst, to = [(self.own, self.got, self.side), (self.own, self.far, self.other), (self.got, self.got, self.side)][kind]
        return pltpu.make_async_remote_copy(
            src_ref=src.at[k], dst_ref=dst.at[k],
            send_sem=self.sems[2 * kind].at[k], recv_sem=self.sems[2 * kind + 1].at[k],
            device_id={"head": to}, device_id_type=MESH,
        )

    def inward(self, k):
        @pl.when(self.end)
        def _():
            self.copy(0, k).start()

    def meet(self, stage, k):
        self.copy(stage, k).wait_recv()
        if stage == 0:
            self.own[k] = (self.own[k].astype(F32) + self.got[k].astype(F32)).astype(BF16)
        else:
            self.got[k] = (self.own[k].astype(F32) + self.far[k].astype(F32)).astype(BF16)

    def onward(self, stage, k):
        @pl.when(jnp.logical_not(self.end))
        def _():
            self.meet(stage - 1, k)
            self.copy(stage, k).start()

    def total(self, k):
        @pl.when(self.end)
        def _():
            self.copy(2, k).wait_recv()

        return self.got[k].astype(F32)

    def drain(self, n):
        def one(k, _):
            @pl.when(self.end)
            def _():
                self.copy(0, k).wait_send()

            @pl.when(jnp.logical_not(self.end))
            def _():
                self.copy(1, k).wait_send()
                self.copy(2, k).wait_send()

            return 0

        lax.fori_loop(0, n, one, 0)


class Rider:
    def __init__(self, first, ticks, count, hbm, own, got, far, sems, local):
        self.first, self.ticks, self.count = first, ticks, count
        self.base = max(first - 2 * LAG, 0)
        self.hbm, self.local = hbm, local
        self.chain = Chain(own, got, far, sems)

    @staticmethod
    def size(first, ticks, count):
        return min(first + ticks, count) - max(first - 2 * LAG, 0)

    @staticmethod
    def scratch(first, ticks, count, width):
        return Chain.scratch(Rider.size(first, ticks, count), CHUNK, width) + [pltpu.SemaphoreType.DMA((2,))]

    def span(self, stage):
        low = self.first - stage * LAG
        return max(low, 0), min(low + self.ticks, self.count)

    def load(self):
        size = self.size(self.first, self.ticks, self.count)
        own = pltpu.make_async_copy(self.hbm.at[pl.ds(self.base, size)], self.chain.own, self.local.at[0])
        own.start()
        ready = min(max(self.first - LAG, 0), self.count) - self.base
        if ready > 0:

            @pl.when(jnp.logical_not(self.chain.end))
            def _():
                got = pltpu.make_async_copy(
                    self.hbm.at[pl.ds(self.base, ready)], self.chain.got.at[pl.ds(0, ready)], self.local.at[1])
                got.start()
                got.wait()

        own.wait()

    def tick(self, t):
        chain = self.chain
        for stage in (2, 1, 0):
            low, high = self.span(stage)
            k = self.first - stage * LAG + t

            @pl.when((k >= low) & (k < high) & (t < self.ticks))
            def _():
                at = k - self.base
                if stage == 0:
                    chain.inward(at)
                else:
                    self.follow(stage, at, t >= LAG)

    def follow(self, stage, at, pending):
        chain = self.chain
        middle = jnp.logical_not(chain.end)

        @pl.when(middle & pending)
        def _():
            chain.meet(stage - 1, at)

        @pl.when(middle)
        def _():
            chain.copy(stage, at).start()

    def drain(self):
        chain = self.chain

        def each(stage):
            low, high = self.span(stage)
            lax.fori_loop(low - self.base, high - self.base, lambda k, _: (chain.copy(stage, k).wait_send(), 0)[1], 0)

        @pl.when(chain.end)
        def _():
            each(0)

        @pl.when(jnp.logical_not(chain.end))
        def _():
            each(1)
            each(2)

    def close(self):
        chain = self.chain
        middle = jnp.logical_not(chain.end)

        def each(low, high, do):
            if high > low:
                lax.fori_loop(low - self.base, high - self.base, lambda k, _: (do(k), 0)[1], 0)

        @pl.when(middle)
        def _():
            for stage in (0, 1):
                low, high = self.span(stage)
                started = max(self.first - stage * LAG + self.ticks - LAG, low)
                each(started, high, lambda k: chain.meet(stage, k))
            for stage in (1, 2):
                each(*self.span(stage), lambda k: chain.copy(stage, k).wait_send())

        @pl.when(chain.end)
        def _():
            each(*self.span(2), lambda k: chain.copy(2, k).wait_recv())
            each(*self.span(0), lambda k: chain.copy(0, k).wait_send())

        def store(ref, low, high):
            if high > low:
                at = pl.ds(low - self.base, high - low)
                copy = pltpu.make_async_copy(ref.at[at], self.hbm.at[pl.ds(low, high - low)], self.local.at[0])
                copy.start()
                copy.wait()

        @pl.when(middle)
        def _():
            reached = self.span(1)[1]
            store(chain.got, self.base, reached)
            store(chain.own, reached, self.span(0)[1])

        @pl.when(chain.end)
        def _():
            store(chain.got, *self.span(2))


class Exchange:
    def __init__(self, rounds, backward, total, before, logs, out, back, send, recv):
        self.rounds, self.backward = rounds, backward
        self.total, self.before, self.logs = total, before, logs
        self.out, self.back, self.send, self.recv = out, back, send, recv
        self.me = lax.axis_index("seq")

    def partner(self, r):
        bit = 1 << r
        return self.me + bit - 2 * bit * (lax.div(self.me, bit) % 2)

    def greet(self, with_head=False):
        barrier = pltpu.get_barrier_semaphore()
        for r in range(self.rounds):
            pl.semaphore_signal(barrier, inc=1, device_id={"seq": self.partner(r)}, device_id_type=MESH)
        if with_head:
            greet_head()
        pl.semaphore_wait(barrier, self.rounds + 3 * with_head)

    def copy(self, r, s):
        return pltpu.make_async_remote_copy(
            src_ref=self.out.at[r, s], dst_ref=self.back.at[r, s],
            send_sem=self.send.at[r, s], recv_sem=self.recv.at[r, s],
            device_id={"seq": self.partner(r)}, device_id_type=MESH,
        )

    def begin(self, s, state, log):
        self.total[s] = state
        self.before[s] = jnp.zeros_like(state)
        self.logs[s] = jnp.zeros(self.logs.shape[1:], F32)
        self.logs[s, 0:1] = log

    def push(self, r, s):
        n = self.total.shape[1]
        self.out[r, s, 0:n] = self.total[s].astype(BF16)
        hi, mid, lo = [v.astype(F32) for v in split(self.logs[s, 0:1], 3)]
        at = lax.broadcasted_iota(jnp.int32, (HALO, hi.shape[1]), 0)
        tail = jnp.where(at == 0, hi, jnp.where(at == 1, mid, jnp.where(at == 2, lo, 0.0)))
        self.out[r, s, n : n + HALO] = tail.astype(BF16)
        self.copy(r, s).start()

    def take(self, r, s):
        n = self.total.shape[1]
        copy = self.copy(r, s)
        copy.wait_recv()
        copy.wait_send()
        state = self.back[r, s, 0:n].astype(F32)
        tail = self.back[r, s, n : n + HALO].astype(F32)
        log = tail[0:1] + tail[1:2] + tail[2:3]
        upper = lax.div(self.me, 1 << r) % 2 == 1
        near = jnp.logical_not(upper) if self.backward else upper
        mine, theirs = self.logs[s, 0:1], self.logs[s, 1:2]
        self.before[s] = self.before[s] + jnp.where(near, jnp.exp(theirs), 0.0) * state
        self.logs[s, 1:2] = theirs + jnp.where(near, log, 0.0)
        own = jnp.where(near, 1.0, jnp.exp(log))
        other = jnp.where(near, jnp.exp(mine), 1.0)
        self.total[s] = own * self.total[s] + other * state
        self.logs[s, 0:1] = mine + log

    def advance(self, i, seqs):
        @pl.when(i < seqs)
        def _():
            self.push(0, i)

        for r in range(self.rounds):
            s = i - 1 - r

            @pl.when((s >= 0) & (s < seqs))
            def _():
                self.take(r, s)
                if r + 1 < self.rounds:
                    self.push(r + 1, s)

    @staticmethod
    def scratch(rounds, seqs, n, inner):
        return [
            pltpu.VMEM((seqs, n, inner), F32), pltpu.VMEM((seqs, n, inner), F32), pltpu.VMEM((seqs, 8, inner), F32),
            pltpu.VMEM((rounds, seqs, n + HALO, inner), BF16), pltpu.VMEM((rounds, seqs, n + HALO, inner), BF16),
            pltpu.SemaphoreType.DMA((rounds, seqs)), pltpu.SemaphoreType.DMA((rounds, seqs)),
        ]


def front(
    tok, halo, ngain, gate_w, value_w, state_w, step_w, vk, vo, sk, so, sbias, rate, wide, tri,
    normed_o, gate_o, xext_o, bcext_o, sraw_o, xact_o, bcact_o, step_o, cum_o, lstart_o, pre_o, entry_o,
    nx, xe, be, st, run, total, before, logs, out, back, send, recv,
    *, seqs, rounds,
):
    i = pl.program_id(0)
    scan = Exchange(rounds, False, total, before, logs, out, back, send, recv)

    @pl.when(i == 0)
    def _():
        scan.greet()

    @pl.when(i < seqs)
    def _():
        front_rows(
            tok, halo, ngain, gate_w, value_w, state_w, step_w, vk, vo, sk, so, sbias, rate, wide, tri,
            normed_o, gate_o, xext_o, bcext_o, sraw_o, xact_o, bcact_o, step_o, cum_o, lstart_o, pre_o,
            nx, xe, be, st, run,
        )
        scan.begin(i, st[...], expand_row(run[0:1], wide[...]))

    scan.advance(i, seqs)

    @pl.when(i == seqs + rounds - 1)
    def _():
        entry_o[...] = before[...]


def front_rows(
    tok, halo, ngain, gate_w, value_w, state_w, step_w, vk, vo, sk, so, sbias, rate, wide, tri,
    normed_o, gate_o, xext_o, bcext_o, sraw_o, xact_o, bcact_o, step_o, cum_o, lstart_o, pre_o,
    nx, xe, be, st, run,
):
    length = tok.shape[1]
    blocks = length // T
    n = bcact_o.shape[2] // 2

    def norm(v):
        v = v.astype(F32)
        inv = lax.rsqrt(jnp.mean(v * v, axis=1, keepdims=True) + EPS)
        return (v * inv * ngain[...]).astype(BF16)

    nx[0:HALO] = norm(halo[0])

    def norm_rows(b, _):
        r = rows_of(b)
        v = norm(tok[0, r, :])
        nx[pl.ds(pl.multiple_of(HALO + b * T, HALO), T), :] = v
        normed_o[0, r, :] = v
        return 0

    lax.fori_loop(0, blocks, norm_rows, 0)
    x = mm(nx[...], value_w[...]).astype(BF16)
    xext_o[0] = x
    xe[...] = x.astype(F32)
    bc = mm(nx[...], state_w[...]).astype(BF16)
    bcext_o[0] = bc
    be[...] = bc.astype(F32)
    gate_o[0] = mm(nx[HALO:], gate_w[...])
    sraw_o[0] = mm(nx[HALO:], step_w[...])
    st[...] = jnp.zeros_like(st)
    run[...] = jnp.zeros_like(run)
    pre_o[0] = jnp.zeros_like(pre_o[0])
    for b in range(blocks):
        r0 = b * T
        r = slice(r0, r0 + T)
        taps = vk.shape[0]
        base = HALO - taps + 1
        xc = vo[...] + vk[0:1] * xe[r0 + base : r0 + base + T]
        bcc = so[...] + sk[0:1] * be[r0 + base : r0 + base + T]
        for k in range(1, taps):
            xc = xc + vk[k : k + 1] * xe[r0 + base + k : r0 + base + k + T]
            bcc = bcc + sk[k : k + 1] * be[r0 + base + k : r0 + base + k + T]
        xa = (xc * sigmoid(xc)).astype(BF16)
        bca = (bcc * sigmoid(bcc)).astype(BF16)
        xact_o[0, r, :] = xa
        bcact_o[0, r, :] = bca
        step = softplus(sraw_o[0, r, :] + sbias[...])
        cum = exact_tri(tri[...], step * rate[...])
        step_o[0, r, :] = step
        cum_o[0, r, :] = cum
        last = cum[T - 1 : T]
        weight = jnp.exp(last - cum) * step
        weighted = (xa.astype(F32) * expand(weight, wide[...])).astype(BF16)
        contrib = t_mm(bca[:, :n], weighted)
        lstart_o[0, b] = st[...]
        st[...] = expand_row(jnp.exp(last), wide[...]) * st[...] + contrib
        run[0:1] = run[0:1] + last
        pre_o[0, b + 1 : b + 2] = run[0:1]


def scan_out(
    xact, bcact, step_i, cum_i, gate, lstart, entry, pre, cot, out_w, mgain, skip, wide,
    ssd_o, gn_o, y_o, sums_o,
    gm,
):
    length = xact.shape[1]
    blocks = length // T
    n = bcact.shape[2] // 2
    inner = xact.shape[2]
    gn_o[0] = mm_t(cot[0], out_w[...])

    def block(b, _):
        r = rows_of(b)
        xa = xact[0, r, :]
        bca = bcact[0, r, :]
        bm, cm = bca[:, :n], bca[:, n:]
        cum = cum_i[0, r, :]
        cum_t = cum.T
        cross = cross_tiles(cm, bm)
        start = expand_row(jnp.exp(pre[0, pl.ds(b, 1), :]), wide[...]) * entry[0] + lstart[0, b]
        start = start.astype(BF16)
        grown = jnp.exp(cum)
        cm = cm.astype(F32)
        xs = (xa.astype(F32) * expand(step_i[0, r, :], wide[...])).astype(BF16)
        for p in range(inner // LANES):
            lanes = slice(p * LANES, (p + 1) * LANES)
            two = (2 * p, 2 * p + 1)
            start_two = pair_rows(start[:, lanes])
            xs_two = [pair_rows(xs[tile(j), lanes]) for j in range(T // SUB)]
            for i in range(T // SUB):
                left = [(cm[tile(i)] * grown[tile(i), h : h + 1]).astype(BF16) for h in two]
                right = [start_two]
                for j in range(i + 1):
                    left += [(cross[i, j] * decay_tile(cum, cum_t, h, i, j)).astype(BF16) for h in two]
                    right.append(xs_two[j])
                rows = pl.ds(pl.multiple_of(b * T + i * SUB, SUB), SUB)
                ssd_o[0, rows, lanes] = mm(jnp.concatenate(left, axis=1), jnp.concatenate(right, axis=0))
        mixed = ssd_o[0, r, :] + skip[...] * xa.astype(F32)
        g = gate[0, r, :]
        gated = mixed * (g * sigmoid(g))
        gg = gated * mgain[...]
        gm[r, :] = gg.astype(BF16)
        squares = jnp.sum(gated * gated, axis=1, keepdims=True)
        dots = jnp.sum(gg * gn_o[0, r, :], axis=1, keepdims=True)
        lane = lax.broadcasted_iota(jnp.int32, (T, LANES), 1)
        both = jnp.where(lane == 0, squares, jnp.where(lane == 1, dots, 0.0))
        sums_o[0, :, r] = both.T[0:8]
        return 0

    lax.fori_loop(0, blocks, block, 0)
    y_o[0] = mm(gm[...], out_w[...]).astype(BF16)


def back_one(
    xact, bcact, step_i, cum_i, gate, ssd, gn, sums, lstart, entry, pre, mgain, skip, wide, y_in,
    gnormed_o, gate_grad_o, xg_o, cumg_o, stepg_o, bcg_o, lend_o, rms_o, mgg_o, skg_o, after_o, y_all,
    z, acc, dys, use, total, before, logs, out, back, send, recv,
    yown, ygot, yfar, ta, tb, tc, td, te, tf, ylocal,
    *, inner_all, seqs, rounds, plan,
):
    i = pl.program_id(0)
    blocks = xact.shape[1] // T
    scan = Exchange(rounds, True, total, before, logs, out, back, send, recv)
    rider = Rider(*plan, y_all, yown, ygot, yfar, (ta, tb, tc, td, te, tf), ylocal)

    @pl.when(i == 0)
    def _():
        scan.greet(with_head=True)
        rider.load()
        mgg_o[...] = jnp.zeros_like(mgg_o)
        skg_o[...] = jnp.zeros_like(skg_o)

    @pl.when(i < seqs)
    def _():
        back_one_rows(
            xact, bcact, step_i, cum_i, gate, ssd, gn, sums, lstart, entry, pre, mgain, skip, wide,
            gnormed_o, gate_grad_o, xg_o, cumg_o, stepg_o, bcg_o, lend_o, rms_o, mgg_o, skg_o,
            z, acc, dys, use, inner_all, lambda b: rider.tick(i * blocks + b),
        )
        scan.begin(i, acc[...], expand_row(pre[0, blocks : blocks + 1], wide[...]))

    scan.advance(i, seqs)

    @pl.when(i >= seqs)
    def _():
        for k in (0, 1):
            rider.tick(seqs * blocks + (i - seqs) * 2 + k)

    @pl.when(i == seqs + rounds - 1)
    def _():
        after_o[...] = before[...]
        rider.close()


def back_one_rows(
    xact, bcact, step_i, cum_i, gate, ssd, gn, sums, lstart, entry, pre, mgain, skip, wide,
    gnormed_o, gate_grad_o, xg_o, cumg_o, stepg_o, bcg_o, lend_o, rms_o, mgg_o, skg_o,
    z, acc, dys, use, inner_all, tick,
):
    length = xact.shape[1]
    blocks = length // T
    n = bcact.shape[2] // 2
    inner = xact.shape[2]
    acc[...] = jnp.zeros_like(acc)

    def block(i, _):
        tick(i)
        b = blocks - 1 - i
        r = rows_of(b)
        sums_b = sums[0, :, r]
        columns = jnp.concatenate([sums_b, jnp.zeros((LANES - 8, T), F32)], axis=0).T
        for i in range(T // SUB):
            ri = pl.ds(pl.multiple_of(b * T + i * SUB, SUB), SUB)
            xa = xact[0, ri, :].astype(F32)
            rms = lax.rsqrt(columns[tile(i), 0:1] / inner_all + EPS)
            rms_o[0, ri, :] = jnp.broadcast_to(rms, (SUB, LANES))
            coef = rms * rms * rms * (columns[tile(i), 1:2] / inner_all)
            mixed = ssd[0, ri, :] + skip[...] * xa
            g = gate[0, ri, :]
            sg = sigmoid(g)
            gated = mixed * (g * sg)
            grad_norm = gn[0, ri, :]
            normalised = gated * rms
            gnormed_o[0, ri, :] = (normalised * mgain[...]).astype(BF16)
            mgg_o[0:1] += jnp.sum(grad_norm * normalised, axis=0, keepdims=True)
            grad_gated = rms * (grad_norm * mgain[...]) - gated * coef
            gate_grad_o[0, ri, :] = (grad_gated * mixed * (sg * (1.0 + g * (1.0 - sg)))).astype(BF16)
            grad_mixed = grad_gated * (g * sg)
            skg_o[0:1] += jnp.sum(grad_mixed * xa, axis=0, keepdims=True)
            xg_o[0, ri, :] = skip[...] * grad_mixed
            dys[tile(i)] = grad_mixed.astype(BF16)
        dy = dys[...]
        xa = xact[0, r, :].astype(F32)
        bca = bcact[0, r, :]
        bm, cm = bca[:, :n], bca[:, n:]
        cm32 = cm.astype(F32)
        cum = cum_i[0, r, :]
        cum_t = cum.T
        grown = jnp.exp(cum)
        start = expand_row(jnp.exp(pre[0, pl.ds(b, 1), :]), wide[...]) * entry[0] + lstart[0, b]
        start = start.astype(BF16)
        gdy_hi, gdy_lo = split(expand(grown, wide[...]) * dy.astype(F32), 2)
        c_grad = mm_t(gdy_hi, start) + mm_t(gdy_lo, start)
        step_wide = expand(step_i[0, r, :], wide[...])
        xs = (xa * step_wide).astype(BF16)
        cross = cross_tiles(cm, bm)
        cross_part = {ij: jnp.zeros((SUB, SUB), F32) for ij in tiles()}
        for p in range(inner // LANES):
            lanes = slice(p * LANES, (p + 1) * LANES)
            two = (2 * p, 2 * p + 1)
            scaled = [(cm32 * grown[:, h : h + 1]).astype(BF16) for h in two]
            used = None
            zs = [None] * (T // SUB)
            for i in range(T // SUB):
                dy_two = pair_rows(dy[tile(i), lanes])
                term = t_mm(jnp.concatenate([v[tile(i)] for v in scaled], axis=0), dy_two)
                used = term if used is None else used + term
                for j in range(i + 1):
                    mix_grad = mm_t(dy_two, xs[tile(j), lanes])
                    mix = []
                    for k, h in enumerate(two):
                        decay = decay_tile(cum, cum_t, h, i, j)
                        mix.append((cross[i, j] * decay).astype(BF16))
                        cross_part[i, j] = cross_part[i, j] + mix_grad[tile(k)] * decay
                    term = t_mm(jnp.concatenate(mix, axis=0), dy_two)
                    zs[j] = term if zs[j] is None else zs[j] + term
            use[:, lanes] = used
            for j in range(T // SUB):
                z[tile(j), lanes] = zs[j]
        lend_o[0, b] = acc[...]
        acc[...] = expand_row(grown[T - 1 : T], wide[...]) * acc[...] + use[...]
        rows = []
        for i in range(T // SUB):
            row = [jnp.where(lower(), cross_part[i, j], 0.0) if i == j else cross_part[i, j] for j in range(i + 1)]
            row += [jnp.zeros((SUB, SUB), F32)] * (T // SUB - 1 - i)
            rows.append(jnp.concatenate(row, axis=1))
        cross_low = jnp.concatenate(rows, axis=0).astype(BF16)
        bcg_o[0, r, 0:n] = t_mm(cross_low, cm)
        bcg_o[0, r, n : 2 * n] = c_grad + mm(cross_low, bm)
        zz = z[...]
        xg_o[0, r, :] = xg_o[0, r, :] + step_wide * zz
        cumg_o[0, r, :] = head_sum(dy.astype(F32) * ssd[0, r, :] - xs.astype(F32) * zz, wide[...])
        stepg_o[0, r, :] = head_sum(xa * zz, wide[...])
        return 0

    lax.fori_loop(0, blocks, block, 0)


def back_two(
    xact, bcact, xext, bcext, step_i, cum_i, sraw, xg, cumg, stepg, bcg, lstart, entry, lend, after, pre,
    vk, vo, sk, so, sbias, rate, wide, tri, y_in,
    xpg_o, xhalo_o, bpg_o, bhalo_o, raw_o, vkg_o, skg_o, heads_o, y_all,
    xe, be, xcg, bcg_s, yown, ygot, yfar, ta, tb, tc, td, te, tf, ylocal,
    *, seqs, plan,
):
    length = xact.shape[1]
    blocks = length // T
    n = bcact.shape[2] // 2
    taps = vk.shape[0]
    base = HALO - taps + 1
    step_at = pl.program_id(0)
    rider = Rider(*plan, y_all, yown, ygot, yfar, (ta, tb, tc, td, te, tf), ylocal)

    @pl.when(step_at == 0)
    def _():
        greet_head()
        pl.semaphore_wait(pltpu.get_barrier_semaphore(), 3)
        rider.load()
        vkg_o[...] = jnp.zeros_like(vkg_o)
        skg_o[...] = jnp.zeros_like(skg_o)
        heads_o[...] = jnp.zeros_like(heads_o)

    xe[...] = xext[0].astype(F32)
    be[...] = bcext[0].astype(F32)
    for ref in (xcg, bcg_s):
        ref[0:HALO] = jnp.zeros((HALO, ref.shape[1]), F32)
        ref[HALO + length :] = jnp.zeros((HALO, ref.shape[1]), F32)

    def conv_rows(ext, kernel, offset, r0):
        total = offset[...] + kernel[0:1] * ext[r0 + base : r0 + base + T]
        for k in range(1, taps):
            total = total + kernel[k : k + 1] * ext[r0 + base + k : r0 + base + k + T]
        sg = sigmoid(total)
        return sg * (1.0 + total * (1.0 - sg))

    def filter_grad(grad, ext, out, r0):
        for k in range(taps):
            out[k : k + 1] += jnp.sum(grad * ext[r0 + base + k : r0 + base + k + T], axis=0, keepdims=True)
        out[taps : taps + 1] += jnp.sum(grad, axis=0, keepdims=True)

    for b in range(blocks):
        rider.tick(step_at * blocks + b)
        r0 = b * T
        r = slice(r0, r0 + T)
        xa = xact[0, r, :].astype(F32)
        bm = bcact[0, r, 0:n]
        cum = cum_i[0, r, :]
        step = step_i[0, r, :]
        last = cum[T - 1 : T]
        start = expand_row(jnp.exp(pre[0, b : b + 1]), wide[...]) * entry[0] + lstart[0, b]
        suffix = jnp.exp(pre[0, blocks : blocks + 1] - pre[0, b + 1 : b + 2])
        end = expand_row(suffix, wide[...]) * after[0] + lend[0, b]
        end_low = end.astype(BF16)
        weighted_grad = mm(bm, end_low)
        reach = jnp.exp(last - cum)
        weight = reach * step
        weight_wide = expand(weight, wide[...])
        weighted = (xa * weight_wide).astype(BF16)
        bcg_b = bcg[0, r, :]
        b_total = bcg_b[:, 0:n] + mm_t(weighted, end_low)
        bc_total = jnp.concatenate([b_total, bcg_b[:, n:]], axis=1)
        w_grad = head_sum(weighted_grad * xa, wide[...])
        part = w_grad * weight
        product = jnp.broadcast_to(jnp.sum(end * start, axis=0, keepdims=True), (16, end.shape[1]))
        fade_grad = jnp.exp(last) * head_sum(product, wide[...])[0:1]
        at_last = lax.broadcasted_iota(jnp.int32, (T, LANES), 0) == T - 1
        extra = fade_grad + jnp.sum(part, axis=0, keepdims=True)
        cum_grad = cumg[0, r, :] - part + jnp.where(at_last, extra, 0.0)
        a, bb, c = split(cum_grad, 3)
        rise = t_mm(tri[...], a) + (t_mm(tri[...], bb) + t_mm(tri[...], c))
        step_grad = stepg[0, r, :] + w_grad * reach + rise * rate[...]
        raw = step_grad * sigmoid(sraw[0, r, :] + sbias[...])
        raw_o[0, r, :] = raw.astype(BF16)
        heads_o[0:1] += jnp.sum(raw, axis=0, keepdims=True)
        heads_o[1:2] += jnp.sum(rise * step, axis=0, keepdims=True)
        grad = (xg[0, r, :] + weighted_grad * weight_wide) * conv_rows(xe, vk, vo, r0)
        filter_grad(grad, xe, vkg_o, r0)
        xcg[HALO + r0 : HALO + r0 + T] = grad
        grad = bc_total * conv_rows(be, sk, so, r0)
        filter_grad(grad, be, skg_o, r0)
        bcg_s[HALO + r0 : HALO + r0 + T] = grad

    def conv_back(ref, kernel, r0, rows):
        total = kernel[0:1] * ref[r0 + taps - 1 : r0 + taps - 1 + rows]
        for k in range(1, taps):
            total = total + kernel[k : k + 1] * ref[r0 + taps - 1 - k : r0 + taps - 1 - k + rows]
        return total.astype(BF16)

    xhalo_o[0] = conv_back(xcg, vk, 0, HALO)
    bhalo_o[0] = conv_back(bcg_s, sk, 0, HALO)
    for b in range(blocks):
        r0 = b * T
        xpg_o[0, r0 : r0 + T] = conv_back(xcg, vk, HALO + r0, T)
        bpg_o[0, r0 : r0 + T] = conv_back(bcg_s, sk, HALO + r0, T)

    @pl.when(step_at == seqs - 1)
    def _():
        rider.close()


def head_sums(mine, out, slots, send, recv):
    z = lax.axis_index("head")
    count = slots.shape[0]
    barrier = pltpu.get_barrier_semaphore()
    for d in range(1, count):
        pl.semaphore_signal(barrier, inc=1, device_id={"head": lax.rem(z + d, count)}, device_id_type=MESH)
    pl.semaphore_wait(barrier, count - 1)
    copies = []
    for d in range(1, count):
        copies.append(pltpu.make_async_remote_copy(
            src_ref=mine, dst_ref=slots.at[z], send_sem=send.at[d], recv_sem=recv.at[d],
            device_id={"head": lax.rem(z + d, count)}, device_id_type=MESH,
        ))
        copies[-1].start()
    slots[z] = mine[...]
    for copy in copies:
        copy.wait_recv()
    total = slots[0]
    for d in range(1, count):
        total = total + slots[d]
    out[...] = total
    for copy in copies:
        copy.wait_send()


class SmallSums:
    def __init__(self, rounds, acc, out, back, zback, done, sems, vec, vback, vsems):
        self.rounds = rounds
        self.acc, self.out, self.back, self.zback, self.done, self.sems = acc, out, back, zback, done, sems
        self.vec, self.vback, self.vsems = vec, vback, vsems
        self.me, self.z = lax.axis_index("seq"), lax.axis_index("head")
        self.stages = 2 * rounds + 2

    @staticmethod
    def scratch(rounds, rows, cols, vec_shape):
        half = pltpu.VMEM((rounds, rows // 2, cols), BF16)
        return [
            pltpu.VMEM((rows, cols), F32), half, half, pltpu.VMEM((4, rows >> rounds, cols), BF16), pltpu.VMEM((rows, cols), BF16),
            pltpu.SemaphoreType.DMA((4 * rounds + 8,)), pltpu.VMEM(vec_shape, F32), pltpu.VMEM((4,) + vec_shape, F32), pltpu.SemaphoreType.DMA((8,)),
        ]

    def partner(self, r):
        bit = 1 << r
        return self.me + bit - 2 * bit * (lax.div(self.me, bit) % 2)

    def start_of(self, r):
        rows = self.acc.shape[0]
        first = 0
        for k in range(r):
            first = first + (lax.div(self.me, 1 << k) % 2) * (rows >> (k + 1))
        return first, rows >> r

    def halving(self, r):
        size = self.acc.shape[0] >> (r + 1)
        return pltpu.make_async_remote_copy(
            src_ref=self.out.at[r, pl.ds(0, size)], dst_ref=self.back.at[r, pl.ds(0, size)],
            send_sem=self.sems.at[r], recv_sem=self.sems.at[self.rounds + r],
            device_id={"seq": self.partner(r)}, device_id_type=MESH,
        )

    def gathering(self, r, mine):
        first, size = self.start_of(r + 1)
        if not mine:
            first = first + size - 2 * size * (lax.div(self.me, 1 << r) % 2)
        at = pl.ds(pl.multiple_of(first, 16), size)
        return pltpu.make_async_remote_copy(
            src_ref=self.done.at[at], dst_ref=self.done.at[at],
            send_sem=self.sems.at[2 * self.rounds + r], recv_sem=self.sems.at[3 * self.rounds + r],
            device_id={"seq": self.partner(r)}, device_id_type=MESH,
        )

    def to_head(self, d, vec):
        src, dst, sems, base = (self.vec, self.vback, self.vsems, 0) if vec else (self.share(), self.zback, self.sems, 4 * self.rounds)
        return pltpu.make_async_remote_copy(
            src_ref=src, dst_ref=dst.at[self.z], send_sem=sems.at[base + d], recv_sem=sems.at[base + 4 + d],
            device_id={"head": lax.rem(self.z + d, 4)}, device_id_type=MESH,
        )

    def share(self):
        first, size = self.start_of(self.rounds)
        return self.done.at[pl.ds(pl.multiple_of(first, 16), size)]

    def push_half(self, r):
        first, size = self.start_of(r)
        half = size // 2
        theirs = first + half - half * (lax.div(self.me, 1 << r) % 2)
        self.out[r, pl.ds(0, half), :] = self.acc[pl.ds(pl.multiple_of(theirs, 16), half), :].astype(BF16)
        self.halving(r).start()

    def stage(self, k):
        rounds = self.rounds
        if k == 0:
            for d in range(1, 4):
                self.to_head(d, True).start()
            self.vback[self.z] = self.vec[...]
        if 0 < k <= rounds:
            r = k - 1
            copy = self.halving(r)
            copy.wait()
            first, size = self.start_of(r + 1)
            at = pl.ds(pl.multiple_of(first, 16), size)
            self.acc[at, :] = self.acc[at, :] + self.back[r, pl.ds(0, size), :].astype(F32)
        if k < rounds:
            self.push_half(k)
        if k == rounds:
            first, size = self.start_of(rounds)
            at = pl.ds(pl.multiple_of(first, 16), size)
            self.done[at, :] = self.acc[at, :].astype(BF16)
            for d in range(1, 4):
                self.to_head(d, False).start()
            self.zback[self.z] = self.done[at, :]
        if k == rounds + 1:
            for d in range(1, 4):
                self.to_head(d, False).wait()
                self.to_head(d, True).wait()
            first, size = self.start_of(rounds)
            at = pl.ds(pl.multiple_of(first, 16), size)
            total = self.zback[0].astype(F32)
            vec = self.vback[0]
            for d in range(1, 4):
                total = total + self.zback[d].astype(F32)
                vec = vec + self.vback[d]
            self.done[at, :] = total.astype(BF16)
            self.vec[...] = vec
            self.gathering(rounds - 1, True).start()
        if k > rounds + 1:
            r = rounds - 1 - (k - rounds - 2)
            self.gathering(r, True).wait_send()
            self.gathering(r, False).wait_recv()
            if r > 0:
                self.gathering(r - 1, True).start()


def finish(
    y, gate_grad, xpg, bpg, raw, tok, cot, rms, gate_w, value_w, state_w, step_w, ngain, small, state_grad, state_rows, y_all,
    result_o, tokens_grad_o, small_o, state_o,
    own, got, far, sa, sb, sc, sd, se, sf, yown, ygot, yfar, ta, tb, tc, td, te, tf, ylocal, rows, out, back, send, recv,
    s_acc, s_out, s_back, s_zback, s_done, s_sems, s_vec, s_vback, s_vsems,
    *, n, rounds, plan,
):
    i = pl.program_id(0)
    sums = SmallSums(rounds, s_acc, s_out, s_back, s_zback, s_done, s_sems, s_vec, s_vback, s_vsems)
    chain = Chain(own, got, far, (sa, sb, sc, sd, se, sf))
    rider = Rider(*plan, y_all, yown, ygot, yfar, (ta, tb, tc, td, te, tf), ylocal)
    me = lax.axis_index("seq")

    def partner(r):
        bit = 1 << r
        return me + bit - 2 * bit * (lax.div(me, bit) % 2)

    @pl.when(i == 0)
    def _():
        barrier = pltpu.get_barrier_semaphore()
        for r in range(rounds):
            pl.semaphore_signal(barrier, inc=1, device_id={"seq": partner(r)}, device_id_type=MESH)
        greet_head()
        pl.semaphore_wait(barrier, rounds + 3)
        rider.load()
        s_acc[...] = state_grad[...].astype(F32)
        s_vec[...] = state_rows[...]
        rows[0:8] = small[...]
        rows[8:] = jnp.zeros_like(rows[8:])

    rider.tick(i)
    for stage in (2, 1):
        k = i - stage * LAG

        @pl.when((k >= 0) & (k < n))
        def _():
            chain.onward(stage, k)

    @pl.when(i < n)
    def _():
        value = mm_t(gate_grad[...], gate_w[...]) + mm_t(xpg[...], value_w[...])
        own[i] = (value + (mm_t(bpg[...], state_w[...]) + mm_t(raw[...], step_w[...]))).astype(BF16)
        chain.inward(i)

    for stage in range(sums.stages):

        @pl.when(i == 1 + 2 * stage)
        def _():
            sums.stage(stage)

    k = i - 3 * LAG

    @pl.when(k >= 0)
    def _():
        grad = chain.total(k)
        rms_k = rms[:, 0:1]
        t = tok[...].astype(F32)
        width = t.shape[1]
        inv = lax.rsqrt(jnp.mean(t * t, axis=1, keepdims=True) + EPS)
        if rider.base > 0:

            @pl.when(k < rider.base)
            def _():
                result_o[...] = (t + y[...].astype(F32) * rms_k).astype(BF16)

        @pl.when(k >= rider.base)
        def _():
            result_o[...] = (t + rider.chain.total(k - rider.base) * rms_k).astype(BF16)

        scaled = grad * ngain[...]
        dot = jnp.sum(scaled * t, axis=1, keepdims=True) / width
        tokens_grad_o[...] = cot[...].astype(F32) + inv * scaled - t * (inv * inv * inv * dot)
        gain = jnp.sum(grad * t * inv, axis=0, keepdims=True)
        half = width // 2
        rows[8:9] += gain[:, :half]
        rows[9:10] += gain[:, half:]

    @pl.when(i == n + 3 * LAG - 1)
    def _():
        chain.drain(n)
        rider.drain()
        rows[16:24, 0 : s_vec.shape[1]] = s_vec[...]
        for r in range(rounds):
            copy = pltpu.make_async_remote_copy(
                src_ref=out.at[r], dst_ref=back.at[r], send_sem=send.at[r], recv_sem=recv.at[r],
                device_id={"seq": partner(r)}, device_id_type=MESH,
            )
            out[r] = rows[...]
            copy.start()
            copy.wait()
            rows[...] = rows[...] + back[r]
        state_o[...] = s_done[...]
        small_o[...] = rows[...]


def call(body, steps, seqs, ins, outs, scratch, flops, collective_id=None, carried=None):
    def cut(shape):
        rest = tuple(shape[1:])
        return pl.BlockSpec((1,) + rest, lambda s: (jnp.minimum(s, seqs - 1),) + (0,) * len(rest))

    def whole(shape):
        return pl.BlockSpec(tuple(shape), lambda s: (0,) * len(shape))

    in_specs = [cut(a.shape) if a.ndim >= 3 else whole(a.shape) for a in ins]
    out_specs = [cut(s) if c else whole(s) for s, _, c in outs]
    out_shape = [jax.ShapeDtypeStruct(s, d) for s, d, _ in outs]
    aliases = {}
    if carried is not None:
        aliases = {len(ins): len(outs)}
        in_specs.append(pl.BlockSpec(memory_space=pl.ANY))
        out_specs.append(pl.BlockSpec(memory_space=pl.ANY))
        out_shape.append(jax.ShapeDtypeStruct(carried.shape, carried.dtype))
        ins = ins + [carried]
    moved = sum(a.size * a.dtype.itemsize for a in ins)
    for s, d, _ in outs:
        size = jnp.dtype(d).itemsize
        for k in s:
            size *= k
        moved += size
    return pl.pallas_call(
        body,
        grid=(steps,),
        in_specs=in_specs,
        out_specs=out_specs,
        out_shape=out_shape,
        scratch_shapes=scratch,
        input_output_aliases=aliases,
        compiler_params=pltpu.CompilerParams(
            dimension_semantics=("arbitrary",), vmem_limit_bytes=60 * 1024 * 1024,
            collective_id=collective_id, has_side_effects=collective_id is not None,
        ),
        cost_estimate=pl.CostEstimate(flops=flops, bytes_accessed=moved, transcendentals=0),
    )(*ins)


def shards(
    tokens, norm_gain, gate_weight, value_weight, state_weight, step_weight, value_kernel, value_offset,
    state_kernel, state_offset, step_bias, log_rate, skip_gain, mixer_gain, out_weight, cotangent,
):
    seqs, length, width = tokens.shape
    flat = seqs * length
    inner = gate_weight.shape[1]
    heads = step_weight.shape[1]
    head_size = inner // heads
    n2 = state_weight.shape[1]
    n = n2 // 2
    taps = value_kernel.shape[0]
    blocks = length // T
    devices = lax.axis_size("seq")
    rounds = devices.bit_length() - 1
    assert devices == 1 << rounds
    inner_all = inner * lax.axis_size("head")

    halo = lax.ppermute(tokens[:, length - HALO :], "seq", [(i, i + 1) for i in range(devices - 1)])
    pad = LANES - heads
    rate_row = -jnp.exp(log_rate)
    rate = jnp.pad(rate_row, (0, pad))[None]
    bias = jnp.pad(step_bias, (0, pad))[None]
    step_w = jnp.pad(step_weight, ((0, 0), (0, pad)))
    skip = jnp.repeat(skip_gain, head_size)[None]
    gain = mixer_gain[None]
    one = (jnp.arange(inner)[None, :] // head_size == jnp.arange(LANES)[:, None]).astype(BF16)
    wide = jnp.concatenate([one, one], axis=0)
    tri = (jnp.arange(T)[:, None] >= jnp.arange(T)[None, :]).astype(BF16)
    vo, so = value_offset[None], state_offset[None]

    def big(cols, dtype, rows=length):
        return ((seqs, rows, cols), dtype, True)

    vmem = pltpu.VMEM
    ext = length + HALO
    (normed, gate, xext, bcext, sraw, xact, bcact, step, cum, lstart, pre, entry) = call(
        functools.partial(front, seqs=seqs, rounds=rounds), seqs + rounds, seqs,
        [tokens, halo, norm_gain[None], gate_weight, value_weight, state_weight, step_w,
         value_kernel, vo, state_kernel, so, bias, rate, wide, tri],
        [big(width, BF16), big(inner, F32), big(inner, BF16, ext), big(n2, BF16, ext), big(LANES, F32),
         big(inner, BF16), big(n2, BF16), big(LANES, F32), big(LANES, F32),
         ((seqs, blocks, n, inner), F32, True), big(LANES, F32, 8),
         ((seqs, n, inner), F32, False)],
        [vmem((ext, width), BF16), vmem((ext, inner), F32), vmem((ext, n2), F32), vmem((n, inner), F32),
         vmem((8, LANES), F32)] + Exchange.scratch(rounds, seqs, n, inner),
        2 * flat * width * (2 * inner + n2 + LANES), 1,
    )
    ssd, gn, y, sums = call(
        scan_out, seqs, seqs,
        [xact, bcact, step, cum, gate, lstart, entry, pre, cotangent, out_weight, gain, skip, wide],
        [big(inner, F32), big(inner, F32), big(width, BF16), ((seqs, 8, length), F32, True)],
        [vmem((length, inner), BF16)],
        4 * flat * width * inner,
    )
    group = lax.axis_size("head")
    sums = pl.pallas_call(
        head_sums,
        out_shape=jax.ShapeDtypeStruct(sums.shape, F32),
        in_specs=[pl.BlockSpec(memory_space=pltpu.VMEM)],
        out_specs=pl.BlockSpec(memory_space=pltpu.VMEM),
        scratch_shapes=[vmem((group,) + sums.shape, F32), pltpu.SemaphoreType.DMA((group,)), pltpu.SemaphoreType.DMA((group,))],
        compiler_params=pltpu.CompilerParams(collective_id=2, has_side_effects=True),
    )(sums)
    n_chunks = flat // CHUNK
    y = y.reshape(n_chunks, CHUNK, width)
    plan = (0, seqs * blocks + 2 * rounds, n_chunks)
    gnormed, gate_grad, xg, cumg, stepg, bcg, lend, rms, mgg, skg, after, y = call(
        functools.partial(back_one, inner_all=inner_all, seqs=seqs, rounds=rounds, plan=plan), seqs + rounds, seqs,
        [xact, bcact, step, cum, gate, ssd, gn, sums, lstart, entry, pre, gain, skip, wide],
        [big(inner, BF16), big(inner, BF16), big(inner, F32), big(LANES, F32), big(LANES, F32), big(n2, F32),
         ((seqs, blocks, n, inner), F32, True), big(LANES, F32),
         ((8, inner), F32, False), ((8, inner), F32, False), ((seqs, n, inner), F32, False)],
        [vmem((T, inner), F32), vmem((n, inner), F32), vmem((T, inner), BF16), vmem((n, inner), F32)]
        + Exchange.scratch(rounds, seqs, n, inner) + Rider.scratch(*plan, width),
        2 * flat * T * inner * 8, 3, y,
    )
    plan = (plan[0] + plan[1], seqs * blocks, n_chunks)
    xpg, xhalo, bpg, bhalo, raw, vkg, skgr, head_rows, y = call(
        functools.partial(back_two, seqs=seqs, plan=plan), seqs, seqs,
        [xact, bcact, xext, bcext, step, cum, sraw, xg, cumg, stepg, bcg, lstart, entry, lend, after, pre,
         value_kernel, vo, state_kernel, so, bias, rate, wide, tri],
        [big(inner, BF16), big(inner, BF16, HALO), big(n2, BF16), big(n2, BF16, HALO), big(LANES, BF16),
         ((8, inner), F32, False), ((8, n2), F32, False), ((8, LANES), F32, False)],
        [vmem((ext, inner), F32), vmem((ext, n2), F32), vmem((ext + HALO, inner), F32),
         vmem((ext + HALO, n2), F32)] + Rider.scratch(*plan, width),
        2 * flat * T * inner * 4, 5, y,
    )
    back = [(i + 1, i) for i in range(devices - 1)]
    xhalo, bhalo = lax.ppermute((xhalo, bhalo), "seq", back)
    xpg = xpg.at[:, length - HALO :].add(xhalo)
    bpg = bpg.at[:, length - HALO :].add(bhalo)

    def flatten(v):
        return v.reshape(flat, v.shape[-1])

    normed_f, xpg_f, bpg_f, raw_f, gg_f = [flatten(v) for v in (normed, xpg, bpg, raw, gate_grad)]
    out_weight_grad = t_mm(flatten(gnormed), flatten(cotangent)).astype(BF16)
    gate_weight_grad = t_mm(normed_f, gg_f).astype(BF16)
    value_weight_grad = t_mm(normed_f, xpg_f).astype(BF16)
    state_weight_grad = t_mm(normed_f, bpg_f).astype(BF16)
    step_weight_grad = t_mm(normed_f, raw_f).astype(BF16)
    head_row = jnp.pad(head_rows[:2].reshape(1, 2 * LANES), ((0, 0), (0, inner - 2 * LANES)))
    small = jnp.concatenate([vkg[: taps + 1], mgg[:1], skg[:1], head_row], axis=0)
    plan = (plan[0] + plan[1], n_chunks - plan[0] - plan[1] + 3 * LAG, n_chunks)

    def lagged(cols, lag):
        return pl.BlockSpec((CHUNK, cols), lambda i: (jnp.clip(i - lag, 0, n_chunks - 1), 0))

    def once(v):
        return pl.BlockSpec(v.shape, lambda i: (0,) * v.ndim, pipeline_mode=pl.Buffered(1))

    late = (gate_weight, value_weight, state_weight, step_w, norm_gain[None], small, state_weight_grad, skgr)
    result, tokens_grad, small, state_weight_grad = pl.pallas_call(
        functools.partial(finish, n=n_chunks, rounds=rounds, plan=plan),
        grid=(n_chunks + 3 * LAG,),
        in_specs=[lagged(width, 3 * LAG)]
        + [lagged(v.shape[1], 0) for v in (gg_f, xpg_f, bpg_f, raw_f)]
        + [lagged(width, 3 * LAG), lagged(width, 3 * LAG), lagged(LANES, 3 * LAG)]
        + [once(v) for v in late] + [pl.BlockSpec(memory_space=pl.ANY)],
        out_specs=[lagged(width, 3 * LAG), lagged(width, 3 * LAG), pl.BlockSpec((24, inner), lambda i: (0, 0)),
                   once(state_weight_grad)],
        out_shape=[
            jax.ShapeDtypeStruct((flat, width), BF16), jax.ShapeDtypeStruct((flat, width), F32),
            jax.ShapeDtypeStruct((24, inner), F32), jax.ShapeDtypeStruct(state_weight_grad.shape, BF16),
        ],
        scratch_shapes=Chain.scratch(n_chunks, CHUNK, width) + Rider.scratch(*plan, width) + [
            vmem((24, inner), F32), vmem((rounds, 24, inner), F32), vmem((rounds, 24, inner), F32),
            pltpu.SemaphoreType.DMA((rounds,)), pltpu.SemaphoreType.DMA((rounds,)),
        ] + SmallSums.scratch(rounds, width, n2, skgr.shape),
        compiler_params=pltpu.CompilerParams(
            dimension_semantics=("arbitrary",), vmem_limit_bytes=62 * 1024 * 1024, collective_id=4, has_side_effects=True
        ),
        cost_estimate=pl.CostEstimate(flops=10**11, bytes_accessed=10**8, transcendentals=0),
    )(y.reshape(flat, width), gg_f, xpg_f, bpg_f, raw_f, flatten(tokens), flatten(cotangent), flatten(rms),
      *late, y)
    result, tokens_grad = result.reshape(tokens.shape), tokens_grad.reshape(tokens.shape)
    vkg, mixer_gain_grad, skg, head_row = small[: taps + 1], small[taps + 1], small[taps + 2], small[taps + 3]
    norm_gain_grad = small[8:10].reshape(width)
    skgr = small[16:24, :n2]
    skip_gain_grad = jnp.sum(skg.reshape(heads, head_size), axis=1)
    step_bias_grad = head_row[:heads]
    log_rate_grad = head_row[LANES : LANES + heads] * rate_row
    out_weight_grad = lax.psum(out_weight_grad, "seq").astype(F32)
    gate_weight_grad = lax.psum(gate_weight_grad, "seq").astype(F32)
    value_weight_grad = lax.psum(value_weight_grad, "seq").astype(F32)
    step_weight_grad = lax.psum(step_weight_grad, "seq")[:, :heads].astype(F32)
    state_weight_grad = state_weight_grad.astype(F32)
    return (
        result, tokens_grad, norm_gain_grad, gate_weight_grad, value_weight_grad, state_weight_grad,
        step_weight_grad, vkg[:taps], vkg[taps], skgr[:taps], skgr[taps], step_bias_grad, log_rate_grad,
        skip_gain_grad, mixer_gain_grad, out_weight_grad,
    )


def solution(mesh):
    rows, cols, vec = P(None, "seq", None), P(None, "head"), P("head")
    in_specs = (rows, P(), cols, cols, P(), cols, cols, vec, P(), P(), vec, vec, vec, vec, P("head", None), rows)
    out_specs = (rows, rows, P(), cols, cols, P(), cols, cols, vec, P(), P(), vec, vec, vec, vec, P("head", None))
    return jax.shard_map(shards, mesh=mesh, in_specs=in_specs, out_specs=out_specs, check_vma=False)
```

```python
import functools

import jax
import jax.numpy as jnp
from jax import lax
from jax.experimental import pallas as pl
from jax.experimental.pallas import tpu as pltpu
from jax.sharding import PartitionSpec as P

EPS = 1e-05
T = 256
SUB = 128
HALO = 16
LANES = 128
F32 = jnp.float32
BF16 = jnp.bfloat16


def mm(a, b):
    return lax.dot_general(a, b, (((1,), (0,)), ((), ())), preferred_element_type=F32)


def mm_t(a, b):
    return lax.dot_general(a, b, (((1,), (1,)), ((), ())), preferred_element_type=F32)


def t_mm(a, b):
    return lax.dot_general(a, b, (((0,), (0,)), ((), ())), preferred_element_type=F32)


def split(v, parts):
    pieces = []
    for _ in range(parts):
        piece = v.astype(BF16)
        pieces.append(piece)
        v = v - piece.astype(F32)
    return pieces


def expand(v, wide):
    return mm(jnp.concatenate(split(v, 2), axis=1), wide)


def expand_row(v, wide):
    return expand(jnp.broadcast_to(v, (16, LANES)), wide)[0:1]


def head_sum(v, wide):
    hi, lo = split(v, 2)
    return mm_t(hi, wide[:LANES]) + mm_t(lo, wide[:LANES])


def exact_tri(tri, v):
    a, b, c = split(v, 3)
    return mm(tri, a) + (mm(tri, b) + mm(tri, c))


def sigmoid(v):
    return 0.5 * jnp.tanh(0.5 * v) + 0.5


def softplus(v):
    return jnp.maximum(v, 0.0) + jnp.log1p(jnp.exp(-jnp.abs(v)))


def lower():
    row = lax.broadcasted_iota(jnp.int32, (SUB, SUB), 0)
    col = lax.broadcasted_iota(jnp.int32, (SUB, SUB), 1)
    return row >= col


def tile(i):
    return slice(i * SUB, (i + 1) * SUB)


def tiles():
    return [(i, j) for i in range(T // SUB) for j in range(i + 1)]


def cross_tiles(cm, bm):
    found = {}
    for i, j in tiles():
        value = mm_t(cm[tile(i)], bm[tile(j)])
        found[i, j] = jnp.where(lower(), value, 0.0) if i == j else value
    return found


def decay_tile(cum, cum_t, h, i, j):
    gap = cum[tile(i), h : h + 1] - cum_t[h : h + 1, tile(j)]
    return jnp.exp(jnp.minimum(gap, 0.0) if i == j else gap)


def half_mask(rows):
    return lax.broadcasted_iota(jnp.int32, (rows, LANES), 1) < LANES // 2


def pair_rows(v):
    left = half_mask(v.shape[0])
    zero = jnp.zeros_like(v)
    return jnp.concatenate([jnp.where(left, v, zero), jnp.where(left, zero, v)], axis=0)


def rows_of(b):
    return pl.ds(pl.multiple_of(b * T, T), T)


MESH = pl.DeviceIdType.MESH
CHUNK = 64
LAG = 2


def greet_head():
    z = lax.axis_index("head")
    for d in range(1, 4):
        pl.semaphore_signal(
            pltpu.get_barrier_semaphore(), inc=1, device_id={"head": lax.rem(z + d, 4)}, device_id_type=MESH)


class Chain:
    def __init__(self, own, got, far, sems):
        z = lax.axis_index("head")
        self.end = (z == 0) | (z == 3)
        self.side = z + 1 - 2 * (z % 2)
        self.other = 3 - z
        self.own, self.got, self.far = own, got, far
        self.sems = sems

    @staticmethod
    def scratch(n, chunk, width):
        buffer = pltpu.VMEM((n, chunk, width), BF16)
        return [buffer, buffer, buffer] + [pltpu.SemaphoreType.DMA((n,))] * 6

    def copy(self, kind, k):
        src, dst, to = [(self.own, self.got, self.side), (self.own, self.far, self.other), (self.got, self.got, self.side)][kind]
        return pltpu.make_async_remote_copy(
            src_ref=src.at[k], dst_ref=dst.at[k],
            send_sem=self.sems[2 * kind].at[k], recv_sem=self.sems[2 * kind + 1].at[k],
            device_id={"head": to}, device_id_type=MESH,
        )

    def inward(self, k):
        @pl.when(self.end)
        def _():
            self.copy(0, k).start()

    def meet(self, stage, k):
        self.copy(stage, k).wait_recv()
        if stage == 0:
            self.own[k] = (self.own[k].astype(F32) + self.got[k].astype(F32)).astype(BF16)
        else:
            self.got[k] = (self.own[k].astype(F32) + self.far[k].astype(F32)).astype(BF16)

    def onward(self, stage, k):
        @pl.when(jnp.logical_not(self.end))
        def _():
            self.meet(stage - 1, k)
            self.copy(stage, k).start()

    def total(self, k):
        @pl.when(self.end)
        def _():
            self.copy(2, k).wait_recv()

        return self.got[k].astype(F32)

    def drain(self, n):
        def one(k, _):
            @pl.when(self.end)
            def _():
                self.copy(0, k).wait_send()

            @pl.when(jnp.logical_not(self.end))
            def _():
                self.copy(1, k).wait_send()
                self.copy(2, k).wait_send()

            return 0

        lax.fori_loop(0, n, one, 0)


class Rider:
    def __init__(self, first, ticks, count, hbm, own, got, far, sems, local):
        self.first, self.ticks, self.count = first, ticks, count
        self.base = max(first - 2 * LAG, 0)
        self.hbm, self.local = hbm, local
        self.chain = Chain(own, got, far, sems)

    @staticmethod
    def size(first, ticks, count):
        return min(first + ticks, count) - max(first - 2 * LAG, 0)

    @staticmethod
    def scratch(first, ticks, count, width):
        return Chain.scratch(Rider.size(first, ticks, count), CHUNK, width) + [pltpu.SemaphoreType.DMA((2,))]

    def span(self, stage):
        low = self.first - stage * LAG
        return max(low, 0), min(low + self.ticks, self.count)

    def load(self):
        size = self.size(self.first, self.ticks, self.count)
        own = pltpu.make_async_copy(self.hbm.at[pl.ds(self.base, size)], self.chain.own, self.local.at[0])
        own.start()
        ready = min(max(self.first - LAG, 0), self.count) - self.base
        if ready > 0:

            @pl.when(jnp.logical_not(self.chain.end))
            def _():
                got = pltpu.make_async_copy(
                    self.hbm.at[pl.ds(self.base, ready)], self.chain.got.at[pl.ds(0, ready)], self.local.at[1])
                got.start()
                got.wait()

        own.wait()

    def tick(self, t):
        chain = self.chain
        for stage in (2, 1, 0):
            low, high = self.span(stage)
            k = self.first - stage * LAG + t

            @pl.when((k >= low) & (k < high) & (t < self.ticks))
            def _():
                at = k - self.base
                if stage == 0:
                    chain.inward(at)
                else:
                    self.follow(stage, at, t >= LAG)

    def follow(self, stage, at, pending):
        chain = self.chain
        middle = jnp.logical_not(chain.end)

        @pl.when(middle & pending)
        def _():
            chain.meet(stage - 1, at)

        @pl.when(middle)
        def _():
            chain.copy(stage, at).start()

    def drain(self):
        chain = self.chain

        def each(stage):
            low, high = self.span(stage)
            lax.fori_loop(low - self.base, high - self.base, lambda k, _: (chain.copy(stage, k).wait_send(), 0)[1], 0)

        @pl.when(chain.end)
        def _():
            each(0)

        @pl.when(jnp.logical_not(chain.end))
        def _():
            each(1)
            each(2)

    def close(self):
        chain = self.chain
        middle = jnp.logical_not(chain.end)

        def each(low, high, do):
            if high > low:
                lax.fori_loop(low - self.base, high - self.base, lambda k, _: (do(k), 0)[1], 0)

        @pl.when(middle)
        def _():
            for stage in (0, 1):
                low, high = self.span(stage)
                started = max(self.first - stage * LAG + self.ticks - LAG, low)
                each(started, high, lambda k: chain.meet(stage, k))
            for stage in (1, 2):
                each(*self.span(stage), lambda k: chain.copy(stage, k).wait_send())

        @pl.when(chain.end)
        def _():
            each(*self.span(2), lambda k: chain.copy(2, k).wait_recv())
            each(*self.span(0), lambda k: chain.copy(0, k).wait_send())

        def store(ref, low, high):
            if high > low:
                at = pl.ds(low - self.base, high - low)
                copy = pltpu.make_async_copy(ref.at[at], self.hbm.at[pl.ds(low, high - low)], self.local.at[0])
                copy.start()
                copy.wait()

        @pl.when(middle)
        def _():
            reached = self.span(1)[1]
            store(chain.got, self.base, reached)
            store(chain.own, reached, self.span(0)[1])

        @pl.when(chain.end)
        def _():
            store(chain.got, *self.span(2))


class Exchange:
    def __init__(self, rounds, backward, total, before, logs, out, back, send, recv):
        self.rounds, self.backward = rounds, backward
        self.total, self.before, self.logs = total, before, logs
        self.out, self.back, self.send, self.recv = out, back, send, recv
        self.me = lax.axis_index("seq")

    def partner(self, r):
        bit = 1 << r
        return self.me + bit - 2 * bit * (lax.div(self.me, bit) % 2)

    def greet(self, with_head=False):
        barrier = pltpu.get_barrier_semaphore()
        for r in range(self.rounds):
            pl.semaphore_signal(barrier, inc=1, device_id={"seq": self.partner(r)}, device_id_type=MESH)
        if with_head:
            greet_head()
        pl.semaphore_wait(barrier, self.rounds + 3 * with_head)

    def copy(self, r, s):
        return pltpu.make_async_remote_copy(
            src_ref=self.out.at[r], dst_ref=self.back.at[r, s],
            send_sem=self.send.at[r], recv_sem=self.recv.at[r, s],
            device_id={"seq": self.partner(r)}, device_id_type=MESH,
        )

    def begin(self, s, state, log):
        self.total[s] = state
        self.before[s] = jnp.zeros_like(state)
        self.logs[s] = jnp.zeros(self.logs.shape[1:], F32)
        self.logs[s, 0:1] = log

    def push(self, r, s):
        n = self.total.shape[1]
        self.out[r, 0:n] = self.total[s].astype(BF16)
        hi, mid, lo = [v.astype(F32) for v in split(self.logs[s, 0:1], 3)]
        at = lax.broadcasted_iota(jnp.int32, (HALO, hi.shape[1]), 0)
        tail = jnp.where(at == 0, hi, jnp.where(at == 1, mid, jnp.where(at == 2, lo, 0.0)))
        self.out[r, n : n + HALO] = tail.astype(BF16)
        self.copy(r, s).start()

    def take(self, r, s):
        n = self.total.shape[1]
        copy = self.copy(r, s)
        copy.wait_recv()
        copy.wait_send()
        state = self.back[r, s, 0:n].astype(F32)
        tail = self.back[r, s, n : n + HALO].astype(F32)
        log = tail[0:1] + tail[1:2] + tail[2:3]
        upper = lax.div(self.me, 1 << r) % 2 == 1
        near = jnp.logical_not(upper) if self.backward else upper
        mine, theirs = self.logs[s, 0:1], self.logs[s, 1:2]
        self.before[s] = self.before[s] + jnp.where(near, jnp.exp(theirs), 0.0) * state
        self.logs[s, 1:2] = theirs + jnp.where(near, log, 0.0)
        own = jnp.where(near, 1.0, jnp.exp(log))
        other = jnp.where(near, jnp.exp(mine), 1.0)
        self.total[s] = own * self.total[s] + other * state
        self.logs[s, 0:1] = mine + log

    def advance(self, i, seqs):
        for r in reversed(range(self.rounds)):
            s = i - 1 - r

            @pl.when((s >= 0) & (s < seqs))
            def _():
                self.take(r, s)
                if r + 1 < self.rounds:
                    self.push(r + 1, s)

        @pl.when(i < seqs)
        def _():
            self.push(0, i)

    @staticmethod
    def scratch(rounds, seqs, n, inner):
        return [
            pltpu.VMEM((seqs, n, inner), F32), pltpu.VMEM((seqs, 8, inner), F32),
            pltpu.VMEM((rounds, n + HALO, inner), BF16), pltpu.VMEM((rounds, seqs, n + HALO, inner), BF16),
            pltpu.SemaphoreType.DMA((rounds,)), pltpu.SemaphoreType.DMA((rounds, seqs)),
        ]


def forward(
    tok, tok_all, cot, ngain, gate_w, value_w, state_w, step_w, vk, vo, sk, so, sbias, rate, wide, tri, out_w, mgain, skip,
    xext_o, bcext_o, sraw_o, pre_o, entry_o, sums_o,
    xact_h, bcact_h, gate_h, step_h, cum_h, lstart_h, normed_h, ssd_h, gn_h, y_h,
    xact, bcact, gate, step, cum, lstart, nx, ssd, gn, y_s, gm, xe, be, st, run, halo, mine, slots,
    kept_sems, slot_sems, halo_send, halo_recv, sum_send, sum_recv,
    total, logs, out, back, send, recv,
    yown, ygot, yfar, ta, tb, tc, td, te, tf, ylocal,
    *, seqs, rounds, plan,
):
    i = pl.program_id(0)
    s = i - rounds
    steps = seqs + rounds
    length = tok.shape[1]
    me, devices = lax.axis_index("seq"), lax.axis_size("seq")
    z = lax.axis_index("head")
    scan = Exchange(rounds, False, total, entry_o, logs, out, back, send, recv)
    rider = Rider(*plan, y_h, yown, ygot, yfar, (ta, tb, tc, td, te, tf), ylocal)
    kept = [(xact, xact_h), (bcact, bcact_h), (gate, gate_h), (step, step_h), (cum, cum_h), (lstart, lstart_h)]
    per_seq = length // CHUNK

    def halo_copy(q):
        return pltpu.make_async_remote_copy(
            src_ref=tok_all.at[q, pl.ds(length - HALO, HALO)], dst_ref=halo.at[q],
            send_sem=halo_send.at[q], recv_sem=halo_recv.at[q],
            device_id={"seq": lax.rem(me + 1, devices)}, device_id_type=MESH,
        )

    def keep(k, q):
        src, dst = kept[k]
        return pltpu.make_async_copy(src.at[q], dst.at[q], kept_sems.at[k, q])

    def normed_copy(q):
        return pltpu.make_async_copy(nx.at[pl.ds(HALO, length)], normed_h.at[q], slot_sems.at[0])

    def scan_copies(q):
        return [
            pltpu.make_async_copy(ssd.at[0], ssd_h.at[q], slot_sems.at[1]),
            pltpu.make_async_copy(gn.at[0], gn_h.at[q], slot_sems.at[2]),
        ]

    def y_copy(q, skip_rider):
        first = plan[1] if skip_rider else 0
        at = pl.ds(q * per_seq + first, per_seq - first)
        return pltpu.make_async_copy(y_s.at[pl.ds(first, per_seq - first)], y_h.at[at], slot_sems.at[3])

    def sum_copy(q, d):
        return pltpu.make_async_remote_copy(
            src_ref=mine.at[q], dst_ref=slots.at[q, z], send_sem=sum_send.at[q, d], recv_sem=sum_recv.at[q, d],
            device_id={"head": lax.rem(z + d, 4)}, device_id_type=MESH,
        )

    @pl.when(i == 0)
    def _():
        barrier = pltpu.get_barrier_semaphore()
        for d in range(1, devices):
            pl.semaphore_signal(barrier, inc=1, device_id={"seq": lax.rem(me + d, devices)}, device_id_type=MESH)
        greet_head()
        pl.semaphore_wait(barrier, devices - 1 + 3)

        @pl.when(me < devices - 1)
        def _():
            for q in range(seqs):
                halo_copy(q).start()

        @pl.when(me == 0)
        def _():
            halo[...] = jnp.zeros_like(halo)

    @pl.when(i < seqs)
    def _():
        @pl.when(i > 0)
        def _():
            normed_copy(i).wait()

        def arrive():
            @pl.when(me > 0)
            def _():
                halo_copy(i).wait_recv()

        one = pl.ds(i, 1)
        front_rows(
            tok, halo.at[one], ngain, gate_w, value_w, state_w, step_w, vk, vo, sk, so, sbias, rate, wide, tri,
            gate.at[one], xext_o, bcext_o, sraw_o, xact.at[one], bcact.at[one], step.at[one], cum.at[one],
            lstart.at[one], pre_o.at[one], nx, xe, be, st, run, arrive,
        )
        normed_copy(i).start()
        for k in range(len(kept)):
            keep(k, i).start()
        scan.begin(i, st[...], expand_row(run[0:1], wide[...]))

    scan.advance(i, seqs)

    @pl.when(s >= 0)
    def _():
        @pl.when(s > 0)
        def _():
            for copy in scan_copies(s):
                copy.wait()

        one = pl.ds(s, 1)
        scan_out(
            xact.at[one], bcact.at[one], step.at[one], cum.at[one], gate.at[one], lstart.at[one], entry_o.at[one],
            pre_o.at[one], cot, out_w, mgain, skip, wide, ssd, gn, mine.at[one], gm, lambda b: rider.tick((s - 1) * 2 + b),
        )
        for copy in scan_copies(s):
            copy.start()
        for d in range(1, 4):
            sum_copy(s, d).start()
        slots[s, z] = mine[s]

        @pl.when(s == 1)
        def _():
            y_copy(0, True).wait()

        @pl.when(s > 1)
        def _():
            y_copy(s, False).wait()

        for b in range(length // T):
            value = mm(gm[b * T : (b + 1) * T], out_w[...]).astype(BF16)
            y_s[b * T // CHUNK : (b + 1) * T // CHUNK] = value.reshape(T // CHUNK, CHUNK, value.shape[1])

        @pl.when(s == 0)
        def _():
            yown[...] = y_s[0 : plan[1]]
            y_copy(0, True).start()

        @pl.when(s > 0)
        def _():
            y_copy(s, False).start()

    @pl.when(i == steps - 1)
    def _():
        rider.close()
        for q in range(seqs):
            for d in range(1, 4):
                sum_copy(q, d).wait()
            sums_o[q] = (slots[q, 0] + slots[q, 1]) + (slots[q, 2] + slots[q, 3])
            for k in range(len(kept)):
                keep(k, q).wait()
        normed_copy(0).wait()
        for copy in scan_copies(0):
            copy.wait()
        y_copy(1, False).wait()

        @pl.when(me < devices - 1)
        def _():
            for q in range(seqs):
                halo_copy(q).wait_send()


def front_rows(
    tok, halo, ngain, gate_w, value_w, state_w, step_w, vk, vo, sk, so, sbias, rate, wide, tri,
    gate_o, xext_o, bcext_o, sraw_o, xact_o, bcact_o, step_o, cum_o, lstart_o, pre_o,
    nx, xe, be, st, run, arrive,
):
    length = tok.shape[1]
    blocks = length // T
    n = bcact_o.shape[2] // 2

    def norm(v):
        v = v.astype(F32)
        inv = lax.rsqrt(jnp.mean(v * v, axis=1, keepdims=True) + EPS)
        return (v * inv * ngain[...]).astype(BF16)

    def norm_rows(b, _):
        nx[pl.ds(pl.multiple_of(HALO + b * SUB, HALO), SUB), :] = norm(tok[0, pl.ds(pl.multiple_of(b * SUB, SUB), SUB), :])
        return 0

    lax.fori_loop(0, length // SUB, norm_rows, 0)
    gate_o[0] = mm(nx[HALO:], gate_w[...])
    sraw_o[0] = mm(nx[HALO:], step_w[...])
    arrive()
    nx[0:HALO] = norm(halo[0])
    x = mm(nx[...], value_w[...]).astype(BF16)
    xext_o[0] = x
    xe[...] = x.astype(F32)
    bc = mm(nx[...], state_w[...]).astype(BF16)
    bcext_o[0] = bc
    be[...] = bc.astype(F32)
    st[...] = jnp.zeros_like(st)
    run[...] = jnp.zeros_like(run)
    pre_o[0] = jnp.zeros_like(pre_o[0])
    for b in range(blocks):
        r0 = b * T
        r = slice(r0, r0 + T)
        taps = vk.shape[0]
        base = HALO - taps + 1
        xc = vo[...] + vk[0:1] * xe[r0 + base : r0 + base + T]
        bcc = so[...] + sk[0:1] * be[r0 + base : r0 + base + T]
        for k in range(1, taps):
            xc = xc + vk[k : k + 1] * xe[r0 + base + k : r0 + base + k + T]
            bcc = bcc + sk[k : k + 1] * be[r0 + base + k : r0 + base + k + T]
        xa = (xc * sigmoid(xc)).astype(BF16)
        bca = (bcc * sigmoid(bcc)).astype(BF16)
        xact_o[0, r, :] = xa
        bcact_o[0, r, :] = bca
        step = softplus(sraw_o[0, r, :] + sbias[...])
        cum = exact_tri(tri[...], step * rate[...])
        step_o[0, r, :] = step
        cum_o[0, r, :] = cum
        last = cum[T - 1 : T]
        weight = jnp.exp(last - cum) * step
        weighted = (xa.astype(F32) * expand(weight, wide[...])).astype(BF16)
        contrib = t_mm(bca[:, :n], weighted)
        lstart_o[0, b] = st[...]
        st[...] = expand_row(jnp.exp(last), wide[...]) * st[...] + contrib
        run[0:1] = run[0:1] + last
        pre_o[0, b + 1 : b + 2] = run[0:1]


def scan_out(
    xact, bcact, step_i, cum_i, gate, lstart, entry, pre, cot, out_w, mgain, skip, wide,
    ssd_o, gn_o, sums_o, gm, tick,
):
    length = xact.shape[1]
    blocks = length // T
    n = bcact.shape[2] // 2
    inner = xact.shape[2]
    gn_o[0] = mm_t(cot[0], out_w[...])

    def block(b, _):
        tick(b)
        r = rows_of(b)
        xa = xact[0, r, :]
        bca = bcact[0, r, :]
        bm, cm = bca[:, :n], bca[:, n:]
        cum = cum_i[0, r, :]
        cum_t = cum.T
        cross = cross_tiles(cm, bm)
        start = expand_row(jnp.exp(pre[0, pl.ds(b, 1), :]), wide[...]) * entry[0] + lstart[0, b]
        start = start.astype(BF16)
        grown = jnp.exp(cum)
        cm = cm.astype(F32)
        xs = (xa.astype(F32) * expand(step_i[0, r, :], wide[...])).astype(BF16)
        for p in range(inner // LANES):
            lanes = slice(p * LANES, (p + 1) * LANES)
            two = (2 * p, 2 * p + 1)
            start_two = pair_rows(start[:, lanes])
            xs_two = [pair_rows(xs[tile(j), lanes]) for j in range(T // SUB)]
            for i in range(T // SUB):
                left = [(cm[tile(i)] * grown[tile(i), h : h + 1]).astype(BF16) for h in two]
                right = [start_two]
                for j in range(i + 1):
                    left += [(cross[i, j] * decay_tile(cum, cum_t, h, i, j)).astype(BF16) for h in two]
                    right.append(xs_two[j])
                rows = pl.ds(pl.multiple_of(b * T + i * SUB, SUB), SUB)
                ssd_o[0, rows, lanes] = mm(jnp.concatenate(left, axis=1), jnp.concatenate(right, axis=0))
        mixed = ssd_o[0, r, :] + skip[...] * xa.astype(F32)
        g = gate[0, r, :]
        gated = mixed * (g * sigmoid(g))
        gg = gated * mgain[...]
        gm[r, :] = gg.astype(BF16)
        squares = jnp.sum(gated * gated, axis=1, keepdims=True)
        dots = jnp.sum(gg * gn_o[0, r, :], axis=1, keepdims=True)
        lane = lax.broadcasted_iota(jnp.int32, (T, LANES), 1)
        both = jnp.where(lane == 0, squares, jnp.where(lane == 1, dots, 0.0))
        sums_o[0, :, r] = both.T[0:8]
        return 0

    lax.fori_loop(0, blocks, block, 0)


def back_one(
    xact, bcact, step_i, cum_i, gate, ssd, gn, sums, lstart, entry, pre, mgain, skip, wide, y_in,
    gnormed_o, gate_grad_o, xg_o, cumg_o, stepg_o, bcg_o, lend_o, rms_o, mgg_o, skg_o, after_o, y_all,
    z, acc, dys, use, total, logs, out, back, send, recv,
    yown, ygot, yfar, ta, tb, tc, td, te, tf, ylocal,
    *, inner_all, seqs, rounds, plan,
):
    i = pl.program_id(0)
    blocks = xact.shape[1] // T
    scan = Exchange(rounds, True, total, after_o, logs, out, back, send, recv)
    rider = Rider(*plan, y_all, yown, ygot, yfar, (ta, tb, tc, td, te, tf), ylocal)

    @pl.when(i == 0)
    def _():
        scan.greet(with_head=True)
        rider.load()
        mgg_o[...] = jnp.zeros_like(mgg_o)
        skg_o[...] = jnp.zeros_like(skg_o)

    @pl.when(i < seqs)
    def _():
        back_one_rows(
            xact, bcact, step_i, cum_i, gate, ssd, gn, sums, lstart, entry, pre, mgain, skip, wide,
            gnormed_o, gate_grad_o, xg_o, cumg_o, stepg_o, bcg_o, lend_o, rms_o, mgg_o, skg_o,
            z, acc, dys, use, inner_all, lambda b: rider.tick(i * blocks + b),
        )
        scan.begin(i, acc[...], expand_row(pre[0, blocks : blocks + 1], wide[...]))

    scan.advance(i, seqs)

    @pl.when(i >= seqs)
    def _():
        for k in (0, 1):
            rider.tick(seqs * blocks + (i - seqs) * 2 + k)

    @pl.when(i == seqs + rounds - 1)
    def _():
        rider.close()


def back_one_rows(
    xact, bcact, step_i, cum_i, gate, ssd, gn, sums, lstart, entry, pre, mgain, skip, wide,
    gnormed_o, gate_grad_o, xg_o, cumg_o, stepg_o, bcg_o, lend_o, rms_o, mgg_o, skg_o,
    z, acc, dys, use, inner_all, tick,
):
    length = xact.shape[1]
    blocks = length // T
    n = bcact.shape[2] // 2
    inner = xact.shape[2]
    acc[...] = jnp.zeros_like(acc)

    def block(i, _):
        tick(i)
        b = blocks - 1 - i
        r = rows_of(b)
        sums_b = sums[0, :, r]
        columns = jnp.concatenate([sums_b, jnp.zeros((LANES - 8, T), F32)], axis=0).T
        for i in range(T // SUB):
            ri = pl.ds(pl.multiple_of(b * T + i * SUB, SUB), SUB)
            xa = xact[0, ri, :].astype(F32)
            rms = lax.rsqrt(columns[tile(i), 0:1] / inner_all + EPS)
            rms_o[0, ri, :] = jnp.broadcast_to(rms, (SUB, LANES))
            coef = rms * rms * rms * (columns[tile(i), 1:2] / inner_all)
            mixed = ssd[0, ri, :] + skip[...] * xa
            g = gate[0, ri, :]
            sg = sigmoid(g)
            gated = mixed * (g * sg)
            grad_norm = gn[0, ri, :]
            normalised = gated * rms
            gnormed_o[0, ri, :] = (normalised * mgain[...]).astype(BF16)
            mgg_o[0:1] += jnp.sum(grad_norm * normalised, axis=0, keepdims=True)
            grad_gated = rms * (grad_norm * mgain[...]) - gated * coef
            gate_grad_o[0, ri, :] = (grad_gated * mixed * (sg * (1.0 + g * (1.0 - sg)))).astype(BF16)
            grad_mixed = grad_gated * (g * sg)
            skg_o[0:1] += jnp.sum(grad_mixed * xa, axis=0, keepdims=True)
            xg_o[0, ri, :] = skip[...] * grad_mixed
            dys[tile(i)] = grad_mixed.astype(BF16)
        dy = dys[...]
        xa = xact[0, r, :].astype(F32)
        bca = bcact[0, r, :]
        bm, cm = bca[:, :n], bca[:, n:]
        cm32 = cm.astype(F32)
        cum = cum_i[0, r, :]
        cum_t = cum.T
        grown = jnp.exp(cum)
        start = expand_row(jnp.exp(pre[0, pl.ds(b, 1), :]), wide[...]) * entry[0] + lstart[0, b]
        start = start.astype(BF16)
        gdy_hi, gdy_lo = split(expand(grown, wide[...]) * dy.astype(F32), 2)
        c_grad = mm_t(gdy_hi, start) + mm_t(gdy_lo, start)
        step_wide = expand(step_i[0, r, :], wide[...])
        xs = (xa * step_wide).astype(BF16)
        cross = cross_tiles(cm, bm)
        cross_part = {ij: jnp.zeros((SUB, SUB), F32) for ij in tiles()}
        for p in range(inner // LANES):
            lanes = slice(p * LANES, (p + 1) * LANES)
            two = (2 * p, 2 * p + 1)
            scaled = [(cm32 * grown[:, h : h + 1]).astype(BF16) for h in two]
            used = None
            zs = [None] * (T // SUB)
            for i in range(T // SUB):
                dy_two = pair_rows(dy[tile(i), lanes])
                term = t_mm(jnp.concatenate([v[tile(i)] for v in scaled], axis=0), dy_two)
                used = term if used is None else used + term
                for j in range(i + 1):
                    mix_grad = mm_t(dy_two, xs[tile(j), lanes])
                    mix = []
                    for k, h in enumerate(two):
                        decay = decay_tile(cum, cum_t, h, i, j)
                        mix.append((cross[i, j] * decay).astype(BF16))
                        cross_part[i, j] = cross_part[i, j] + mix_grad[tile(k)] * decay
                    term = t_mm(jnp.concatenate(mix, axis=0), dy_two)
                    zs[j] = term if zs[j] is None else zs[j] + term
            use[:, lanes] = used
            for j in range(T // SUB):
                z[tile(j), lanes] = zs[j]
        lend_o[0, b] = acc[...]
        acc[...] = expand_row(grown[T - 1 : T], wide[...]) * acc[...] + use[...]
        rows = []
        for i in range(T // SUB):
            row = [jnp.where(lower(), cross_part[i, j], 0.0) if i == j else cross_part[i, j] for j in range(i + 1)]
            row += [jnp.zeros((SUB, SUB), F32)] * (T // SUB - 1 - i)
            rows.append(jnp.concatenate(row, axis=1))
        cross_low = jnp.concatenate(rows, axis=0).astype(BF16)
        bcg_o[0, r, 0:n] = t_mm(cross_low, cm)
        bcg_o[0, r, n : 2 * n] = c_grad + mm(cross_low, bm)
        zz = z[...]
        xg_o[0, r, :] = xg_o[0, r, :] + step_wide * zz
        cumg_o[0, r, :] = head_sum(dy.astype(F32) * ssd[0, r, :] - xs.astype(F32) * zz, wide[...])
        stepg_o[0, r, :] = head_sum(xa * zz, wide[...])
        return 0

    lax.fori_loop(0, blocks, block, 0)


def back_two(
    xact, bcact, xext, bcext, step_i, cum_i, sraw, xg, cumg, stepg, bcg, lstart, entry, lend, after, pre,
    vk, vo, sk, so, sbias, rate, wide, tri, y_in,
    xpg_o, xhalo_o, bpg_o, bhalo_o, raw_o, vkg_o, skg_o, heads_o, y_all,
    xe, be, xcg, bcg_s, yown, ygot, yfar, ta, tb, tc, td, te, tf, ylocal,
    *, seqs, plan,
):
    length = xact.shape[1]
    blocks = length // T
    n = bcact.shape[2] // 2
    taps = vk.shape[0]
    base = HALO - taps + 1
    step_at = pl.program_id(0)
    rider = Rider(*plan, y_all, yown, ygot, yfar, (ta, tb, tc, td, te, tf), ylocal)

    @pl.when(step_at == 0)
    def _():
        greet_head()
        pl.semaphore_wait(pltpu.get_barrier_semaphore(), 3)
        rider.load()
        vkg_o[...] = jnp.zeros_like(vkg_o)
        skg_o[...] = jnp.zeros_like(skg_o)
        heads_o[...] = jnp.zeros_like(heads_o)

    xe[...] = xext[0].astype(F32)
    be[...] = bcext[0].astype(F32)
    for ref in (xcg, bcg_s):
        ref[0:HALO] = jnp.zeros((HALO, ref.shape[1]), F32)
        ref[HALO + length :] = jnp.zeros((HALO, ref.shape[1]), F32)

    def conv_rows(ext, kernel, offset, r0):
        total = offset[...] + kernel[0:1] * ext[r0 + base : r0 + base + T]
        for k in range(1, taps):
            total = total + kernel[k : k + 1] * ext[r0 + base + k : r0 + base + k + T]
        sg = sigmoid(total)
        return sg * (1.0 + total * (1.0 - sg))

    def filter_grad(grad, ext, out, r0):
        for k in range(taps):
            out[k : k + 1] += jnp.sum(grad * ext[r0 + base + k : r0 + base + k + T], axis=0, keepdims=True)
        out[taps : taps + 1] += jnp.sum(grad, axis=0, keepdims=True)

    for b in range(blocks):
        rider.tick(step_at * blocks + b)
        r0 = b * T
        r = slice(r0, r0 + T)
        xa = xact[0, r, :].astype(F32)
        bm = bcact[0, r, 0:n]
        cum = cum_i[0, r, :]
        step = step_i[0, r, :]
        last = cum[T - 1 : T]
        start = expand_row(jnp.exp(pre[0, b : b + 1]), wide[...]) * entry[0] + lstart[0, b]
        suffix = jnp.exp(pre[0, blocks : blocks + 1] - pre[0, b + 1 : b + 2])
        end = expand_row(suffix, wide[...]) * after[0] + lend[0, b]
        end_low = end.astype(BF16)
        weighted_grad = mm(bm, end_low)
        reach = jnp.exp(last - cum)
        weight = reach * step
        weight_wide = expand(weight, wide[...])
        weighted = (xa * weight_wide).astype(BF16)
        bcg_b = bcg[0, r, :]
        b_total = bcg_b[:, 0:n] + mm_t(weighted, end_low)
        bc_total = jnp.concatenate([b_total, bcg_b[:, n:]], axis=1)
        w_grad = head_sum(weighted_grad * xa, wide[...])
        part = w_grad * weight
        product = jnp.broadcast_to(jnp.sum(end * start, axis=0, keepdims=True), (16, end.shape[1]))
        fade_grad = jnp.exp(last) * head_sum(product, wide[...])[0:1]
        at_last = lax.broadcasted_iota(jnp.int32, (T, LANES), 0) == T - 1
        extra = fade_grad + jnp.sum(part, axis=0, keepdims=True)
        cum_grad = cumg[0, r, :] - part + jnp.where(at_last, extra, 0.0)
        a, bb, c = split(cum_grad, 3)
        rise = t_mm(tri[...], a) + (t_mm(tri[...], bb) + t_mm(tri[...], c))
        step_grad = stepg[0, r, :] + w_grad * reach + rise * rate[...]
        raw = step_grad * sigmoid(sraw[0, r, :] + sbias[...])
        raw_o[0, r, :] = raw.astype(BF16)
        heads_o[0:1] += jnp.sum(raw, axis=0, keepdims=True)
        heads_o[1:2] += jnp.sum(rise * step, axis=0, keepdims=True)
        grad = (xg[0, r, :] + weighted_grad * weight_wide) * conv_rows(xe, vk, vo, r0)
        filter_grad(grad, xe, vkg_o, r0)
        xcg[HALO + r0 : HALO + r0 + T] = grad
        grad = bc_total * conv_rows(be, sk, so, r0)
        filter_grad(grad, be, skg_o, r0)
        bcg_s[HALO + r0 : HALO + r0 + T] = grad

    def conv_back(ref, kernel, r0, rows):
        total = kernel[0:1] * ref[r0 + taps - 1 : r0 + taps - 1 + rows]
        for k in range(1, taps):
            total = total + kernel[k : k + 1] * ref[r0 + taps - 1 - k : r0 + taps - 1 - k + rows]
        return total.astype(BF16)

    xhalo_o[0] = conv_back(xcg, vk, 0, HALO)
    bhalo_o[0] = conv_back(bcg_s, sk, 0, HALO)
    for b in range(blocks):
        r0 = b * T
        xpg_o[0, r0 : r0 + T] = conv_back(xcg, vk, HALO + r0, T)
        bpg_o[0, r0 : r0 + T] = conv_back(bcg_s, sk, HALO + r0, T)

    @pl.when(step_at == seqs - 1)
    def _():
        rider.close()


class SmallSums:
    def __init__(self, rounds, acc, out, back, zback, done, sems, vec, vback, vsems):
        self.rounds = rounds
        self.acc, self.out, self.back, self.zback, self.done, self.sems = acc, out, back, zback, done, sems
        self.vec, self.vback, self.vsems = vec, vback, vsems
        self.me, self.z = lax.axis_index("seq"), lax.axis_index("head")
        self.stages = 2 * rounds + 2

    @staticmethod
    def scratch(rounds, rows, cols, vec_shape):
        half = pltpu.VMEM((rounds, rows // 2, cols), BF16)
        return [
            pltpu.VMEM((rows, cols), F32), half, half, pltpu.VMEM((4, rows >> rounds, cols), BF16), pltpu.VMEM((rows, cols), BF16),
            pltpu.SemaphoreType.DMA((4 * rounds + 8,)), pltpu.VMEM(vec_shape, F32), pltpu.VMEM((4,) + vec_shape, F32), pltpu.SemaphoreType.DMA((8,)),
        ]

    def partner(self, r):
        bit = 1 << r
        return self.me + bit - 2 * bit * (lax.div(self.me, bit) % 2)

    def start_of(self, r):
        rows = self.acc.shape[0]
        first = 0
        for k in range(r):
            first = first + (lax.div(self.me, 1 << k) % 2) * (rows >> (k + 1))
        return first, rows >> r

    def halving(self, r):
        size = self.acc.shape[0] >> (r + 1)
        return pltpu.make_async_remote_copy(
            src_ref=self.out.at[r, pl.ds(0, size)], dst_ref=self.back.at[r, pl.ds(0, size)],
            send_sem=self.sems.at[r], recv_sem=self.sems.at[self.rounds + r],
            device_id={"seq": self.partner(r)}, device_id_type=MESH,
        )

    def gathering(self, r, mine):
        first, size = self.start_of(r + 1)
        if not mine:
            first = first + size - 2 * size * (lax.div(self.me, 1 << r) % 2)
        at = pl.ds(pl.multiple_of(first, 16), size)
        return pltpu.make_async_remote_copy(
            src_ref=self.done.at[at], dst_ref=self.done.at[at],
            send_sem=self.sems.at[2 * self.rounds + r], recv_sem=self.sems.at[3 * self.rounds + r],
            device_id={"seq": self.partner(r)}, device_id_type=MESH,
        )

    def to_head(self, d, vec):
        src, dst, sems, base = (self.vec, self.vback, self.vsems, 0) if vec else (self.share(), self.zback, self.sems, 4 * self.rounds)
        return pltpu.make_async_remote_copy(
            src_ref=src, dst_ref=dst.at[self.z], send_sem=sems.at[base + d], recv_sem=sems.at[base + 4 + d],
            device_id={"head": lax.rem(self.z + d, 4)}, device_id_type=MESH,
        )

    def share(self):
        first, size = self.start_of(self.rounds)
        return self.done.at[pl.ds(pl.multiple_of(first, 16), size)]

    def push_half(self, r):
        first, size = self.start_of(r)
        half = size // 2
        theirs = first + half - half * (lax.div(self.me, 1 << r) % 2)
        self.out[r, pl.ds(0, half), :] = self.acc[pl.ds(pl.multiple_of(theirs, 16), half), :].astype(BF16)
        self.halving(r).start()

    def stage(self, k):
        rounds = self.rounds
        if k == 0:
            for d in range(1, 4):
                self.to_head(d, True).start()
            self.vback[self.z] = self.vec[...]
        if 0 < k <= rounds:
            r = k - 1
            copy = self.halving(r)
            copy.wait()
            first, size = self.start_of(r + 1)
            at = pl.ds(pl.multiple_of(first, 16), size)
            self.acc[at, :] = self.acc[at, :] + self.back[r, pl.ds(0, size), :].astype(F32)
        if k < rounds:
            self.push_half(k)
        if k == rounds:
            first, size = self.start_of(rounds)
            at = pl.ds(pl.multiple_of(first, 16), size)
            self.done[at, :] = self.acc[at, :].astype(BF16)
            for d in range(1, 4):
                self.to_head(d, False).start()
            self.zback[self.z] = self.done[at, :]
        if k == rounds + 1:
            for d in range(1, 4):
                self.to_head(d, False).wait()
                self.to_head(d, True).wait()
            first, size = self.start_of(rounds)
            at = pl.ds(pl.multiple_of(first, 16), size)
            total = self.zback[0].astype(F32)
            vec = self.vback[0]
            for d in range(1, 4):
                total = total + self.zback[d].astype(F32)
                vec = vec + self.vback[d]
            self.done[at, :] = total.astype(BF16)
            self.vec[...] = vec
            self.gathering(rounds - 1, True).start()
        if k > rounds + 1:
            r = rounds - 1 - (k - rounds - 2)
            self.gathering(r, True).wait_send()
            self.gathering(r, False).wait_recv()
            if r > 0:
                self.gathering(r - 1, True).start()


def finish(
    y, gate_grad, xpg, bpg, raw, tok, cot, rms, gate_w, value_w, state_w, step_w, ngain, small, state_grad, state_rows, y_all,
    result_o, tokens_grad_o, small_o, state_o,
    own, got, far, sa, sb, sc, sd, se, sf, yown, ygot, yfar, ta, tb, tc, td, te, tf, ylocal, rows, out, back, send, recv,
    s_acc, s_out, s_back, s_zback, s_done, s_sems, s_vec, s_vback, s_vsems,
    *, n, rounds, plan,
):
    i = pl.program_id(0)
    sums = SmallSums(rounds, s_acc, s_out, s_back, s_zback, s_done, s_sems, s_vec, s_vback, s_vsems)
    chain = Chain(own, got, far, (sa, sb, sc, sd, se, sf))
    rider = Rider(*plan, y_all, yown, ygot, yfar, (ta, tb, tc, td, te, tf), ylocal)
    me = lax.axis_index("seq")

    def partner(r):
        bit = 1 << r
        return me + bit - 2 * bit * (lax.div(me, bit) % 2)

    @pl.when(i == 0)
    def _():
        barrier = pltpu.get_barrier_semaphore()
        for r in range(rounds):
            pl.semaphore_signal(barrier, inc=1, device_id={"seq": partner(r)}, device_id_type=MESH)
        greet_head()
        pl.semaphore_wait(barrier, rounds + 3)
        rider.load()
        s_acc[...] = state_grad[...].astype(F32)
        s_vec[...] = state_rows[...]
        rows[0:8] = small[...]
        rows[8:] = jnp.zeros_like(rows[8:])

    rider.tick(i)
    for stage in (2, 1):
        k = i - stage * LAG

        @pl.when((k >= 0) & (k < n))
        def _():
            chain.onward(stage, k)

    @pl.when(i < n)
    def _():
        value = mm_t(gate_grad[...], gate_w[...]) + mm_t(xpg[...], value_w[...])
        own[i] = (value + (mm_t(bpg[...], state_w[...]) + mm_t(raw[...], step_w[...]))).astype(BF16)
        chain.inward(i)

    for stage in range(sums.stages):

        @pl.when(i == 1 + 2 * stage)
        def _():
            sums.stage(stage)

    k = i - 3 * LAG

    @pl.when(k >= 0)
    def _():
        grad = chain.total(k)
        rms_k = rms[:, 0:1]
        t = tok[...].astype(F32)
        width = t.shape[1]
        inv = lax.rsqrt(jnp.mean(t * t, axis=1, keepdims=True) + EPS)
        if rider.base > 0:

            @pl.when(k < rider.base)
            def _():
                result_o[...] = (t + y[...].astype(F32) * rms_k).astype(BF16)

        @pl.when(k >= rider.base)
        def _():
            result_o[...] = (t + rider.chain.total(k - rider.base) * rms_k).astype(BF16)

        scaled = grad * ngain[...]
        dot = jnp.sum(scaled * t, axis=1, keepdims=True) / width
        tokens_grad_o[...] = cot[...].astype(F32) + inv * scaled - t * (inv * inv * inv * dot)
        gain = jnp.sum(grad * t * inv, axis=0, keepdims=True)
        half = width // 2
        rows[8:9] += gain[:, :half]
        rows[9:10] += gain[:, half:]

    @pl.when(i == n + 3 * LAG - 1)
    def _():
        chain.drain(n)
        rider.drain()
        rows[16:24, 0 : s_vec.shape[1]] = s_vec[...]
        for r in range(rounds):
            copy = pltpu.make_async_remote_copy(
                src_ref=out.at[r], dst_ref=back.at[r], send_sem=send.at[r], recv_sem=recv.at[r],
                device_id={"seq": partner(r)}, device_id_type=MESH,
            )
            out[r] = rows[...]
            copy.start()
            copy.wait()
            rows[...] = rows[...] + back[r]
        state_o[...] = s_done[...]
        small_o[...] = rows[...]


def call(body, steps, seqs, ins, outs, scratch, flops, collective_id=None, carried=None):
    def cut(shape):
        rest = tuple(shape[1:])
        return pl.BlockSpec((1,) + rest, lambda s: (jnp.minimum(s, seqs - 1),) + (0,) * len(rest))

    def whole(shape):
        return pl.BlockSpec(tuple(shape), lambda s: (0,) * len(shape))

    in_specs = [cut(a.shape) if a.ndim >= 3 else whole(a.shape) for a in ins]
    out_specs = [cut(s) if c else whole(s) for s, _, c in outs]
    out_shape = [jax.ShapeDtypeStruct(s, d) for s, d, _ in outs]
    aliases = {}
    if carried is not None:
        aliases = {len(ins): len(outs)}
        in_specs.append(pl.BlockSpec(memory_space=pl.ANY))
        out_specs.append(pl.BlockSpec(memory_space=pl.ANY))
        out_shape.append(jax.ShapeDtypeStruct(carried.shape, carried.dtype))
        ins = ins + [carried]
    moved = sum(a.size * a.dtype.itemsize for a in ins)
    for s, d, _ in outs:
        size = jnp.dtype(d).itemsize
        for k in s:
            size *= k
        moved += size
    return pl.pallas_call(
        body,
        grid=(steps,),
        in_specs=in_specs,
        out_specs=out_specs,
        out_shape=out_shape,
        scratch_shapes=scratch,
        input_output_aliases=aliases,
        compiler_params=pltpu.CompilerParams(
            dimension_semantics=("arbitrary",), vmem_limit_bytes=60 * 1024 * 1024,
            collective_id=collective_id, has_side_effects=collective_id is not None,
        ),
        cost_estimate=pl.CostEstimate(flops=flops, bytes_accessed=moved, transcendentals=0),
    )(*ins)


def shards(
    tokens, norm_gain, gate_weight, value_weight, state_weight, step_weight, value_kernel, value_offset,
    state_kernel, state_offset, step_bias, log_rate, skip_gain, mixer_gain, out_weight, cotangent,
):
    seqs, length, width = tokens.shape
    flat = seqs * length
    inner = gate_weight.shape[1]
    heads = step_weight.shape[1]
    head_size = inner // heads
    n2 = state_weight.shape[1]
    n = n2 // 2
    taps = value_kernel.shape[0]
    blocks = length // T
    devices = lax.axis_size("seq")
    rounds = devices.bit_length() - 1
    assert devices == 1 << rounds
    inner_all = inner * lax.axis_size("head")

    pad = LANES - heads
    rate_row = -jnp.exp(log_rate)
    rate = jnp.pad(rate_row, (0, pad))[None]
    bias = jnp.pad(step_bias, (0, pad))[None]
    step_w = jnp.pad(step_weight, ((0, 0), (0, pad)))
    skip = jnp.repeat(skip_gain, head_size)[None]
    gain = mixer_gain[None]
    one = (jnp.arange(inner)[None, :] // head_size == jnp.arange(LANES)[:, None]).astype(BF16)
    wide = jnp.concatenate([one, one], axis=0)
    tri = (jnp.arange(T)[:, None] >= jnp.arange(T)[None, :]).astype(BF16)
    vo, so = value_offset[None], state_offset[None]

    def big(cols, dtype, rows=length):
        return ((seqs, rows, cols), dtype, True)

    vmem = pltpu.VMEM
    ext = length + HALO
    n_chunks = flat // CHUNK
    steps = seqs + rounds
    plan = (0, min(2 * (seqs - 1), length // CHUNK), n_chunks)
    dma = pltpu.SemaphoreType.DMA

    def block(shape, lag):
        return pl.BlockSpec((1,) + shape, lambda i: (jnp.clip(i - lag, 0, seqs - 1), 0, 0))

    def once(v):
        return pl.BlockSpec(v.shape, lambda i: (0,) * len(v.shape), pipeline_mode=pl.Buffered(1))

    def shape_of(cols, dtype, rows=length):
        return jax.ShapeDtypeStruct((seqs, rows, cols), dtype)

    fixed = (norm_gain[None], gate_weight, value_weight, state_weight, step_w, value_kernel, vo, state_kernel, so, bias, rate,
             wide, tri, out_weight, gain, skip)
    held = (shape_of(LANES, F32, 8), shape_of(inner, F32, n), shape_of(length, F32, 8))
    anywhere = pl.BlockSpec(memory_space=pl.ANY)
    (xext, bcext, sraw, pre, entry, sums, xact, bcact, gate, step, cum, lstart, normed, ssd, gn, y) = pl.pallas_call(
        functools.partial(forward, seqs=seqs, rounds=rounds, plan=plan),
        grid=(steps,),
        in_specs=[block((length, width), 0), anywhere, block((length, width), rounds)] + [once(v) for v in fixed],
        out_specs=[block((ext, inner), 0), block((ext, n2), 0), block((length, LANES), 0)] + [once(v) for v in held] + [anywhere] * 10,
        out_shape=[shape_of(inner, BF16, ext), shape_of(n2, BF16, ext), shape_of(LANES, F32), *held,
                   shape_of(inner, BF16), shape_of(n2, BF16), shape_of(inner, F32), shape_of(LANES, F32), shape_of(LANES, F32),
                   jax.ShapeDtypeStruct((seqs, blocks, n, inner), F32), shape_of(width, BF16), shape_of(inner, F32),
                   shape_of(inner, F32), jax.ShapeDtypeStruct((n_chunks, CHUNK, width), BF16)],
        scratch_shapes=[
            vmem((seqs, length, inner), BF16), vmem((seqs, length, n2), BF16), vmem((seqs, length, inner), F32),
            vmem((seqs, length, LANES), F32), vmem((seqs, length, LANES), F32), vmem((seqs, blocks, n, inner), F32),
            vmem((ext, width), BF16), vmem((1, length, inner), F32), vmem((1, length, inner), F32),
            vmem((length // CHUNK, CHUNK, width), BF16), vmem((length, inner), BF16),
            vmem((ext, inner), F32), vmem((ext, n2), F32), vmem((n, inner), F32), vmem((8, LANES), F32),
            vmem((seqs, HALO, width), BF16), vmem((seqs, 8, length), F32), vmem((seqs, 4, 8, length), F32),
            dma((6, seqs)), dma((4,)), dma((seqs,)), dma((seqs,)), dma((seqs, 4)), dma((seqs, 4)),
        ] + Exchange.scratch(rounds, seqs, n, inner) + Rider.scratch(*plan, width),
        compiler_params=pltpu.CompilerParams(
            dimension_semantics=("arbitrary",), vmem_limit_bytes=62 * 1024 * 1024, collective_id=1, has_side_effects=True
        ),
        cost_estimate=pl.CostEstimate(flops=2 * flat * width * 4 * inner, bytes_accessed=10**8, transcendentals=0),
    )(tokens, tokens, cotangent, *fixed)
    plan = (plan[1], seqs * blocks + 2 * rounds, n_chunks)
    gnormed, gate_grad, xg, cumg, stepg, bcg, lend, rms, mgg, skg, after, y = call(
        functools.partial(back_one, inner_all=inner_all, seqs=seqs, rounds=rounds, plan=plan), seqs + rounds, seqs,
        [xact, bcact, step, cum, gate, ssd, gn, sums, lstart, entry, pre, gain, skip, wide],
        [big(inner, BF16), big(inner, BF16), big(inner, F32), big(LANES, F32), big(LANES, F32), big(n2, F32),
         ((seqs, blocks, n, inner), F32, True), big(LANES, F32),
         ((8, inner), F32, False), ((8, inner), F32, False), ((seqs, n, inner), F32, False)],
        [vmem((T, inner), F32), vmem((n, inner), F32), vmem((T, inner), BF16), vmem((n, inner), F32)]
        + Exchange.scratch(rounds, seqs, n, inner) + Rider.scratch(*plan, width),
        2 * flat * T * inner * 8, 3, y,
    )
    plan = (plan[0] + plan[1], seqs * blocks, n_chunks)
    xpg, xhalo, bpg, bhalo, raw, vkg, skgr, head_rows, y = call(
        functools.partial(back_two, seqs=seqs, plan=plan), seqs, seqs,
        [xact, bcact, xext, bcext, step, cum, sraw, xg, cumg, stepg, bcg, lstart, entry, lend, after, pre,
         value_kernel, vo, state_kernel, so, bias, rate, wide, tri],
        [big(inner, BF16), big(inner, BF16, HALO), big(n2, BF16), big(n2, BF16, HALO), big(LANES, BF16),
         ((8, inner), F32, False), ((8, n2), F32, False), ((8, LANES), F32, False)],
        [vmem((ext, inner), F32), vmem((ext, n2), F32), vmem((ext + HALO, inner), F32),
         vmem((ext + HALO, n2), F32)] + Rider.scratch(*plan, width),
        2 * flat * T * inner * 4, 5, y,
    )
    back = [(i + 1, i) for i in range(devices - 1)]
    xhalo, bhalo = lax.ppermute((xhalo, bhalo), "seq", back)
    xpg = xpg.at[:, length - HALO :].add(xhalo)
    bpg = bpg.at[:, length - HALO :].add(bhalo)

    def flatten(v):
        return v.reshape(flat, v.shape[-1])

    normed_f, xpg_f, bpg_f, raw_f, gg_f = [flatten(v) for v in (normed, xpg, bpg, raw, gate_grad)]
    out_weight_grad = t_mm(flatten(gnormed), flatten(cotangent)).astype(BF16)
    gate_weight_grad = t_mm(normed_f, gg_f).astype(BF16)
    value_weight_grad = t_mm(normed_f, xpg_f).astype(BF16)
    state_weight_grad = t_mm(normed_f, bpg_f).astype(BF16)
    step_weight_grad = t_mm(normed_f, raw_f).astype(BF16)
    head_row = jnp.pad(head_rows[:2].reshape(1, 2 * LANES), ((0, 0), (0, inner - 2 * LANES)))
    small = jnp.concatenate([vkg[: taps + 1], mgg[:1], skg[:1], head_row], axis=0)
    plan = (plan[0] + plan[1], n_chunks - plan[0] - plan[1] + 3 * LAG, n_chunks)

    def lagged(cols, lag):
        return pl.BlockSpec((CHUNK, cols), lambda i: (jnp.clip(i - lag, 0, n_chunks - 1), 0))

    late = (gate_weight, value_weight, state_weight, step_w, norm_gain[None], small, state_weight_grad, skgr)
    result, tokens_grad, small, state_weight_grad = pl.pallas_call(
        functools.partial(finish, n=n_chunks, rounds=rounds, plan=plan),
        grid=(n_chunks + 3 * LAG,),
        in_specs=[lagged(width, 3 * LAG)]
        + [lagged(v.shape[1], 0) for v in (gg_f, xpg_f, bpg_f, raw_f)]
        + [lagged(width, 3 * LAG), lagged(width, 3 * LAG), lagged(LANES, 3 * LAG)]
        + [once(v) for v in late] + [pl.BlockSpec(memory_space=pl.ANY)],
        out_specs=[lagged(width, 3 * LAG), lagged(width, 3 * LAG), pl.BlockSpec((24, inner), lambda i: (0, 0)),
                   once(state_weight_grad)],
        out_shape=[
            jax.ShapeDtypeStruct((flat, width), BF16), jax.ShapeDtypeStruct((flat, width), F32),
            jax.ShapeDtypeStruct((24, inner), F32), jax.ShapeDtypeStruct(state_weight_grad.shape, BF16),
        ],
        scratch_shapes=Chain.scratch(n_chunks, CHUNK, width) + Rider.scratch(*plan, width) + [
            vmem((24, inner), F32), vmem((rounds, 24, inner), F32), vmem((rounds, 24, inner), F32),
            pltpu.SemaphoreType.DMA((rounds,)), pltpu.SemaphoreType.DMA((rounds,)),
        ] + SmallSums.scratch(rounds, width, n2, skgr.shape),
        compiler_params=pltpu.CompilerParams(
            dimension_semantics=("arbitrary",), vmem_limit_bytes=62 * 1024 * 1024, collective_id=4, has_side_effects=True
        ),
        cost_estimate=pl.CostEstimate(flops=10**11, bytes_accessed=10**8, transcendentals=0),
    )(y.reshape(flat, width), gg_f, xpg_f, bpg_f, raw_f, flatten(tokens), flatten(cotangent), flatten(rms),
      *late, y)
    result, tokens_grad = result.reshape(tokens.shape), tokens_grad.reshape(tokens.shape)
    vkg, mixer_gain_grad, skg, head_row = small[: taps + 1], small[taps + 1], small[taps + 2], small[taps + 3]
    norm_gain_grad = small[8:10].reshape(width)
    skgr = small[16:24, :n2]
    skip_gain_grad = jnp.sum(skg.reshape(heads, head_size), axis=1)
    step_bias_grad = head_row[:heads]
    log_rate_grad = head_row[LANES : LANES + heads] * rate_row
    out_weight_grad = lax.psum(out_weight_grad, "seq").astype(F32)
    gate_weight_grad = lax.psum(gate_weight_grad, "seq").astype(F32)
    value_weight_grad = lax.psum(value_weight_grad, "seq").astype(F32)
    step_weight_grad = lax.psum(step_weight_grad, "seq")[:, :heads].astype(F32)
    state_weight_grad = state_weight_grad.astype(F32)
    return (
        result, tokens_grad, norm_gain_grad, gate_weight_grad, value_weight_grad, state_weight_grad,
        step_weight_grad, vkg[:taps], vkg[taps], skgr[:taps], skgr[taps], step_bias_grad, log_rate_grad,
        skip_gain_grad, mixer_gain_grad, out_weight_grad,
    )


def solution(mesh):
    rows, cols, vec = P(None, "seq", None), P(None, "head"), P("head")
    in_specs = (rows, P(), cols, cols, P(), cols, cols, vec, P(), P(), vec, vec, vec, vec, P("head", None), rows)
    out_specs = (rows, rows, P(), cols, cols, P(), cols, cols, vec, P(), P(), vec, vec, vec, vec, P("head", None))
    return jax.shard_map(shards, mesh=mesh, in_specs=in_specs, out_specs=out_specs, check_vma=False)
```

```python
import functools

import jax
import jax.numpy as jnp
from jax import lax
from jax.experimental import pallas as pl
from jax.experimental.pallas import tpu as pltpu
from jax.sharding import PartitionSpec as P

EPS = 1e-05
T = 256
SUB = 128
HALO = 16
LANES = 128
F32 = jnp.float32
BF16 = jnp.bfloat16


def mm(a, b):
    return lax.dot_general(a, b, (((1,), (0,)), ((), ())), preferred_element_type=F32)


def mm_t(a, b):
    return lax.dot_general(a, b, (((1,), (1,)), ((), ())), preferred_element_type=F32)


def t_mm(a, b):
    return lax.dot_general(a, b, (((0,), (0,)), ((), ())), preferred_element_type=F32)


def split(v, parts):
    pieces = []
    for _ in range(parts):
        piece = v.astype(BF16)
        pieces.append(piece)
        v = v - piece.astype(F32)
    return pieces


def expand(v, wide):
    return mm(jnp.concatenate(split(v, 2), axis=1), wide)


def expand_row(v, wide):
    return expand(jnp.broadcast_to(v, (16, LANES)), wide)[0:1]


def head_sum(v, wide):
    hi, lo = split(v, 2)
    return mm_t(hi, wide[:LANES]) + mm_t(lo, wide[:LANES])


def exact_tri(tri, v):
    a, b, c = split(v, 3)
    return mm(tri, a) + (mm(tri, b) + mm(tri, c))


def sigmoid(v):
    return 0.5 * jnp.tanh(0.5 * v) + 0.5


def softplus(v):
    return jnp.maximum(v, 0.0) + jnp.log1p(jnp.exp(-jnp.abs(v)))


def lower():
    row = lax.broadcasted_iota(jnp.int32, (SUB, SUB), 0)
    col = lax.broadcasted_iota(jnp.int32, (SUB, SUB), 1)
    return row >= col


def tile(i):
    return slice(i * SUB, (i + 1) * SUB)


def tiles():
    return [(i, j) for i in range(T // SUB) for j in range(i + 1)]


def cross_tiles(cm, bm):
    found = {}
    for i, j in tiles():
        value = mm_t(cm[tile(i)], bm[tile(j)])
        found[i, j] = jnp.where(lower(), value, 0.0) if i == j else value
    return found


def decay_tile(cum, cum_t, h, i, j):
    gap = cum[tile(i), h : h + 1] - cum_t[h : h + 1, tile(j)]
    return jnp.exp(jnp.minimum(gap, 0.0) if i == j else gap)


def half_mask(rows):
    return lax.broadcasted_iota(jnp.int32, (rows, LANES), 1) < LANES // 2


def pair_rows(v):
    left = half_mask(v.shape[0])
    zero = jnp.zeros_like(v)
    return jnp.concatenate([jnp.where(left, v, zero), jnp.where(left, zero, v)], axis=0)


def rows_of(b):
    return pl.ds(pl.multiple_of(b * T, T), T)


MESH = pl.DeviceIdType.MESH
CHUNK = 64
LAG = 2


def greet_head():
    z = lax.axis_index("head")
    for d in range(1, 4):
        pl.semaphore_signal(
            pltpu.get_barrier_semaphore(), inc=1, device_id={"head": lax.rem(z + d, 4)}, device_id_type=MESH)


class Chain:
    def __init__(self, own, got, far, sems):
        z = lax.axis_index("head")
        self.end = (z == 0) | (z == 3)
        self.side = z + 1 - 2 * (z % 2)
        self.other = 3 - z
        self.own, self.got, self.far = own, got, far
        self.sems = sems

    @staticmethod
    def scratch(n, chunk, width):
        buffer = pltpu.VMEM((n, chunk, width), BF16)
        return [buffer, buffer, buffer] + [pltpu.SemaphoreType.DMA((n,))] * 6

    def copy(self, kind, k):
        src, dst, to = [(self.own, self.got, self.side), (self.own, self.far, self.other), (self.got, self.got, self.side)][kind]
        return pltpu.make_async_remote_copy(
            src_ref=src.at[k], dst_ref=dst.at[k],
            send_sem=self.sems[2 * kind].at[k], recv_sem=self.sems[2 * kind + 1].at[k],
            device_id={"head": to}, device_id_type=MESH,
        )

    def inward(self, k):
        @pl.when(self.end)
        def _():
            self.copy(0, k).start()

    def meet(self, stage, k):
        self.copy(stage, k).wait_recv()
        if stage == 0:
            self.own[k] = (self.own[k].astype(F32) + self.got[k].astype(F32)).astype(BF16)
        else:
            self.got[k] = (self.own[k].astype(F32) + self.far[k].astype(F32)).astype(BF16)

    def onward(self, stage, k):
        @pl.when(jnp.logical_not(self.end))
        def _():
            self.meet(stage - 1, k)
            self.copy(stage, k).start()

    def total(self, k):
        @pl.when(self.end)
        def _():
            self.copy(2, k).wait_recv()

        return self.got[k].astype(F32)

    def drain(self, n):
        def one(k, _):
            @pl.when(self.end)
            def _():
                self.copy(0, k).wait_send()

            @pl.when(jnp.logical_not(self.end))
            def _():
                self.copy(1, k).wait_send()
                self.copy(2, k).wait_send()

            return 0

        lax.fori_loop(0, n, one, 0)


class Rider:
    def __init__(self, first, ticks, count, hbm, own, got, far, sems, local):
        self.first, self.ticks, self.count = first, ticks, count
        self.done = min(max(first - 2 * LAG, 0), count)
        self.base = min(self.done, count - 1)
        self.hbm, self.local = hbm, local
        self.chain = Chain(own, got, far, sems)

    @staticmethod
    def size(first, ticks, count):
        return max(min(first + ticks, count) - min(max(first - 2 * LAG, 0), count - 1), 1)

    @staticmethod
    def scratch(first, ticks, count, width):
        return Chain.scratch(Rider.size(first, ticks, count), CHUNK, width) + [pltpu.SemaphoreType.DMA((2,))]

    def span(self, stage):
        low = self.first - stage * LAG
        return max(low, 0), min(low + self.ticks, self.count)

    def load(self):
        size = self.size(self.first, self.ticks, self.count)
        own = pltpu.make_async_copy(self.hbm.at[pl.ds(self.base, size)], self.chain.own, self.local.at[0])
        own.start()
        ready = min(max(self.first - LAG, 0), self.count) - self.base
        if ready > 0 and self.done < self.count:

            @pl.when(jnp.logical_not(self.chain.end))
            def _():
                got = pltpu.make_async_copy(
                    self.hbm.at[pl.ds(self.base, ready)], self.chain.got.at[pl.ds(0, ready)], self.local.at[1])
                got.start()
                got.wait()

        own.wait()

    def tick(self, t):
        chain = self.chain
        for stage in (2, 1, 0):
            low, high = self.span(stage)
            k = self.first - stage * LAG + t

            @pl.when((k >= low) & (k < high) & (t < self.ticks))
            def _():
                at = k - self.base
                if stage == 0:
                    chain.inward(at)
                else:
                    self.follow(stage, at, t >= LAG)

    def follow(self, stage, at, pending):
        chain = self.chain
        middle = jnp.logical_not(chain.end)

        @pl.when(middle & pending)
        def _():
            chain.meet(stage - 1, at)

        @pl.when(middle)
        def _():
            chain.copy(stage, at).start()

    def drain(self):
        chain = self.chain

        def each(stage):
            low, high = self.span(stage)
            lax.fori_loop(low - self.base, high - self.base, lambda k, _: (chain.copy(stage, k).wait_send(), 0)[1], 0)

        @pl.when(chain.end)
        def _():
            each(0)

        @pl.when(jnp.logical_not(chain.end))
        def _():
            each(1)
            each(2)

    def close(self):
        chain = self.chain
        middle = jnp.logical_not(chain.end)

        def each(low, high, do):
            if high > low:
                lax.fori_loop(low - self.base, high - self.base, lambda k, _: (do(k), 0)[1], 0)

        @pl.when(middle)
        def _():
            for stage in (0, 1):
                low, high = self.span(stage)
                started = max(self.first - stage * LAG + self.ticks - LAG, low)
                each(started, high, lambda k: chain.meet(stage, k))
            for stage in (1, 2):
                each(*self.span(stage), lambda k: chain.copy(stage, k).wait_send())

        @pl.when(chain.end)
        def _():
            each(*self.span(2), lambda k: chain.copy(2, k).wait_recv())
            each(*self.span(0), lambda k: chain.copy(0, k).wait_send())

        def store(ref, low, high):
            if high > low:
                at = pl.ds(low - self.base, high - low)
                copy = pltpu.make_async_copy(ref.at[at], self.hbm.at[pl.ds(low, high - low)], self.local.at[0])
                copy.start()
                copy.wait()

        @pl.when(middle)
        def _():
            reached = self.span(1)[1]
            store(chain.got, self.done, reached)
            store(chain.own, reached, self.span(0)[1])

        @pl.when(chain.end)
        def _():
            store(chain.got, *self.span(2))


class Exchange:
    def __init__(self, rounds, backward, total, before, logs, out, back, send, recv):
        self.rounds, self.backward = rounds, backward
        self.total, self.before, self.logs = total, before, logs
        self.out, self.back, self.send, self.recv = out, back, send, recv
        self.me = lax.axis_index("seq")

    def partner(self, r):
        bit = 1 << r
        return self.me + bit - 2 * bit * (lax.div(self.me, bit) % 2)

    def greet(self, with_head=False):
        barrier = pltpu.get_barrier_semaphore()
        for r in range(self.rounds):
            pl.semaphore_signal(barrier, inc=1, device_id={"seq": self.partner(r)}, device_id_type=MESH)
        if with_head:
            greet_head()
        pl.semaphore_wait(barrier, self.rounds + 3 * with_head)

    def copy(self, r, s):
        return pltpu.make_async_remote_copy(
            src_ref=self.out.at[r], dst_ref=self.back.at[r, s],
            send_sem=self.send.at[r], recv_sem=self.recv.at[r, s],
            device_id={"seq": self.partner(r)}, device_id_type=MESH,
        )

    def begin(self, s, state, log):
        self.total[s] = state
        self.before[s] = jnp.zeros_like(state)
        self.logs[s] = jnp.zeros(self.logs.shape[1:], F32)
        self.logs[s, 0:1] = log

    def push(self, r, s):
        n = self.total.shape[1]
        self.out[r, 0:n] = self.total[s].astype(BF16)
        hi, mid, lo = [v.astype(F32) for v in split(self.logs[s, 0:1], 3)]
        at = lax.broadcasted_iota(jnp.int32, (HALO, hi.shape[1]), 0)
        tail = jnp.where(at == 0, hi, jnp.where(at == 1, mid, jnp.where(at == 2, lo, 0.0)))
        self.out[r, n : n + HALO] = tail.astype(BF16)
        self.copy(r, s).start()

    def take(self, r, s):
        n = self.total.shape[1]
        copy = self.copy(r, s)
        copy.wait_recv()
        copy.wait_send()
        state = self.back[r, s, 0:n].astype(F32)
        tail = self.back[r, s, n : n + HALO].astype(F32)
        log = tail[0:1] + tail[1:2] + tail[2:3]
        upper = lax.div(self.me, 1 << r) % 2 == 1
        near = jnp.logical_not(upper) if self.backward else upper
        mine, theirs = self.logs[s, 0:1], self.logs[s, 1:2]
        self.before[s] = self.before[s] + jnp.where(near, jnp.exp(theirs), 0.0) * state
        self.logs[s, 1:2] = theirs + jnp.where(near, log, 0.0)
        own = jnp.where(near, 1.0, jnp.exp(log))
        other = jnp.where(near, jnp.exp(mine), 1.0)
        self.total[s] = own * self.total[s] + other * state
        self.logs[s, 0:1] = mine + log

    def advance(self, i, seqs):
        for r in reversed(range(self.rounds)):
            s = i - 1 - r

            @pl.when((s >= 0) & (s < seqs))
            def _():
                self.take(r, s)
                if r + 1 < self.rounds:
                    self.push(r + 1, s)

    @staticmethod
    def scratch(rounds, seqs, n, inner):
        return [
            pltpu.VMEM((seqs, n, inner), F32), pltpu.VMEM((seqs, 8, inner), F32),
            pltpu.VMEM((rounds, n + HALO, inner), BF16), pltpu.VMEM((rounds, seqs, n + HALO, inner), BF16),
            pltpu.SemaphoreType.DMA((rounds,)), pltpu.SemaphoreType.DMA((rounds, seqs)),
        ]


def forward(
    tok, tok_all, cot, ngain, gate_w, value_w, state_w, step_w, vk, vo, sk, so, sbias, rate, wide, tri, out_w, mgain, skip,
    xext_o, bcext_o, sraw_o, pre_o, entry_o, sums_o,
    xact_h, bcact_h, gate_h, step_h, cum_h, lstart_h, normed_h, ssd_h, gn_h, y_h,
    xact, bcact, gate, step, cum, lstart, nx, ssd, gn, y_s, gm, xe, be, st, run, halo, mine, slots,
    kept_sems, slot_sems, halo_send, halo_recv, sum_send, sum_recv,
    total, logs, out, back, send, recv,
    yown, ygot, yfar, ta, tb, tc, td, te, tf, ylocal,
    *, seqs, rounds, plan,
):
    i = pl.program_id(0)
    s = i - rounds
    steps = seqs + rounds
    length = tok.shape[1]
    me, devices = lax.axis_index("seq"), lax.axis_size("seq")
    z = lax.axis_index("head")
    scan = Exchange(rounds, False, total, entry_o, logs, out, back, send, recv)
    rider = Rider(*plan, y_h, yown, ygot, yfar, (ta, tb, tc, td, te, tf), ylocal)
    kept = [(xact, xact_h), (bcact, bcact_h), (gate, gate_h), (step, step_h), (cum, cum_h), (lstart, lstart_h)]
    per_seq = length // CHUNK

    def halo_copy(q):
        return pltpu.make_async_remote_copy(
            src_ref=tok_all.at[q, pl.ds(length - HALO, HALO)], dst_ref=halo.at[q],
            send_sem=halo_send.at[q], recv_sem=halo_recv.at[q],
            device_id={"seq": lax.rem(me + 1, devices)}, device_id_type=MESH,
        )

    def keep(k, q):
        src, dst = kept[k]
        return pltpu.make_async_copy(src.at[q], dst.at[q], kept_sems.at[k, q])

    def normed_copy(q):
        return pltpu.make_async_copy(nx.at[pl.ds(HALO, length)], normed_h.at[q], slot_sems.at[0])

    def scan_copies(q):
        return [
            pltpu.make_async_copy(ssd.at[0], ssd_h.at[q], slot_sems.at[1]),
            pltpu.make_async_copy(gn.at[0], gn_h.at[q], slot_sems.at[2]),
        ]

    def y_copy(q, skip_rider):
        first = plan[1] if skip_rider else 0
        at = pl.ds(q * per_seq + first, per_seq - first)
        return pltpu.make_async_copy(y_s.at[pl.ds(first, per_seq - first)], y_h.at[at], slot_sems.at[3])

    def sum_copy(q, d):
        return pltpu.make_async_remote_copy(
            src_ref=mine.at[q], dst_ref=slots.at[q, z], send_sem=sum_send.at[q, d], recv_sem=sum_recv.at[q, d],
            device_id={"head": lax.rem(z + d, 4)}, device_id_type=MESH,
        )

    @pl.when(i == 0)
    def _():
        barrier = pltpu.get_barrier_semaphore()
        for d in range(1, devices):
            pl.semaphore_signal(barrier, inc=1, device_id={"seq": lax.rem(me + d, devices)}, device_id_type=MESH)
        greet_head()
        pl.semaphore_wait(barrier, devices - 1 + 3)

        @pl.when(me < devices - 1)
        def _():
            for q in range(seqs):
                halo_copy(q).start()

        @pl.when(me == 0)
        def _():
            halo[...] = jnp.zeros_like(halo)

    @pl.when(i < seqs)
    def _():
        @pl.when(i > 0)
        def _():
            normed_copy(i).wait()

        def arrive():
            @pl.when(me > 0)
            def _():
                halo_copy(i).wait_recv()

        one = pl.ds(i, 1)
        front_rows(
            tok, halo.at[one], ngain, gate_w, value_w, state_w, step_w, vk, vo, sk, so, sbias, rate, wide, tri,
            gate.at[one], xext_o, bcext_o, sraw_o, xact.at[one], bcact.at[one], step.at[one], cum.at[one],
            lstart.at[one], pre_o.at[one], nx, xe, be, st, run, arrive,
        )
        normed_copy(i).start()
        for k in range(len(kept)):
            keep(k, i).start()
        scan.begin(i, st[...], expand_row(run[0:1], wide[...]))

    scan.advance(i, seqs)

    @pl.when(i < seqs)
    def _():
        scan.push(0, i)

    @pl.when(s >= 0)
    def _():
        @pl.when(s > 0)
        def _():
            for copy in scan_copies(s):
                copy.wait()

        one = pl.ds(s, 1)
        scan_out(
            xact.at[one], bcact.at[one], step.at[one], cum.at[one], gate.at[one], lstart.at[one], entry_o.at[one],
            pre_o.at[one], cot, out_w, mgain, skip, wide, ssd, gn, mine.at[one], gm, lambda b: rider.tick((s - 1) * 2 + b),
        )
        for copy in scan_copies(s):
            copy.start()
        for d in range(1, 4):
            sum_copy(s, d).start()
        slots[s, z] = mine[s]

        @pl.when(s == 1)
        def _():
            y_copy(0, True).wait()

        @pl.when(s > 1)
        def _():
            y_copy(s, False).wait()

        for b in range(length // T):
            value = mm(gm[b * T : (b + 1) * T], out_w[...]).astype(BF16)
            y_s[b * T // CHUNK : (b + 1) * T // CHUNK] = value.reshape(T // CHUNK, CHUNK, value.shape[1])

        @pl.when(s == 0)
        def _():
            yown[...] = y_s[0 : plan[1]]
            y_copy(0, True).start()

        @pl.when(s > 0)
        def _():
            y_copy(s, False).start()

    @pl.when(i == steps - 1)
    def _():
        rider.close()
        for q in range(seqs):
            for d in range(1, 4):
                sum_copy(q, d).wait()
            sums_o[q] = (slots[q, 0] + slots[q, 1]) + (slots[q, 2] + slots[q, 3])
            for k in range(len(kept)):
                keep(k, q).wait()
        normed_copy(0).wait()
        for copy in scan_copies(0):
            copy.wait()
        y_copy(1, False).wait()

        @pl.when(me < devices - 1)
        def _():
            for q in range(seqs):
                halo_copy(q).wait_send()


def front_rows(
    tok, halo, ngain, gate_w, value_w, state_w, step_w, vk, vo, sk, so, sbias, rate, wide, tri,
    gate_o, xext_o, bcext_o, sraw_o, xact_o, bcact_o, step_o, cum_o, lstart_o, pre_o,
    nx, xe, be, st, run, arrive,
):
    length = tok.shape[1]
    blocks = length // T
    n = bcact_o.shape[2] // 2

    def norm(v):
        v = v.astype(F32)
        inv = lax.rsqrt(jnp.mean(v * v, axis=1, keepdims=True) + EPS)
        return (v * inv * ngain[...]).astype(BF16)

    def norm_rows(b, _):
        nx[pl.ds(pl.multiple_of(HALO + b * SUB, HALO), SUB), :] = norm(tok[0, pl.ds(pl.multiple_of(b * SUB, SUB), SUB), :])
        return 0

    lax.fori_loop(0, length // SUB, norm_rows, 0)
    gate_o[0] = mm(nx[HALO:], gate_w[...])
    sraw_o[0] = mm(nx[HALO:], step_w[...])
    arrive()
    nx[0:HALO] = norm(halo[0])
    x = mm(nx[...], value_w[...]).astype(BF16)
    xext_o[0] = x
    xe[...] = x.astype(F32)
    bc = mm(nx[...], state_w[...]).astype(BF16)
    bcext_o[0] = bc
    be[...] = bc.astype(F32)
    st[...] = jnp.zeros_like(st)
    run[...] = jnp.zeros_like(run)
    pre_o[0] = jnp.zeros_like(pre_o[0])
    for b in range(blocks):
        r0 = b * T
        r = slice(r0, r0 + T)
        taps = vk.shape[0]
        base = HALO - taps + 1
        xc = vo[...] + vk[0:1] * xe[r0 + base : r0 + base + T]
        bcc = so[...] + sk[0:1] * be[r0 + base : r0 + base + T]
        for k in range(1, taps):
            xc = xc + vk[k : k + 1] * xe[r0 + base + k : r0 + base + k + T]
            bcc = bcc + sk[k : k + 1] * be[r0 + base + k : r0 + base + k + T]
        xa = (xc * sigmoid(xc)).astype(BF16)
        bca = (bcc * sigmoid(bcc)).astype(BF16)
        xact_o[0, r, :] = xa
        bcact_o[0, r, :] = bca
        step = softplus(sraw_o[0, r, :] + sbias[...])
        cum = exact_tri(tri[...], step * rate[...])
        step_o[0, r, :] = step
        cum_o[0, r, :] = cum
        last = cum[T - 1 : T]
        weight = jnp.exp(last - cum) * step
        weighted = (xa.astype(F32) * expand(weight, wide[...])).astype(BF16)
        contrib = t_mm(bca[:, :n], weighted)
        lstart_o[0, b] = st[...]
        st[...] = expand_row(jnp.exp(last), wide[...]) * st[...] + contrib
        run[0:1] = run[0:1] + last
        pre_o[0, b + 1 : b + 2] = run[0:1]


def scan_out(
    xact, bcact, step_i, cum_i, gate, lstart, entry, pre, cot, out_w, mgain, skip, wide,
    ssd_o, gn_o, sums_o, gm, tick,
):
    length = xact.shape[1]
    blocks = length // T
    n = bcact.shape[2] // 2
    inner = xact.shape[2]
    gn_o[0] = mm_t(cot[0], out_w[...])

    def block(b, _):
        tick(b)
        r = rows_of(b)
        xa = xact[0, r, :]
        bca = bcact[0, r, :]
        bm, cm = bca[:, :n], bca[:, n:]
        cum = cum_i[0, r, :]
        cum_t = cum.T
        cross = cross_tiles(cm, bm)
        start = expand_row(jnp.exp(pre[0, pl.ds(b, 1), :]), wide[...]) * entry[0] + lstart[0, b]
        start = start.astype(BF16)
        grown = jnp.exp(cum)
        cm = cm.astype(F32)
        xs = (xa.astype(F32) * expand(step_i[0, r, :], wide[...])).astype(BF16)
        for p in range(inner // LANES):
            lanes = slice(p * LANES, (p + 1) * LANES)
            two = (2 * p, 2 * p + 1)
            start_two = pair_rows(start[:, lanes])
            xs_two = [pair_rows(xs[tile(j), lanes]) for j in range(T // SUB)]
            for i in range(T // SUB):
                left = [(cm[tile(i)] * grown[tile(i), h : h + 1]).astype(BF16) for h in two]
                right = [start_two]
                for j in range(i + 1):
                    left += [(cross[i, j] * decay_tile(cum, cum_t, h, i, j)).astype(BF16) for h in two]
                    right.append(xs_two[j])
                rows = pl.ds(pl.multiple_of(b * T + i * SUB, SUB), SUB)
                ssd_o[0, rows, lanes] = mm(jnp.concatenate(left, axis=1), jnp.concatenate(right, axis=0))
        mixed = ssd_o[0, r, :] + skip[...] * xa.astype(F32)
        g = gate[0, r, :]
        gated = mixed * (g * sigmoid(g))
        gg = gated * mgain[...]
        gm[r, :] = gg.astype(BF16)
        squares = jnp.sum(gated * gated, axis=1, keepdims=True)
        dots = jnp.sum(gg * gn_o[0, r, :], axis=1, keepdims=True)
        lane = lax.broadcasted_iota(jnp.int32, (T, LANES), 1)
        both = jnp.where(lane == 0, squares, jnp.where(lane == 1, dots, 0.0))
        sums_o[0, :, r] = both.T[0:8]
        return 0

    lax.fori_loop(0, blocks, block, 0)


def back_one(
    xact, bcact, cum_i, gate, ssd, gn, sums, pre, mgain, skip, wide,
    xact_b, bcact_b, step_b, cum_b, lstart_b, entry_b, pre_b, y_in,
    gnormed_o, gate_grad_o, lend_o, rms_o, xg_o, cumg_o, stepg_o, bcg_o, mgg_o, skg_o, after_o, y_all,
    z, acc, use, dys, cumg, total, logs, out, back, send, recv,
    yown, ygot, yfar, ta, tb, tc, td, te, tf, ylocal,
    *, inner_all, seqs, rounds, plan,
):
    i = pl.program_id(0)
    s = i - rounds
    blocks = xact.shape[1] // T
    scan = Exchange(rounds, True, total, after_o, logs, out, back, send, recv)
    rider = Rider(*plan, y_all, yown, ygot, yfar, (ta, tb, tc, td, te, tf), ylocal)
    per_step = plan[1] // (seqs + rounds)

    @pl.when(i == 0)
    def _():
        scan.greet(with_head=True)
        rider.load()
        mgg_o[...] = jnp.zeros_like(mgg_o)
        skg_o[...] = jnp.zeros_like(skg_o)

    ticks = min(per_step, 3)
    rider.tick(i * per_step)

    @pl.when(i < seqs)
    def _():
        one = pl.ds(i, 1)
        gate_back(
            xact, bcact, cum_i, gate, ssd, gn, sums, mgain, skip, wide, gnormed_o, gate_grad_o, lend_o, rms_o, mgg_o, skg_o,
            dys.at[one], cumg.at[one], acc, use, inner_all,
        )
        scan.begin(i, acc[...], expand_row(pre[0, blocks : blocks + 1], wide[...]))

    scan.advance(i, seqs)

    @pl.when(i < seqs)
    def _():
        scan.push(0, i)

    @pl.when(s >= 0)
    def _():
        one = pl.ds(s, 1)
        scan_back(
            xact_b, bcact_b, step_b, cum_b, lstart_b, entry_b, pre_b, skip, wide, dys.at[one], cumg.at[one],
            xg_o, cumg_o, stepg_o, bcg_o, z, lambda b: rider.tick(jnp.where(1 + b < ticks, i * per_step + 1 + b, plan[1])),
        )

    @pl.when(s < 0)
    def _():
        for k in range(1, per_step):
            rider.tick(i * per_step + k)

    @pl.when(i == seqs + rounds - 1)
    def _():
        rider.close()


def gate_back(
    xact, bcact, cum_i, gate, ssd, gn, sums, mgain, skip, wide, gnormed_o, gate_grad_o, lend_o, rms_o, mgg_o, skg_o,
    dys, cumg, acc, use, inner_all,
):
    length = xact.shape[1]
    blocks = length // T
    n = bcact.shape[2] // 2
    inner = xact.shape[2]
    acc[...] = jnp.zeros_like(acc)

    def block(k, _):
        b = blocks - 1 - k
        r = rows_of(b)
        sums_b = sums[0, :, r]
        columns = jnp.concatenate([sums_b, jnp.zeros((LANES - 8, T), F32)], axis=0).T
        for i in range(T // SUB):
            ri = pl.ds(pl.multiple_of(b * T + i * SUB, SUB), SUB)
            xa = xact[0, ri, :].astype(F32)
            rms = lax.rsqrt(columns[tile(i), 0:1] / inner_all + EPS)
            rms_o[0, ri, :] = jnp.broadcast_to(rms, (SUB, LANES))
            coef = rms * rms * rms * (columns[tile(i), 1:2] / inner_all)
            ssd_r = ssd[0, ri, :]
            mixed = ssd_r + skip[...] * xa
            g = gate[0, ri, :]
            sg = sigmoid(g)
            gated = mixed * (g * sg)
            grad_norm = gn[0, ri, :]
            normalised = gated * rms
            gnormed_o[0, ri, :] = (normalised * mgain[...]).astype(BF16)
            mgg_o[0:1] += jnp.sum(grad_norm * normalised, axis=0, keepdims=True)
            grad_gated = rms * (grad_norm * mgain[...]) - gated * coef
            gate_grad_o[0, ri, :] = (grad_gated * mixed * (sg * (1.0 + g * (1.0 - sg)))).astype(BF16)
            grad_mixed = grad_gated * (g * sg)
            skg_o[0:1] += jnp.sum(grad_mixed * xa, axis=0, keepdims=True)
            dy = grad_mixed.astype(BF16)
            dys[0, ri, :] = dy
            cumg[0, ri, :] = head_sum(dy.astype(F32) * ssd_r, wide[...])
        cm = bcact[0, r, n:].astype(F32)
        grown = jnp.exp(cum_i[0, r, :])
        for p in range(inner // LANES):
            lanes = slice(p * LANES, (p + 1) * LANES)
            scaled = [(cm * grown[:, h : h + 1]).astype(BF16) for h in (2 * p, 2 * p + 1)]
            used = None
            for i in range(T // SUB):
                ri = pl.ds(pl.multiple_of(b * T + i * SUB, SUB), SUB)
                term = t_mm(jnp.concatenate([v[tile(i)] for v in scaled], axis=0), pair_rows(dys[0, ri, lanes]))
                used = term if used is None else used + term
            use[:, lanes] = used
        lend_o[0, b] = acc[...]
        acc[...] = expand_row(grown[T - 1 : T], wide[...]) * acc[...] + use[...]
        return 0

    lax.fori_loop(0, blocks, block, 0)


def scan_back(
    xact, bcact, step_i, cum_i, lstart, entry, pre, skip, wide, dys, cumg, xg_o, cumg_o, stepg_o, bcg_o, z, tick,
):
    length = xact.shape[1]
    blocks = length // T
    n = bcact.shape[2] // 2
    inner = xact.shape[2]

    def block(b, _):
        tick(b)
        r = rows_of(b)
        dy = dys[0, r, :]
        xa = xact[0, r, :].astype(F32)
        bca = bcact[0, r, :]
        bm, cm = bca[:, :n], bca[:, n:]
        cum = cum_i[0, r, :]
        cum_t = cum.T
        start = expand_row(jnp.exp(pre[0, pl.ds(b, 1), :]), wide[...]) * entry[0] + lstart[0, b]
        start = start.astype(BF16)
        dy32 = dy.astype(F32)
        gdy_hi, gdy_lo = split(expand(jnp.exp(cum), wide[...]) * dy32, 2)
        c_grad = mm_t(gdy_hi, start) + mm_t(gdy_lo, start)
        step_wide = expand(step_i[0, r, :], wide[...])
        xs = (xa * step_wide).astype(BF16)
        cross = cross_tiles(cm, bm)
        cross_part = {ij: jnp.zeros((SUB, SUB), F32) for ij in tiles()}
        for p in range(inner // LANES):
            lanes = slice(p * LANES, (p + 1) * LANES)
            zs = [None] * (T // SUB)
            for i in range(T // SUB):
                dy_two = pair_rows(dy[tile(i), lanes])
                for j in range(i + 1):
                    mix_grad = mm_t(dy_two, xs[tile(j), lanes])
                    mix = []
                    for k, h in enumerate((2 * p, 2 * p + 1)):
                        decay = decay_tile(cum, cum_t, h, i, j)
                        mix.append((cross[i, j] * decay).astype(BF16))
                        cross_part[i, j] = cross_part[i, j] + mix_grad[tile(k)] * decay
                    term = t_mm(jnp.concatenate(mix, axis=0), dy_two)
                    zs[j] = term if zs[j] is None else zs[j] + term
            for j in range(T // SUB):
                z[tile(j), lanes] = zs[j]
        rows = []
        for i in range(T // SUB):
            row = [jnp.where(lower(), cross_part[i, j], 0.0) if i == j else cross_part[i, j] for j in range(i + 1)]
            row += [jnp.zeros((SUB, SUB), F32)] * (T // SUB - 1 - i)
            rows.append(jnp.concatenate(row, axis=1))
        cross_low = jnp.concatenate(rows, axis=0).astype(BF16)
        bcg_o[0, r, 0:n] = t_mm(cross_low, cm)
        bcg_o[0, r, n : 2 * n] = c_grad + mm(cross_low, bm)
        zz = z[...]
        xg_o[0, r, :] = skip[...] * dy32 + step_wide * zz
        cumg_o[0, r, :] = cumg[0, r, :] - head_sum(xs.astype(F32) * zz, wide[...])
        stepg_o[0, r, :] = head_sum(xa * zz, wide[...])
        return 0

    lax.fori_loop(0, blocks, block, 0)


def back_two(
    xact, bcact, xext, bcext, step_i, cum_i, sraw, xg, cumg, stepg, bcg, lstart, entry, lend, after, pre,
    vk, vo, sk, so, sbias, rate, wide, tri, y_in,
    xpg_o, xhalo_o, bpg_o, bhalo_o, raw_o, vkg_o, skg_o, heads_o, y_all,
    xe, be, xcg, bcg_s, yown, ygot, yfar, ta, tb, tc, td, te, tf, ylocal,
    *, seqs, plan,
):
    length = xact.shape[1]
    blocks = length // T
    n = bcact.shape[2] // 2
    taps = vk.shape[0]
    base = HALO - taps + 1
    step_at = pl.program_id(0)
    rider = Rider(*plan, y_all, yown, ygot, yfar, (ta, tb, tc, td, te, tf), ylocal)

    @pl.when(step_at == 0)
    def _():
        greet_head()
        pl.semaphore_wait(pltpu.get_barrier_semaphore(), 3)
        rider.load()
        vkg_o[...] = jnp.zeros_like(vkg_o)
        skg_o[...] = jnp.zeros_like(skg_o)
        heads_o[...] = jnp.zeros_like(heads_o)

    xe[...] = xext[0].astype(F32)
    be[...] = bcext[0].astype(F32)
    for ref in (xcg, bcg_s):
        ref[0:HALO] = jnp.zeros((HALO, ref.shape[1]), F32)
        ref[HALO + length :] = jnp.zeros((HALO, ref.shape[1]), F32)

    def conv_rows(ext, kernel, offset, r0):
        total = offset[...] + kernel[0:1] * ext[r0 + base : r0 + base + T]
        for k in range(1, taps):
            total = total + kernel[k : k + 1] * ext[r0 + base + k : r0 + base + k + T]
        sg = sigmoid(total)
        return sg * (1.0 + total * (1.0 - sg))

    def filter_grad(grad, ext, out, r0):
        for k in range(taps):
            out[k : k + 1] += jnp.sum(grad * ext[r0 + base + k : r0 + base + k + T], axis=0, keepdims=True)
        out[taps : taps + 1] += jnp.sum(grad, axis=0, keepdims=True)

    per_step = plan[1] // seqs
    for b in range(blocks):
        rider.tick(step_at * per_step + b)
        r0 = b * T
        r = slice(r0, r0 + T)
        xa = xact[0, r, :].astype(F32)
        bm = bcact[0, r, 0:n]
        cum = cum_i[0, r, :]
        step = step_i[0, r, :]
        last = cum[T - 1 : T]
        start = expand_row(jnp.exp(pre[0, b : b + 1]), wide[...]) * entry[0] + lstart[0, b]
        suffix = jnp.exp(pre[0, blocks : blocks + 1] - pre[0, b + 1 : b + 2])
        end = expand_row(suffix, wide[...]) * after[0] + lend[0, b]
        end_low = end.astype(BF16)
        weighted_grad = mm(bm, end_low)
        reach = jnp.exp(last - cum)
        weight = reach * step
        weight_wide = expand(weight, wide[...])
        weighted = (xa * weight_wide).astype(BF16)
        bcg_b = bcg[0, r, :]
        b_total = bcg_b[:, 0:n] + mm_t(weighted, end_low)
        bc_total = jnp.concatenate([b_total, bcg_b[:, n:]], axis=1)
        w_grad = head_sum(weighted_grad * xa, wide[...])
        part = w_grad * weight
        product = jnp.broadcast_to(jnp.sum(end * start, axis=0, keepdims=True), (16, end.shape[1]))
        fade_grad = jnp.exp(last) * head_sum(product, wide[...])[0:1]
        at_last = lax.broadcasted_iota(jnp.int32, (T, LANES), 0) == T - 1
        extra = fade_grad + jnp.sum(part, axis=0, keepdims=True)
        cum_grad = cumg[0, r, :] - part + jnp.where(at_last, extra, 0.0)
        a, bb, c = split(cum_grad, 3)
        rise = t_mm(tri[...], a) + (t_mm(tri[...], bb) + t_mm(tri[...], c))
        step_grad = stepg[0, r, :] + w_grad * reach + rise * rate[...]
        raw = step_grad * sigmoid(sraw[0, r, :] + sbias[...])
        raw_o[0, r, :] = raw.astype(BF16)
        heads_o[0:1] += jnp.sum(raw, axis=0, keepdims=True)
        heads_o[1:2] += jnp.sum(rise * step, axis=0, keepdims=True)
        grad = (xg[0, r, :] + weighted_grad * weight_wide) * conv_rows(xe, vk, vo, r0)
        filter_grad(grad, xe, vkg_o, r0)
        xcg[HALO + r0 : HALO + r0 + T] = grad
        grad = bc_total * conv_rows(be, sk, so, r0)
        filter_grad(grad, be, skg_o, r0)
        bcg_s[HALO + r0 : HALO + r0 + T] = grad

    def conv_back(ref, kernel, r0, rows):
        total = kernel[0:1] * ref[r0 + taps - 1 : r0 + taps - 1 + rows]
        for k in range(1, taps):
            total = total + kernel[k : k + 1] * ref[r0 + taps - 1 - k : r0 + taps - 1 - k + rows]
        return total.astype(BF16)

    xhalo_o[0] = conv_back(xcg, vk, 0, HALO)
    bhalo_o[0] = conv_back(bcg_s, sk, 0, HALO)
    for b in range(blocks):
        if blocks + b < per_step:
            rider.tick(step_at * per_step + blocks + b)
        r0 = b * T
        xpg_o[0, r0 : r0 + T] = conv_back(xcg, vk, HALO + r0, T)
        bpg_o[0, r0 : r0 + T] = conv_back(bcg_s, sk, HALO + r0, T)

    @pl.when(step_at == seqs - 1)
    def _():
        rider.close()


class GradSum:
    def __init__(self, rounds, mine, back, out, sems, zback=None, shared=0):
        self.rounds, self.mine, self.back, self.out, self.sems = rounds, mine, back, out, sems
        self.zback, self.shared = zback, shared
        self.me, self.z = lax.axis_index("seq"), lax.axis_index("head")
        self.rows = mine.shape[0]
        self.share = self.rows >> rounds

    @staticmethod
    def sem_count(rounds):
        return 4 * rounds + 9

    def bit(self, r):
        return lax.div(self.me, 1 << r) % 2

    def partner(self, r):
        return self.me + (1 << r) - (2 << r) * self.bit(r)

    def first(self, r):
        row = 0
        for k in range(r):
            row = row + self.bit(k) * (self.rows >> (k + 1))
        return row

    def at(self, row, size):
        return pl.ds(pl.multiple_of(row, 16), size)

    def halving(self, r):
        half = self.rows >> (r + 1)
        theirs = self.first(r) + half - half * self.bit(r)
        return pltpu.make_async_remote_copy(
            src_ref=self.mine.at[self.at(theirs, half)], dst_ref=self.back.at[pl.ds(self.rows - 2 * half, half)],
            send_sem=self.sems.at[r], recv_sem=self.sems.at[self.rounds + r],
            device_id={"seq": self.partner(r)}, device_id_type=MESH,
        )

    def add_half(self, r):
        copy = self.halving(r)
        copy.wait()
        half = self.rows >> (r + 1)
        row = self.first(r + 1)

        def one(k, _):
            at = self.at(row + k * self.share, self.share)
            come = self.back[pl.ds(pl.multiple_of(self.rows - 2 * half + k * self.share, 16), self.share), :]
            self.mine[at, :] = (self.mine[at, :].astype(F32) + come.astype(F32)).astype(BF16)
            return 0

        lax.fori_loop(0, half // self.share, one, 0)

    def gathering(self, r, arriving):
        size = self.rows >> (r + 1)
        row = self.first(r + 1)
        if arriving:
            row = row + size - 2 * size * self.bit(r)
        at = self.at(row, size)
        return pltpu.make_async_remote_copy(
            src_ref=self.out.at[at], dst_ref=self.out.at[at],
            send_sem=self.sems.at[2 * self.rounds + r], recv_sem=self.sems.at[3 * self.rounds + r],
            device_id={"seq": self.partner(r)}, device_id_type=MESH,
        )

    def to_head(self, d):
        base = 4 * self.rounds + 1
        src = self.mine.at[self.at(self.first(self.rounds), self.share), pl.ds(0, self.shared)]
        return pltpu.make_async_remote_copy(
            src_ref=src, dst_ref=self.zback.at[self.z], send_sem=self.sems.at[base + d], recv_sem=self.sems.at[base + 4 + d],
            device_id={"head": lax.rem(self.z + d, 4)}, device_id_type=MESH,
        )

    def publish(self):
        at = self.at(self.first(self.rounds), self.share)
        copy = pltpu.make_async_copy(self.mine.at[at], self.out.at[at], self.sems.at[4 * self.rounds])
        copy.start()
        copy.wait()
        self.gathering(self.rounds - 1, False).start()

    def stages(self):
        spans = [2, 5, 3] + [2] * self.rounds
        acts = [(spans[0], lambda: self.halving(0).start())]
        for r in range(self.rounds):
            def act(r=r):
                self.add_half(r)
                if r + 1 < self.rounds:
                    self.halving(r + 1).start()
                elif not self.shared:
                    self.publish()
                else:
                    for d in range(1, 4):
                        self.to_head(d).start()
                    self.zback[self.z] = self.mine[self.at(self.first(self.rounds), self.share), 0 : self.shared]

            acts.append((spans[r + 1] if r + 1 < self.rounds else spans[r], act))
        if self.shared:
            def meet():
                for d in range(1, 4):
                    self.to_head(d).wait()
                at = self.at(self.first(self.rounds), self.share)
                low = [self.zback[k].astype(F32) for k in range(4)]
                self.mine[at, 0 : self.shared] = ((low[0] + low[1]) + (low[2] + low[3])).astype(BF16)
                self.publish()

            acts.append((spans[self.rounds - 1], meet))
        for r in reversed(range(self.rounds)):
            def act(r=r):
                self.gathering(r, False).wait_send()
                self.gathering(r, True).wait_recv()
                if r > 0:
                    self.gathering(r - 1, False).start()

            acts.append((spans[max(r - 1, 0)], act))
        return acts


def finish(
    y, gate_grad, xpg, bpg, raw, tok, cot, rms, gate_w, value_w, state_w, step_w, ngain, small, state_rows,
    normed, tok_k, out_grad, gate_grad_w, y_all,
    result_o, tokens_grad_o, small_o, wout_o, wgate_o, wvalue_o, wmixed_o,
    own, got, far, sa, sb, sc, sd, se, sf, yown, ygot, yfar, ta, tb, tc, td, te, tf, ylocal, rows, out, back, send, recv,
    w_mine, w_back, m_mine, m_back, m_zback, w_acc, m_acc, w_sems, w_local, vec, vback, vsems,
    *, n, rounds, plan,
):
    i = pl.program_id(0)
    z = lax.axis_index("head")
    last = n + 3 * LAG - 1
    outs = (wout_o, wgate_o, wvalue_o)
    grads = [GradSum(rounds, w_mine.at[k], w_back.at[k], outs[k], w_sems.at[k]) for k in range(3)]
    grads.append(GradSum(rounds, m_mine, m_back, wmixed_o, w_sems.at[3], m_zback, bpg.shape[1]))
    products = 2 * (n * CHUNK // T)

    def vec_copy(d):
        return pltpu.make_async_remote_copy(
            src_ref=vec, dst_ref=vback.at[z], send_sem=vsems.at[d], recv_sem=vsems.at[4 + d],
            device_id={"head": lax.rem(z + d, 4)}, device_id_type=MESH,
        )

    def local_copies():
        rows_out, half = out_grad.shape[0], out_grad.shape[1] // 2
        return [
            pltpu.make_async_copy(gate_grad_w, w_mine.at[1], w_local.at[0]),
            pltpu.make_async_copy(out_grad.at[:, pl.ds(0, half)], w_mine.at[0, pl.ds(0, rows_out)], w_local.at[1]),
            pltpu.make_async_copy(out_grad.at[:, pl.ds(half, half)], w_mine.at[0, pl.ds(rows_out, rows_out)], w_local.at[2]),
        ]

    chain = Chain(own, got, far, (sa, sb, sc, sd, se, sf))
    rider = Rider(*plan, y_all, yown, ygot, yfar, (ta, tb, tc, td, te, tf), ylocal)
    me = lax.axis_index("seq")

    def partner(r):
        bit = 1 << r
        return me + bit - 2 * bit * (lax.div(me, bit) % 2)

    @pl.when(i == 0)
    def _():
        barrier = pltpu.get_barrier_semaphore()
        for r in range(rounds):
            pl.semaphore_signal(barrier, inc=1, device_id={"seq": partner(r)}, device_id_type=MESH)
        greet_head()
        pl.semaphore_wait(barrier, rounds + 3)
        rider.load()
        for copy in local_copies():
            copy.start()
        w_acc[...] = jnp.zeros_like(w_acc)
        m_acc[...] = jnp.zeros_like(m_acc)
        rows[0:8] = small[...]
        rows[8:] = jnp.zeros_like(rows[8:])
        rows[16:24, 0 : state_rows.shape[1]] = state_rows[...]

    rider.tick(i)
    for stage in (2, 1):
        k = i - stage * LAG

        @pl.when((k >= 0) & (k < n))
        def _():
            chain.onward(stage, k)

    @pl.when((i < products) & (i % 2 == 0))
    def _():
        value = mm_t(gate_grad[...], gate_w[...]) + mm_t(xpg[...], value_w[...])
        value = value + (mm_t(bpg[...], state_w[...]) + mm_t(raw[...], step_w[...]))
        t = tok_k[...].astype(F32)
        inv = lax.rsqrt(jnp.mean(t * t, axis=1, keepdims=True) + EPS)
        gain = jnp.sum(value * (t * inv), axis=0, keepdims=True)
        half = t.shape[1] // 2
        rows[8:9] += gain[:, :half]
        rows[9:10] += gain[:, half:]
        chunks = T // CHUNK
        first = lax.div(i, 2) * chunks
        own[pl.ds(first, chunks)] = value.astype(BF16).reshape(chunks, CHUNK, value.shape[1])
        mixed = jnp.concatenate([bpg[...], raw[...]], axis=1)
        for m in range(w_acc.shape[0] // 256):
            rows_m = slice(m * 256, (m + 1) * 256)
            part = normed[:, rows_m]
            w_acc[rows_m] += t_mm(part, xpg[...])
            m_acc[rows_m] += t_mm(part, mixed)

    @pl.when(i < n)
    def _():
        chain.inward(i)

    @pl.when(i == products)
    def _():
        w_mine[2] = w_acc[...].astype(BF16)
        m_mine[...] = m_acc[...].astype(BF16)

    @pl.when(i == 1)
    def _():
        for copy in local_copies():
            copy.wait()

    for grad_sum, begin in zip(grads, (1, 5, products, products + 2)):
        at = begin
        for span, act in grad_sum.stages():
            pl.when(i == min(at, last))(act)
            at += span

    @pl.when(i == products)
    def _():
        vec[...] = rows[8:24]
        for d in range(1, 4):
            vec_copy(d).start()
        vback[z] = vec[...]

    def row_copy(r):
        return pltpu.make_async_remote_copy(
            src_ref=out.at[r], dst_ref=back.at[r], send_sem=send.at[r], recv_sem=recv.at[r],
            device_id={"seq": partner(r)}, device_id_type=MESH,
        )

    @pl.when(i == products + 4)
    def _():
        for d in range(1, 4):
            vec_copy(d).wait()
        rows[8:24] = (vback[0] + vback[1]) + (vback[2] + vback[3])
        out[0] = rows[...]
        row_copy(0).start()

    for r in range(rounds):

        @pl.when(i == products + 4 + 3 * (r + 1))
        def _():
            row_copy(r).wait()
            rows[...] = rows[...] + back[r]
            if r + 1 < rounds:
                out[r + 1] = rows[...]
                row_copy(r + 1).start()

    k = i - 3 * LAG

    @pl.when(k >= 0)
    def _():
        grad = chain.total(k)
        rms_k = rms[:, 0:1]
        t = tok[...].astype(F32)
        width = t.shape[1]
        inv = lax.rsqrt(jnp.mean(t * t, axis=1, keepdims=True) + EPS)
        if rider.done > 0:

            @pl.when(k < rider.done)
            def _():
                result_o[...] = (t + y[...].astype(F32) * rms_k).astype(BF16)

        if rider.done < n:

            @pl.when(k >= rider.done)
            def _():
                result_o[...] = (t + rider.chain.total(k - rider.base) * rms_k).astype(BF16)

        scaled = grad * ngain[...]
        dot = jnp.sum(scaled * t, axis=1, keepdims=True) / width
        tokens_grad_o[...] = (cot[...].astype(F32) + inv * scaled - t * (inv * inv * inv * dot)).astype(BF16)

    @pl.when(i == last)
    def _():
        chain.drain(n)
        rider.drain()
        small_o[...] = rows[...]


def call(body, steps, seqs, ins, outs, scratch, flops, collective_id=None, carried=None):
    def cut(shape, lag):
        rest = tuple(shape[1:])
        return pl.BlockSpec((1,) + rest, lambda s: (jnp.clip(s - lag, 0, seqs - 1),) + (0,) * len(rest))

    def whole(shape):
        return pl.BlockSpec(tuple(shape), lambda s: (0,) * len(shape), pipeline_mode=pl.Buffered(1))

    pairs = [v if isinstance(v, tuple) else (v, 0) for v in ins]
    ins = [v for v, _ in pairs]
    in_specs = [cut(v.shape, lag) if v.ndim >= 3 else whole(v.shape) for v, lag in pairs]
    out_specs = [whole(s) if lag is None else cut(s, lag) for s, _, lag in outs]
    out_shape = [jax.ShapeDtypeStruct(s, d) for s, d, _ in outs]
    aliases = {}
    if carried is not None:
        aliases = {len(ins): len(outs)}
        in_specs.append(pl.BlockSpec(memory_space=pl.ANY))
        out_specs.append(pl.BlockSpec(memory_space=pl.ANY))
        out_shape.append(jax.ShapeDtypeStruct(carried.shape, carried.dtype))
        ins = ins + [carried]
    moved = sum(a.size * a.dtype.itemsize for a in ins)
    for s, d, _ in outs:
        size = jnp.dtype(d).itemsize
        for k in s:
            size *= k
        moved += size
    return pl.pallas_call(
        body,
        grid=(steps,),
        in_specs=in_specs,
        out_specs=out_specs,
        out_shape=out_shape,
        scratch_shapes=scratch,
        input_output_aliases=aliases,
        compiler_params=pltpu.CompilerParams(
            dimension_semantics=("arbitrary",), vmem_limit_bytes=60 * 1024 * 1024,
            collective_id=collective_id, has_side_effects=collective_id is not None,
        ),
        cost_estimate=pl.CostEstimate(flops=flops, bytes_accessed=moved, transcendentals=0),
    )(*ins)


def shards(
    tokens, norm_gain, gate_weight, value_weight, state_weight, step_weight, value_kernel, value_offset,
    state_kernel, state_offset, step_bias, log_rate, skip_gain, mixer_gain, out_weight, cotangent,
):
    seqs, length, width = tokens.shape
    flat = seqs * length
    inner = gate_weight.shape[1]
    heads = step_weight.shape[1]
    head_size = inner // heads
    n2 = state_weight.shape[1]
    n = n2 // 2
    taps = value_kernel.shape[0]
    blocks = length // T
    devices = lax.axis_size("seq")
    rounds = devices.bit_length() - 1
    assert devices == 1 << rounds
    inner_all = inner * lax.axis_size("head")

    pad = LANES - heads
    rate_row = -jnp.exp(log_rate)
    rate = jnp.pad(rate_row, (0, pad))[None]
    bias = jnp.pad(step_bias, (0, pad))[None]
    step_w = jnp.pad(step_weight, ((0, 0), (0, pad)))
    skip = jnp.repeat(skip_gain, head_size)[None]
    gain = mixer_gain[None]
    one = (jnp.arange(inner)[None, :] // head_size == jnp.arange(LANES)[:, None]).astype(BF16)
    wide = jnp.concatenate([one, one], axis=0)
    tri = (jnp.arange(T)[:, None] >= jnp.arange(T)[None, :]).astype(BF16)
    vo, so = value_offset[None], state_offset[None]

    def big(cols, dtype, rows=length, lag=0):
        return ((seqs, rows, cols), dtype, lag)

    vmem = pltpu.VMEM
    ext = length + HALO
    n_chunks = flat // CHUNK
    steps = seqs + rounds
    plan = (0, min(2 * (seqs - 1), length // CHUNK), n_chunks)
    dma = pltpu.SemaphoreType.DMA

    def block(shape, lag):
        return pl.BlockSpec((1,) + shape, lambda i: (jnp.clip(i - lag, 0, seqs - 1), 0, 0))

    def once(v):
        return pl.BlockSpec(v.shape, lambda i: (0,) * len(v.shape), pipeline_mode=pl.Buffered(1))

    def shape_of(cols, dtype, rows=length):
        return jax.ShapeDtypeStruct((seqs, rows, cols), dtype)

    fixed = (norm_gain[None], gate_weight, value_weight, state_weight, step_w, value_kernel, vo, state_kernel, so, bias, rate,
             wide, tri, out_weight, gain, skip)
    held = (shape_of(LANES, F32, 8), shape_of(inner, F32, n), shape_of(length, F32, 8))
    anywhere = pl.BlockSpec(memory_space=pl.ANY)
    (xext, bcext, sraw, pre, entry, sums, xact, bcact, gate, step, cum, lstart, normed, ssd, gn, y) = pl.pallas_call(
        functools.partial(forward, seqs=seqs, rounds=rounds, plan=plan),
        grid=(steps,),
        in_specs=[block((length, width), 0), anywhere, block((length, width), rounds)] + [once(v) for v in fixed],
        out_specs=[block((ext, inner), 0), block((ext, n2), 0), block((length, LANES), 0)] + [once(v) for v in held] + [anywhere] * 10,
        out_shape=[shape_of(inner, BF16, ext), shape_of(n2, BF16, ext), shape_of(LANES, F32), *held,
                   shape_of(inner, BF16), shape_of(n2, BF16), shape_of(inner, F32), shape_of(LANES, F32), shape_of(LANES, F32),
                   jax.ShapeDtypeStruct((seqs, blocks, n, inner), F32), shape_of(width, BF16), shape_of(inner, F32),
                   shape_of(inner, F32), jax.ShapeDtypeStruct((n_chunks, CHUNK, width), BF16)],
        scratch_shapes=[
            vmem((seqs, length, inner), BF16), vmem((seqs, length, n2), BF16), vmem((seqs, length, inner), F32),
            vmem((seqs, length, LANES), F32), vmem((seqs, length, LANES), F32), vmem((seqs, blocks, n, inner), F32),
            vmem((ext, width), BF16), vmem((1, length, inner), F32), vmem((1, length, inner), F32),
            vmem((length // CHUNK, CHUNK, width), BF16), vmem((length, inner), BF16),
            vmem((ext, inner), F32), vmem((ext, n2), F32), vmem((n, inner), F32), vmem((8, LANES), F32),
            vmem((seqs, HALO, width), BF16), vmem((seqs, 8, length), F32), vmem((seqs, 4, 8, length), F32),
            dma((6, seqs)), dma((4,)), dma((seqs,)), dma((seqs,)), dma((seqs, 4)), dma((seqs, 4)),
        ] + Exchange.scratch(rounds, seqs, n, inner) + Rider.scratch(*plan, width),
        compiler_params=pltpu.CompilerParams(
            dimension_semantics=("arbitrary",), vmem_limit_bytes=62 * 1024 * 1024, collective_id=1, has_side_effects=True
        ),
        cost_estimate=pl.CostEstimate(flops=2 * flat * width * 4 * inner, bytes_accessed=10**8, transcendentals=0),
    )(tokens, tokens, cotangent, *fixed)
    plan = (plan[1], 2 * (seqs + rounds), n_chunks)
    gnormed, gate_grad, lend, rms, xg, cumg, stepg, bcg, mgg, skg, after, y = call(
        functools.partial(back_one, inner_all=inner_all, seqs=seqs, rounds=rounds, plan=plan), seqs + rounds, seqs,
        [xact, bcact, cum, gate, ssd, gn, sums, pre, gain, skip, wide]
        + [(v, rounds) for v in (xact, bcact, step, cum, lstart, entry, pre)],
        [big(inner, BF16), big(inner, BF16), ((seqs, blocks, n, inner), F32, 0), big(LANES, F32),
         big(inner, F32, lag=rounds), big(LANES, F32, lag=rounds), big(LANES, F32, lag=rounds), big(n2, F32, lag=rounds),
         ((8, inner), F32, None), ((8, inner), F32, None), ((seqs, n, inner), F32, None)],
        [vmem((T, inner), F32), vmem((n, inner), F32), vmem((n, inner), F32), vmem((seqs, length, inner), BF16),
         vmem((seqs, length, LANES), F32)]
        + Exchange.scratch(rounds, seqs, n, inner) + Rider.scratch(*plan, width),
        2 * flat * T * inner * 8, 3, y,
    )
    plan = (plan[0] + plan[1], 3 * seqs, n_chunks)
    xpg, xhalo, bpg, bhalo, raw, vkg, skgr, head_rows, y = call(
        functools.partial(back_two, seqs=seqs, plan=plan), seqs, seqs,
        [xact, bcact, xext, bcext, step, cum, sraw, xg, cumg, stepg, bcg, lstart, entry, lend, after, pre,
         value_kernel, vo, state_kernel, so, bias, rate, wide, tri],
        [big(inner, BF16), big(inner, BF16, HALO), big(n2, BF16), big(n2, BF16, HALO), big(LANES, BF16),
         ((8, inner), F32, None), ((8, n2), F32, None), ((8, LANES), F32, None)],
        [vmem((ext, inner), F32), vmem((ext, n2), F32), vmem((ext + HALO, inner), F32),
         vmem((ext + HALO, n2), F32)] + Rider.scratch(*plan, width),
        2 * flat * T * inner * 4, 5, y,
    )
    back = [(i + 1, i) for i in range(devices - 1)]
    xhalo, bhalo = lax.ppermute((xhalo, bhalo), "seq", back)
    xpg = xpg.at[:, length - HALO :].add(xhalo)
    bpg = bpg.at[:, length - HALO :].add(bhalo)

    def flatten(v):
        return v.reshape(flat, v.shape[-1])

    normed_f, xpg_f, bpg_f, raw_f, gg_f = [flatten(v) for v in (normed, xpg, bpg, raw, gate_grad)]
    out_weight_grad = t_mm(flatten(gnormed), flatten(cotangent)).astype(BF16)
    gate_weight_grad = t_mm(normed_f, gg_f).astype(BF16)
    head_row = jnp.pad(head_rows[:2].reshape(1, 2 * LANES), ((0, 0), (0, inner - 2 * LANES)))
    small = jnp.concatenate([vkg[: taps + 1], mgg[:1], skg[:1], head_row], axis=0)
    first = min(plan[0] + plan[1], n_chunks + 2 * LAG)
    plan = (first, max(n_chunks - first, 0) + 3 * LAG, n_chunks)

    def product_rows(v):
        return pl.BlockSpec((T, v.shape[1]), lambda i: (jnp.minimum(i // 2, flat // T - 1), 0))

    def lagged(cols, lag):
        return pl.BlockSpec((CHUNK, cols), lambda i: (jnp.clip(i - lag, 0, n_chunks - 1), 0))

    late = (gate_weight, value_weight, state_weight, step_w, norm_gain[None], small, skgr)
    result, tokens_grad, small, wout, wgate, wvalue, wmixed = pl.pallas_call(
        functools.partial(finish, n=n_chunks, rounds=rounds, plan=plan),
        grid=(n_chunks + 3 * LAG,),
        in_specs=[lagged(width, 3 * LAG)]
        + [product_rows(v) for v in (gg_f, xpg_f, bpg_f, raw_f)]
        + [lagged(width, 3 * LAG), lagged(width, 3 * LAG), lagged(LANES, 3 * LAG)]
        + [once(v) for v in late] + [product_rows(normed_f), product_rows(flatten(tokens))] + [anywhere] * 3,
        out_specs=[lagged(width, 3 * LAG), lagged(width, 3 * LAG), pl.BlockSpec((24, inner), lambda i: (0, 0)),
                   anywhere, anywhere, anywhere, anywhere],
        out_shape=[
            jax.ShapeDtypeStruct((flat, width), BF16), jax.ShapeDtypeStruct((flat, width), BF16),
            jax.ShapeDtypeStruct((24, inner), F32), *[jax.ShapeDtypeStruct((width, c), BF16) for c in (inner, inner, inner, n2 + LANES)],
        ],
        scratch_shapes=Chain.scratch(n_chunks, CHUNK, width) + Rider.scratch(*plan, width) + [
            vmem((24, inner), F32), vmem((rounds, 24, inner), F32), vmem((rounds, 24, inner), F32),
            pltpu.SemaphoreType.DMA((rounds,)), pltpu.SemaphoreType.DMA((rounds,)),

            vmem((3, width, inner), BF16), vmem((3, width, inner), BF16), vmem((width, n2 + LANES), BF16),
            vmem((width, n2 + LANES), BF16), vmem((4, width >> rounds, n2), BF16), vmem((width, inner), F32),
            vmem((width, n2 + LANES), F32), dma((4, GradSum.sem_count(rounds))), dma((3,)),
            vmem((16, inner), F32), vmem((4, 16, inner), F32), dma((8,)),
        ],
        compiler_params=pltpu.CompilerParams(
            dimension_semantics=("arbitrary",), vmem_limit_bytes=62 * 1024 * 1024, collective_id=4, has_side_effects=True
        ),
        cost_estimate=pl.CostEstimate(flops=10**11, bytes_accessed=10**8, transcendentals=0),
    )(y.reshape(flat, width), gg_f, xpg_f, bpg_f, raw_f, flatten(tokens), flatten(cotangent), flatten(rms),
      *late, normed_f, flatten(tokens), out_weight_grad, gate_weight_grad, y)
    result, tokens_grad = result.reshape(tokens.shape), tokens_grad.reshape(tokens.shape).astype(F32)
    vkg, mixer_gain_grad, skg, head_row = small[: taps + 1], small[taps + 1], small[taps + 2], small[taps + 3]
    norm_gain_grad = small[8:10].reshape(width)
    skgr = small[16:24, :n2]
    skip_gain_grad = jnp.sum(skg.reshape(heads, head_size), axis=1)
    step_bias_grad = head_row[:heads]
    log_rate_grad = head_row[LANES : LANES + heads] * rate_row
    out_weight_grad = jnp.concatenate([wout[:inner], wout[inner:]], axis=1).astype(F32)
    gate_weight_grad, value_weight_grad = wgate.astype(F32), wvalue.astype(F32)
    state_weight_grad = wmixed[:, :n2].astype(F32)
    step_weight_grad = wmixed[:, n2 : n2 + heads].astype(F32)
    return (
        result, tokens_grad, norm_gain_grad, gate_weight_grad, value_weight_grad, state_weight_grad,
        step_weight_grad, vkg[:taps], vkg[taps], skgr[:taps], skgr[taps], step_bias_grad, log_rate_grad,
        skip_gain_grad, mixer_gain_grad, out_weight_grad,
    )


def solution(mesh):
    rows, cols, vec = P(None, "seq", None), P(None, "head"), P("head")
    in_specs = (rows, P(), cols, cols, P(), cols, cols, vec, P(), P(), vec, vec, vec, vec, P("head", None), rows)
    out_specs = (rows, rows, P(), cols, cols, P(), cols, cols, vec, P(), P(), vec, vec, vec, vec, P("head", None))
    return jax.shard_map(shards, mesh=mesh, in_specs=in_specs, out_specs=out_specs, check_vma=False)
```

```python
import functools

import jax
import jax.numpy as jnp
from jax import lax
from jax.experimental import pallas as pl
from jax.experimental.pallas import tpu as pltpu
from jax.sharding import PartitionSpec as P

EPS = 1e-05
T = 256
SUB = 128
HALO = 16
LANES = 128
F32 = jnp.float32
BF16 = jnp.bfloat16


def mm(a, b):
    return lax.dot_general(a, b, (((1,), (0,)), ((), ())), preferred_element_type=F32)


def mm_t(a, b):
    return lax.dot_general(a, b, (((1,), (1,)), ((), ())), preferred_element_type=F32)


def t_mm(a, b):
    return lax.dot_general(a, b, (((0,), (0,)), ((), ())), preferred_element_type=F32)


def split(v, parts):
    pieces = []
    for _ in range(parts):
        piece = v.astype(BF16)
        pieces.append(piece)
        v = v - piece.astype(F32)
    return pieces


def expand(v, wide):
    return mm(jnp.concatenate(split(v, 2), axis=1), wide)


def expand_row(v, wide):
    return expand(jnp.broadcast_to(v, (16, LANES)), wide)[0:1]


def head_sum(v, wide):
    hi, lo = split(v, 2)
    return mm_t(hi, wide[:LANES]) + mm_t(lo, wide[:LANES])


def exact_tri(tri, v):
    a, b, c = split(v, 3)
    return mm(tri, a) + (mm(tri, b) + mm(tri, c))


def sigmoid(v):
    return 0.5 * jnp.tanh(0.5 * v) + 0.5


def softplus(v):
    return jnp.maximum(v, 0.0) + jnp.log1p(jnp.exp(-jnp.abs(v)))


def lower():
    row = lax.broadcasted_iota(jnp.int32, (SUB, SUB), 0)
    col = lax.broadcasted_iota(jnp.int32, (SUB, SUB), 1)
    return row >= col


def tile(i):
    return slice(i * SUB, (i + 1) * SUB)


def tiles():
    return [(i, j) for i in range(T // SUB) for j in range(i + 1)]


def cross_tiles(cm, bm):
    found = {}
    for i, j in tiles():
        value = mm_t(cm[tile(i)], bm[tile(j)])
        found[i, j] = jnp.where(lower(), value, 0.0) if i == j else value
    return found


def decay_tile(cum, cum_t, h, i, j):
    gap = cum[tile(i), h : h + 1] - cum_t[h : h + 1, tile(j)]
    return jnp.exp(jnp.minimum(gap, 0.0) if i == j else gap)


def half_mask(rows):
    return lax.broadcasted_iota(jnp.int32, (rows, LANES), 1) < LANES // 2


def pair_rows(v):
    left = half_mask(v.shape[0])
    zero = jnp.zeros_like(v)
    return jnp.concatenate([jnp.where(left, v, zero), jnp.where(left, zero, v)], axis=0)


def rows_of(b):
    return pl.ds(pl.multiple_of(b * T, T), T)


MESH = pl.DeviceIdType.MESH
CHUNK = 64
LAG = 2


def greet_head():
    z = lax.axis_index("head")
    for d in range(1, 4):
        pl.semaphore_signal(
            pltpu.get_barrier_semaphore(), inc=1, device_id={"head": lax.rem(z + d, 4)}, device_id_type=MESH)


class Chain:
    def __init__(self, own, got, far, sems):
        z = lax.axis_index("head")
        self.end = (z == 0) | (z == 3)
        self.side = z + 1 - 2 * (z % 2)
        self.other = 3 - z
        self.own, self.got, self.far = own, got, far
        self.sems = sems

    @staticmethod
    def scratch(n, chunk, width):
        buffer = pltpu.VMEM((n, chunk, width), BF16)
        return [buffer, buffer, buffer] + [pltpu.SemaphoreType.DMA((n,))] * 6

    def copy(self, kind, k):
        src, dst, to = [(self.own, self.got, self.side), (self.own, self.far, self.other), (self.got, self.got, self.side)][kind]
        return pltpu.make_async_remote_copy(
            src_ref=src.at[k], dst_ref=dst.at[k],
            send_sem=self.sems[2 * kind].at[k], recv_sem=self.sems[2 * kind + 1].at[k],
            device_id={"head": to}, device_id_type=MESH,
        )

    def inward(self, k):
        @pl.when(self.end)
        def _():
            self.copy(0, k).start()

    def meet(self, stage, k):
        self.copy(stage, k).wait_recv()
        if stage == 0:
            self.own[k] = (self.own[k].astype(F32) + self.got[k].astype(F32)).astype(BF16)
        else:
            self.got[k] = (self.own[k].astype(F32) + self.far[k].astype(F32)).astype(BF16)

    def onward(self, stage, k):
        @pl.when(jnp.logical_not(self.end))
        def _():
            self.meet(stage - 1, k)
            self.copy(stage, k).start()

    def total(self, k):
        @pl.when(self.end)
        def _():
            self.copy(2, k).wait_recv()

        return self.got[k].astype(F32)

    def drain(self, n):
        def one(k, _):
            @pl.when(self.end)
            def _():
                self.copy(0, k).wait_send()

            @pl.when(jnp.logical_not(self.end))
            def _():
                self.copy(1, k).wait_send()
                self.copy(2, k).wait_send()

            return 0

        lax.fori_loop(0, n, one, 0)


class Rider:
    def __init__(self, first, ticks, count, hbm, own, got, far, sems, local):
        self.first, self.ticks, self.count = first, ticks, count
        self.done = min(max(first - 2 * LAG, 0), count)
        self.base = min(self.done, count - 1)
        self.hbm, self.local = hbm, local
        self.chain = Chain(own, got, far, sems)

    @staticmethod
    def size(first, ticks, count):
        return max(min(first + ticks, count) - min(max(first - 2 * LAG, 0), count - 1), 1)

    @staticmethod
    def scratch(first, ticks, count, width):
        return Chain.scratch(Rider.size(first, ticks, count), CHUNK, width) + [pltpu.SemaphoreType.DMA((2,))]

    def span(self, stage):
        low = self.first - stage * LAG
        return max(low, 0), min(low + self.ticks, self.count)

    def load(self):
        size = self.size(self.first, self.ticks, self.count)
        own = pltpu.make_async_copy(self.hbm.at[pl.ds(self.base, size)], self.chain.own, self.local.at[0])
        own.start()
        ready = min(max(self.first - LAG, 0), self.count) - self.base
        if ready > 0 and self.done < self.count:

            @pl.when(jnp.logical_not(self.chain.end))
            def _():
                got = pltpu.make_async_copy(
                    self.hbm.at[pl.ds(self.base, ready)], self.chain.got.at[pl.ds(0, ready)], self.local.at[1])
                got.start()
                got.wait()

        own.wait()

    def tick(self, t):
        chain = self.chain
        for stage in (2, 1, 0):
            low, high = self.span(stage)
            k = self.first - stage * LAG + t

            @pl.when((k >= low) & (k < high) & (t < self.ticks))
            def _():
                at = k - self.base
                if stage == 0:
                    chain.inward(at)
                else:
                    self.follow(stage, at, t >= LAG)

    def follow(self, stage, at, pending):
        chain = self.chain
        middle = jnp.logical_not(chain.end)

        @pl.when(middle & pending)
        def _():
            chain.meet(stage - 1, at)

        @pl.when(middle)
        def _():
            chain.copy(stage, at).start()

    def drain(self):
        chain = self.chain

        def each(stage):
            low, high = self.span(stage)
            lax.fori_loop(low - self.base, high - self.base, lambda k, _: (chain.copy(stage, k).wait_send(), 0)[1], 0)

        @pl.when(chain.end)
        def _():
            each(0)

        @pl.when(jnp.logical_not(chain.end))
        def _():
            each(1)
            each(2)

    def close(self):
        chain = self.chain
        middle = jnp.logical_not(chain.end)

        def each(low, high, do):
            if high > low:
                lax.fori_loop(low - self.base, high - self.base, lambda k, _: (do(k), 0)[1], 0)

        @pl.when(middle)
        def _():
            for stage in (0, 1):
                low, high = self.span(stage)
                started = max(self.first - stage * LAG + self.ticks - LAG, low)
                each(started, high, lambda k: chain.meet(stage, k))
            for stage in (1, 2):
                each(*self.span(stage), lambda k: chain.copy(stage, k).wait_send())

        @pl.when(chain.end)
        def _():
            each(*self.span(2), lambda k: chain.copy(2, k).wait_recv())
            each(*self.span(0), lambda k: chain.copy(0, k).wait_send())

        def store(ref, low, high):
            if high > low:
                at = pl.ds(low - self.base, high - low)
                copy = pltpu.make_async_copy(ref.at[at], self.hbm.at[pl.ds(low, high - low)], self.local.at[0])
                copy.start()
                copy.wait()

        @pl.when(middle)
        def _():
            reached = self.span(1)[1]
            store(chain.got, self.done, reached)
            store(chain.own, reached, self.span(0)[1])

        @pl.when(chain.end)
        def _():
            store(chain.got, *self.span(2))


class Exchange:
    def __init__(self, rounds, backward, total, before, logs, out, back, send, recv):
        self.rounds, self.backward = rounds, backward
        self.total, self.before, self.logs = total, before, logs
        self.out, self.back, self.send, self.recv = out, back, send, recv
        self.me = lax.axis_index("seq")

    def partner(self, r):
        bit = 1 << r
        return self.me + bit - 2 * bit * (lax.div(self.me, bit) % 2)

    def greet(self, with_head=False):
        barrier = pltpu.get_barrier_semaphore()
        for r in range(self.rounds):
            pl.semaphore_signal(barrier, inc=1, device_id={"seq": self.partner(r)}, device_id_type=MESH)
        if with_head:
            greet_head()
        pl.semaphore_wait(barrier, self.rounds + 3 * with_head)

    def copy(self, r, s):
        return pltpu.make_async_remote_copy(
            src_ref=self.out.at[r], dst_ref=self.back.at[r, s],
            send_sem=self.send.at[r], recv_sem=self.recv.at[r, s],
            device_id={"seq": self.partner(r)}, device_id_type=MESH,
        )

    def begin(self, s, state, log):
        self.total[s] = state
        self.before[s] = jnp.zeros_like(state)
        self.logs[s] = jnp.zeros(self.logs.shape[1:], F32)
        self.logs[s, 0:1] = log

    def push(self, r, s):
        n = self.total.shape[1]
        self.out[r, 0:n] = self.total[s].astype(BF16)
        hi, mid, lo = [v.astype(F32) for v in split(self.logs[s, 0:1], 3)]
        at = lax.broadcasted_iota(jnp.int32, (HALO, hi.shape[1]), 0)
        tail = jnp.where(at == 0, hi, jnp.where(at == 1, mid, jnp.where(at == 2, lo, 0.0)))
        self.out[r, n : n + HALO] = tail.astype(BF16)
        self.copy(r, s).start()

    def take(self, r, s):
        n = self.total.shape[1]
        copy = self.copy(r, s)
        copy.wait_recv()
        copy.wait_send()
        state = self.back[r, s, 0:n].astype(F32)
        tail = self.back[r, s, n : n + HALO].astype(F32)
        log = tail[0:1] + tail[1:2] + tail[2:3]
        upper = lax.div(self.me, 1 << r) % 2 == 1
        near = jnp.logical_not(upper) if self.backward else upper
        mine, theirs = self.logs[s, 0:1], self.logs[s, 1:2]
        self.before[s] = self.before[s] + jnp.where(near, jnp.exp(theirs), 0.0) * state
        self.logs[s, 1:2] = theirs + jnp.where(near, log, 0.0)
        own = jnp.where(near, 1.0, jnp.exp(log))
        other = jnp.where(near, jnp.exp(mine), 1.0)
        self.total[s] = own * self.total[s] + other * state
        self.logs[s, 0:1] = mine + log

    def advance(self, i, seqs):
        for r in reversed(range(self.rounds)):
            s = i - 1 - r

            @pl.when((s >= 0) & (s < seqs))
            def _():
                self.take(r, s)
                if r + 1 < self.rounds:
                    self.push(r + 1, s)

    @staticmethod
    def scratch(rounds, seqs, n, inner):
        return [
            pltpu.VMEM((seqs, n, inner), F32), pltpu.VMEM((seqs, 8, inner), F32),
            pltpu.VMEM((rounds, n + HALO, inner), BF16), pltpu.VMEM((rounds, seqs, n + HALO, inner), BF16),
            pltpu.SemaphoreType.DMA((rounds,)), pltpu.SemaphoreType.DMA((rounds, seqs)),
        ]


class Row:
    def __init__(self, ref):
        self.ref = ref

    def __getitem__(self, _):
        return self.ref[...].reshape(1, self.ref.shape[0])


def forward(
    tok, tok_all, cot, ngain, gate_w, value_w, state_w, step_w, vk, vo, sk, so, sbias, rate, wide, tri, out_w, mgain, skip,
    xext_o, bcext_o, sraw_o, pre_o, entry_o, sums_o,
    xact_h, bcact_h, gate_h, step_h, cum_h, lstart_h, normed_h, ssd_h, gn_h, y_h,
    xact, bcact, gate, step, cum, lstart, nx, ssd, gn, y_s, gm, xe, be, st, run, halo, mine, slots,
    kept_sems, slot_sems, halo_send, halo_recv, sum_send, sum_recv,
    total, logs, out, back, send, recv,
    yown, ygot, yfar, ta, tb, tc, td, te, tf, ylocal,
    *, seqs, rounds, plan,
):
    ngain, vo, so, mgain = Row(ngain), Row(vo), Row(so), Row(mgain)
    i = pl.program_id(0)
    s = i - rounds
    steps = seqs + rounds
    length = tok.shape[1]
    me, devices = lax.axis_index("seq"), lax.axis_size("seq")
    z = lax.axis_index("head")
    scan = Exchange(rounds, False, total, entry_o, logs, out, back, send, recv)
    rider = Rider(*plan, y_h, yown, ygot, yfar, (ta, tb, tc, td, te, tf), ylocal)
    kept = [(xact, xact_h), (bcact, bcact_h), (gate, gate_h), (step, step_h), (cum, cum_h), (lstart, lstart_h)]
    per_seq = length // CHUNK

    def halo_copy(q):
        return pltpu.make_async_remote_copy(
            src_ref=tok_all.at[q, pl.ds(length - HALO, HALO)], dst_ref=halo.at[q],
            send_sem=halo_send.at[q], recv_sem=halo_recv.at[q],
            device_id={"seq": lax.rem(me + 1, devices)}, device_id_type=MESH,
        )

    def keep(k, q):
        src, dst = kept[k]
        return pltpu.make_async_copy(src.at[q], dst.at[q], kept_sems.at[k, q])

    def normed_copy(q):
        return pltpu.make_async_copy(nx.at[pl.ds(HALO, length)], normed_h.at[q], slot_sems.at[0])

    def scan_copies(q):
        return [
            pltpu.make_async_copy(ssd.at[0], ssd_h.at[q], slot_sems.at[1]),
            pltpu.make_async_copy(gn.at[0], gn_h.at[q], slot_sems.at[2]),
        ]

    def y_copy(q, skip_rider):
        first = plan[1] if skip_rider else 0
        at = pl.ds(q * per_seq + first, per_seq - first)
        return pltpu.make_async_copy(y_s.at[pl.ds(first, per_seq - first)], y_h.at[at], slot_sems.at[3])

    def sum_copy(q, d):
        return pltpu.make_async_remote_copy(
            src_ref=mine.at[q], dst_ref=slots.at[q, z], send_sem=sum_send.at[q, d], recv_sem=sum_recv.at[q, d],
            device_id={"head": lax.rem(z + d, 4)}, device_id_type=MESH,
        )

    @pl.when(i == 0)
    def _():
        barrier = pltpu.get_barrier_semaphore()
        for d in range(1, devices):
            pl.semaphore_signal(barrier, inc=1, device_id={"seq": lax.rem(me + d, devices)}, device_id_type=MESH)
        greet_head()
        pl.semaphore_wait(barrier, devices - 1 + 3)

        @pl.when(me < devices - 1)
        def _():
            for q in range(seqs):
                halo_copy(q).start()

        @pl.when(me == 0)
        def _():
            halo[...] = jnp.zeros_like(halo)

    @pl.when(i < seqs)
    def _():
        @pl.when(i > 0)
        def _():
            normed_copy(i).wait()

        def arrive():
            @pl.when(me > 0)
            def _():
                halo_copy(i).wait_recv()

        one = pl.ds(i, 1)
        front_rows(
            tok, halo.at[one], ngain, gate_w, value_w, state_w, step_w, vk, vo, sk, so, sbias, rate, wide, tri,
            gate.at[one], xext_o, bcext_o, sraw_o, xact.at[one], bcact.at[one], step.at[one], cum.at[one],
            lstart.at[one], pre_o.at[one], nx, xe, be, st, run, arrive,
        )
        normed_copy(i).start()
        for k in range(len(kept)):
            keep(k, i).start()
        scan.begin(i, st[...], expand_row(run[0:1], wide[...]))

    scan.advance(i, seqs)

    @pl.when(i < seqs)
    def _():
        scan.push(0, i)

    @pl.when(s >= 0)
    def _():
        @pl.when(s > 0)
        def _():
            for copy in scan_copies(s):
                copy.wait()

        one = pl.ds(s, 1)
        scan_out(
            xact.at[one], bcact.at[one], step.at[one], cum.at[one], gate.at[one], lstart.at[one], entry_o.at[one],
            pre_o.at[one], cot, out_w, mgain, skip, wide, ssd, gn, mine.at[one], gm, lambda b: rider.tick((s - 1) * 2 + b),
        )
        for copy in scan_copies(s):
            copy.start()
        for d in range(1, 4):
            sum_copy(s, d).start()
        slots[s, z] = mine[s]

        @pl.when(s == 1)
        def _():
            y_copy(0, True).wait()

        @pl.when(s > 1)
        def _():
            y_copy(s, False).wait()

        for b in range(length // T):
            value = mm(gm[b * T : (b + 1) * T], out_w[...]).astype(BF16)
            y_s[b * T // CHUNK : (b + 1) * T // CHUNK] = value.reshape(T // CHUNK, CHUNK, value.shape[1])

        @pl.when(s == 0)
        def _():
            yown[...] = y_s[0 : plan[1]]
            y_copy(0, True).start()

        @pl.when(s > 0)
        def _():
            y_copy(s, False).start()

    @pl.when(i == steps - 1)
    def _():
        rider.close()
        for q in range(seqs):
            for d in range(1, 4):
                sum_copy(q, d).wait()
            sums_o[q] = (slots[q, 0] + slots[q, 1]) + (slots[q, 2] + slots[q, 3])
            for k in range(len(kept)):
                keep(k, q).wait()
        normed_copy(0).wait()
        for copy in scan_copies(0):
            copy.wait()
        y_copy(1, False).wait()

        @pl.when(me < devices - 1)
        def _():
            for q in range(seqs):
                halo_copy(q).wait_send()


def front_rows(
    tok, halo, ngain, gate_w, value_w, state_w, step_w, vk, vo, sk, so, sbias, rate, wide, tri,
    gate_o, xext_o, bcext_o, sraw_o, xact_o, bcact_o, step_o, cum_o, lstart_o, pre_o,
    nx, xe, be, st, run, arrive,
):
    length = tok.shape[1]
    blocks = length // T
    n = bcact_o.shape[2] // 2

    def norm(v):
        v = v.astype(F32)
        inv = lax.rsqrt(jnp.mean(v * v, axis=1, keepdims=True) + EPS)
        return (v * inv * ngain[...]).astype(BF16)

    def norm_rows(b, _):
        nx[pl.ds(pl.multiple_of(HALO + b * SUB, HALO), SUB), :] = norm(tok[0, pl.ds(pl.multiple_of(b * SUB, SUB), SUB), :])
        return 0

    lax.fori_loop(0, length // SUB, norm_rows, 0)
    gate_o[0] = mm(nx[HALO:], gate_w[...])
    sraw_o[0] = mm(nx[HALO:], step_w[...])
    arrive()
    nx[0:HALO] = norm(halo[0])
    x = mm(nx[...], value_w[...]).astype(BF16)
    xext_o[0] = x
    xe[...] = x.astype(F32)
    bc = mm(nx[...], state_w[...]).astype(BF16)
    bcext_o[0] = bc
    be[...] = bc.astype(F32)
    st[...] = jnp.zeros_like(st)
    run[...] = jnp.zeros_like(run)
    pre_o[0] = jnp.zeros_like(pre_o[0])
    for b in range(blocks):
        r0 = b * T
        r = slice(r0, r0 + T)
        taps = vk.shape[0]
        base = HALO - taps + 1
        xc = vo[...] + vk[0:1] * xe[r0 + base : r0 + base + T]
        bcc = so[...] + sk[0:1] * be[r0 + base : r0 + base + T]
        for k in range(1, taps):
            xc = xc + vk[k : k + 1] * xe[r0 + base + k : r0 + base + k + T]
            bcc = bcc + sk[k : k + 1] * be[r0 + base + k : r0 + base + k + T]
        xa = (xc * sigmoid(xc)).astype(BF16)
        bca = (bcc * sigmoid(bcc)).astype(BF16)
        xact_o[0, r, :] = xa
        bcact_o[0, r, :] = bca
        step = softplus(sraw_o[0, r, :] + sbias[...])
        cum = exact_tri(tri[...], step * rate[...])
        step_o[0, r, :] = step
        cum_o[0, r, :] = cum
        last = cum[T - 1 : T]
        weight = jnp.exp(last - cum) * step
        weighted = (xa.astype(F32) * expand(weight, wide[...])).astype(BF16)
        contrib = t_mm(bca[:, :n], weighted)
        lstart_o[0, b] = st[...]
        st[...] = expand_row(jnp.exp(last), wide[...]) * st[...] + contrib
        run[0:1] = run[0:1] + last
        pre_o[0, b + 1 : b + 2] = run[0:1]


def scan_out(
    xact, bcact, step_i, cum_i, gate, lstart, entry, pre, cot, out_w, mgain, skip, wide,
    ssd_o, gn_o, sums_o, gm, tick,
):
    length = xact.shape[1]
    blocks = length // T
    n = bcact.shape[2] // 2
    inner = xact.shape[2]
    gn_o[0] = mm_t(cot[0], out_w[...])

    def block(b, _):
        tick(b)
        r = rows_of(b)
        xa = xact[0, r, :]
        bca = bcact[0, r, :]
        bm, cm = bca[:, :n], bca[:, n:]
        cum = cum_i[0, r, :]
        cum_t = cum.T
        cross = cross_tiles(cm, bm)
        start = expand_row(jnp.exp(pre[0, pl.ds(b, 1), :]), wide[...]) * entry[0] + lstart[0, b]
        start = start.astype(BF16)
        grown = jnp.exp(cum)
        cm = cm.astype(F32)
        xs = (xa.astype(F32) * expand(step_i[0, r, :], wide[...])).astype(BF16)
        for p in range(inner // LANES):
            lanes = slice(p * LANES, (p + 1) * LANES)
            two = (2 * p, 2 * p + 1)
            start_two = pair_rows(start[:, lanes])
            xs_two = [pair_rows(xs[tile(j), lanes]) for j in range(T // SUB)]
            for i in range(T // SUB):
                left = [(cm[tile(i)] * grown[tile(i), h : h + 1]).astype(BF16) for h in two]
                right = [start_two]
                for j in range(i + 1):
                    left += [(cross[i, j] * decay_tile(cum, cum_t, h, i, j)).astype(BF16) for h in two]
                    right.append(xs_two[j])
                rows = pl.ds(pl.multiple_of(b * T + i * SUB, SUB), SUB)
                ssd_o[0, rows, lanes] = mm(jnp.concatenate(left, axis=1), jnp.concatenate(right, axis=0))
        mixed = ssd_o[0, r, :] + skip[...] * xa.astype(F32)
        g = gate[0, r, :]
        gated = mixed * (g * sigmoid(g))
        gg = gated * mgain[...]
        gm[r, :] = gg.astype(BF16)
        squares = jnp.sum(gated * gated, axis=1, keepdims=True)
        dots = jnp.sum(gg * gn_o[0, r, :], axis=1, keepdims=True)
        lane = lax.broadcasted_iota(jnp.int32, (T, LANES), 1)
        both = jnp.where(lane == 0, squares, jnp.where(lane == 1, dots, 0.0))
        sums_o[0, :, r] = both.T[0:8]
        return 0

    lax.fori_loop(0, blocks, block, 0)


def back_one(
    xact, bcact, cum_i, gate, ssd, gn, sums, pre, mgain, skip, wide,
    xact_b, bcact_b, step_b, cum_b, lstart_b, entry_b, pre_b, y_in,
    gnormed_o, gate_grad_o, lend_o, rms_o, xg_o, cumg_o, stepg_o, bcg_o, mgg_o, skg_o, after_o, y_all,
    z, acc, use, dys, cumg, total, logs, out, back, send, recv,
    yown, ygot, yfar, ta, tb, tc, td, te, tf, ylocal,
    *, inner_all, seqs, rounds, plan,
):
    mgain = Row(mgain)
    i = pl.program_id(0)
    s = i - rounds
    blocks = xact.shape[1] // T
    scan = Exchange(rounds, True, total, after_o, logs, out, back, send, recv)
    rider = Rider(*plan, y_all, yown, ygot, yfar, (ta, tb, tc, td, te, tf), ylocal)
    per_step = plan[1] // (seqs + rounds)

    @pl.when(i == 0)
    def _():
        scan.greet(with_head=True)
        rider.load()
        mgg_o[...] = jnp.zeros_like(mgg_o)
        skg_o[...] = jnp.zeros_like(skg_o)

    ticks = min(per_step, 3)
    rider.tick(i * per_step)

    @pl.when(i < seqs)
    def _():
        one = pl.ds(i, 1)
        gate_back(
            xact, bcact, cum_i, gate, ssd, gn, sums, mgain, skip, wide, gnormed_o, gate_grad_o, lend_o, rms_o, mgg_o, skg_o,
            dys.at[one], cumg.at[one], acc, use, inner_all,
        )
        scan.begin(i, acc[...], expand_row(pre[0, blocks : blocks + 1], wide[...]))

    scan.advance(i, seqs)

    @pl.when(i < seqs)
    def _():
        scan.push(0, i)

    @pl.when(s >= 0)
    def _():
        one = pl.ds(s, 1)
        scan_back(
            xact_b, bcact_b, step_b, cum_b, lstart_b, entry_b, pre_b, skip, wide, dys.at[one], cumg.at[one],
            xg_o, cumg_o, stepg_o, bcg_o, z, lambda b: rider.tick(jnp.where(1 + b < ticks, i * per_step + 1 + b, plan[1])),
        )

    @pl.when(s < 0)
    def _():
        for k in range(1, per_step):
            rider.tick(i * per_step + k)

    @pl.when(i == seqs + rounds - 1)
    def _():
        rider.close()


def gate_back(
    xact, bcact, cum_i, gate, ssd, gn, sums, mgain, skip, wide, gnormed_o, gate_grad_o, lend_o, rms_o, mgg_o, skg_o,
    dys, cumg, acc, use, inner_all,
):
    length = xact.shape[1]
    blocks = length // T
    n = bcact.shape[2] // 2
    inner = xact.shape[2]
    acc[...] = jnp.zeros_like(acc)

    def block(k, _):
        b = blocks - 1 - k
        r = rows_of(b)
        sums_b = sums[0, :, r]
        columns = jnp.concatenate([sums_b, jnp.zeros((LANES - 8, T), F32)], axis=0).T
        for i in range(T // SUB):
            ri = pl.ds(pl.multiple_of(b * T + i * SUB, SUB), SUB)
            xa = xact[0, ri, :].astype(F32)
            rms = lax.rsqrt(columns[tile(i), 0:1] / inner_all + EPS)
            rms_o[0, ri, :] = jnp.broadcast_to(rms, (SUB, LANES))
            coef = rms * rms * rms * (columns[tile(i), 1:2] / inner_all)
            ssd_r = ssd[0, ri, :]
            mixed = ssd_r + skip[...] * xa
            g = gate[0, ri, :]
            sg = sigmoid(g)
            gated = mixed * (g * sg)
            grad_norm = gn[0, ri, :]
            normalised = gated * rms
            gnormed_o[0, ri, :] = (normalised * mgain[...]).astype(BF16)
            mgg_o[0:1] += jnp.sum(grad_norm * normalised, axis=0, keepdims=True)
            grad_gated = rms * (grad_norm * mgain[...]) - gated * coef
            gate_grad_o[0, ri, :] = (grad_gated * mixed * (sg * (1.0 + g * (1.0 - sg)))).astype(BF16)
            grad_mixed = grad_gated * (g * sg)
            skg_o[0:1] += jnp.sum(grad_mixed * xa, axis=0, keepdims=True)
            dy = grad_mixed.astype(BF16)
            dys[0, ri, :] = dy
            cumg[0, ri, :] = head_sum(dy.astype(F32) * ssd_r, wide[...])
        cm = bcact[0, r, n:].astype(F32)
        grown = jnp.exp(cum_i[0, r, :])
        for p in range(inner // LANES):
            lanes = slice(p * LANES, (p + 1) * LANES)
            scaled = [(cm * grown[:, h : h + 1]).astype(BF16) for h in (2 * p, 2 * p + 1)]
            used = None
            for i in range(T // SUB):
                ri = pl.ds(pl.multiple_of(b * T + i * SUB, SUB), SUB)
                term = t_mm(jnp.concatenate([v[tile(i)] for v in scaled], axis=0), pair_rows(dys[0, ri, lanes]))
                used = term if used is None else used + term
            use[:, lanes] = used
        lend_o[0, b] = acc[...]
        acc[...] = expand_row(grown[T - 1 : T], wide[...]) * acc[...] + use[...]
        return 0

    lax.fori_loop(0, blocks, block, 0)


def scan_back(
    xact, bcact, step_i, cum_i, lstart, entry, pre, skip, wide, dys, cumg, xg_o, cumg_o, stepg_o, bcg_o, z, tick,
):
    length = xact.shape[1]
    blocks = length // T
    n = bcact.shape[2] // 2
    inner = xact.shape[2]

    def block(b, _):
        tick(b)
        r = rows_of(b)
        dy = dys[0, r, :]
        xa = xact[0, r, :].astype(F32)
        bca = bcact[0, r, :]
        bm, cm = bca[:, :n], bca[:, n:]
        cum = cum_i[0, r, :]
        cum_t = cum.T
        start = expand_row(jnp.exp(pre[0, pl.ds(b, 1), :]), wide[...]) * entry[0] + lstart[0, b]
        start = start.astype(BF16)
        dy32 = dy.astype(F32)
        gdy_hi, gdy_lo = split(expand(jnp.exp(cum), wide[...]) * dy32, 2)
        c_grad = mm_t(gdy_hi, start) + mm_t(gdy_lo, start)
        step_wide = expand(step_i[0, r, :], wide[...])
        xs = (xa * step_wide).astype(BF16)
        cross = cross_tiles(cm, bm)
        cross_part = {ij: jnp.zeros((SUB, SUB), F32) for ij in tiles()}
        for p in range(inner // LANES):
            lanes = slice(p * LANES, (p + 1) * LANES)
            zs = [None] * (T // SUB)
            for i in range(T // SUB):
                dy_two = pair_rows(dy[tile(i), lanes])
                for j in range(i + 1):
                    mix_grad = mm_t(dy_two, xs[tile(j), lanes])
                    mix = []
                    for k, h in enumerate((2 * p, 2 * p + 1)):
                        decay = decay_tile(cum, cum_t, h, i, j)
                        mix.append((cross[i, j] * decay).astype(BF16))
                        cross_part[i, j] = cross_part[i, j] + mix_grad[tile(k)] * decay
                    term = t_mm(jnp.concatenate(mix, axis=0), dy_two)
                    zs[j] = term if zs[j] is None else zs[j] + term
            for j in range(T // SUB):
                z[tile(j), lanes] = zs[j]
        rows = []
        for i in range(T // SUB):
            row = [jnp.where(lower(), cross_part[i, j], 0.0) if i == j else cross_part[i, j] for j in range(i + 1)]
            row += [jnp.zeros((SUB, SUB), F32)] * (T // SUB - 1 - i)
            rows.append(jnp.concatenate(row, axis=1))
        cross_low = jnp.concatenate(rows, axis=0).astype(BF16)
        bcg_o[0, r, 0:n] = t_mm(cross_low, cm)
        bcg_o[0, r, n : 2 * n] = c_grad + mm(cross_low, bm)
        zz = z[...]
        xg_o[0, r, :] = skip[...] * dy32 + step_wide * zz
        cumg_o[0, r, :] = cumg[0, r, :] - head_sum(xs.astype(F32) * zz, wide[...])
        stepg_o[0, r, :] = head_sum(xa * zz, wide[...])
        return 0

    lax.fori_loop(0, blocks, block, 0)


def back_two(
    xact, bcact, xext, bcext, step_i, cum_i, sraw, xg, cumg, stepg, bcg, lstart, entry, lend, after, pre,
    gnormed, cot, normed, gate_grad, vk, vo, sk, so, sbias, rate, wide, tri, y_in,
    xpg_o, xhalo_o, bpg_o, bhalo_o, raw_o, vkg_o, skg_o, heads_o, wout_o, wgate_o, y_all,
    xe, be, xcg, bcg_s, out_acc, gate_acc, yown, ygot, yfar, ta, tb, tc, td, te, tf, ylocal,
    *, seqs, plan,
):
    length = xact.shape[1]
    blocks = length // T
    n = bcact.shape[2] // 2
    taps = vk.shape[0]
    base = HALO - taps + 1
    vo, so = Row(vo), Row(so)
    step_at = pl.program_id(0)
    rider = Rider(*plan, y_all, yown, ygot, yfar, (ta, tb, tc, td, te, tf), ylocal)

    @pl.when(step_at == 0)
    def _():
        greet_head()
        pl.semaphore_wait(pltpu.get_barrier_semaphore(), 3)
        rider.load()
        out_acc[...] = jnp.zeros_like(out_acc)
        gate_acc[...] = jnp.zeros_like(gate_acc)
        vkg_o[...] = jnp.zeros_like(vkg_o)
        skg_o[...] = jnp.zeros_like(skg_o)
        heads_o[...] = jnp.zeros_like(heads_o)

    xe[...] = xext[0].astype(F32)
    be[...] = bcext[0].astype(F32)
    for ref in (xcg, bcg_s):
        ref[0:HALO] = jnp.zeros((HALO, ref.shape[1]), F32)
        ref[HALO + length :] = jnp.zeros((HALO, ref.shape[1]), F32)

    def conv_rows(ext, kernel, offset, r0):
        total = offset[...] + kernel[0:1] * ext[r0 + base : r0 + base + T]
        for k in range(1, taps):
            total = total + kernel[k : k + 1] * ext[r0 + base + k : r0 + base + k + T]
        sg = sigmoid(total)
        return sg * (1.0 + total * (1.0 - sg))

    def filter_grad(grad, ext, out, r0):
        for k in range(taps):
            out[k : k + 1] += jnp.sum(grad * ext[r0 + base + k : r0 + base + k + T], axis=0, keepdims=True)
        out[taps : taps + 1] += jnp.sum(grad, axis=0, keepdims=True)

    per_step = plan[1] // seqs
    for b in range(blocks):
        rider.tick(step_at * per_step + b)
        r0 = b * T
        r = slice(r0, r0 + T)
        xa = xact[0, r, :].astype(F32)
        bm = bcact[0, r, 0:n]
        cum = cum_i[0, r, :]
        step = step_i[0, r, :]
        last = cum[T - 1 : T]
        start = expand_row(jnp.exp(pre[0, b : b + 1]), wide[...]) * entry[0] + lstart[0, b]
        suffix = jnp.exp(pre[0, blocks : blocks + 1] - pre[0, b + 1 : b + 2])
        end = expand_row(suffix, wide[...]) * after[0] + lend[0, b]
        end_low = end.astype(BF16)
        weighted_grad = mm(bm, end_low)
        reach = jnp.exp(last - cum)
        weight = reach * step
        weight_wide = expand(weight, wide[...])
        weighted = (xa * weight_wide).astype(BF16)
        bcg_b = bcg[0, r, :]
        b_total = bcg_b[:, 0:n] + mm_t(weighted, end_low)
        bc_total = jnp.concatenate([b_total, bcg_b[:, n:]], axis=1)
        w_grad = head_sum(weighted_grad * xa, wide[...])
        part = w_grad * weight
        product = jnp.broadcast_to(jnp.sum(end * start, axis=0, keepdims=True), (16, end.shape[1]))
        fade_grad = jnp.exp(last) * head_sum(product, wide[...])[0:1]
        at_last = lax.broadcasted_iota(jnp.int32, (T, LANES), 0) == T - 1
        extra = fade_grad + jnp.sum(part, axis=0, keepdims=True)
        cum_grad = cumg[0, r, :] - part + jnp.where(at_last, extra, 0.0)
        a, bb, c = split(cum_grad, 3)
        rise = t_mm(tri[...], a) + (t_mm(tri[...], bb) + t_mm(tri[...], c))
        step_grad = stepg[0, r, :] + w_grad * reach + rise * rate[...]
        raw = step_grad * sigmoid(sraw[0, r, :] + sbias[...])
        raw_o[0, r, :] = raw.astype(BF16)
        heads_o[0:1] += jnp.sum(raw, axis=0, keepdims=True)
        heads_o[1:2] += jnp.sum(rise * step, axis=0, keepdims=True)
        grad = (xg[0, r, :] + weighted_grad * weight_wide) * conv_rows(xe, vk, vo, r0)
        filter_grad(grad, xe, vkg_o, r0)
        xcg[HALO + r0 : HALO + r0 + T] = grad
        grad = bc_total * conv_rows(be, sk, so, r0)
        filter_grad(grad, be, skg_o, r0)
        bcg_s[HALO + r0 : HALO + r0 + T] = grad

    def conv_back(ref, kernel, r0, rows):
        total = kernel[0:1] * ref[r0 + taps - 1 : r0 + taps - 1 + rows]
        for k in range(1, taps):
            total = total + kernel[k : k + 1] * ref[r0 + taps - 1 - k : r0 + taps - 1 - k + rows]
        return total.astype(BF16)

    for acc, left, right in ((out_acc, gnormed, cot), (gate_acc, normed, gate_grad)):
        for m in range(acc.shape[0] // 256):
            at = slice(m * 256, (m + 1) * 256)
            acc[at] += t_mm(left[0, :, at], right[0])

    xhalo_o[0] = conv_back(xcg, vk, 0, HALO)
    bhalo_o[0] = conv_back(bcg_s, sk, 0, HALO)
    for b in range(blocks):
        if blocks + b < per_step:
            rider.tick(step_at * per_step + blocks + b)
        r0 = b * T
        xpg_o[0, r0 : r0 + T] = conv_back(xcg, vk, HALO + r0, T)
        bpg_o[0, r0 : r0 + T] = conv_back(bcg_s, sk, HALO + r0, T)

    @pl.when(step_at == seqs - 1)
    def _():
        wout_o[...] = out_acc[...].astype(BF16)
        wgate_o[...] = gate_acc[...].astype(BF16)
        rider.close()


class GradSum:
    def __init__(self, rounds, mine, back, out, sems, zback=None, shared=0):
        self.rounds, self.mine, self.back, self.out, self.sems = rounds, mine, back, out, sems
        self.zback, self.shared = zback, shared
        self.me, self.z = lax.axis_index("seq"), lax.axis_index("head")
        self.rows = mine.shape[0]
        self.share = self.rows >> rounds

    @staticmethod
    def sem_count(rounds):
        return 4 * rounds + 9

    def bit(self, r):
        return lax.div(self.me, 1 << r) % 2

    def partner(self, r):
        return self.me + (1 << r) - (2 << r) * self.bit(r)

    def first(self, r):
        row = 0
        for k in range(r):
            row = row + self.bit(k) * (self.rows >> (k + 1))
        return row

    def at(self, row, size):
        return pl.ds(pl.multiple_of(row, 16), size)

    def halving(self, r):
        half = self.rows >> (r + 1)
        theirs = self.first(r) + half - half * self.bit(r)
        return pltpu.make_async_remote_copy(
            src_ref=self.mine.at[self.at(theirs, half)], dst_ref=self.back.at[pl.ds(self.rows - 2 * half, half)],
            send_sem=self.sems.at[r], recv_sem=self.sems.at[self.rounds + r],
            device_id={"seq": self.partner(r)}, device_id_type=MESH,
        )

    def add_half(self, r):
        copy = self.halving(r)
        copy.wait()
        half = self.rows >> (r + 1)
        row = self.first(r + 1)

        def one(k, _):
            at = self.at(row + k * self.share, self.share)
            come = self.back[pl.ds(pl.multiple_of(self.rows - 2 * half + k * self.share, 16), self.share), :]
            self.mine[at, :] = (self.mine[at, :].astype(F32) + come.astype(F32)).astype(BF16)
            return 0

        lax.fori_loop(0, half // self.share, one, 0)

    def gathering(self, r, arriving):
        size = self.rows >> (r + 1)
        row = self.first(r + 1)
        if arriving:
            row = row + size - 2 * size * self.bit(r)
        at = self.at(row, size)
        return pltpu.make_async_remote_copy(
            src_ref=self.out.at[at], dst_ref=self.out.at[at],
            send_sem=self.sems.at[2 * self.rounds + r], recv_sem=self.sems.at[3 * self.rounds + r],
            device_id={"seq": self.partner(r)}, device_id_type=MESH,
        )

    def to_head(self, d):
        base = 4 * self.rounds + 1
        src = self.mine.at[self.at(self.first(self.rounds), self.share), pl.ds(0, self.shared)]
        return pltpu.make_async_remote_copy(
            src_ref=src, dst_ref=self.zback.at[self.z], send_sem=self.sems.at[base + d], recv_sem=self.sems.at[base + 4 + d],
            device_id={"head": lax.rem(self.z + d, 4)}, device_id_type=MESH,
        )

    def publish(self):
        at = self.at(self.first(self.rounds), self.share)
        copy = pltpu.make_async_copy(self.mine.at[at], self.out.at[at], self.sems.at[4 * self.rounds])
        copy.start()
        copy.wait()
        self.gathering(self.rounds - 1, False).start()

    def stages(self):
        spans = [2, 5, 3] + [2] * self.rounds
        acts = [(spans[0], lambda: self.halving(0).start())]
        for r in range(self.rounds):
            def act(r=r):
                self.add_half(r)
                if r + 1 < self.rounds:
                    self.halving(r + 1).start()
                elif not self.shared:
                    self.publish()
                else:
                    for d in range(1, 4):
                        self.to_head(d).start()
                    self.zback[self.z] = self.mine[self.at(self.first(self.rounds), self.share), 0 : self.shared]

            acts.append((spans[r + 1] if r + 1 < self.rounds else spans[r], act))
        if self.shared:
            def meet():
                for d in range(1, 4):
                    self.to_head(d).wait()
                at = self.at(self.first(self.rounds), self.share)
                low = [self.zback[k].astype(F32) for k in range(4)]
                self.mine[at, 0 : self.shared] = ((low[0] + low[1]) + (low[2] + low[3])).astype(BF16)
                self.publish()

            acts.append((spans[self.rounds - 1], meet))
        for r in reversed(range(self.rounds)):
            def act(r=r):
                self.gathering(r, False).wait_send()
                self.gathering(r, True).wait_recv()
                if r > 0:
                    self.gathering(r - 1, False).start()

            acts.append((spans[max(r - 1, 0)], act))
        return acts


def finish(
    y, gate_grad, xpg, bpg, raw, tok, cot, rms, gate_w, value_w, state_w, step_w, ngain, filter_rows, gain_rows, skip_rows, head_rows, state_rows, xtail, btail,
    normed, tok_k, out_grad, gate_grad_w, y_all,
    result_o, tokens_grad_o, small_o, wout_o, wgate_o, wvalue_o, wmixed_o,
    own, got, far, sa, sb, sc, sd, se, sf, yown, ygot, yfar, ta, tb, tc, td, te, tf, ylocal, rows, out, back, send, recv,
    w_mine, w_back, m_mine, m_back, m_zback, w_acc, m_acc, w_sems, w_local, vec, vback, vsems,
    *, n, rounds, plan, per_seq,
):
    i = pl.program_id(0)
    ngain = Row(ngain)
    z = lax.axis_index("head")
    last = n + 3 * LAG - 1
    outs = (wout_o, wgate_o, wvalue_o)
    grads = [GradSum(rounds, w_mine.at[k], w_back.at[k], outs[k], w_sems.at[k]) for k in range(3)]
    grads.append(GradSum(rounds, m_mine, m_back, wmixed_o, w_sems.at[3], m_zback, bpg.shape[1]))
    products = 2 * (n * CHUNK // T)

    def vec_copy(d):
        return pltpu.make_async_remote_copy(
            src_ref=vec, dst_ref=vback.at[z], send_sem=vsems.at[d], recv_sem=vsems.at[4 + d],
            device_id={"head": lax.rem(z + d, 4)}, device_id_type=MESH,
        )

    def local_copies():
        rows_out, half = out_grad.shape[0], out_grad.shape[1] // 2
        return [
            pltpu.make_async_copy(gate_grad_w, w_mine.at[1], w_local.at[0]),
            pltpu.make_async_copy(out_grad.at[:, pl.ds(0, half)], w_mine.at[0, pl.ds(0, rows_out)], w_local.at[1]),
            pltpu.make_async_copy(out_grad.at[:, pl.ds(half, half)], w_mine.at[0, pl.ds(rows_out, rows_out)], w_local.at[2]),
        ]

    chain = Chain(own, got, far, (sa, sb, sc, sd, se, sf))
    rider = Rider(*plan, y_all, yown, ygot, yfar, (ta, tb, tc, td, te, tf), ylocal)
    me = lax.axis_index("seq")

    def partner(r):
        bit = 1 << r
        return me + bit - 2 * bit * (lax.div(me, bit) % 2)

    @pl.when(i == 0)
    def _():
        barrier = pltpu.get_barrier_semaphore()
        for r in range(rounds):
            pl.semaphore_signal(barrier, inc=1, device_id={"seq": partner(r)}, device_id_type=MESH)
        greet_head()
        pl.semaphore_wait(barrier, rounds + 3)
        rider.load()
        for copy in local_copies():
            copy.start()
        w_acc[...] = jnp.zeros_like(w_acc)
        m_acc[...] = jnp.zeros_like(m_acc)
        rows[...] = jnp.zeros_like(rows)
        rows[0:5] = filter_rows[0:5]
        rows[5:6] = gain_rows[0:1]
        rows[6:7] = skip_rows[0:1]
        rows[7:8, 0:LANES] = head_rows[0:1]
        rows[7:8, LANES : 2 * LANES] = head_rows[1:2]
        rows[16:24, 0 : state_rows.shape[1]] = state_rows[...]

    rider.tick(i)
    for stage in (2, 1):
        k = i - stage * LAG

        @pl.when((k >= 0) & (k < n))
        def _():
            chain.onward(stage, k)

    @pl.when((i < products) & (i % 2 == 0))
    def _():
        part = lax.div(i, 2)
        ends = lax.rem(part, per_seq) == per_seq - 1
        tails = [jnp.where(ends, v[lax.div(part, per_seq)].astype(F32), 0.0) for v in (xtail, btail)]
        x_rows, b_rows = [
            jnp.concatenate([v[0 : T - HALO], (v[T - HALO : T].astype(F32) + tail).astype(BF16)], axis=0)
            for v, tail in zip((xpg, bpg), tails)
        ]
        value = mm_t(gate_grad[...], gate_w[...]) + mm_t(x_rows, value_w[...])
        value = value + (mm_t(b_rows, state_w[...]) + mm_t(raw[...], step_w[...]))
        t = tok_k[...].astype(F32)
        inv = lax.rsqrt(jnp.mean(t * t, axis=1, keepdims=True) + EPS)
        gain = jnp.sum(value * (t * inv), axis=0, keepdims=True)
        half = t.shape[1] // 2
        rows[8:9] += gain[:, :half]
        rows[9:10] += gain[:, half:]
        chunks = T // CHUNK
        first = lax.div(i, 2) * chunks
        own[pl.ds(first, chunks)] = value.astype(BF16).reshape(chunks, CHUNK, value.shape[1])
        mixed = jnp.concatenate([b_rows, raw[...]], axis=1)
        for m in range(w_acc.shape[0] // 256):
            rows_m = slice(m * 256, (m + 1) * 256)
            left = normed[:, rows_m]
            w_acc[rows_m] += t_mm(left, x_rows)
            m_acc[rows_m] += t_mm(left, mixed)

    @pl.when(i < n)
    def _():
        chain.inward(i)

    @pl.when(i == products)
    def _():
        w_mine[2] = w_acc[...].astype(BF16)
        m_mine[...] = m_acc[...].astype(BF16)

    @pl.when(i == 1)
    def _():
        for copy in local_copies():
            copy.wait()

    for grad_sum, begin in zip(grads, (1, 5, products, products + 2)):
        at = begin
        for span, act in grad_sum.stages():
            pl.when(i == min(at, last))(act)
            at += span

    @pl.when(i == products)
    def _():
        vec[...] = rows[8:24]
        for d in range(1, 4):
            vec_copy(d).start()
        vback[z] = vec[...]

    def row_copy(r):
        return pltpu.make_async_remote_copy(
            src_ref=out.at[r], dst_ref=back.at[r], send_sem=send.at[r], recv_sem=recv.at[r],
            device_id={"seq": partner(r)}, device_id_type=MESH,
        )

    @pl.when(i == products + 4)
    def _():
        for d in range(1, 4):
            vec_copy(d).wait()
        rows[8:24] = (vback[0] + vback[1]) + (vback[2] + vback[3])
        out[0] = rows[...]
        row_copy(0).start()

    for r in range(rounds):

        @pl.when(i == products + 4 + 3 * (r + 1))
        def _():
            row_copy(r).wait()
            rows[...] = rows[...] + back[r]
            if r + 1 < rounds:
                out[r + 1] = rows[...]
                row_copy(r + 1).start()

    k = i - 3 * LAG

    @pl.when(k >= 0)
    def _():
        grad = chain.total(k)
        rms_k = rms[:, 0:1]
        t = tok[...].astype(F32)
        width = t.shape[1]
        inv = lax.rsqrt(jnp.mean(t * t, axis=1, keepdims=True) + EPS)
        if rider.done > 0:

            @pl.when(k < rider.done)
            def _():
                result_o[...] = (t + y[...].astype(F32) * rms_k).astype(BF16)

        if rider.done < n:

            @pl.when(k >= rider.done)
            def _():
                result_o[...] = (t + rider.chain.total(k - rider.base) * rms_k).astype(BF16)

        scaled = grad * ngain[...]
        dot = jnp.sum(scaled * t, axis=1, keepdims=True) / width
        tokens_grad_o[...] = (cot[...].astype(F32) + inv * scaled - t * (inv * inv * inv * dot)).astype(BF16)

    @pl.when(i == last)
    def _():
        chain.drain(n)
        rider.drain()
        small_o[...] = rows[...]


def unpack(
    tgrad, res, wout_l, wout_r, wgate, wvalue, wmixed, small, rate, wide,
    res_o, tgrad_o, ngain_o, wgate_o, wvalue_o, state_o, step_o, vk_o, vo_o, sk_o, so_o, sbias_o, rate_o, skip_o, mgain_o, wout_o,
    *, taps, heads,
):
    res_o[...] = res[...]
    tgrad_o[...] = tgrad[...].astype(F32)
    wgate_o[...] = wgate[...].astype(F32)
    wvalue_o[...] = wvalue[...].astype(F32)
    half = wout_l.shape[1]
    wout_o[:, :half] = wout_l[...].astype(F32)
    wout_o[:, half:] = wout_r[...].astype(F32)
    n2 = state_o.shape[1]
    state_o[...] = wmixed[:, :n2].astype(F32)
    step_o[...] = wmixed[:, n2 : n2 + heads].astype(F32)

    @pl.when(pl.program_id(0) == 0)
    def _():
        vk_o[...] = small[0:taps]
        vo_o[...] = small[taps]
        mgain_o[...] = small[taps + 1]
        skip_o[...] = head_sum(jnp.broadcast_to(small[taps + 2 : taps + 3], (16, half)), wide[...])[0, 0:heads]
        sbias_o[...] = small[taps + 3, 0:heads]
        rate_o[...] = small[taps + 3, LANES : LANES + heads] * rate[0, 0:heads]
        ngain_o[pl.ds(0, half)] = small[8]
        ngain_o[pl.ds(half, half)] = small[9]
        sk_o[...] = small[16 : 16 + taps, 0:n2]
        so_o[...] = small[16 + taps, 0:n2]


def call(body, steps, seqs, ins, outs, scratch, flops, collective_id=None, carried=None):
    def cut(shape, lag):
        rest = tuple(shape[1:])
        return pl.BlockSpec((1,) + rest, lambda s: (jnp.clip(s - lag, 0, seqs - 1),) + (0,) * len(rest))

    def whole(shape):
        return pl.BlockSpec(tuple(shape), lambda s: (0,) * len(shape), pipeline_mode=pl.Buffered(1))

    pairs = [v if isinstance(v, tuple) else (v, 0) for v in ins]
    ins = [v for v, _ in pairs]
    in_specs = [cut(v.shape, lag) if v.ndim >= 3 else whole(v.shape) for v, lag in pairs]
    out_specs = [whole(s) if lag is None else cut(s, lag) for s, _, lag in outs]
    out_shape = [jax.ShapeDtypeStruct(s, d) for s, d, _ in outs]
    aliases = {}
    if carried is not None:
        aliases = {len(ins): len(outs)}
        in_specs.append(pl.BlockSpec(memory_space=pl.ANY))
        out_specs.append(pl.BlockSpec(memory_space=pl.ANY))
        out_shape.append(jax.ShapeDtypeStruct(carried.shape, carried.dtype))
        ins = ins + [carried]
    moved = sum(a.size * a.dtype.itemsize for a in ins)
    for s, d, _ in outs:
        size = jnp.dtype(d).itemsize
        for k in s:
            size *= k
        moved += size
    return pl.pallas_call(
        body,
        grid=(steps,),
        in_specs=in_specs,
        out_specs=out_specs,
        out_shape=out_shape,
        scratch_shapes=scratch,
        input_output_aliases=aliases,
        compiler_params=pltpu.CompilerParams(
            dimension_semantics=("arbitrary",), vmem_limit_bytes=60 * 1024 * 1024,
            collective_id=collective_id, has_side_effects=collective_id is not None,
        ),
        cost_estimate=pl.CostEstimate(flops=flops, bytes_accessed=moved, transcendentals=0),
    )(*ins)


def shards(
    tokens, norm_gain, gate_weight, value_weight, state_weight, step_weight, value_kernel, value_offset,
    state_kernel, state_offset, step_bias, log_rate, skip_gain, mixer_gain, out_weight, cotangent,
):
    seqs, length, width = tokens.shape
    flat = seqs * length
    inner = gate_weight.shape[1]
    heads = step_weight.shape[1]
    head_size = inner // heads
    n2 = state_weight.shape[1]
    n = n2 // 2
    taps = value_kernel.shape[0]
    blocks = length // T
    devices = lax.axis_size("seq")
    rounds = devices.bit_length() - 1
    assert devices == 1 << rounds and taps == 4
    inner_all = inner * lax.axis_size("head")

    pad = LANES - heads
    rate_row = -jnp.exp(log_rate)
    rate = jnp.pad(rate_row, (0, pad))[None]
    bias = jnp.pad(step_bias, (0, pad))[None]
    step_w = jnp.pad(step_weight, ((0, 0), (0, pad)))
    skip = jnp.repeat(skip_gain, head_size)[None]
    gain = mixer_gain
    one = (jnp.arange(inner)[None, :] // head_size == jnp.arange(LANES)[:, None]).astype(BF16)
    wide = jnp.concatenate([one, one], axis=0)
    tri = (jnp.arange(T)[:, None] >= jnp.arange(T)[None, :]).astype(BF16)
    vo, so = value_offset, state_offset

    def big(cols, dtype, rows=length, lag=0):
        return ((seqs, rows, cols), dtype, lag)

    vmem = pltpu.VMEM
    ext = length + HALO
    n_chunks = flat // CHUNK
    steps = seqs + rounds
    plan = (0, min(2 * (seqs - 1), length // CHUNK), n_chunks)
    dma = pltpu.SemaphoreType.DMA

    def block(shape, lag):
        return pl.BlockSpec((1,) + shape, lambda i: (jnp.clip(i - lag, 0, seqs - 1), 0, 0))

    def once(v):
        return pl.BlockSpec(v.shape, lambda i: (0,) * len(v.shape), pipeline_mode=pl.Buffered(1))

    def shape_of(cols, dtype, rows=length):
        return jax.ShapeDtypeStruct((seqs, rows, cols), dtype)

    fixed = (norm_gain, gate_weight, value_weight, state_weight, step_w, value_kernel, vo, state_kernel, so, bias, rate,
             wide, tri, out_weight, gain, skip)
    held = (shape_of(LANES, F32, 8), shape_of(inner, F32, n), shape_of(length, F32, 8))
    anywhere = pl.BlockSpec(memory_space=pl.ANY)
    (xext, bcext, sraw, pre, entry, sums, xact, bcact, gate, step, cum, lstart, normed, ssd, gn, y) = pl.pallas_call(
        functools.partial(forward, seqs=seqs, rounds=rounds, plan=plan),
        grid=(steps,),
        in_specs=[block((length, width), 0), anywhere, block((length, width), rounds)] + [once(v) for v in fixed],
        out_specs=[block((ext, inner), 0), block((ext, n2), 0), block((length, LANES), 0)] + [once(v) for v in held] + [anywhere] * 10,
        out_shape=[shape_of(inner, BF16, ext), shape_of(n2, BF16, ext), shape_of(LANES, F32), *held,
                   shape_of(inner, BF16), shape_of(n2, BF16), shape_of(inner, F32), shape_of(LANES, F32), shape_of(LANES, F32),
                   jax.ShapeDtypeStruct((seqs, blocks, n, inner), F32), shape_of(width, BF16), shape_of(inner, F32),
                   shape_of(inner, F32), jax.ShapeDtypeStruct((n_chunks, CHUNK, width), BF16)],
        scratch_shapes=[
            vmem((seqs, length, inner), BF16), vmem((seqs, length, n2), BF16), vmem((seqs, length, inner), F32),
            vmem((seqs, length, LANES), F32), vmem((seqs, length, LANES), F32), vmem((seqs, blocks, n, inner), F32),
            vmem((ext, width), BF16), vmem((1, length, inner), F32), vmem((1, length, inner), F32),
            vmem((length // CHUNK, CHUNK, width), BF16), vmem((length, inner), BF16),
            vmem((ext, inner), F32), vmem((ext, n2), F32), vmem((n, inner), F32), vmem((8, LANES), F32),
            vmem((seqs, HALO, width), BF16), vmem((seqs, 8, length), F32), vmem((seqs, 4, 8, length), F32),
            dma((6, seqs)), dma((4,)), dma((seqs,)), dma((seqs,)), dma((seqs, 4)), dma((seqs, 4)),
        ] + Exchange.scratch(rounds, seqs, n, inner) + Rider.scratch(*plan, width),
        compiler_params=pltpu.CompilerParams(
            dimension_semantics=("arbitrary",), vmem_limit_bytes=62 * 1024 * 1024, collective_id=1, has_side_effects=True
        ),
        cost_estimate=pl.CostEstimate(flops=2 * flat * width * 4 * inner, bytes_accessed=10**8, transcendentals=0),
    )(tokens, tokens, cotangent, *fixed)
    plan = (plan[1], 2 * (seqs + rounds), n_chunks)
    gnormed, gate_grad, lend, rms, xg, cumg, stepg, bcg, mgg, skg, after, y = call(
        functools.partial(back_one, inner_all=inner_all, seqs=seqs, rounds=rounds, plan=plan), seqs + rounds, seqs,
        [xact, bcact, cum, gate, ssd, gn, sums, pre, gain, skip, wide]
        + [(v, rounds) for v in (xact, bcact, step, cum, lstart, entry, pre)],
        [big(inner, BF16), big(inner, BF16), ((seqs, blocks, n, inner), F32, 0), big(LANES, F32),
         big(inner, F32, lag=rounds), big(LANES, F32, lag=rounds), big(LANES, F32, lag=rounds), big(n2, F32, lag=rounds),
         ((8, inner), F32, None), ((8, inner), F32, None), ((seqs, n, inner), F32, None)],
        [vmem((T, inner), F32), vmem((n, inner), F32), vmem((n, inner), F32), vmem((seqs, length, inner), BF16),
         vmem((seqs, length, LANES), F32)]
        + Exchange.scratch(rounds, seqs, n, inner) + Rider.scratch(*plan, width),
        2 * flat * T * inner * 8, 3, y,
    )
    plan = (plan[0] + plan[1], 3 * seqs, n_chunks)
    xpg, xhalo, bpg, bhalo, raw, vkg, skgr, head_rows, out_weight_grad, gate_weight_grad, y = call(
        functools.partial(back_two, seqs=seqs, plan=plan), seqs, seqs,
        [xact, bcact, xext, bcext, step, cum, sraw, xg, cumg, stepg, bcg, lstart, entry, lend, after, pre,
         gnormed, cotangent, normed, gate_grad, value_kernel, vo, state_kernel, so, bias, rate, wide, tri],
        [big(inner, BF16), big(inner, BF16, HALO), big(n2, BF16), big(n2, BF16, HALO), big(LANES, BF16),
         ((8, inner), F32, None), ((8, n2), F32, None), ((8, LANES), F32, None),
         ((inner, width), BF16, None), ((width, inner), BF16, None)],
        [vmem((ext, inner), F32), vmem((ext, n2), F32), vmem((ext + HALO, inner), F32),
         vmem((ext + HALO, n2), F32), vmem((inner, width), F32), vmem((width, inner), F32)] + Rider.scratch(*plan, width),
        2 * flat * T * inner * 4, 5, y,
    )
    back = [(i + 1, i) for i in range(devices - 1)]
    xhalo, bhalo = lax.ppermute((xhalo, bhalo), "seq", back)
    def flatten(v):
        return v.reshape(flat, v.shape[-1])

    normed_f, xpg_f, bpg_f, raw_f, gg_f = [flatten(v) for v in (normed, xpg, bpg, raw, gate_grad)]
    first = min(plan[0] + plan[1], n_chunks + 2 * LAG)
    plan = (first, max(n_chunks - first, 0) + 3 * LAG, n_chunks)

    def product_rows(v):
        return pl.BlockSpec((T, v.shape[1]), lambda i: (jnp.minimum(i // 2, flat // T - 1), 0))

    def lagged(cols, lag):
        return pl.BlockSpec((CHUNK, cols), lambda i: (jnp.clip(i - lag, 0, n_chunks - 1), 0))

    late = (gate_weight, value_weight, state_weight, step_w, norm_gain, vkg, mgg, skg, head_rows, skgr, xhalo, bhalo)
    result, tokens_grad, small, wout, wgate, wvalue, wmixed = pl.pallas_call(
        functools.partial(finish, n=n_chunks, rounds=rounds, plan=plan, per_seq=blocks),
        grid=(n_chunks + 3 * LAG,),
        in_specs=[lagged(width, 3 * LAG)]
        + [product_rows(v) for v in (gg_f, xpg_f, bpg_f, raw_f)]
        + [lagged(width, 3 * LAG), lagged(width, 3 * LAG), lagged(LANES, 3 * LAG)]
        + [once(v) for v in late] + [product_rows(normed_f), product_rows(flatten(tokens))] + [anywhere] * 3,
        out_specs=[lagged(width, 3 * LAG), lagged(width, 3 * LAG), pl.BlockSpec((24, inner), lambda i: (0, 0)),
                   anywhere, anywhere, anywhere, anywhere],
        out_shape=[
            jax.ShapeDtypeStruct((flat, width), BF16), jax.ShapeDtypeStruct((flat, width), BF16),
            jax.ShapeDtypeStruct((24, inner), F32), *[jax.ShapeDtypeStruct((width, c), BF16) for c in (inner, inner, inner, n2 + LANES)],
        ],
        scratch_shapes=Chain.scratch(n_chunks, CHUNK, width) + Rider.scratch(*plan, width) + [
            vmem((24, inner), F32), vmem((rounds, 24, inner), F32), vmem((rounds, 24, inner), F32),
            pltpu.SemaphoreType.DMA((rounds,)), pltpu.SemaphoreType.DMA((rounds,)),

            vmem((3, width, inner), BF16), vmem((3, width, inner), BF16), vmem((width, n2 + LANES), BF16),
            vmem((width, n2 + LANES), BF16), vmem((4, width >> rounds, n2), BF16), vmem((width, inner), F32),
            vmem((width, n2 + LANES), F32), dma((4, GradSum.sem_count(rounds))), dma((3,)),
            vmem((16, inner), F32), vmem((4, 16, inner), F32), dma((8,)),
        ],
        compiler_params=pltpu.CompilerParams(
            dimension_semantics=("arbitrary",), vmem_limit_bytes=62 * 1024 * 1024, collective_id=4, has_side_effects=True
        ),
        cost_estimate=pl.CostEstimate(flops=10**11, bytes_accessed=10**8, transcendentals=0),
    )(y.reshape(flat, width), gg_f, xpg_f, bpg_f, raw_f, flatten(tokens), flatten(cotangent), flatten(rms),
      *late, normed_f, flatten(tokens), out_weight_grad, gate_weight_grad, y)
    parts = 16

    def strip(rows, cols, at=0):
        return pl.BlockSpec((rows // parts, cols), lambda i: (i + at, 0))

    def entire(shape):
        return pl.BlockSpec(shape, lambda i: (0,) * len(shape))

    fine = [strip(inner, inner), strip(inner, inner, parts)]
    flat_out = [
        ((flat, width), BF16), ((flat, width), F32), ((width,), F32), ((width, inner), F32), ((width, inner), F32), ((width, n2), F32),
        ((width, heads), F32), ((taps, inner), F32), ((inner,), F32), ((taps, n2), F32), ((n2,), F32), ((heads,), F32), ((heads,), F32),
        ((heads,), F32), ((inner,), F32), ((inner, width), F32),
    ]
    cut = (0, 1, 3, 4, 5, 6, 15)
    found = pl.pallas_call(
        functools.partial(unpack, taps=taps, heads=heads),
        grid=(parts,),
        in_specs=[strip(flat, width), strip(flat, width)] + fine + [strip(width, inner)] * 2 + [strip(width, n2 + LANES)]
        + [entire(small.shape), entire(rate.shape), entire(wide.shape)],
        out_specs=[strip(*shape) if k in cut else entire(shape) for k, (shape, _) in enumerate(flat_out)],
        out_shape=[jax.ShapeDtypeStruct(shape, dtype) for shape, dtype in flat_out],
        compiler_params=pltpu.CompilerParams(dimension_semantics=("arbitrary",), vmem_limit_bytes=60 * 1024 * 1024),
    )(tokens_grad, result, wout, wout, wgate, wvalue, wmixed, small, rate, wide)
    return (found[0].reshape(tokens.shape), found[1].reshape(tokens.shape)) + tuple(found[2:])


def solution(mesh):
    rows, cols, vec = P(None, "seq", None), P(None, "head"), P("head")
    in_specs = (rows, P(), cols, cols, P(), cols, cols, vec, P(), P(), vec, vec, vec, vec, P("head", None), rows)
    out_specs = (rows, rows, P(), cols, cols, P(), cols, cols, vec, P(), P(), vec, vec, vec, vec, P("head", None))
    return jax.shard_map(shards, mesh=mesh, in_specs=in_specs, out_specs=out_specs, check_vma=False)
```

```python
import functools

import jax
import jax.numpy as jnp
from jax import lax
from jax.experimental import pallas as pl
from jax.experimental.pallas import tpu as pltpu
from jax.sharding import PartitionSpec as P

EPS = 1e-05
T = 256
SUB = 128
HALO = 16
LANES = 128
F32 = jnp.float32
BF16 = jnp.bfloat16


def mm(a, b):
    return lax.dot_general(a, b, (((1,), (0,)), ((), ())), preferred_element_type=F32)


def mm_t(a, b):
    return lax.dot_general(a, b, (((1,), (1,)), ((), ())), preferred_element_type=F32)


def t_mm(a, b):
    return lax.dot_general(a, b, (((0,), (0,)), ((), ())), preferred_element_type=F32)


def split(v, parts):
    pieces = []
    for _ in range(parts):
        piece = v.astype(BF16)
        pieces.append(piece)
        v = v - piece.astype(F32)
    return pieces


def expand(v, wide):
    return mm(jnp.concatenate(split(v, 2), axis=1), wide)


def expand_row(v, wide):
    return expand(jnp.broadcast_to(v, (16, LANES)), wide)[0:1]


def head_sum(v, wide):
    hi, lo = split(v, 2)
    return mm_t(hi, wide[:LANES]) + mm_t(lo, wide[:LANES])


def exact_tri(tri, v):
    a, b, c = split(v, 3)
    return mm(tri, a) + (mm(tri, b) + mm(tri, c))


def sigmoid(v):
    return 0.5 * jnp.tanh(0.5 * v) + 0.5


def softplus(v):
    return jnp.maximum(v, 0.0) + jnp.log1p(jnp.exp(-jnp.abs(v)))


def lower():
    row = lax.broadcasted_iota(jnp.int32, (SUB, SUB), 0)
    col = lax.broadcasted_iota(jnp.int32, (SUB, SUB), 1)
    return row >= col


def tile(i):
    return slice(i * SUB, (i + 1) * SUB)


def tiles():
    return [(i, j) for i in range(T // SUB) for j in range(i + 1)]


def cross_tiles(cm, bm):
    found = {}
    for i, j in tiles():
        value = mm_t(cm[tile(i)], bm[tile(j)])
        found[i, j] = jnp.where(lower(), value, 0.0) if i == j else value
    return found


def decay_tile(cum, cum_t, h, i, j):
    gap = cum[tile(i), h : h + 1] - cum_t[h : h + 1, tile(j)]
    return jnp.exp(jnp.minimum(gap, 0.0) if i == j else gap)


def half_mask(rows):
    return lax.broadcasted_iota(jnp.int32, (rows, LANES), 1) < LANES // 2


def pair_rows(v):
    left = half_mask(v.shape[0])
    zero = jnp.zeros_like(v)
    return jnp.concatenate([jnp.where(left, v, zero), jnp.where(left, zero, v)], axis=0)


def rows_of(b):
    return pl.ds(pl.multiple_of(b * T, T), T)


MESH = pl.DeviceIdType.MESH
CHUNK = 64
LAG = 2


def greet_head():
    z = lax.axis_index("head")
    for d in range(1, 4):
        pl.semaphore_signal(
            pltpu.get_barrier_semaphore(), inc=1, device_id={"head": lax.rem(z + d, 4)}, device_id_type=MESH)


class Chain:
    def __init__(self, own, got, far, sems):
        z = lax.axis_index("head")
        self.end = (z == 0) | (z == 3)
        self.side = z + 1 - 2 * (z % 2)
        self.other = 3 - z
        self.own, self.got, self.far = own, got, far
        self.sems = sems

    @staticmethod
    def scratch(n, chunk, width):
        buffer = pltpu.VMEM((n, chunk, width), BF16)
        return [buffer, buffer, buffer] + [pltpu.SemaphoreType.DMA((n,))] * 6

    def copy(self, kind, k):
        src, dst, to = [(self.own, self.got, self.side), (self.own, self.far, self.other), (self.got, self.got, self.side)][kind]
        return pltpu.make_async_remote_copy(
            src_ref=src.at[k], dst_ref=dst.at[k],
            send_sem=self.sems[2 * kind].at[k], recv_sem=self.sems[2 * kind + 1].at[k],
            device_id={"head": to}, device_id_type=MESH,
        )

    def inward(self, k):
        @pl.when(self.end)
        def _():
            self.copy(0, k).start()

    def meet(self, stage, k):
        self.copy(stage, k).wait_recv()
        if stage == 0:
            self.own[k] = (self.own[k].astype(F32) + self.got[k].astype(F32)).astype(BF16)
        else:
            self.got[k] = (self.own[k].astype(F32) + self.far[k].astype(F32)).astype(BF16)

    def onward(self, stage, k):
        @pl.when(jnp.logical_not(self.end))
        def _():
            self.meet(stage - 1, k)
            self.copy(stage, k).start()

    def total(self, k):
        @pl.when(self.end)
        def _():
            self.copy(2, k).wait_recv()

        return self.got[k].astype(F32)

    def drain(self, n):
        def one(k, _):
            @pl.when(self.end)
            def _():
                self.copy(0, k).wait_send()

            @pl.when(jnp.logical_not(self.end))
            def _():
                self.copy(1, k).wait_send()
                self.copy(2, k).wait_send()

            return 0

        lax.fori_loop(0, n, one, 0)


class Rider:
    def __init__(self, first, ticks, count, hbm, own, got, far, sems, local):
        self.first, self.ticks, self.count = first, ticks, count
        self.done = min(max(first - 2 * LAG, 0), count)
        self.base = min(self.done, count - 1)
        self.hbm, self.local = hbm, local
        self.chain = Chain(own, got, far, sems)

    @staticmethod
    def size(first, ticks, count):
        return max(min(first + ticks, count) - min(max(first - 2 * LAG, 0), count - 1), 1)

    @staticmethod
    def scratch(first, ticks, count, width):
        return Chain.scratch(Rider.size(first, ticks, count), CHUNK, width) + [pltpu.SemaphoreType.DMA((2,))]

    def span(self, stage):
        low = self.first - stage * LAG
        return max(low, 0), min(low + self.ticks, self.count)

    def load(self):
        size = self.size(self.first, self.ticks, self.count)
        own = pltpu.make_async_copy(self.hbm.at[pl.ds(self.base, size)], self.chain.own, self.local.at[0])
        own.start()
        ready = min(max(self.first - LAG, 0), self.count) - self.base
        if ready > 0 and self.done < self.count:

            @pl.when(jnp.logical_not(self.chain.end))
            def _():
                got = pltpu.make_async_copy(
                    self.hbm.at[pl.ds(self.base, ready)], self.chain.got.at[pl.ds(0, ready)], self.local.at[1])
                got.start()
                got.wait()

        own.wait()

    def tick(self, t):
        chain = self.chain
        for stage in (2, 1, 0):
            low, high = self.span(stage)
            k = self.first - stage * LAG + t

            @pl.when((k >= low) & (k < high) & (t < self.ticks))
            def _():
                at = k - self.base
                if stage == 0:
                    chain.inward(at)
                else:
                    self.follow(stage, at, t >= LAG)

    def follow(self, stage, at, pending):
        chain = self.chain
        middle = jnp.logical_not(chain.end)

        @pl.when(middle & pending)
        def _():
            chain.meet(stage - 1, at)

        @pl.when(middle)
        def _():
            chain.copy(stage, at).start()

    def drain(self):
        chain = self.chain

        def each(stage):
            low, high = self.span(stage)
            lax.fori_loop(low - self.base, high - self.base, lambda k, _: (chain.copy(stage, k).wait_send(), 0)[1], 0)

        @pl.when(chain.end)
        def _():
            each(0)

        @pl.when(jnp.logical_not(chain.end))
        def _():
            each(1)
            each(2)

    def close(self):
        chain = self.chain
        middle = jnp.logical_not(chain.end)

        def each(low, high, do):
            if high > low:
                lax.fori_loop(low - self.base, high - self.base, lambda k, _: (do(k), 0)[1], 0)

        @pl.when(middle)
        def _():
            for stage in (0, 1):
                low, high = self.span(stage)
                started = max(self.first - stage * LAG + self.ticks - LAG, low)
                each(started, high, lambda k: chain.meet(stage, k))
            for stage in (1, 2):
                each(*self.span(stage), lambda k: chain.copy(stage, k).wait_send())

        @pl.when(chain.end)
        def _():
            each(*self.span(2), lambda k: chain.copy(2, k).wait_recv())
            each(*self.span(0), lambda k: chain.copy(0, k).wait_send())

        def store(ref, low, high):
            if high > low:
                at = pl.ds(low - self.base, high - low)
                copy = pltpu.make_async_copy(ref.at[at], self.hbm.at[pl.ds(low, high - low)], self.local.at[0])
                copy.start()
                copy.wait()

        @pl.when(middle)
        def _():
            reached = self.span(1)[1]
            store(chain.got, self.done, reached)
            store(chain.own, reached, self.span(0)[1])

        @pl.when(chain.end)
        def _():
            store(chain.got, *self.span(2))


class Exchange:
    def __init__(self, rounds, backward, total, before, logs, out, back, send, recv):
        self.rounds, self.backward = rounds, backward
        self.total, self.before, self.logs = total, before, logs
        self.out, self.back, self.send, self.recv = out, back, send, recv
        self.me = lax.axis_index("seq")

    def partner(self, r):
        bit = 1 << r
        return self.me + bit - 2 * bit * (lax.div(self.me, bit) % 2)

    def greet(self, with_head=False):
        barrier = pltpu.get_barrier_semaphore()
        for r in range(self.rounds):
            pl.semaphore_signal(barrier, inc=1, device_id={"seq": self.partner(r)}, device_id_type=MESH)
        if with_head:
            greet_head()
        pl.semaphore_wait(barrier, self.rounds + 3 * with_head)

    def copy(self, r, s):
        return pltpu.make_async_remote_copy(
            src_ref=self.out.at[r], dst_ref=self.back.at[r, s],
            send_sem=self.send.at[r], recv_sem=self.recv.at[r, s],
            device_id={"seq": self.partner(r)}, device_id_type=MESH,
        )

    def begin(self, s, state, log):
        self.total[s] = state
        self.before[s] = jnp.zeros_like(state)
        self.logs[s] = jnp.zeros(self.logs.shape[1:], F32)
        self.logs[s, 0:1] = log

    def push(self, r, s):
        n = self.total.shape[1]
        self.out[r, 0:n] = self.total[s].astype(BF16)
        hi, mid, lo = [v.astype(F32) for v in split(self.logs[s, 0:1], 3)]
        at = lax.broadcasted_iota(jnp.int32, (HALO, hi.shape[1]), 0)
        tail = jnp.where(at == 0, hi, jnp.where(at == 1, mid, jnp.where(at == 2, lo, 0.0)))
        self.out[r, n : n + HALO] = tail.astype(BF16)
        self.copy(r, s).start()

    def take(self, r, s):
        n = self.total.shape[1]
        copy = self.copy(r, s)
        copy.wait_recv()
        copy.wait_send()
        state = self.back[r, s, 0:n].astype(F32)
        tail = self.back[r, s, n : n + HALO].astype(F32)
        log = tail[0:1] + tail[1:2] + tail[2:3]
        upper = lax.div(self.me, 1 << r) % 2 == 1
        near = jnp.logical_not(upper) if self.backward else upper
        mine, theirs = self.logs[s, 0:1], self.logs[s, 1:2]
        self.before[s] = self.before[s] + jnp.where(near, jnp.exp(theirs), 0.0) * state
        self.logs[s, 1:2] = theirs + jnp.where(near, log, 0.0)
        own = jnp.where(near, 1.0, jnp.exp(log))
        other = jnp.where(near, jnp.exp(mine), 1.0)
        self.total[s] = own * self.total[s] + other * state
        self.logs[s, 0:1] = mine + log

    def advance(self, i, seqs):
        for r in reversed(range(self.rounds)):
            s = i - 1 - r

            @pl.when((s >= 0) & (s < seqs))
            def _():
                self.take(r, s)
                if r + 1 < self.rounds:
                    self.push(r + 1, s)

    @staticmethod
    def scratch(rounds, seqs, n, inner):
        return [
            pltpu.VMEM((seqs, n, inner), F32), pltpu.VMEM((seqs, 8, inner), F32),
            pltpu.VMEM((rounds, n + HALO, inner), BF16), pltpu.VMEM((rounds, seqs, n + HALO, inner), BF16),
            pltpu.SemaphoreType.DMA((rounds,)), pltpu.SemaphoreType.DMA((rounds, seqs)),
        ]


class Row:
    def __init__(self, ref):
        self.ref = ref

    def __getitem__(self, _):
        return self.ref[...].reshape(1, self.ref.shape[0])


def forward(
    tok, tok_all, cot, ngain, gate_w, value_w, state_w, step_w, vk, vo, sk, so, sbias, rate, wide, tri, out_w, mgain, skip,
    xext_o, bcext_o, sraw_o, pre_o, entry_o, sums_o,
    xact_h, bcact_h, gate_h, step_h, cum_h, lstart_h, normed_h, ssd_h, gn_h, y_h,
    xact, bcact, gate, step, cum, lstart, nx, ssd, gn, y_s, gm, xe, be, st, run, halo, mine, slots,
    kept_sems, slot_sems, halo_send, halo_recv, sum_send, sum_recv,
    total, logs, out, back, send, recv,
    yown, ygot, yfar, ta, tb, tc, td, te, tf, ylocal,
    *, seqs, rounds, plan,
):
    ngain, vo, so, mgain = Row(ngain), Row(vo), Row(so), Row(mgain)
    i = pl.program_id(0)
    s = i - rounds
    steps = seqs + rounds
    length = tok.shape[1]
    me, devices = lax.axis_index("seq"), lax.axis_size("seq")
    z = lax.axis_index("head")
    scan = Exchange(rounds, False, total, entry_o, logs, out, back, send, recv)
    rider = Rider(*plan, y_h, yown, ygot, yfar, (ta, tb, tc, td, te, tf), ylocal)
    kept = [(xact, xact_h), (bcact, bcact_h), (gate, gate_h), (step, step_h), (cum, cum_h), (lstart, lstart_h)]
    per_seq = length // CHUNK

    def halo_copy(q):
        return pltpu.make_async_remote_copy(
            src_ref=tok_all.at[q, pl.ds(length - HALO, HALO)], dst_ref=halo.at[q],
            send_sem=halo_send.at[q], recv_sem=halo_recv.at[q],
            device_id={"seq": lax.rem(me + 1, devices)}, device_id_type=MESH,
        )

    def keep(k, q):
        src, dst = kept[k]
        return pltpu.make_async_copy(src.at[q], dst.at[q], kept_sems.at[k, q])

    def normed_copy(q):
        return pltpu.make_async_copy(nx.at[pl.ds(HALO, length)], normed_h.at[q], slot_sems.at[0])

    def scan_copies(q):
        return [
            pltpu.make_async_copy(ssd.at[0], ssd_h.at[q], slot_sems.at[1]),
            pltpu.make_async_copy(gn.at[0], gn_h.at[q], slot_sems.at[2]),
        ]

    def y_copy(q, skip_rider):
        first = plan[1] if skip_rider else 0
        at = pl.ds(q * per_seq + first, per_seq - first)
        return pltpu.make_async_copy(y_s.at[pl.ds(first, per_seq - first)], y_h.at[at], slot_sems.at[3])

    def sum_copy(q, d):
        return pltpu.make_async_remote_copy(
            src_ref=mine.at[q], dst_ref=slots.at[q, z], send_sem=sum_send.at[q, d], recv_sem=sum_recv.at[q, d],
            device_id={"head": lax.rem(z + d, 4)}, device_id_type=MESH,
        )

    @pl.when(i == 0)
    def _():
        barrier = pltpu.get_barrier_semaphore()
        for d in range(1, devices):
            pl.semaphore_signal(barrier, inc=1, device_id={"seq": lax.rem(me + d, devices)}, device_id_type=MESH)
        greet_head()
        pl.semaphore_wait(barrier, devices - 1 + 3)

        @pl.when(me < devices - 1)
        def _():
            for q in range(seqs):
                halo_copy(q).start()

        @pl.when(me == 0)
        def _():
            halo[...] = jnp.zeros_like(halo)

    @pl.when(i < seqs)
    def _():
        @pl.when(i > 0)
        def _():
            normed_copy(i).wait()

        def arrive():
            @pl.when(me > 0)
            def _():
                halo_copy(i).wait_recv()

        one = pl.ds(i, 1)
        front_rows(
            tok, halo.at[one], ngain, gate_w, value_w, state_w, step_w, vk, vo, sk, so, sbias, rate, wide, tri,
            gate.at[one], xext_o, bcext_o, sraw_o, xact.at[one], bcact.at[one], step.at[one], cum.at[one],
            lstart.at[one], pre_o.at[one], nx, xe, be, st, run, arrive,
        )
        normed_copy(i).start()
        for k in range(len(kept)):
            keep(k, i).start()
        scan.begin(i, st[...], expand_row(run[0:1], wide[...]))

    scan.advance(i, seqs)

    @pl.when(i < seqs)
    def _():
        scan.push(0, i)

    @pl.when(s >= 0)
    def _():
        @pl.when(s > 0)
        def _():
            for copy in scan_copies(s):
                copy.wait()

        one = pl.ds(s, 1)
        scan_out(
            xact.at[one], bcact.at[one], step.at[one], cum.at[one], gate.at[one], lstart.at[one], entry_o.at[one],
            pre_o.at[one], cot, out_w, mgain, skip, wide, ssd, gn, mine.at[one], gm, lambda b: rider.tick((s - 1) * 2 + b),
        )
        for copy in scan_copies(s):
            copy.start()
        for d in range(1, 4):
            sum_copy(s, d).start()
        slots[s, z] = mine[s]

        @pl.when(s == 1)
        def _():
            y_copy(0, True).wait()

        @pl.when(s > 1)
        def _():
            y_copy(s, False).wait()

        for b in range(length // T):
            value = mm(gm[b * T : (b + 1) * T], out_w[...]).astype(BF16)
            y_s[b * T // CHUNK : (b + 1) * T // CHUNK] = value.reshape(T // CHUNK, CHUNK, value.shape[1])

        @pl.when(s == 0)
        def _():
            yown[...] = y_s[0 : plan[1]]
            y_copy(0, True).start()

        @pl.when(s > 0)
        def _():
            y_copy(s, False).start()

    @pl.when(i == steps - 1)
    def _():
        rider.close()
        for q in range(seqs):
            for d in range(1, 4):
                sum_copy(q, d).wait()
            sums_o[q] = (slots[q, 0] + slots[q, 1]) + (slots[q, 2] + slots[q, 3])
            for k in range(len(kept)):
                keep(k, q).wait()
        normed_copy(0).wait()
        for copy in scan_copies(0):
            copy.wait()
        y_copy(1, False).wait()

        @pl.when(me < devices - 1)
        def _():
            for q in range(seqs):
                halo_copy(q).wait_send()


def front_rows(
    tok, halo, ngain, gate_w, value_w, state_w, step_w, vk, vo, sk, so, sbias, rate, wide, tri,
    gate_o, xext_o, bcext_o, sraw_o, xact_o, bcact_o, step_o, cum_o, lstart_o, pre_o,
    nx, xe, be, st, run, arrive,
):
    length = tok.shape[1]
    blocks = length // T
    n = bcact_o.shape[2] // 2

    def norm(v):
        v = v.astype(F32)
        inv = lax.rsqrt(jnp.mean(v * v, axis=1, keepdims=True) + EPS)
        return (v * inv * ngain[...]).astype(BF16)

    def norm_rows(b, _):
        nx[pl.ds(pl.multiple_of(HALO + b * SUB, HALO), SUB), :] = norm(tok[0, pl.ds(pl.multiple_of(b * SUB, SUB), SUB), :])
        return 0

    lax.fori_loop(0, length // SUB, norm_rows, 0)
    gate_o[0] = mm(nx[HALO:], gate_w[...])
    sraw_o[0] = mm(nx[HALO:], step_w[...])
    arrive()
    nx[0:HALO] = norm(halo[0])
    x = mm(nx[...], value_w[...]).astype(BF16)
    xext_o[0] = x
    xe[...] = x.astype(F32)
    bc = mm(nx[...], state_w[...]).astype(BF16)
    bcext_o[0] = bc
    be[...] = bc.astype(F32)
    st[...] = jnp.zeros_like(st)
    run[...] = jnp.zeros_like(run)
    pre_o[0] = jnp.zeros_like(pre_o[0])
    for b in range(blocks):
        r0 = b * T
        r = slice(r0, r0 + T)
        taps = vk.shape[0]
        base = HALO - taps + 1
        xc = vo[...] + vk[0:1] * xe[r0 + base : r0 + base + T]
        bcc = so[...] + sk[0:1] * be[r0 + base : r0 + base + T]
        for k in range(1, taps):
            xc = xc + vk[k : k + 1] * xe[r0 + base + k : r0 + base + k + T]
            bcc = bcc + sk[k : k + 1] * be[r0 + base + k : r0 + base + k + T]
        xa = (xc * sigmoid(xc)).astype(BF16)
        bca = (bcc * sigmoid(bcc)).astype(BF16)
        xact_o[0, r, :] = xa
        bcact_o[0, r, :] = bca
        step = softplus(sraw_o[0, r, :] + sbias[...])
        cum = exact_tri(tri[...], step * rate[...])
        step_o[0, r, :] = step
        cum_o[0, r, :] = cum
        last = cum[T - 1 : T]
        weight = jnp.exp(last - cum) * step
        weighted = (xa.astype(F32) * expand(weight, wide[...])).astype(BF16)
        contrib = t_mm(bca[:, :n], weighted)
        lstart_o[0, b] = st[...]
        st[...] = expand_row(jnp.exp(last), wide[...]) * st[...] + contrib
        run[0:1] = run[0:1] + last
        pre_o[0, b + 1 : b + 2] = run[0:1]


def scan_out(
    xact, bcact, step_i, cum_i, gate, lstart, entry, pre, cot, out_w, mgain, skip, wide,
    ssd_o, gn_o, sums_o, gm, tick,
):
    length = xact.shape[1]
    blocks = length // T
    n = bcact.shape[2] // 2
    inner = xact.shape[2]
    gn_o[0] = mm_t(cot[0], out_w[...])

    def block(b, _):
        tick(b)
        r = rows_of(b)
        xa = xact[0, r, :]
        bca = bcact[0, r, :]
        bm, cm = bca[:, :n], bca[:, n:]
        cum = cum_i[0, r, :]
        cum_t = cum.T
        cross = cross_tiles(cm, bm)
        start = expand_row(jnp.exp(pre[0, pl.ds(b, 1), :]), wide[...]) * entry[0] + lstart[0, b]
        start = start.astype(BF16)
        grown = jnp.exp(cum)
        cm = cm.astype(F32)
        xs = (xa.astype(F32) * expand(step_i[0, r, :], wide[...])).astype(BF16)
        for p in range(inner // LANES):
            lanes = slice(p * LANES, (p + 1) * LANES)
            two = (2 * p, 2 * p + 1)
            start_two = pair_rows(start[:, lanes])
            xs_two = [pair_rows(xs[tile(j), lanes]) for j in range(T // SUB)]
            for i in range(T // SUB):
                left = [(cm[tile(i)] * grown[tile(i), h : h + 1]).astype(BF16) for h in two]
                right = [start_two]
                for j in range(i + 1):
                    left += [(cross[i, j] * decay_tile(cum, cum_t, h, i, j)).astype(BF16) for h in two]
                    right.append(xs_two[j])
                rows = pl.ds(pl.multiple_of(b * T + i * SUB, SUB), SUB)
                ssd_o[0, rows, lanes] = mm(jnp.concatenate(left, axis=1), jnp.concatenate(right, axis=0))
        mixed = ssd_o[0, r, :] + skip[...] * xa.astype(F32)
        g = gate[0, r, :]
        gated = mixed * (g * sigmoid(g))
        gg = gated * mgain[...]
        gm[r, :] = gg.astype(BF16)
        squares = jnp.sum(gated * gated, axis=1, keepdims=True)
        dots = jnp.sum(gg * gn_o[0, r, :], axis=1, keepdims=True)
        lane = lax.broadcasted_iota(jnp.int32, (T, LANES), 1)
        both = jnp.where(lane == 0, squares, jnp.where(lane == 1, dots, 0.0))
        sums_o[0, :, r] = both.T[0:8]
        return 0

    lax.fori_loop(0, blocks, block, 0)


def back_one(
    xact, bcact, cum_i, gate, ssd, gn, sums, pre, mgain, skip, wide,
    xact_b, bcact_b, step_b, cum_b, lstart_b, entry_b, pre_b, y_in,
    gnormed_o, gate_grad_o, lend_o, rms_o, xg_o, cumg_o, stepg_o, bcg_o, mgg_o, skg_o, after_o, y_all,
    z, acc, use, dys, cumg, total, logs, out, back, send, recv,
    yown, ygot, yfar, ta, tb, tc, td, te, tf, ylocal,
    *, inner_all, seqs, rounds, plan,
):
    mgain = Row(mgain)
    i = pl.program_id(0)
    s = i - rounds
    blocks = xact.shape[1] // T
    scan = Exchange(rounds, True, total, after_o, logs, out, back, send, recv)
    rider = Rider(*plan, y_all, yown, ygot, yfar, (ta, tb, tc, td, te, tf), ylocal)
    per_step = plan[1] // (seqs + rounds)

    @pl.when(i == 0)
    def _():
        scan.greet(with_head=True)
        rider.load()
        mgg_o[...] = jnp.zeros_like(mgg_o)
        skg_o[...] = jnp.zeros_like(skg_o)

    ticks = min(per_step, 3)
    rider.tick(i * per_step)

    @pl.when(i < seqs)
    def _():
        one = pl.ds(i, 1)
        gate_back(
            xact, bcact, cum_i, gate, ssd, gn, sums, mgain, skip, wide, gnormed_o, gate_grad_o, lend_o, rms_o, mgg_o, skg_o,
            dys.at[one], cumg.at[one], acc, use, inner_all,
        )
        scan.begin(i, acc[...], expand_row(pre[0, blocks : blocks + 1], wide[...]))

    scan.advance(i, seqs)

    @pl.when(i < seqs)
    def _():
        scan.push(0, i)

    @pl.when(s >= 0)
    def _():
        one = pl.ds(s, 1)
        scan_back(
            xact_b, bcact_b, step_b, cum_b, lstart_b, entry_b, pre_b, skip, wide, dys.at[one], cumg.at[one],
            xg_o, cumg_o, stepg_o, bcg_o, z, lambda b: rider.tick(jnp.where(1 + b < ticks, i * per_step + 1 + b, plan[1])),
        )

    @pl.when(s < 0)
    def _():
        for k in range(1, per_step):
            rider.tick(i * per_step + k)

    @pl.when(i == seqs + rounds - 1)
    def _():
        rider.close()


def gate_back(
    xact, bcact, cum_i, gate, ssd, gn, sums, mgain, skip, wide, gnormed_o, gate_grad_o, lend_o, rms_o, mgg_o, skg_o,
    dys, cumg, acc, use, inner_all,
):
    length = xact.shape[1]
    blocks = length // T
    n = bcact.shape[2] // 2
    inner = xact.shape[2]
    acc[...] = jnp.zeros_like(acc)

    def block(k, _):
        b = blocks - 1 - k
        r = rows_of(b)
        sums_b = sums[0, :, r]
        columns = jnp.concatenate([sums_b, jnp.zeros((LANES - 8, T), F32)], axis=0).T
        for i in range(T // SUB):
            ri = pl.ds(pl.multiple_of(b * T + i * SUB, SUB), SUB)
            xa = xact[0, ri, :].astype(F32)
            rms = lax.rsqrt(columns[tile(i), 0:1] / inner_all + EPS)
            rms_o[0, ri, :] = jnp.broadcast_to(rms, (SUB, LANES))
            coef = rms * rms * rms * (columns[tile(i), 1:2] / inner_all)
            ssd_r = ssd[0, ri, :]
            mixed = ssd_r + skip[...] * xa
            g = gate[0, ri, :]
            sg = sigmoid(g)
            gated = mixed * (g * sg)
            grad_norm = gn[0, ri, :]
            normalised = gated * rms
            gnormed_o[0, ri, :] = (normalised * mgain[...]).astype(BF16)
            mgg_o[0:1] += jnp.sum(grad_norm * normalised, axis=0, keepdims=True)
            grad_gated = rms * (grad_norm * mgain[...]) - gated * coef
            gate_grad_o[0, ri, :] = (grad_gated * mixed * (sg * (1.0 + g * (1.0 - sg)))).astype(BF16)
            grad_mixed = grad_gated * (g * sg)
            skg_o[0:1] += jnp.sum(grad_mixed * xa, axis=0, keepdims=True)
            dy = grad_mixed.astype(BF16)
            dys[0, ri, :] = dy
            cumg[0, ri, :] = head_sum(dy.astype(F32) * ssd_r, wide[...])
        cm = bcact[0, r, n:].astype(F32)
        grown = jnp.exp(cum_i[0, r, :])
        for p in range(inner // LANES):
            lanes = slice(p * LANES, (p + 1) * LANES)
            scaled = [(cm * grown[:, h : h + 1]).astype(BF16) for h in (2 * p, 2 * p + 1)]
            used = None
            for i in range(T // SUB):
                ri = pl.ds(pl.multiple_of(b * T + i * SUB, SUB), SUB)
                term = t_mm(jnp.concatenate([v[tile(i)] for v in scaled], axis=0), pair_rows(dys[0, ri, lanes]))
                used = term if used is None else used + term
            use[:, lanes] = used
        lend_o[0, b] = acc[...]
        acc[...] = expand_row(grown[T - 1 : T], wide[...]) * acc[...] + use[...]
        return 0

    lax.fori_loop(0, blocks, block, 0)


def scan_back(
    xact, bcact, step_i, cum_i, lstart, entry, pre, skip, wide, dys, cumg, xg_o, cumg_o, stepg_o, bcg_o, z, tick,
):
    length = xact.shape[1]
    blocks = length // T
    n = bcact.shape[2] // 2
    inner = xact.shape[2]

    def block(b, _):
        tick(b)
        r = rows_of(b)
        dy = dys[0, r, :]
        xa = xact[0, r, :].astype(F32)
        bca = bcact[0, r, :]
        bm, cm = bca[:, :n], bca[:, n:]
        cum = cum_i[0, r, :]
        cum_t = cum.T
        start = expand_row(jnp.exp(pre[0, pl.ds(b, 1), :]), wide[...]) * entry[0] + lstart[0, b]
        start = start.astype(BF16)
        dy32 = dy.astype(F32)
        gdy_hi, gdy_lo = split(expand(jnp.exp(cum), wide[...]) * dy32, 2)
        c_grad = mm_t(gdy_hi, start) + mm_t(gdy_lo, start)
        step_wide = expand(step_i[0, r, :], wide[...])
        xs = (xa * step_wide).astype(BF16)
        cross = cross_tiles(cm, bm)
        cross_part = {ij: jnp.zeros((SUB, SUB), F32) for ij in tiles()}
        for p in range(inner // LANES):
            lanes = slice(p * LANES, (p + 1) * LANES)
            zs = [None] * (T // SUB)
            for i in range(T // SUB):
                dy_two = pair_rows(dy[tile(i), lanes])
                for j in range(i + 1):
                    mix_grad = mm_t(dy_two, xs[tile(j), lanes])
                    mix = []
                    for k, h in enumerate((2 * p, 2 * p + 1)):
                        decay = decay_tile(cum, cum_t, h, i, j)
                        mix.append((cross[i, j] * decay).astype(BF16))
                        cross_part[i, j] = cross_part[i, j] + mix_grad[tile(k)] * decay
                    term = t_mm(jnp.concatenate(mix, axis=0), dy_two)
                    zs[j] = term if zs[j] is None else zs[j] + term
            for j in range(T // SUB):
                z[tile(j), lanes] = zs[j]
        rows = []
        for i in range(T // SUB):
            row = [jnp.where(lower(), cross_part[i, j], 0.0) if i == j else cross_part[i, j] for j in range(i + 1)]
            row += [jnp.zeros((SUB, SUB), F32)] * (T // SUB - 1 - i)
            rows.append(jnp.concatenate(row, axis=1))
        cross_low = jnp.concatenate(rows, axis=0).astype(BF16)
        bcg_o[0, r, 0:n] = t_mm(cross_low, cm)
        bcg_o[0, r, n : 2 * n] = c_grad + mm(cross_low, bm)
        zz = z[...]
        xg_o[0, r, :] = skip[...] * dy32 + step_wide * zz
        cumg_o[0, r, :] = cumg[0, r, :] - head_sum(xs.astype(F32) * zz, wide[...])
        stepg_o[0, r, :] = head_sum(xa * zz, wide[...])
        return 0

    lax.fori_loop(0, blocks, block, 0)


def back_two(
    xact, bcact, xext, bcext, step_i, cum_i, sraw, xg, cumg, stepg, bcg, lstart, entry, lend, after, pre,
    gnormed, cot, normed, gate_grad, vk, vo, sk, so, sbias, rate, wide, tri, y_in,
    xpg_o, xhalo_o, bpg_o, bhalo_o, raw_o, vkg_o, skg_o, heads_o, wout_o, wgate_o, y_all,
    xe, be, xcg, bcg_s, out_acc, gate_acc, yown, ygot, yfar, ta, tb, tc, td, te, tf, ylocal,
    *, seqs, plan,
):
    length = xact.shape[1]
    blocks = length // T
    n = bcact.shape[2] // 2
    taps = vk.shape[0]
    base = HALO - taps + 1
    vo, so = Row(vo), Row(so)
    step_at = pl.program_id(0)
    rider = Rider(*plan, y_all, yown, ygot, yfar, (ta, tb, tc, td, te, tf), ylocal)

    @pl.when(step_at == 0)
    def _():
        greet_head()
        pl.semaphore_wait(pltpu.get_barrier_semaphore(), 3)
        rider.load()
        out_acc[...] = jnp.zeros_like(out_acc)
        gate_acc[...] = jnp.zeros_like(gate_acc)
        vkg_o[...] = jnp.zeros_like(vkg_o)
        skg_o[...] = jnp.zeros_like(skg_o)
        heads_o[...] = jnp.zeros_like(heads_o)

    xe[...] = xext[0].astype(F32)
    be[...] = bcext[0].astype(F32)
    for ref in (xcg, bcg_s):
        ref[0:HALO] = jnp.zeros((HALO, ref.shape[1]), F32)
        ref[HALO + length :] = jnp.zeros((HALO, ref.shape[1]), F32)

    def conv_rows(ext, kernel, offset, r0):
        total = offset[...] + kernel[0:1] * ext[r0 + base : r0 + base + T]
        for k in range(1, taps):
            total = total + kernel[k : k + 1] * ext[r0 + base + k : r0 + base + k + T]
        sg = sigmoid(total)
        return sg * (1.0 + total * (1.0 - sg))

    def filter_grad(grad, ext, out, r0):
        for k in range(taps):
            out[k : k + 1] += jnp.sum(grad * ext[r0 + base + k : r0 + base + k + T], axis=0, keepdims=True)
        out[taps : taps + 1] += jnp.sum(grad, axis=0, keepdims=True)

    per_step = plan[1] // seqs
    for b in range(blocks):
        rider.tick(step_at * per_step + b)
        r0 = b * T
        r = slice(r0, r0 + T)
        xa = xact[0, r, :].astype(F32)
        bm = bcact[0, r, 0:n]
        cum = cum_i[0, r, :]
        step = step_i[0, r, :]
        last = cum[T - 1 : T]
        start = expand_row(jnp.exp(pre[0, b : b + 1]), wide[...]) * entry[0] + lstart[0, b]
        suffix = jnp.exp(pre[0, blocks : blocks + 1] - pre[0, b + 1 : b + 2])
        end = expand_row(suffix, wide[...]) * after[0] + lend[0, b]
        end_low = end.astype(BF16)
        weighted_grad = mm(bm, end_low)
        reach = jnp.exp(last - cum)
        weight = reach * step
        weight_wide = expand(weight, wide[...])
        weighted = (xa * weight_wide).astype(BF16)
        bcg_b = bcg[0, r, :]
        b_total = bcg_b[:, 0:n] + mm_t(weighted, end_low)
        bc_total = jnp.concatenate([b_total, bcg_b[:, n:]], axis=1)
        w_grad = head_sum(weighted_grad * xa, wide[...])
        part = w_grad * weight
        product = jnp.broadcast_to(jnp.sum(end * start, axis=0, keepdims=True), (16, end.shape[1]))
        fade_grad = jnp.exp(last) * head_sum(product, wide[...])[0:1]
        at_last = lax.broadcasted_iota(jnp.int32, (T, LANES), 0) == T - 1
        extra = fade_grad + jnp.sum(part, axis=0, keepdims=True)
        cum_grad = cumg[0, r, :] - part + jnp.where(at_last, extra, 0.0)
        a, bb, c = split(cum_grad, 3)
        rise = t_mm(tri[...], a) + (t_mm(tri[...], bb) + t_mm(tri[...], c))
        step_grad = stepg[0, r, :] + w_grad * reach + rise * rate[...]
        raw = step_grad * sigmoid(sraw[0, r, :] + sbias[...])
        raw_o[0, r, :] = raw.astype(BF16)
        heads_o[0:1] += jnp.sum(raw, axis=0, keepdims=True)
        heads_o[1:2] += jnp.sum(rise * step, axis=0, keepdims=True)
        grad = (xg[0, r, :] + weighted_grad * weight_wide) * conv_rows(xe, vk, vo, r0)
        filter_grad(grad, xe, vkg_o, r0)
        xcg[HALO + r0 : HALO + r0 + T] = grad
        grad = bc_total * conv_rows(be, sk, so, r0)
        filter_grad(grad, be, skg_o, r0)
        bcg_s[HALO + r0 : HALO + r0 + T] = grad

    def conv_back(ref, kernel, r0, rows):
        total = kernel[0:1] * ref[r0 + taps - 1 : r0 + taps - 1 + rows]
        for k in range(1, taps):
            total = total + kernel[k : k + 1] * ref[r0 + taps - 1 - k : r0 + taps - 1 - k + rows]
        return total.astype(BF16)

    for acc, left, right in ((out_acc, gnormed, cot), (gate_acc, normed, gate_grad)):
        for m in range(acc.shape[0] // 256):
            at = slice(m * 256, (m + 1) * 256)
            acc[at] += t_mm(left[0, :, at], right[0])

    xhalo_o[0] = conv_back(xcg, vk, 0, HALO)
    bhalo_o[0] = conv_back(bcg_s, sk, 0, HALO)
    for b in range(blocks):
        if blocks + b < per_step:
            rider.tick(step_at * per_step + blocks + b)
        r0 = b * T
        xpg_o[0, r0 : r0 + T] = conv_back(xcg, vk, HALO + r0, T)
        bpg_o[0, r0 : r0 + T] = conv_back(bcg_s, sk, HALO + r0, T)

    @pl.when(step_at == seqs - 1)
    def _():
        wout_o[...] = out_acc[...].astype(BF16)
        wgate_o[...] = gate_acc[...].astype(BF16)
        rider.close()


class GradSum:
    def __init__(self, rounds, mine, back, out, sems, zback=None, shared=0):
        self.rounds, self.mine, self.back, self.out, self.sems = rounds, mine, back, out, sems
        self.zback, self.shared = zback, shared
        self.me, self.z = lax.axis_index("seq"), lax.axis_index("head")
        self.rows = mine.shape[0]
        self.share = self.rows >> rounds

    @staticmethod
    def sem_count(rounds):
        return 4 * rounds + 9

    def bit(self, r):
        return lax.div(self.me, 1 << r) % 2

    def partner(self, r):
        return self.me + (1 << r) - (2 << r) * self.bit(r)

    def first(self, r):
        row = 0
        for k in range(r):
            row = row + self.bit(k) * (self.rows >> (k + 1))
        return row

    def at(self, row, size):
        return pl.ds(pl.multiple_of(row, 16), size)

    def halving(self, r):
        half = self.rows >> (r + 1)
        theirs = self.first(r) + half - half * self.bit(r)
        return pltpu.make_async_remote_copy(
            src_ref=self.mine.at[self.at(theirs, half)], dst_ref=self.back.at[pl.ds(self.rows - 2 * half, half)],
            send_sem=self.sems.at[r], recv_sem=self.sems.at[self.rounds + r],
            device_id={"seq": self.partner(r)}, device_id_type=MESH,
        )

    def add_half(self, r):
        copy = self.halving(r)
        copy.wait()
        half = self.rows >> (r + 1)
        row = self.first(r + 1)

        def one(k, _):
            at = self.at(row + k * self.share, self.share)
            come = self.back[pl.ds(pl.multiple_of(self.rows - 2 * half + k * self.share, 16), self.share), :]
            self.mine[at, :] = (self.mine[at, :].astype(F32) + come.astype(F32)).astype(BF16)
            return 0

        lax.fori_loop(0, half // self.share, one, 0)

    def gathering(self, r, arriving):
        size = self.rows >> (r + 1)
        row = self.first(r + 1)
        if arriving:
            row = row + size - 2 * size * self.bit(r)
        at = self.at(row, size)
        return pltpu.make_async_remote_copy(
            src_ref=self.out.at[at], dst_ref=self.out.at[at],
            send_sem=self.sems.at[2 * self.rounds + r], recv_sem=self.sems.at[3 * self.rounds + r],
            device_id={"seq": self.partner(r)}, device_id_type=MESH,
        )

    def to_head(self, d):
        base = 4 * self.rounds + 1
        src = self.mine.at[self.at(self.first(self.rounds), self.share), pl.ds(0, self.shared)]
        return pltpu.make_async_remote_copy(
            src_ref=src, dst_ref=self.zback.at[self.z], send_sem=self.sems.at[base + d], recv_sem=self.sems.at[base + 4 + d],
            device_id={"head": lax.rem(self.z + d, 4)}, device_id_type=MESH,
        )

    def publish(self):
        at = self.at(self.first(self.rounds), self.share)
        copy = pltpu.make_async_copy(self.mine.at[at], self.out.at[at], self.sems.at[4 * self.rounds])
        copy.start()
        copy.wait()
        self.gathering(self.rounds - 1, False).start()

    def stages(self):
        spans = [2, 5, 3] + [2] * self.rounds
        acts = [(spans[0], lambda: self.halving(0).start())]
        for r in range(self.rounds):
            def act(r=r):
                self.add_half(r)
                if r + 1 < self.rounds:
                    self.halving(r + 1).start()
                elif not self.shared:
                    self.publish()
                else:
                    for d in range(1, 4):
                        self.to_head(d).start()
                    self.zback[self.z] = self.mine[self.at(self.first(self.rounds), self.share), 0 : self.shared]

            acts.append((spans[r + 1] if r + 1 < self.rounds else spans[r], act))
        if self.shared:
            def meet():
                for d in range(1, 4):
                    self.to_head(d).wait()
                at = self.at(self.first(self.rounds), self.share)
                low = [self.zback[k].astype(F32) for k in range(4)]
                self.mine[at, 0 : self.shared] = ((low[0] + low[1]) + (low[2] + low[3])).astype(BF16)
                self.publish()

            acts.append((spans[self.rounds - 1], meet))
        for r in reversed(range(self.rounds)):
            def act(r=r):
                self.gathering(r, False).wait_send()
                self.gathering(r, True).wait_recv()
                if r > 0:
                    self.gathering(r - 1, False).start()

            acts.append((spans[max(r - 1, 0)], act))
        return acts


def finish(
    y, gate_grad, xpg, bpg, raw, tok, cot, rms, gate_w, value_w, state_w, step_w, ngain, filter_rows, gain_rows, skip_rows, head_rows, state_rows, xhalo, bhalo,
    normed, tok_k, out_grad, gate_grad_w, y_all,
    result_o, tokens_grad_o, small_o, wout_o, wgate_o, wvalue_o, wmixed_o,
    own, got, far, sa, sb, sc, sd, se, sf, yown, ygot, yfar, ta, tb, tc, td, te, tf, ylocal, rows, out, back, send, recv,
    w_mine, w_back, m_mine, m_back, m_zback, w_acc, m_acc, w_sems, w_local, vec, vback, vsems, xtail, btail, halo_sems, xnow, bnow,
    *, n, rounds, plan, per_seq,
):
    i = pl.program_id(0)
    ngain = Row(ngain)
    z, me = lax.axis_index("head"), lax.axis_index("seq")
    last = n + 3 * LAG - 1
    outs = (wout_o, wgate_o, wvalue_o)
    grads = [GradSum(rounds, w_mine.at[k], w_back.at[k], outs[k], w_sems.at[k]) for k in range(3)]
    grads.append(GradSum(rounds, m_mine, m_back, wmixed_o, w_sems.at[3], m_zback, bpg.shape[1]))
    products = n * CHUNK // T

    devices = lax.axis_size("seq")

    def halo_copies():
        return [
            pltpu.make_async_remote_copy(
                src_ref=src, dst_ref=dst, send_sem=halo_sems.at[k], recv_sem=halo_sems.at[2 + k],
                device_id={"seq": lax.rem(me + devices - 1, devices)}, device_id_type=MESH,
            )
            for k, (src, dst) in enumerate(((xhalo, xtail), (bhalo, btail)))
        ]

    def vec_copy(d):
        return pltpu.make_async_remote_copy(
            src_ref=vec, dst_ref=vback.at[z], send_sem=vsems.at[d], recv_sem=vsems.at[4 + d],
            device_id={"head": lax.rem(z + d, 4)}, device_id_type=MESH,
        )

    def local_copies():
        rows_out, half = out_grad.shape[0], out_grad.shape[1] // 2
        return [
            pltpu.make_async_copy(gate_grad_w, w_mine.at[1], w_local.at[0]),
            pltpu.make_async_copy(out_grad.at[:, pl.ds(0, half)], w_mine.at[0, pl.ds(0, rows_out)], w_local.at[1]),
            pltpu.make_async_copy(out_grad.at[:, pl.ds(half, half)], w_mine.at[0, pl.ds(rows_out, rows_out)], w_local.at[2]),
        ]

    chain = Chain(own, got, far, (sa, sb, sc, sd, se, sf))
    rider = Rider(*plan, y_all, yown, ygot, yfar, (ta, tb, tc, td, te, tf), ylocal)
    me = lax.axis_index("seq")

    def partner(r):
        bit = 1 << r
        return me + bit - 2 * bit * (lax.div(me, bit) % 2)

    @pl.when(i == 0)
    def _():
        barrier = pltpu.get_barrier_semaphore()
        for d in range(1, devices):
            pl.semaphore_signal(barrier, inc=1, device_id={"seq": lax.rem(me + d, devices)}, device_id_type=MESH)
        greet_head()
        pl.semaphore_wait(barrier, devices - 1 + 3)

        @pl.when(me > 0)
        def _():
            for copy in halo_copies():
                copy.start()

        @pl.when(me == devices - 1)
        def _():
            xtail[...] = jnp.zeros_like(xtail)
            btail[...] = jnp.zeros_like(btail)

        rider.load()
        for copy in local_copies():
            copy.start()
        w_acc[...] = jnp.zeros_like(w_acc)
        m_acc[...] = jnp.zeros_like(m_acc)
        rows[...] = jnp.zeros_like(rows)
        rows[0:5] = filter_rows[0:5]
        rows[5:6] = gain_rows[0:1]
        rows[6:7] = skip_rows[0:1]
        rows[7:8, 0:LANES] = head_rows[0:1]
        rows[7:8, LANES : 2 * LANES] = head_rows[1:2]
        rows[16:24, 0 : state_rows.shape[1]] = state_rows[...]

    rider.tick(i)
    for stage in (2, 1):
        k = i - stage * LAG

        @pl.when((k >= 0) & (k < n))
        def _():
            chain.onward(stage, k)

    def with_tails():
        return [
            jnp.concatenate([v[0 : T - HALO], (v[T - HALO : T].astype(F32) + tail[...]).astype(BF16)], axis=0)
            for v, tail in ((xpg, xnow), (bpg, bnow))
        ]

    @pl.when((i == per_seq - 1) & (me < devices - 1))
    def _():
        for copy in halo_copies():
            copy.wait_recv()

    ends = lax.rem(i, per_seq) == per_seq - 1

    @pl.when((i < products) & ends)
    def _():
        xnow[...] = xtail[lax.div(i, per_seq)].astype(F32)
        bnow[...] = btail[lax.div(i, per_seq)].astype(F32)

    @pl.when((i < products) & jnp.logical_not(ends))
    def _():
        xnow[...] = jnp.zeros_like(xnow)
        bnow[...] = jnp.zeros_like(bnow)

    @pl.when(i < products)
    def _():
        x_rows, b_rows = with_tails()
        value = mm_t(gate_grad[...], gate_w[...]) + mm_t(x_rows, value_w[...])
        value = value + (mm_t(b_rows, state_w[...]) + mm_t(raw[...], step_w[...]))
        chunks = T // CHUNK
        own[pl.ds(i * chunks, chunks)] = value.astype(BF16).reshape(chunks, CHUNK, value.shape[1])
        t = tok_k[...].astype(F32)
        inv = lax.rsqrt(jnp.mean(t * t, axis=1, keepdims=True) + EPS)
        gain = jnp.sum(value * (t * inv), axis=0, keepdims=True)
        half = t.shape[1] // 2
        rows[8:9] += gain[:, :half]
        rows[9:10] += gain[:, half:]

    @pl.when(i < n)
    def _():
        chain.inward(i)

    @pl.when(i < products)
    def _():
        x_rows, b_rows = with_tails()
        mixed = jnp.concatenate([b_rows, raw[...]], axis=1)
        for m in range(w_acc.shape[0] // 256):
            rows_m = slice(m * 256, (m + 1) * 256)
            left = normed[:, rows_m]
            w_acc[rows_m] += t_mm(left, x_rows)
            m_acc[rows_m] += t_mm(left, mixed)

    @pl.when(i == products)
    def _():
        w_mine[2] = w_acc[...].astype(BF16)
        m_mine[...] = m_acc[...].astype(BF16)

    @pl.when(i == 1)
    def _():
        for copy in local_copies():
            copy.wait()

    for grad_sum, begin in zip(grads, (1, 4, products + 1, products + 5)):
        at = begin
        for span, act in grad_sum.stages():
            pl.when(i == min(at, last))(act)
            at += span

    @pl.when(i == products)
    def _():
        vec[...] = rows[8:24]
        for d in range(1, 4):
            vec_copy(d).start()
        vback[z] = vec[...]

    def row_copy(r):
        return pltpu.make_async_remote_copy(
            src_ref=out.at[r], dst_ref=back.at[r], send_sem=send.at[r], recv_sem=recv.at[r],
            device_id={"seq": partner(r)}, device_id_type=MESH,
        )

    @pl.when(i == products + 4)
    def _():
        for d in range(1, 4):
            vec_copy(d).wait()
        rows[8:24] = (vback[0] + vback[1]) + (vback[2] + vback[3])
        out[0] = rows[...]
        row_copy(0).start()

    for r in range(rounds):

        @pl.when(i == products + 4 + 3 * (r + 1))
        def _():
            row_copy(r).wait()
            rows[...] = rows[...] + back[r]
            if r + 1 < rounds:
                out[r + 1] = rows[...]
                row_copy(r + 1).start()

    k = i - 3 * LAG

    @pl.when(k >= 0)
    def _():
        grad = chain.total(k)
        rms_k = rms[:, 0:1]
        t = tok[...].astype(F32)
        width = t.shape[1]
        inv = lax.rsqrt(jnp.mean(t * t, axis=1, keepdims=True) + EPS)
        if rider.done > 0:

            @pl.when(k < rider.done)
            def _():
                result_o[...] = (t + y[...].astype(F32) * rms_k).astype(BF16)

        if rider.done < n:

            @pl.when(k >= rider.done)
            def _():
                result_o[...] = (t + rider.chain.total(k - rider.base) * rms_k).astype(BF16)

        scaled = grad * ngain[...]
        dot = jnp.sum(scaled * t, axis=1, keepdims=True) / width
        tokens_grad_o[...] = (cot[...].astype(F32) + inv * scaled - t * (inv * inv * inv * dot)).astype(BF16)

    @pl.when(i == last)
    def _():
        chain.drain(n)
        rider.drain()

        @pl.when(me > 0)
        def _():
            for copy in halo_copies():
                copy.wait_send()

        small_o[...] = rows[...]


def unpack(
    tgrad, res, wout_l, wout_r, wgate, wvalue, wmixed, mixed_all, small, rate, wide,
    res_o, tgrad_o, ngain_o, wgate_o, wvalue_o, state_o, step_o, vk_o, vo_o, sk_o, so_o, sbias_o, rate_o, skip_o, mgain_o, wout_o,
    *, taps, heads,
):
    res_o[...] = res[...]
    tgrad_o[...] = tgrad[...].astype(F32)
    wgate_o[...] = wgate[...].astype(F32)
    wvalue_o[...] = wvalue[...].astype(F32)
    half = wout_l.shape[1]
    wout_o[:, :half] = wout_l[...].astype(F32)
    wout_o[:, half:] = wout_r[...].astype(F32)
    n2 = state_o.shape[1]
    state_o[...] = wmixed[:, :n2].astype(F32)

    @pl.when(pl.program_id(0) == 0)
    def _():
        for k in range(mixed_all.shape[0] // LANES):
            at = slice(k * LANES, (k + 1) * LANES)
            step_o[:, at] = mixed_all[at, n2 : n2 + LANES].astype(F32).T[0:heads]
        vk_o[...] = small[0:taps]
        vo_o[...] = small[taps]
        mgain_o[...] = small[taps + 1]
        skip_o[...] = head_sum(jnp.broadcast_to(small[taps + 2 : taps + 3], (16, half)), wide[...])[0, 0:heads]
        sbias_o[...] = small[taps + 3, 0:heads]
        rate_o[...] = small[taps + 3, LANES : LANES + heads] * rate[0, 0:heads]
        ngain_o[pl.ds(0, half)] = small[8]
        ngain_o[pl.ds(half, half)] = small[9]
        sk_o[...] = small[16 : 16 + taps, 0:n2]
        so_o[...] = small[16 + taps, 0:n2]


def call(body, steps, seqs, ins, outs, scratch, flops, collective_id=None, carried=None):
    def cut(shape, lag):
        rest = tuple(shape[1:])
        return pl.BlockSpec((1,) + rest, lambda s: (jnp.clip(s - lag, 0, seqs - 1),) + (0,) * len(rest))

    def whole(shape):
        return pl.BlockSpec(tuple(shape), lambda s: (0,) * len(shape), pipeline_mode=pl.Buffered(1))

    pairs = [v if isinstance(v, tuple) else (v, 0) for v in ins]
    ins = [v for v, _ in pairs]
    in_specs = [cut(v.shape, lag) if v.ndim >= 3 else whole(v.shape) for v, lag in pairs]
    out_specs = [whole(s) if lag is None else cut(s, lag) for s, _, lag in outs]
    out_shape = [jax.ShapeDtypeStruct(s, d) for s, d, _ in outs]
    aliases = {}
    if carried is not None:
        aliases = {len(ins): len(outs)}
        in_specs.append(pl.BlockSpec(memory_space=pl.ANY))
        out_specs.append(pl.BlockSpec(memory_space=pl.ANY))
        out_shape.append(jax.ShapeDtypeStruct(carried.shape, carried.dtype))
        ins = ins + [carried]
    moved = sum(a.size * a.dtype.itemsize for a in ins)
    for s, d, _ in outs:
        size = jnp.dtype(d).itemsize
        for k in s:
            size *= k
        moved += size
    return pl.pallas_call(
        body,
        grid=(steps,),
        in_specs=in_specs,
        out_specs=out_specs,
        out_shape=out_shape,
        scratch_shapes=scratch,
        input_output_aliases=aliases,
        compiler_params=pltpu.CompilerParams(
            dimension_semantics=("arbitrary",), vmem_limit_bytes=60 * 1024 * 1024,
            collective_id=collective_id, has_side_effects=collective_id is not None,
        ),
        cost_estimate=pl.CostEstimate(flops=flops, bytes_accessed=moved, transcendentals=0),
    )(*ins)


def shards(
    tokens, norm_gain, gate_weight, value_weight, state_weight, step_weight, value_kernel, value_offset,
    state_kernel, state_offset, step_bias, log_rate, skip_gain, mixer_gain, out_weight, cotangent,
):
    seqs, length, width = tokens.shape
    flat = seqs * length
    inner = gate_weight.shape[1]
    heads = step_weight.shape[1]
    head_size = inner // heads
    n2 = state_weight.shape[1]
    n = n2 // 2
    taps = value_kernel.shape[0]
    blocks = length // T
    devices = lax.axis_size("seq")
    rounds = devices.bit_length() - 1
    assert devices == 1 << rounds and taps == 4
    inner_all = inner * lax.axis_size("head")

    pad = LANES - heads
    rate_row = -jnp.exp(log_rate)
    rate = jnp.pad(rate_row, (0, pad))[None]
    bias = jnp.pad(step_bias, (0, pad))[None]
    step_w = jnp.pad(step_weight, ((0, 0), (0, pad)))
    skip = jnp.repeat(skip_gain, head_size)[None]
    gain = mixer_gain
    one = (jnp.arange(inner)[None, :] // head_size == jnp.arange(LANES)[:, None]).astype(BF16)
    wide = jnp.concatenate([one, one], axis=0)
    tri = (jnp.arange(T)[:, None] >= jnp.arange(T)[None, :]).astype(BF16)
    vo, so = value_offset, state_offset

    def big(cols, dtype, rows=length, lag=0):
        return ((seqs, rows, cols), dtype, lag)

    vmem = pltpu.VMEM
    ext = length + HALO
    n_chunks = flat // CHUNK
    steps = seqs + rounds
    plan = (0, min(2 * (seqs - 1), length // CHUNK), n_chunks)
    dma = pltpu.SemaphoreType.DMA

    def block(shape, lag):
        return pl.BlockSpec((1,) + shape, lambda i: (jnp.clip(i - lag, 0, seqs - 1), 0, 0))

    def once(v):
        return pl.BlockSpec(v.shape, lambda i: (0,) * len(v.shape), pipeline_mode=pl.Buffered(1))

    def shape_of(cols, dtype, rows=length):
        return jax.ShapeDtypeStruct((seqs, rows, cols), dtype)

    fixed = (norm_gain, gate_weight, value_weight, state_weight, step_w, value_kernel, vo, state_kernel, so, bias, rate,
             wide, tri, out_weight, gain, skip)
    held = (shape_of(LANES, F32, 8), shape_of(inner, F32, n), shape_of(length, F32, 8))
    anywhere = pl.BlockSpec(memory_space=pl.ANY)
    (xext, bcext, sraw, pre, entry, sums, xact, bcact, gate, step, cum, lstart, normed, ssd, gn, y) = pl.pallas_call(
        functools.partial(forward, seqs=seqs, rounds=rounds, plan=plan),
        grid=(steps,),
        in_specs=[block((length, width), 0), anywhere, block((length, width), rounds)] + [once(v) for v in fixed],
        out_specs=[block((ext, inner), 0), block((ext, n2), 0), block((length, LANES), 0)] + [once(v) for v in held] + [anywhere] * 10,
        out_shape=[shape_of(inner, BF16, ext), shape_of(n2, BF16, ext), shape_of(LANES, F32), *held,
                   shape_of(inner, BF16), shape_of(n2, BF16), shape_of(inner, F32), shape_of(LANES, F32), shape_of(LANES, F32),
                   jax.ShapeDtypeStruct((seqs, blocks, n, inner), F32), shape_of(width, BF16), shape_of(inner, F32),
                   shape_of(inner, F32), jax.ShapeDtypeStruct((n_chunks, CHUNK, width), BF16)],
        scratch_shapes=[
            vmem((seqs, length, inner), BF16), vmem((seqs, length, n2), BF16), vmem((seqs, length, inner), F32),
            vmem((seqs, length, LANES), F32), vmem((seqs, length, LANES), F32), vmem((seqs, blocks, n, inner), F32),
            vmem((ext, width), BF16), vmem((1, length, inner), F32), vmem((1, length, inner), F32),
            vmem((length // CHUNK, CHUNK, width), BF16), vmem((length, inner), BF16),
            vmem((ext, inner), F32), vmem((ext, n2), F32), vmem((n, inner), F32), vmem((8, LANES), F32),
            vmem((seqs, HALO, width), BF16), vmem((seqs, 8, length), F32), vmem((seqs, 4, 8, length), F32),
            dma((6, seqs)), dma((4,)), dma((seqs,)), dma((seqs,)), dma((seqs, 4)), dma((seqs, 4)),
        ] + Exchange.scratch(rounds, seqs, n, inner) + Rider.scratch(*plan, width),
        compiler_params=pltpu.CompilerParams(
            dimension_semantics=("arbitrary",), vmem_limit_bytes=62 * 1024 * 1024, collective_id=1, has_side_effects=True
        ),
        cost_estimate=pl.CostEstimate(flops=2 * flat * width * 4 * inner, bytes_accessed=10**8, transcendentals=0),
    )(tokens, tokens, cotangent, *fixed)
    plan = (plan[1], 2 * (seqs + rounds), n_chunks)
    gnormed, gate_grad, lend, rms, xg, cumg, stepg, bcg, mgg, skg, after, y = call(
        functools.partial(back_one, inner_all=inner_all, seqs=seqs, rounds=rounds, plan=plan), seqs + rounds, seqs,
        [xact, bcact, cum, gate, ssd, gn, sums, pre, gain, skip, wide]
        + [(v, rounds) for v in (xact, bcact, step, cum, lstart, entry, pre)],
        [big(inner, BF16), big(inner, BF16), ((seqs, blocks, n, inner), F32, 0), big(LANES, F32),
         big(inner, F32, lag=rounds), big(LANES, F32, lag=rounds), big(LANES, F32, lag=rounds), big(n2, F32, lag=rounds),
         ((8, inner), F32, None), ((8, inner), F32, None), ((seqs, n, inner), F32, None)],
        [vmem((T, inner), F32), vmem((n, inner), F32), vmem((n, inner), F32), vmem((seqs, length, inner), BF16),
         vmem((seqs, length, LANES), F32)]
        + Exchange.scratch(rounds, seqs, n, inner) + Rider.scratch(*plan, width),
        2 * flat * T * inner * 8, 3, y,
    )
    plan = (plan[0] + plan[1], 3 * seqs, n_chunks)
    xpg, xhalo, bpg, bhalo, raw, vkg, skgr, head_rows, out_weight_grad, gate_weight_grad, y = call(
        functools.partial(back_two, seqs=seqs, plan=plan), seqs, seqs,
        [xact, bcact, xext, bcext, step, cum, sraw, xg, cumg, stepg, bcg, lstart, entry, lend, after, pre,
         gnormed, cotangent, normed, gate_grad, value_kernel, vo, state_kernel, so, bias, rate, wide, tri],
        [big(inner, BF16), big(inner, BF16, HALO), big(n2, BF16), big(n2, BF16, HALO), big(LANES, BF16),
         ((8, inner), F32, None), ((8, n2), F32, None), ((8, LANES), F32, None),
         ((inner, width), BF16, None), ((width, inner), BF16, None)],
        [vmem((ext, inner), F32), vmem((ext, n2), F32), vmem((ext + HALO, inner), F32),
         vmem((ext + HALO, n2), F32), vmem((inner, width), F32), vmem((width, inner), F32)] + Rider.scratch(*plan, width),
        2 * flat * T * inner * 4, 5, y,
    )
    def flatten(v):
        return v.reshape(flat, v.shape[-1])

    normed_f, xpg_f, bpg_f, raw_f, gg_f = [flatten(v) for v in (normed, xpg, bpg, raw, gate_grad)]
    first = min(plan[0] + plan[1], n_chunks + 2 * LAG)
    plan = (first, max(n_chunks - first, 0) + 3 * LAG, n_chunks)

    def product_rows(v):
        return pl.BlockSpec((T, v.shape[1]), lambda i: (jnp.minimum(i, flat // T - 1), 0))

    def lagged(cols, lag):
        return pl.BlockSpec((CHUNK, cols), lambda i: (jnp.clip(i - lag, 0, n_chunks - 1), 0))

    late = (gate_weight, value_weight, state_weight, step_w, norm_gain, vkg, mgg, skg, head_rows, skgr, xhalo, bhalo)
    result, tokens_grad, small, wout, wgate, wvalue, wmixed = pl.pallas_call(
        functools.partial(finish, n=n_chunks, rounds=rounds, plan=plan, per_seq=blocks),
        grid=(n_chunks + 3 * LAG,),
        in_specs=[lagged(width, 3 * LAG)]
        + [product_rows(v) for v in (gg_f, xpg_f, bpg_f, raw_f)]
        + [lagged(width, 3 * LAG), lagged(width, 3 * LAG), lagged(LANES, 3 * LAG)]
        + [once(v) for v in late] + [product_rows(normed_f), product_rows(flatten(tokens))] + [anywhere] * 3,
        out_specs=[lagged(width, 3 * LAG), lagged(width, 3 * LAG), pl.BlockSpec((24, inner), lambda i: (0, 0)),
                   anywhere, anywhere, anywhere, anywhere],
        out_shape=[
            jax.ShapeDtypeStruct((flat, width), BF16), jax.ShapeDtypeStruct((flat, width), BF16),
            jax.ShapeDtypeStruct((24, inner), F32), *[jax.ShapeDtypeStruct((width, c), BF16) for c in (inner, inner, inner, n2 + LANES)],
        ],
        scratch_shapes=Chain.scratch(n_chunks, CHUNK, width) + Rider.scratch(*plan, width) + [
            vmem((24, inner), F32), vmem((rounds, 24, inner), F32), vmem((rounds, 24, inner), F32),
            pltpu.SemaphoreType.DMA((rounds,)), pltpu.SemaphoreType.DMA((rounds,)),

            vmem((3, width, inner), BF16), vmem((3, width, inner), BF16), vmem((width, n2 + LANES), BF16),
            vmem((width, n2 + LANES), BF16), vmem((4, width >> rounds, n2), BF16), vmem((width, inner), F32),
            vmem((width, n2 + LANES), F32), dma((4, GradSum.sem_count(rounds))), dma((3,)),
            vmem((16, inner), F32), vmem((4, 16, inner), F32), dma((8,)), vmem(xhalo.shape, BF16), vmem(bhalo.shape, BF16), dma((4,)),
            vmem((HALO, inner), F32), vmem((HALO, n2), F32),
        ],
        compiler_params=pltpu.CompilerParams(
            dimension_semantics=("arbitrary",), vmem_limit_bytes=62 * 1024 * 1024, collective_id=4, has_side_effects=True
        ),
        cost_estimate=pl.CostEstimate(flops=10**11, bytes_accessed=10**8, transcendentals=0),
    )(y.reshape(flat, width), gg_f, xpg_f, bpg_f, raw_f, flatten(tokens), flatten(cotangent), flatten(rms),
      *late, normed_f, flatten(tokens), out_weight_grad, gate_weight_grad, y)
    parts = 8

    def strip(rows, cols, at=0):
        return pl.BlockSpec((rows // parts, cols), lambda i: (i + at, 0))

    def entire(shape):
        return pl.BlockSpec(shape, lambda i: (0,) * len(shape))

    fine = [strip(inner, inner), strip(inner, inner, parts)]
    flat_out = [
        ((flat, width), BF16), ((flat, width), F32), ((width,), F32), ((width, inner), F32), ((width, inner), F32), ((width, n2), F32),
        ((heads, width), F32), ((taps, inner), F32), ((inner,), F32), ((taps, n2), F32), ((n2,), F32), ((heads,), F32), ((heads,), F32),
        ((heads,), F32), ((inner,), F32), ((inner, width), F32),
    ]
    cut = (0, 1, 3, 4, 5, 15)
    found = pl.pallas_call(
        functools.partial(unpack, taps=taps, heads=heads),
        grid=(parts,),
        in_specs=[strip(flat, width), strip(flat, width)] + fine + [strip(width, inner)] * 2 + [strip(width, n2 + LANES)]
        + [entire(wmixed.shape), entire(small.shape), entire(rate.shape), entire(wide.shape)],
        out_specs=[strip(*shape) if k in cut else entire(shape) for k, (shape, _) in enumerate(flat_out)],
        out_shape=[jax.ShapeDtypeStruct(shape, dtype) for shape, dtype in flat_out],
        compiler_params=pltpu.CompilerParams(dimension_semantics=("arbitrary",), vmem_limit_bytes=60 * 1024 * 1024),
    )(tokens_grad, result, wout, wout, wgate, wvalue, wmixed, wmixed, small, rate, wide)
    found = [found[0].reshape(tokens.shape), found[1].reshape(tokens.shape), *found[2:6], found[6].T, *found[7:]]
    return tuple(found)


def solution(mesh):
    rows, cols, vec = P(None, "seq", None), P(None, "head"), P("head")
    in_specs = (rows, P(), cols, cols, P(), cols, cols, vec, P(), P(), vec, vec, vec, vec, P("head", None), rows)
    out_specs = (rows, rows, P(), cols, cols, P(), cols, cols, vec, P(), P(), vec, vec, vec, vec, P("head", None))
    return jax.shard_map(shards, mesh=mesh, in_specs=in_specs, out_specs=out_specs, check_vma=False)
```

```python
import functools

import jax
import jax.numpy as jnp
import numpy as np
from jax import lax
from jax.experimental import pallas as pl
from jax.experimental.pallas import tpu as pltpu
from jax.sharding import PartitionSpec as P

EPS = 1e-05
T = 256
SUB = 128
HALO = 16
LANES = 128
F32 = jnp.float32
BF16 = jnp.bfloat16


def mm(a, b):
    return lax.dot_general(a, b, (((1,), (0,)), ((), ())), preferred_element_type=F32)


def mm_t(a, b):
    return lax.dot_general(a, b, (((1,), (1,)), ((), ())), preferred_element_type=F32)


def t_mm(a, b):
    return lax.dot_general(a, b, (((0,), (0,)), ((), ())), preferred_element_type=F32)


def split(v, parts):
    pieces = []
    for _ in range(parts):
        piece = v.astype(BF16)
        pieces.append(piece)
        v = v - piece.astype(F32)
    return pieces


def expand(v, wide):
    return mm(jnp.concatenate(split(v, 2), axis=1), wide)


def expand_row(v, wide):
    return expand(jnp.broadcast_to(v, (16, LANES)), wide)[0:1]


def head_sum(v, wide):
    hi, lo = split(v, 2)
    return mm_t(hi, wide[:LANES]) + mm_t(lo, wide[:LANES])


def exact_tri(tri, v):
    a, b, c = split(v, 3)
    return mm(tri, a) + (mm(tri, b) + mm(tri, c))


def sigmoid(v):
    return 0.5 * jnp.tanh(0.5 * v) + 0.5


def softplus(v):
    return jnp.maximum(v, 0.0) + jnp.log1p(jnp.exp(-jnp.abs(v)))


def lower():
    row = lax.broadcasted_iota(jnp.int32, (SUB, SUB), 0)
    col = lax.broadcasted_iota(jnp.int32, (SUB, SUB), 1)
    return row >= col


def tile(i):
    return slice(i * SUB, (i + 1) * SUB)


def tiles():
    return [(i, j) for i in range(T // SUB) for j in range(i + 1)]


def cross_tiles(cm, bm):
    found = {}
    for i, j in tiles():
        value = mm_t(cm[tile(i)], bm[tile(j)])
        found[i, j] = jnp.where(lower(), value, 0.0) if i == j else value
    return found


def decay_tile(cum, cum_t, h, i, j):
    gap = cum[tile(i), h : h + 1] - cum_t[h : h + 1, tile(j)]
    return jnp.exp(jnp.minimum(gap, 0.0) if i == j else gap)


def half_mask(rows):
    return lax.broadcasted_iota(jnp.int32, (rows, LANES), 1) < LANES // 2


def pair_rows(v):
    left = half_mask(v.shape[0])
    zero = jnp.zeros_like(v)
    return jnp.concatenate([jnp.where(left, v, zero), jnp.where(left, zero, v)], axis=0)


def rows_of(b):
    return pl.ds(pl.multiple_of(b * T, T), T)


MESH = pl.DeviceIdType.MESH
CHUNK = 64
LAG = 2


def greet_head():
    z = lax.axis_index("head")
    for d in range(1, 4):
        pl.semaphore_signal(
            pltpu.get_barrier_semaphore(), inc=1, device_id={"head": lax.rem(z + d, 4)}, device_id_type=MESH)


class Chain:
    def __init__(self, own, got, far, sems):
        z = lax.axis_index("head")
        self.end = (z == 0) | (z == 3)
        self.side = z + 1 - 2 * (z % 2)
        self.other = 3 - z
        self.own, self.got, self.far = own, got, far
        self.sems = sems

    @staticmethod
    def scratch(n, chunk, width):
        buffer = pltpu.VMEM((n, chunk, width), BF16)
        return [buffer, buffer, buffer] + [pltpu.SemaphoreType.DMA((n,))] * 6

    def copy(self, kind, k):
        src, dst, to = [(self.own, self.got, self.side), (self.own, self.far, self.other), (self.got, self.got, self.side)][kind]
        return pltpu.make_async_remote_copy(
            src_ref=src.at[k], dst_ref=dst.at[k],
            send_sem=self.sems[2 * kind].at[k], recv_sem=self.sems[2 * kind + 1].at[k],
            device_id={"head": to}, device_id_type=MESH,
        )

    def inward(self, k):
        @pl.when(self.end)
        def _():
            self.copy(0, k).start()

    def meet(self, stage, k):
        self.copy(stage, k).wait_recv()
        if stage == 0:
            self.own[k] = (self.own[k].astype(F32) + self.got[k].astype(F32)).astype(BF16)
        else:
            self.got[k] = (self.own[k].astype(F32) + self.far[k].astype(F32)).astype(BF16)

    def onward(self, stage, k):
        @pl.when(jnp.logical_not(self.end))
        def _():
            self.meet(stage - 1, k)
            self.copy(stage, k).start()

    def total(self, k):
        @pl.when(self.end)
        def _():
            self.copy(2, k).wait_recv()

        return self.got[k].astype(F32)

    def drain(self, n):
        def one(k, _):
            @pl.when(self.end)
            def _():
                self.copy(0, k).wait_send()

            @pl.when(jnp.logical_not(self.end))
            def _():
                self.copy(1, k).wait_send()
                self.copy(2, k).wait_send()

            return 0

        lax.fori_loop(0, n, one, 0)


class Rider:
    def __init__(self, first, ticks, count, hbm, own, got, far, sems, local):
        self.first, self.ticks, self.count = first, ticks, count
        self.done = min(max(first - 2 * LAG, 0), count)
        self.base = min(self.done, count - 1)
        self.hbm, self.local = hbm, local
        self.chain = Chain(own, got, far, sems)

    @staticmethod
    def size(first, ticks, count):
        return max(min(first + ticks, count) - min(max(first - 2 * LAG, 0), count - 1), 1)

    @staticmethod
    def scratch(first, ticks, count, width):
        return Chain.scratch(Rider.size(first, ticks, count), CHUNK, width) + [pltpu.SemaphoreType.DMA((2,))]

    def span(self, stage):
        low = self.first - stage * LAG
        return max(low, 0), min(low + self.ticks, self.count)

    def load(self):
        size = self.size(self.first, self.ticks, self.count)
        own = pltpu.make_async_copy(self.hbm.at[pl.ds(self.base, size)], self.chain.own, self.local.at[0])
        own.start()
        ready = min(max(self.first - LAG, 0), self.count) - self.base
        if ready > 0 and self.done < self.count:

            @pl.when(jnp.logical_not(self.chain.end))
            def _():
                got = pltpu.make_async_copy(
                    self.hbm.at[pl.ds(self.base, ready)], self.chain.got.at[pl.ds(0, ready)], self.local.at[1])
                got.start()
                got.wait()

        own.wait()

    def tick(self, t):
        chain = self.chain
        for stage in (2, 1, 0):
            low, high = self.span(stage)
            k = self.first - stage * LAG + t

            @pl.when((k >= low) & (k < high) & (t < self.ticks))
            def _():
                at = k - self.base
                if stage == 0:
                    chain.inward(at)
                else:
                    self.follow(stage, at, t >= LAG)

    def follow(self, stage, at, pending):
        chain = self.chain
        middle = jnp.logical_not(chain.end)

        @pl.when(middle & pending)
        def _():
            chain.meet(stage - 1, at)

        @pl.when(middle)
        def _():
            chain.copy(stage, at).start()

    def drain(self):
        chain = self.chain

        def each(stage):
            low, high = self.span(stage)
            lax.fori_loop(low - self.base, high - self.base, lambda k, _: (chain.copy(stage, k).wait_send(), 0)[1], 0)

        @pl.when(chain.end)
        def _():
            each(0)

        @pl.when(jnp.logical_not(chain.end))
        def _():
            each(1)
            each(2)

    def close(self):
        chain = self.chain
        middle = jnp.logical_not(chain.end)

        def each(low, high, do):
            if high > low:
                lax.fori_loop(low - self.base, high - self.base, lambda k, _: (do(k), 0)[1], 0)

        @pl.when(middle)
        def _():
            for stage in (0, 1):
                low, high = self.span(stage)
                started = max(self.first - stage * LAG + self.ticks - LAG, low)
                each(started, high, lambda k: chain.meet(stage, k))
            for stage in (1, 2):
                each(*self.span(stage), lambda k: chain.copy(stage, k).wait_send())

        @pl.when(chain.end)
        def _():
            each(*self.span(2), lambda k: chain.copy(2, k).wait_recv())
            each(*self.span(0), lambda k: chain.copy(0, k).wait_send())

        def store(ref, low, high):
            if high > low:
                at = pl.ds(low - self.base, high - low)
                copy = pltpu.make_async_copy(ref.at[at], self.hbm.at[pl.ds(low, high - low)], self.local.at[0])
                copy.start()
                copy.wait()

        @pl.when(middle)
        def _():
            reached = self.span(1)[1]
            store(chain.got, self.done, reached)
            store(chain.own, reached, self.span(0)[1])

        @pl.when(chain.end)
        def _():
            store(chain.got, *self.span(2))


class Exchange:
    def __init__(self, rounds, backward, total, before, logs, out, back, send, recv):
        self.rounds, self.backward = rounds, backward
        self.total, self.before, self.logs = total, before, logs
        self.out, self.back, self.send, self.recv = out, back, send, recv
        self.me = lax.axis_index("seq")

    def partner(self, r):
        bit = 1 << r
        return self.me + bit - 2 * bit * (lax.div(self.me, bit) % 2)

    def greet(self, with_head=False):
        barrier = pltpu.get_barrier_semaphore()
        for r in range(self.rounds):
            pl.semaphore_signal(barrier, inc=1, device_id={"seq": self.partner(r)}, device_id_type=MESH)
        if with_head:
            greet_head()
        pl.semaphore_wait(barrier, self.rounds + 3 * with_head)

    def copy(self, r, s):
        return pltpu.make_async_remote_copy(
            src_ref=self.out.at[r], dst_ref=self.back.at[r, s],
            send_sem=self.send.at[r], recv_sem=self.recv.at[r, s],
            device_id={"seq": self.partner(r)}, device_id_type=MESH,
        )

    def begin(self, s, state, log):
        self.total[s] = state
        self.before[s] = jnp.zeros_like(state)
        self.logs[s] = jnp.zeros(self.logs.shape[1:], F32)
        self.logs[s, 0:1] = log

    def push(self, r, s):
        n = self.total.shape[1]
        self.out[r, 0:n] = self.total[s].astype(BF16)
        hi, mid, lo = [v.astype(F32) for v in split(self.logs[s, 0:1], 3)]
        at = lax.broadcasted_iota(jnp.int32, (HALO, hi.shape[1]), 0)
        tail = jnp.where(at == 0, hi, jnp.where(at == 1, mid, jnp.where(at == 2, lo, 0.0)))
        self.out[r, n : n + HALO] = tail.astype(BF16)
        self.copy(r, s).start()

    def take(self, r, s):
        n = self.total.shape[1]
        copy = self.copy(r, s)
        copy.wait_recv()
        copy.wait_send()
        state = self.back[r, s, 0:n].astype(F32)
        tail = self.back[r, s, n : n + HALO].astype(F32)
        log = tail[0:1] + tail[1:2] + tail[2:3]
        upper = lax.div(self.me, 1 << r) % 2 == 1
        near = jnp.logical_not(upper) if self.backward else upper
        mine, theirs = self.logs[s, 0:1], self.logs[s, 1:2]
        self.before[s] = self.before[s] + jnp.where(near, jnp.exp(theirs), 0.0) * state
        self.logs[s, 1:2] = theirs + jnp.where(near, log, 0.0)
        own = jnp.where(near, 1.0, jnp.exp(log))
        other = jnp.where(near, jnp.exp(mine), 1.0)
        self.total[s] = own * self.total[s] + other * state
        self.logs[s, 0:1] = mine + log

    def advance(self, i, seqs):
        for r in reversed(range(self.rounds)):
            s = i - 1 - r

            @pl.when((s >= 0) & (s < seqs))
            def _():
                self.take(r, s)
                if r + 1 < self.rounds:
                    self.push(r + 1, s)

    @staticmethod
    def scratch(rounds, seqs, n, inner):
        return [
            pltpu.VMEM((seqs, n, inner), F32), pltpu.VMEM((seqs, 8, inner), F32),
            pltpu.VMEM((rounds, n + HALO, inner), BF16), pltpu.VMEM((rounds, seqs, n + HALO, inner), BF16),
            pltpu.SemaphoreType.DMA((rounds,)), pltpu.SemaphoreType.DMA((rounds, seqs)),
        ]


class Row:
    def __init__(self, ref):
        self.ref = ref

    def __getitem__(self, _):
        return self.ref[...].reshape(1, self.ref.shape[0])


def forward(
    tok, tok_all, cot, ngain, gate_w, value_w, state_w, step_w, vk, vo, sk, so, sbias, rate, wide, tri, out_w, mgain, skip,
    xext_o, bcext_o, sraw_o, pre_o, entry_o, sums_o,
    xact_h, bcact_h, gate_h, step_h, cum_h, lstart_h, normed_h, ssd_h, gn_h, y_h,
    xact, bcact, gate, step, cum, lstart, nx, ssd, gn, y_s, gm, xe, be, st, run, halo, mine, slots,
    kept_sems, slot_sems, halo_send, halo_recv, sum_send, sum_recv,
    total, logs, out, back, send, recv,
    yown, ygot, yfar, ta, tb, tc, td, te, tf, ylocal,
    *, seqs, rounds, plan,
):
    ngain, vo, so, mgain = Row(ngain), Row(vo), Row(so), Row(mgain)
    i = pl.program_id(0)
    s = i - rounds
    steps = seqs + rounds
    length = tok.shape[1]
    me, devices = lax.axis_index("seq"), lax.axis_size("seq")
    z = lax.axis_index("head")
    scan = Exchange(rounds, False, total, entry_o, logs, out, back, send, recv)
    rider = Rider(*plan, y_h, yown, ygot, yfar, (ta, tb, tc, td, te, tf), ylocal)
    kept = [(xact, xact_h), (bcact, bcact_h), (gate, gate_h), (step, step_h), (cum, cum_h), (lstart, lstart_h)]
    per_seq = length // CHUNK

    def halo_copy(q):
        return pltpu.make_async_remote_copy(
            src_ref=tok_all.at[q, pl.ds(length - HALO, HALO)], dst_ref=halo.at[q],
            send_sem=halo_send.at[q], recv_sem=halo_recv.at[q],
            device_id={"seq": lax.rem(me + 1, devices)}, device_id_type=MESH,
        )

    def keep(k, q):
        src, dst = kept[k]
        return pltpu.make_async_copy(src.at[q], dst.at[q], kept_sems.at[k, q])

    def normed_copy(q):
        return pltpu.make_async_copy(nx.at[pl.ds(HALO, length)], normed_h.at[q], slot_sems.at[0])

    def scan_copies(q):
        return [
            pltpu.make_async_copy(ssd.at[0], ssd_h.at[q], slot_sems.at[1]),
            pltpu.make_async_copy(gn.at[0], gn_h.at[q], slot_sems.at[2]),
        ]

    def y_copy(q, skip_rider):
        first = plan[1] if skip_rider else 0
        at = pl.ds(q * per_seq + first, per_seq - first)
        return pltpu.make_async_copy(y_s.at[pl.ds(first, per_seq - first)], y_h.at[at], slot_sems.at[3])

    def sum_copy(q, d):
        return pltpu.make_async_remote_copy(
            src_ref=mine.at[q], dst_ref=slots.at[q, z], send_sem=sum_send.at[q, d], recv_sem=sum_recv.at[q, d],
            device_id={"head": lax.rem(z + d, 4)}, device_id_type=MESH,
        )

    @pl.when(i == 0)
    def _():
        barrier = pltpu.get_barrier_semaphore()
        for d in range(1, devices):
            pl.semaphore_signal(barrier, inc=1, device_id={"seq": lax.rem(me + d, devices)}, device_id_type=MESH)
        greet_head()
        pl.semaphore_wait(barrier, devices - 1 + 3)

        @pl.when(me < devices - 1)
        def _():
            for q in range(seqs):
                halo_copy(q).start()

        @pl.when(me == 0)
        def _():
            halo[...] = jnp.zeros_like(halo)

    @pl.when(i < seqs)
    def _():
        @pl.when(i > 0)
        def _():
            normed_copy(i).wait()

        def arrive():
            @pl.when(me > 0)
            def _():
                halo_copy(i).wait_recv()

        one = pl.ds(i, 1)
        front_rows(
            tok, halo.at[one], ngain, gate_w, value_w, state_w, step_w, vk, vo, sk, so, sbias, rate, wide, tri,
            gate.at[one], xext_o, bcext_o, sraw_o, xact.at[one], bcact.at[one], step.at[one], cum.at[one],
            lstart.at[one], pre_o.at[one], nx, xe, be, st, run, arrive,
        )
        normed_copy(i).start()
        for k in range(len(kept)):
            keep(k, i).start()
        scan.begin(i, st[...], expand_row(run[0:1], wide[...]))

    scan.advance(i, seqs)

    @pl.when(i < seqs)
    def _():
        scan.push(0, i)

    @pl.when(s >= 0)
    def _():
        @pl.when(s > 0)
        def _():
            for copy in scan_copies(s):
                copy.wait()

        one = pl.ds(s, 1)
        scan_out(
            xact.at[one], bcact.at[one], step.at[one], cum.at[one], gate.at[one], lstart.at[one], entry_o.at[one],
            pre_o.at[one], cot, out_w, mgain, skip, wide, ssd, gn, mine.at[one], gm, lambda b: rider.tick((s - 1) * 2 + b),
        )
        for copy in scan_copies(s):
            copy.start()
        for d in range(1, 4):
            sum_copy(s, d).start()
        slots[s, z] = mine[s]

        @pl.when(s == 1)
        def _():
            y_copy(0, True).wait()

        @pl.when(s > 1)
        def _():
            y_copy(s, False).wait()

        for b in range(length // T):
            value = mm(gm[b * T : (b + 1) * T], out_w[...]).astype(BF16)
            y_s[b * T // CHUNK : (b + 1) * T // CHUNK] = value.reshape(T // CHUNK, CHUNK, value.shape[1])

        @pl.when(s == 0)
        def _():
            yown[...] = y_s[0 : plan[1]]
            y_copy(0, True).start()

        @pl.when(s > 0)
        def _():
            y_copy(s, False).start()

    @pl.when(i == steps - 1)
    def _():
        rider.close()
        for q in range(seqs):
            for d in range(1, 4):
                sum_copy(q, d).wait()
            sums_o[q] = (slots[q, 0] + slots[q, 1]) + (slots[q, 2] + slots[q, 3])
            for k in range(len(kept)):
                keep(k, q).wait()
        normed_copy(0).wait()
        for copy in scan_copies(0):
            copy.wait()
        y_copy(1, False).wait()

        @pl.when(me < devices - 1)
        def _():
            for q in range(seqs):
                halo_copy(q).wait_send()


def front_rows(
    tok, halo, ngain, gate_w, value_w, state_w, step_w, vk, vo, sk, so, sbias, rate, wide, tri,
    gate_o, xext_o, bcext_o, sraw_o, xact_o, bcact_o, step_o, cum_o, lstart_o, pre_o,
    nx, xe, be, st, run, arrive,
):
    length = tok.shape[1]
    blocks = length // T
    n = bcact_o.shape[2] // 2

    def norm(v):
        v = v.astype(F32)
        inv = lax.rsqrt(jnp.mean(v * v, axis=1, keepdims=True) + EPS)
        return (v * inv * ngain[...]).astype(BF16)

    def norm_rows(b, _):
        nx[pl.ds(pl.multiple_of(HALO + b * SUB, HALO), SUB), :] = norm(tok[0, pl.ds(pl.multiple_of(b * SUB, SUB), SUB), :])
        return 0

    lax.fori_loop(0, length // SUB, norm_rows, 0)
    gate_o[0] = mm(nx[HALO:], gate_w[...])
    sraw_o[0] = mm(nx[HALO:], step_w[...])
    arrive()
    nx[0:HALO] = norm(halo[0])
    x = mm(nx[...], value_w[...]).astype(BF16)
    xext_o[0] = x
    xe[...] = x.astype(F32)
    bc = mm(nx[...], state_w[...]).astype(BF16)
    bcext_o[0] = bc
    be[...] = bc.astype(F32)
    st[...] = jnp.zeros_like(st)
    run[...] = jnp.zeros_like(run)
    pre_o[0] = jnp.zeros_like(pre_o[0])
    for b in range(blocks):
        r0 = b * T
        r = slice(r0, r0 + T)
        taps = vk.shape[0]
        base = HALO - taps + 1
        xc = vo[...] + vk[0:1] * xe[r0 + base : r0 + base + T]
        bcc = so[...] + sk[0:1] * be[r0 + base : r0 + base + T]
        for k in range(1, taps):
            xc = xc + vk[k : k + 1] * xe[r0 + base + k : r0 + base + k + T]
            bcc = bcc + sk[k : k + 1] * be[r0 + base + k : r0 + base + k + T]
        xa = (xc * sigmoid(xc)).astype(BF16)
        bca = (bcc * sigmoid(bcc)).astype(BF16)
        xact_o[0, r, :] = xa
        bcact_o[0, r, :] = bca
        step = softplus(sraw_o[0, r, :] + sbias[...])
        cum = exact_tri(tri[...], step * rate[...])
        step_o[0, r, :] = step
        cum_o[0, r, :] = cum
        last = cum[T - 1 : T]
        weight = jnp.exp(last - cum) * step
        weighted = (xa.astype(F32) * expand(weight, wide[...])).astype(BF16)
        contrib = t_mm(bca[:, :n], weighted)
        lstart_o[0, b] = st[...]
        st[...] = expand_row(jnp.exp(last), wide[...]) * st[...] + contrib
        run[0:1] = run[0:1] + last
        pre_o[0, b + 1 : b + 2] = run[0:1]


def scan_out(
    xact, bcact, step_i, cum_i, gate, lstart, entry, pre, cot, out_w, mgain, skip, wide,
    ssd_o, gn_o, sums_o, gm, tick,
):
    length = xact.shape[1]
    blocks = length // T
    n = bcact.shape[2] // 2
    inner = xact.shape[2]
    gn_o[0] = mm_t(cot[0], out_w[...])

    def block(b, _):
        tick(b)
        r = rows_of(b)
        xa = xact[0, r, :]
        bca = bcact[0, r, :]
        bm, cm = bca[:, :n], bca[:, n:]
        cum = cum_i[0, r, :]
        cum_t = cum.T
        cross = cross_tiles(cm, bm)
        start = expand_row(jnp.exp(pre[0, pl.ds(b, 1), :]), wide[...]) * entry[0] + lstart[0, b]
        start = start.astype(BF16)
        grown = jnp.exp(cum)
        cm = cm.astype(F32)
        xs = (xa.astype(F32) * expand(step_i[0, r, :], wide[...])).astype(BF16)
        for p in range(inner // LANES):
            lanes = slice(p * LANES, (p + 1) * LANES)
            two = (2 * p, 2 * p + 1)
            start_two = pair_rows(start[:, lanes])
            xs_two = [pair_rows(xs[tile(j), lanes]) for j in range(T // SUB)]
            for i in range(T // SUB):
                left = [(cm[tile(i)] * grown[tile(i), h : h + 1]).astype(BF16) for h in two]
                right = [start_two]
                for j in range(i + 1):
                    left += [(cross[i, j] * decay_tile(cum, cum_t, h, i, j)).astype(BF16) for h in two]
                    right.append(xs_two[j])
                rows = pl.ds(pl.multiple_of(b * T + i * SUB, SUB), SUB)
                ssd_o[0, rows, lanes] = mm(jnp.concatenate(left, axis=1), jnp.concatenate(right, axis=0))
        mixed = ssd_o[0, r, :] + skip[...] * xa.astype(F32)
        g = gate[0, r, :]
        gated = mixed * (g * sigmoid(g))
        gg = gated * mgain[...]
        gm[r, :] = gg.astype(BF16)
        squares = jnp.sum(gated * gated, axis=1, keepdims=True)
        dots = jnp.sum(gg * gn_o[0, r, :], axis=1, keepdims=True)
        lane = lax.broadcasted_iota(jnp.int32, (T, LANES), 1)
        both = jnp.where(lane == 0, squares, jnp.where(lane == 1, dots, 0.0))
        sums_o[0, :, r] = both.T[0:8]
        return 0

    lax.fori_loop(0, blocks, block, 0)


def back_one(
    xact, bcact, cum_i, gate, ssd, gn, sums, pre, mgain, skip, wide,
    xact_b, bcact_b, step_b, cum_b, lstart_b, entry_b, pre_b, y_in,
    gnormed_o, gate_grad_o, lend_o, rms_o, xg_o, cumg_o, stepg_o, bcg_o, mgg_o, skg_o, after_o, y_all,
    z, acc, use, dys, cumg, total, logs, out, back, send, recv,
    yown, ygot, yfar, ta, tb, tc, td, te, tf, ylocal,
    *, inner_all, seqs, rounds, plan,
):
    mgain = Row(mgain)
    i = pl.program_id(0)
    s = i - rounds
    blocks = xact.shape[1] // T
    scan = Exchange(rounds, True, total, after_o, logs, out, back, send, recv)
    rider = Rider(*plan, y_all, yown, ygot, yfar, (ta, tb, tc, td, te, tf), ylocal)
    per_step = plan[1] // (seqs + rounds)

    @pl.when(i == 0)
    def _():
        scan.greet(with_head=True)
        rider.load()
        mgg_o[...] = jnp.zeros_like(mgg_o)
        skg_o[...] = jnp.zeros_like(skg_o)

    ticks = min(per_step, 3)
    rider.tick(i * per_step)

    @pl.when(i < seqs)
    def _():
        one = pl.ds(i, 1)
        gate_back(
            xact, bcact, cum_i, gate, ssd, gn, sums, mgain, skip, wide, gnormed_o, gate_grad_o, lend_o, rms_o, mgg_o, skg_o,
            dys.at[one], cumg.at[one], acc, use, inner_all,
        )
        scan.begin(i, acc[...], expand_row(pre[0, blocks : blocks + 1], wide[...]))

    scan.advance(i, seqs)

    @pl.when(i < seqs)
    def _():
        scan.push(0, i)

    @pl.when(s >= 0)
    def _():
        one = pl.ds(s, 1)
        scan_back(
            xact_b, bcact_b, step_b, cum_b, lstart_b, entry_b, pre_b, skip, wide, dys.at[one], cumg.at[one],
            xg_o, cumg_o, stepg_o, bcg_o, z, lambda b: rider.tick(jnp.where(1 + b < ticks, i * per_step + 1 + b, plan[1])),
        )

    @pl.when(s < 0)
    def _():
        for k in range(1, per_step):
            rider.tick(i * per_step + k)

    @pl.when(i == seqs + rounds - 1)
    def _():
        rider.close()


def gate_back(
    xact, bcact, cum_i, gate, ssd, gn, sums, mgain, skip, wide, gnormed_o, gate_grad_o, lend_o, rms_o, mgg_o, skg_o,
    dys, cumg, acc, use, inner_all,
):
    length = xact.shape[1]
    blocks = length // T
    n = bcact.shape[2] // 2
    inner = xact.shape[2]
    acc[...] = jnp.zeros_like(acc)

    def block(k, _):
        b = blocks - 1 - k
        r = rows_of(b)
        sums_b = sums[0, :, r]
        columns = jnp.concatenate([sums_b, jnp.zeros((LANES - 8, T), F32)], axis=0).T
        for i in range(T // SUB):
            ri = pl.ds(pl.multiple_of(b * T + i * SUB, SUB), SUB)
            xa = xact[0, ri, :].astype(F32)
            rms = lax.rsqrt(columns[tile(i), 0:1] / inner_all + EPS)
            rms_o[0, ri, :] = jnp.broadcast_to(rms, (SUB, LANES))
            coef = rms * rms * rms * (columns[tile(i), 1:2] / inner_all)
            ssd_r = ssd[0, ri, :]
            mixed = ssd_r + skip[...] * xa
            g = gate[0, ri, :]
            sg = sigmoid(g)
            gated = mixed * (g * sg)
            grad_norm = gn[0, ri, :]
            normalised = gated * rms
            gnormed_o[0, ri, :] = (normalised * mgain[...]).astype(BF16)
            mgg_o[0:1] += jnp.sum(grad_norm * normalised, axis=0, keepdims=True)
            grad_gated = rms * (grad_norm * mgain[...]) - gated * coef
            gate_grad_o[0, ri, :] = (grad_gated * mixed * (sg * (1.0 + g * (1.0 - sg)))).astype(BF16)
            grad_mixed = grad_gated * (g * sg)
            skg_o[0:1] += jnp.sum(grad_mixed * xa, axis=0, keepdims=True)
            dy = grad_mixed.astype(BF16)
            dys[0, ri, :] = dy
            cumg[0, ri, :] = head_sum(dy.astype(F32) * ssd_r, wide[...])
        cm = bcact[0, r, n:].astype(F32)
        grown = jnp.exp(cum_i[0, r, :])
        for p in range(inner // LANES):
            lanes = slice(p * LANES, (p + 1) * LANES)
            scaled = [(cm * grown[:, h : h + 1]).astype(BF16) for h in (2 * p, 2 * p + 1)]
            used = None
            for i in range(T // SUB):
                ri = pl.ds(pl.multiple_of(b * T + i * SUB, SUB), SUB)
                term = t_mm(jnp.concatenate([v[tile(i)] for v in scaled], axis=0), pair_rows(dys[0, ri, lanes]))
                used = term if used is None else used + term
            use[:, lanes] = used
        lend_o[0, b] = acc[...]
        acc[...] = expand_row(grown[T - 1 : T], wide[...]) * acc[...] + use[...]
        return 0

    lax.fori_loop(0, blocks, block, 0)


def scan_back(
    xact, bcact, step_i, cum_i, lstart, entry, pre, skip, wide, dys, cumg, xg_o, cumg_o, stepg_o, bcg_o, z, tick,
):
    length = xact.shape[1]
    blocks = length // T
    n = bcact.shape[2] // 2
    inner = xact.shape[2]

    def block(b, _):
        tick(b)
        r = rows_of(b)
        dy = dys[0, r, :]
        xa = xact[0, r, :].astype(F32)
        bca = bcact[0, r, :]
        bm, cm = bca[:, :n], bca[:, n:]
        cum = cum_i[0, r, :]
        cum_t = cum.T
        start = expand_row(jnp.exp(pre[0, pl.ds(b, 1), :]), wide[...]) * entry[0] + lstart[0, b]
        start = start.astype(BF16)
        dy32 = dy.astype(F32)
        gdy_hi, gdy_lo = split(expand(jnp.exp(cum), wide[...]) * dy32, 2)
        c_grad = mm_t(gdy_hi, start) + mm_t(gdy_lo, start)
        step_wide = expand(step_i[0, r, :], wide[...])
        xs = (xa * step_wide).astype(BF16)
        cross = cross_tiles(cm, bm)
        cross_part = {ij: jnp.zeros((SUB, SUB), F32) for ij in tiles()}
        for p in range(inner // LANES):
            lanes = slice(p * LANES, (p + 1) * LANES)
            zs = [None] * (T // SUB)
            for i in range(T // SUB):
                dy_two = pair_rows(dy[tile(i), lanes])
                for j in range(i + 1):
                    mix_grad = mm_t(dy_two, xs[tile(j), lanes])
                    mix = []
                    for k, h in enumerate((2 * p, 2 * p + 1)):
                        decay = decay_tile(cum, cum_t, h, i, j)
                        mix.append((cross[i, j] * decay).astype(BF16))
                        cross_part[i, j] = cross_part[i, j] + mix_grad[tile(k)] * decay
                    term = t_mm(jnp.concatenate(mix, axis=0), dy_two)
                    zs[j] = term if zs[j] is None else zs[j] + term
            for j in range(T // SUB):
                z[tile(j), lanes] = zs[j]
        rows = []
        for i in range(T // SUB):
            row = [jnp.where(lower(), cross_part[i, j], 0.0) if i == j else cross_part[i, j] for j in range(i + 1)]
            row += [jnp.zeros((SUB, SUB), F32)] * (T // SUB - 1 - i)
            rows.append(jnp.concatenate(row, axis=1))
        cross_low = jnp.concatenate(rows, axis=0).astype(BF16)
        bcg_o[0, r, 0:n] = t_mm(cross_low, cm)
        bcg_o[0, r, n : 2 * n] = c_grad + mm(cross_low, bm)
        zz = z[...]
        xg_o[0, r, :] = skip[...] * dy32 + step_wide * zz
        cumg_o[0, r, :] = cumg[0, r, :] - head_sum(xs.astype(F32) * zz, wide[...])
        stepg_o[0, r, :] = head_sum(xa * zz, wide[...])
        return 0

    lax.fori_loop(0, blocks, block, 0)


def back_two(
    xact, bcact, xext, bcext, step_i, cum_i, sraw, xg, cumg, stepg, bcg, lstart, entry, lend, after, pre,
    gnormed, cot, normed, gate_grad, vk, vo, sk, so, sbias, rate, wide, tri, y_in,
    xpg_o, xhalo_o, bpg_o, bhalo_o, raw_o, vkg_o, skg_o, heads_o, wout_o, wgate_o, y_all,
    xe, be, xcg, bcg_s, out_acc, gate_acc, yown, ygot, yfar, ta, tb, tc, td, te, tf, ylocal,
    *, seqs, plan,
):
    length = xact.shape[1]
    blocks = length // T
    n = bcact.shape[2] // 2
    taps = vk.shape[0]
    base = HALO - taps + 1
    vo, so = Row(vo), Row(so)
    step_at = pl.program_id(0)
    rider = Rider(*plan, y_all, yown, ygot, yfar, (ta, tb, tc, td, te, tf), ylocal)

    @pl.when(step_at == 0)
    def _():
        greet_head()
        pl.semaphore_wait(pltpu.get_barrier_semaphore(), 3)
        rider.load()
        out_acc[...] = jnp.zeros_like(out_acc)
        gate_acc[...] = jnp.zeros_like(gate_acc)
        vkg_o[...] = jnp.zeros_like(vkg_o)
        skg_o[...] = jnp.zeros_like(skg_o)
        heads_o[...] = jnp.zeros_like(heads_o)

    xe[...] = xext[0].astype(F32)
    be[...] = bcext[0].astype(F32)
    for ref in (xcg, bcg_s):
        ref[0:HALO] = jnp.zeros((HALO, ref.shape[1]), F32)
        ref[HALO + length :] = jnp.zeros((HALO, ref.shape[1]), F32)

    def conv_rows(ext, kernel, offset, r0):
        total = offset[...] + kernel[0:1] * ext[r0 + base : r0 + base + T]
        for k in range(1, taps):
            total = total + kernel[k : k + 1] * ext[r0 + base + k : r0 + base + k + T]
        sg = sigmoid(total)
        return sg * (1.0 + total * (1.0 - sg))

    def filter_grad(grad, ext, out, r0):
        for k in range(taps):
            out[k : k + 1] += jnp.sum(grad * ext[r0 + base + k : r0 + base + k + T], axis=0, keepdims=True)
        out[taps : taps + 1] += jnp.sum(grad, axis=0, keepdims=True)

    per_step = plan[1] // seqs
    for b in range(blocks):
        rider.tick(step_at * per_step + b)
        r0 = b * T
        r = slice(r0, r0 + T)
        xa = xact[0, r, :].astype(F32)
        bm = bcact[0, r, 0:n]
        cum = cum_i[0, r, :]
        step = step_i[0, r, :]
        last = cum[T - 1 : T]
        start = expand_row(jnp.exp(pre[0, b : b + 1]), wide[...]) * entry[0] + lstart[0, b]
        suffix = jnp.exp(pre[0, blocks : blocks + 1] - pre[0, b + 1 : b + 2])
        end = expand_row(suffix, wide[...]) * after[0] + lend[0, b]
        end_low = end.astype(BF16)
        weighted_grad = mm(bm, end_low)
        reach = jnp.exp(last - cum)
        weight = reach * step
        weight_wide = expand(weight, wide[...])
        weighted = (xa * weight_wide).astype(BF16)
        bcg_b = bcg[0, r, :]
        b_total = bcg_b[:, 0:n] + mm_t(weighted, end_low)
        bc_total = jnp.concatenate([b_total, bcg_b[:, n:]], axis=1)
        w_grad = head_sum(weighted_grad * xa, wide[...])
        part = w_grad * weight
        product = jnp.broadcast_to(jnp.sum(end * start, axis=0, keepdims=True), (16, end.shape[1]))
        fade_grad = jnp.exp(last) * head_sum(product, wide[...])[0:1]
        at_last = lax.broadcasted_iota(jnp.int32, (T, LANES), 0) == T - 1
        extra = fade_grad + jnp.sum(part, axis=0, keepdims=True)
        cum_grad = cumg[0, r, :] - part + jnp.where(at_last, extra, 0.0)
        a, bb, c = split(cum_grad, 3)
        rise = t_mm(tri[...], a) + (t_mm(tri[...], bb) + t_mm(tri[...], c))
        step_grad = stepg[0, r, :] + w_grad * reach + rise * rate[...]
        raw = step_grad * sigmoid(sraw[0, r, :] + sbias[...])
        raw_o[0, r, :] = raw.astype(BF16)
        heads_o[0:1] += jnp.sum(raw, axis=0, keepdims=True)
        heads_o[1:2] += jnp.sum(rise * step, axis=0, keepdims=True)
        grad = (xg[0, r, :] + weighted_grad * weight_wide) * conv_rows(xe, vk, vo, r0)
        filter_grad(grad, xe, vkg_o, r0)
        xcg[HALO + r0 : HALO + r0 + T] = grad
        grad = bc_total * conv_rows(be, sk, so, r0)
        filter_grad(grad, be, skg_o, r0)
        bcg_s[HALO + r0 : HALO + r0 + T] = grad

    def conv_back(ref, kernel, r0, rows):
        total = kernel[0:1] * ref[r0 + taps - 1 : r0 + taps - 1 + rows]
        for k in range(1, taps):
            total = total + kernel[k : k + 1] * ref[r0 + taps - 1 - k : r0 + taps - 1 - k + rows]
        return total.astype(BF16)

    for acc, left, right in ((out_acc, gnormed, cot), (gate_acc, normed, gate_grad)):
        for m in range(acc.shape[0] // 256):
            at = slice(m * 256, (m + 1) * 256)
            acc[at] += t_mm(left[0, :, at], right[0])

    xhalo_o[0] = conv_back(xcg, vk, 0, HALO)
    bhalo_o[0] = conv_back(bcg_s, sk, 0, HALO)
    for b in range(blocks):
        if blocks + b < per_step:
            rider.tick(step_at * per_step + blocks + b)
        r0 = b * T
        xpg_o[0, r0 : r0 + T] = conv_back(xcg, vk, HALO + r0, T)
        bpg_o[0, r0 : r0 + T] = conv_back(bcg_s, sk, HALO + r0, T)

    @pl.when(step_at == seqs - 1)
    def _():
        wout_o[...] = out_acc[...].astype(BF16)
        wgate_o[...] = gate_acc[...].astype(BF16)
        rider.close()


class GradSum:
    def __init__(self, rounds, mine, back, out, sems, zback=None, shared=0):
        self.rounds, self.mine, self.back, self.out, self.sems = rounds, mine, back, out, sems
        self.zback, self.shared = zback, shared
        self.me, self.z = lax.axis_index("seq"), lax.axis_index("head")
        self.rows = mine.shape[0]
        self.share = self.rows >> rounds

    @staticmethod
    def sem_count(rounds):
        return 4 * rounds + 9

    def bit(self, r):
        return lax.div(self.me, 1 << r) % 2

    def partner(self, r):
        return self.me + (1 << r) - (2 << r) * self.bit(r)

    def first(self, r):
        row = 0
        for k in range(r):
            row = row + self.bit(k) * (self.rows >> (k + 1))
        return row

    def at(self, row, size):
        return pl.ds(pl.multiple_of(row, 16), size)

    def halving(self, r):
        half = self.rows >> (r + 1)
        theirs = self.first(r) + half - half * self.bit(r)
        return pltpu.make_async_remote_copy(
            src_ref=self.mine.at[self.at(theirs, half)], dst_ref=self.back.at[pl.ds(self.rows - 2 * half, half)],
            send_sem=self.sems.at[r], recv_sem=self.sems.at[self.rounds + r],
            device_id={"seq": self.partner(r)}, device_id_type=MESH,
        )

    def add_half(self, r):
        copy = self.halving(r)
        copy.wait()
        half = self.rows >> (r + 1)
        row = self.first(r + 1)

        def one(k, _):
            at = self.at(row + k * self.share, self.share)
            come = self.back[pl.ds(pl.multiple_of(self.rows - 2 * half + k * self.share, 16), self.share), :]
            self.mine[at, :] = (self.mine[at, :].astype(F32) + come.astype(F32)).astype(BF16)
            return 0

        lax.fori_loop(0, half // self.share, one, 0)

    def gathering(self, r, arriving):
        size = self.rows >> (r + 1)
        row = self.first(r + 1)
        if arriving:
            row = row + size - 2 * size * self.bit(r)
        at = self.at(row, size)
        return pltpu.make_async_remote_copy(
            src_ref=self.out.at[at], dst_ref=self.out.at[at],
            send_sem=self.sems.at[2 * self.rounds + r], recv_sem=self.sems.at[3 * self.rounds + r],
            device_id={"seq": self.partner(r)}, device_id_type=MESH,
        )

    def to_head(self, d):
        base = 4 * self.rounds + 1
        src = self.mine.at[self.at(self.first(self.rounds), self.share), pl.ds(0, self.shared)]
        return pltpu.make_async_remote_copy(
            src_ref=src, dst_ref=self.zback.at[self.z], send_sem=self.sems.at[base + d], recv_sem=self.sems.at[base + 4 + d],
            device_id={"head": lax.rem(self.z + d, 4)}, device_id_type=MESH,
        )

    def publish(self):
        at = self.at(self.first(self.rounds), self.share)
        copy = pltpu.make_async_copy(self.mine.at[at], self.out.at[at], self.sems.at[4 * self.rounds])
        copy.start()
        copy.wait()
        self.gathering(self.rounds - 1, False).start()

    def stages(self):
        spans = [2, 5, 3] + [2] * self.rounds
        acts = [(spans[0], lambda: self.halving(0).start())]
        for r in range(self.rounds):
            def act(r=r):
                self.add_half(r)
                if r + 1 < self.rounds:
                    self.halving(r + 1).start()
                elif not self.shared:
                    self.publish()
                else:
                    for d in range(1, 4):
                        self.to_head(d).start()
                    self.zback[self.z] = self.mine[self.at(self.first(self.rounds), self.share), 0 : self.shared]

            acts.append((spans[r + 1] if r + 1 < self.rounds else spans[r], act))
        if self.shared:
            def meet():
                for d in range(1, 4):
                    self.to_head(d).wait()
                at = self.at(self.first(self.rounds), self.share)
                low = [self.zback[k].astype(F32) for k in range(4)]
                self.mine[at, 0 : self.shared] = ((low[0] + low[1]) + (low[2] + low[3])).astype(BF16)
                self.publish()

            acts.append((spans[self.rounds - 1], meet))
        for r in reversed(range(self.rounds)):
            def act(r=r):
                self.gathering(r, False).wait_send()
                self.gathering(r, True).wait_recv()
                if r > 0:
                    self.gathering(r - 1, False).start()

            acts.append((spans[max(r - 1, 0)], act))
        return acts


def finish(
    y, gate_grad, xpg, bpg, raw, tok, cot, rms, gate_w, value_w, state_w, step_w, ngain, filter_rows, gain_rows, skip_rows, head_rows, state_rows, xhalo, bhalo,
    normed, tok_k, out_grad, gate_grad_w, y_all,
    result_o, tokens_grad_o, small_o, wout_o, wgate_o, wvalue_o, wmixed_o,
    own, got, far, sa, sb, sc, sd, se, sf, yown, ygot, yfar, ta, tb, tc, td, te, tf, ylocal, rows, out, back, send, recv,
    w_mine, w_back, m_mine, m_back, m_zback, w_acc, m_acc, w_sems, w_local, vec, vback, vsems, xtail, btail, halo_sems, xnow, bnow,
    *, n, rounds, plan, per_seq,
):
    i = pl.program_id(0)
    ngain = Row(ngain)
    z, me = lax.axis_index("head"), lax.axis_index("seq")
    last = n + 3 * LAG - 1
    outs = (wout_o, wgate_o, wvalue_o)
    grads = [GradSum(rounds, w_mine.at[k], w_back.at[k], outs[k], w_sems.at[k]) for k in range(3)]
    grads.append(GradSum(rounds, m_mine, m_back, wmixed_o, w_sems.at[3], m_zback, bpg.shape[1]))
    products = n * CHUNK // T

    devices = lax.axis_size("seq")

    def halo_copies():
        return [
            pltpu.make_async_remote_copy(
                src_ref=src, dst_ref=dst, send_sem=halo_sems.at[k], recv_sem=halo_sems.at[2 + k],
                device_id={"seq": lax.rem(me + devices - 1, devices)}, device_id_type=MESH,
            )
            for k, (src, dst) in enumerate(((xhalo, xtail), (bhalo, btail)))
        ]

    def vec_copy(d):
        return pltpu.make_async_remote_copy(
            src_ref=vec, dst_ref=vback.at[z], send_sem=vsems.at[d], recv_sem=vsems.at[4 + d],
            device_id={"head": lax.rem(z + d, 4)}, device_id_type=MESH,
        )

    def local_copies():
        rows_out, half = out_grad.shape[0], out_grad.shape[1] // 2
        return [
            pltpu.make_async_copy(gate_grad_w, w_mine.at[1], w_local.at[0]),
            pltpu.make_async_copy(out_grad.at[:, pl.ds(0, half)], w_mine.at[0, pl.ds(0, rows_out)], w_local.at[1]),
            pltpu.make_async_copy(out_grad.at[:, pl.ds(half, half)], w_mine.at[0, pl.ds(rows_out, rows_out)], w_local.at[2]),
        ]

    chain = Chain(own, got, far, (sa, sb, sc, sd, se, sf))
    rider = Rider(*plan, y_all, yown, ygot, yfar, (ta, tb, tc, td, te, tf), ylocal)
    me = lax.axis_index("seq")

    def partner(r):
        bit = 1 << r
        return me + bit - 2 * bit * (lax.div(me, bit) % 2)

    @pl.when(i == 0)
    def _():
        barrier = pltpu.get_barrier_semaphore()
        for d in range(1, devices):
            pl.semaphore_signal(barrier, inc=1, device_id={"seq": lax.rem(me + d, devices)}, device_id_type=MESH)
        greet_head()
        pl.semaphore_wait(barrier, devices - 1 + 3)

        @pl.when(me > 0)
        def _():
            for copy in halo_copies():
                copy.start()

        @pl.when(me == devices - 1)
        def _():
            xtail[...] = jnp.zeros_like(xtail)
            btail[...] = jnp.zeros_like(btail)

        rider.load()
        for copy in local_copies():
            copy.start()
        w_acc[...] = jnp.zeros_like(w_acc)
        m_acc[...] = jnp.zeros_like(m_acc)
        rows[...] = jnp.zeros_like(rows)
        rows[0:5] = filter_rows[0:5]
        rows[5:6] = gain_rows[0:1]
        rows[6:7] = skip_rows[0:1]
        rows[7:8, 0:LANES] = head_rows[0:1]
        rows[7:8, LANES : 2 * LANES] = head_rows[1:2]
        rows[16:24, 0 : state_rows.shape[1]] = state_rows[...]

    rider.tick(i)
    for stage in (2, 1):
        k = i - stage * LAG

        @pl.when((k >= 0) & (k < n))
        def _():
            chain.onward(stage, k)

    def with_tails():
        return [
            jnp.concatenate([v[0 : T - HALO], (v[T - HALO : T].astype(F32) + tail[...]).astype(BF16)], axis=0)
            for v, tail in ((xpg, xnow), (bpg, bnow))
        ]

    @pl.when((i == per_seq - 1) & (me < devices - 1))
    def _():
        for copy in halo_copies():
            copy.wait_recv()

    ends = lax.rem(i, per_seq) == per_seq - 1

    @pl.when((i < products) & ends)
    def _():
        xnow[...] = xtail[lax.div(i, per_seq)].astype(F32)
        bnow[...] = btail[lax.div(i, per_seq)].astype(F32)

    @pl.when((i < products) & jnp.logical_not(ends))
    def _():
        xnow[...] = jnp.zeros_like(xnow)
        bnow[...] = jnp.zeros_like(bnow)

    @pl.when(i < products)
    def _():
        x_rows, b_rows = with_tails()
        value = mm_t(gate_grad[...], gate_w[...]) + mm_t(x_rows, value_w[...])
        value = value + (mm_t(b_rows, state_w[...]) + mm_t(raw[...], step_w[...]))
        chunks = T // CHUNK
        own[pl.ds(i * chunks, chunks)] = value.astype(BF16).reshape(chunks, CHUNK, value.shape[1])
        t = tok_k[...].astype(F32)
        inv = lax.rsqrt(jnp.mean(t * t, axis=1, keepdims=True) + EPS)
        gain = jnp.sum(value * (t * inv), axis=0, keepdims=True)
        half = t.shape[1] // 2
        rows[8:9] += gain[:, :half]
        rows[9:10] += gain[:, half:]

    @pl.when(i < n)
    def _():
        chain.inward(i)

    @pl.when(i < products)
    def _():
        x_rows, b_rows = with_tails()
        mixed = jnp.concatenate([b_rows, raw[...]], axis=1)
        for m in range(w_acc.shape[0] // 256):
            rows_m = slice(m * 256, (m + 1) * 256)
            left = normed[:, rows_m]
            w_acc[rows_m] += t_mm(left, x_rows)
            m_acc[rows_m] += t_mm(left, mixed)

    @pl.when(i == products)
    def _():
        w_mine[2] = w_acc[...].astype(BF16)
        m_mine[...] = m_acc[...].astype(BF16)

    @pl.when(i == 1)
    def _():
        for copy in local_copies():
            copy.wait()

    for grad_sum, begin in zip(grads, (1, 4, products + 1, products + 5)):
        at = begin
        for span, act in grad_sum.stages():
            pl.when(i == min(at, last))(act)
            at += span

    @pl.when(i == products)
    def _():
        vec[...] = rows[8:24]
        for d in range(1, 4):
            vec_copy(d).start()
        vback[z] = vec[...]

    def row_copy(r):
        return pltpu.make_async_remote_copy(
            src_ref=out.at[r], dst_ref=back.at[r], send_sem=send.at[r], recv_sem=recv.at[r],
            device_id={"seq": partner(r)}, device_id_type=MESH,
        )

    @pl.when(i == products + 4)
    def _():
        for d in range(1, 4):
            vec_copy(d).wait()
        rows[8:24] = (vback[0] + vback[1]) + (vback[2] + vback[3])
        out[0] = rows[...]
        row_copy(0).start()

    for r in range(rounds):

        @pl.when(i == products + 4 + 3 * (r + 1))
        def _():
            row_copy(r).wait()
            rows[...] = rows[...] + back[r]
            if r + 1 < rounds:
                out[r + 1] = rows[...]
                row_copy(r + 1).start()

    k = i - 3 * LAG

    @pl.when(k >= 0)
    def _():
        grad = chain.total(k)
        rms_k = rms[:, 0:1]
        t = tok[...].astype(F32)
        width = t.shape[1]
        inv = lax.rsqrt(jnp.mean(t * t, axis=1, keepdims=True) + EPS)
        if rider.done > 0:

            @pl.when(k < rider.done)
            def _():
                result_o[...] = (t + y[...].astype(F32) * rms_k).astype(BF16)

        if rider.done < n:

            @pl.when(k >= rider.done)
            def _():
                result_o[...] = (t + rider.chain.total(k - rider.base) * rms_k).astype(BF16)

        scaled = grad * ngain[...]
        dot = jnp.sum(scaled * t, axis=1, keepdims=True) / width
        tokens_grad_o[...] = (cot[...].astype(F32) + inv * scaled - t * (inv * inv * inv * dot)).astype(BF16)

    @pl.when(i == last)
    def _():
        chain.drain(n)
        rider.drain()

        @pl.when(me > 0)
        def _():
            for copy in halo_copies():
                copy.wait_send()

        small_o[...] = rows[...]


def unpack(
    tgrad, res, wout_l, wout_r, wgate, wvalue, wmixed, mixed_all, small, rate, wide,
    res_o, tgrad_o, ngain_o, wgate_o, wvalue_o, state_o, step_o, vk_o, vo_o, sk_o, so_o, sbias_o, rate_o, skip_o, mgain_o, wout_o,
    *, taps, heads,
):
    res_o[...] = res[...]
    tgrad_o[...] = tgrad[...].astype(F32)
    wgate_o[...] = wgate[...].astype(F32)
    wvalue_o[...] = wvalue[...].astype(F32)
    half = wout_l.shape[1]
    wout_o[:, :half] = wout_l[...].astype(F32)
    wout_o[:, half:] = wout_r[...].astype(F32)
    n2 = state_o.shape[1]
    state_o[...] = wmixed[:, :n2].astype(F32)

    @pl.when(pl.program_id(0) == 0)
    def _():
        for k in range(mixed_all.shape[0] // LANES):
            at = slice(k * LANES, (k + 1) * LANES)
            step_o[:, at] = mixed_all[at, n2 : n2 + LANES].astype(F32).T[0:heads]
        vk_o[...] = small[0:taps]
        vo_o[...] = small[taps]
        mgain_o[...] = small[taps + 1]
        skip_o[...] = head_sum(jnp.broadcast_to(small[taps + 2 : taps + 3], (16, half)), wide[...])[0, 0:heads]
        sbias_o[...] = small[taps + 3, 0:heads]
        rate_o[...] = small[taps + 3, LANES : LANES + heads] * rate[0, 0:heads]
        ngain_o[pl.ds(0, half)] = small[8]
        ngain_o[pl.ds(half, half)] = small[9]
        sk_o[...] = small[16 : 16 + taps, 0:n2]
        so_o[...] = small[16 + taps, 0:n2]


def call(body, steps, seqs, ins, outs, scratch, flops, collective_id=None, carried=None):
    def cut(shape, lag):
        rest = tuple(shape[1:])
        return pl.BlockSpec((1,) + rest, lambda s: (jnp.clip(s - lag, 0, seqs - 1),) + (0,) * len(rest))

    def whole(shape):
        return pl.BlockSpec(tuple(shape), lambda s: (0,) * len(shape), pipeline_mode=pl.Buffered(1))

    pairs = [v if isinstance(v, tuple) else (v, 0) for v in ins]
    ins = [v for v, _ in pairs]
    in_specs = [cut(v.shape, lag) if v.ndim >= 3 else whole(v.shape) for v, lag in pairs]
    out_specs = [whole(s) if lag is None else cut(s, lag) for s, _, lag in outs]
    out_shape = [jax.ShapeDtypeStruct(s, d) for s, d, _ in outs]
    aliases = {}
    if carried is not None:
        aliases = {len(ins): len(outs)}
        in_specs.append(pl.BlockSpec(memory_space=pl.ANY))
        out_specs.append(pl.BlockSpec(memory_space=pl.ANY))
        out_shape.append(jax.ShapeDtypeStruct(carried.shape, carried.dtype))
        ins = ins + [carried]
    moved = sum(a.size * a.dtype.itemsize for a in ins)
    for s, d, _ in outs:
        size = jnp.dtype(d).itemsize
        for k in s:
            size *= k
        moved += size
    return pl.pallas_call(
        body,
        grid=(steps,),
        in_specs=in_specs,
        out_specs=out_specs,
        out_shape=out_shape,
        scratch_shapes=scratch,
        input_output_aliases=aliases,
        compiler_params=pltpu.CompilerParams(
            dimension_semantics=("arbitrary",), vmem_limit_bytes=60 * 1024 * 1024,
            collective_id=collective_id, has_side_effects=collective_id is not None,
        ),
        cost_estimate=pl.CostEstimate(flops=flops, bytes_accessed=moved, transcendentals=0),
    )(*ins)


def shards(
    tokens, norm_gain, gate_weight, value_weight, state_weight, step_weight, value_kernel, value_offset,
    state_kernel, state_offset, step_bias, log_rate, skip_gain, mixer_gain, out_weight, cotangent,
):
    seqs, length, width = tokens.shape
    flat = seqs * length
    inner = gate_weight.shape[1]
    heads = step_weight.shape[1]
    head_size = inner // heads
    n2 = state_weight.shape[1]
    n = n2 // 2
    taps = value_kernel.shape[0]
    blocks = length // T
    devices = lax.axis_size("seq")
    rounds = devices.bit_length() - 1
    assert devices == 1 << rounds and taps == 4
    inner_all = inner * lax.axis_size("head")

    pad = LANES - heads
    rate_row = -jnp.exp(log_rate)
    rate = jnp.pad(rate_row, (0, pad))[None]
    bias = jnp.pad(step_bias, (0, pad))[None]
    step_w = jnp.pad(step_weight, ((0, 0), (0, pad)))
    skip = jnp.repeat(skip_gain, head_size)[None]
    gain = mixer_gain
    one = np.arange(inner)[None, :] // head_size == np.arange(LANES)[:, None]
    wide = jnp.asarray(np.concatenate([one, one], axis=0).astype(BF16))
    tri = jnp.asarray(np.tril(np.ones((T, T))).astype(BF16))
    vo, so = value_offset, state_offset

    def big(cols, dtype, rows=length, lag=0):
        return ((seqs, rows, cols), dtype, lag)

    vmem = pltpu.VMEM
    ext = length + HALO
    n_chunks = flat // CHUNK
    steps = seqs + rounds
    plan = (0, min(2 * (seqs - 1), length // CHUNK), n_chunks)
    dma = pltpu.SemaphoreType.DMA

    def block(shape, lag):
        return pl.BlockSpec((1,) + shape, lambda i: (jnp.clip(i - lag, 0, seqs - 1), 0, 0))

    def once(v):
        return pl.BlockSpec(v.shape, lambda i: (0,) * len(v.shape), pipeline_mode=pl.Buffered(1))

    def shape_of(cols, dtype, rows=length):
        return jax.ShapeDtypeStruct((seqs, rows, cols), dtype)

    fixed = (norm_gain, gate_weight, value_weight, state_weight, step_w, value_kernel, vo, state_kernel, so, bias, rate,
             wide, tri, out_weight, gain, skip)
    held = (shape_of(LANES, F32, 8), shape_of(inner, F32, n), shape_of(length, F32, 8))
    anywhere = pl.BlockSpec(memory_space=pl.ANY)
    (xext, bcext, sraw, pre, entry, sums, xact, bcact, gate, step, cum, lstart, normed, ssd, gn, y) = pl.pallas_call(
        functools.partial(forward, seqs=seqs, rounds=rounds, plan=plan),
        grid=(steps,),
        in_specs=[block((length, width), 0), anywhere, block((length, width), rounds)] + [once(v) for v in fixed],
        out_specs=[block((ext, inner), 0), block((ext, n2), 0), block((length, LANES), 0)] + [once(v) for v in held] + [anywhere] * 10,
        out_shape=[shape_of(inner, BF16, ext), shape_of(n2, BF16, ext), shape_of(LANES, F32), *held,
                   shape_of(inner, BF16), shape_of(n2, BF16), shape_of(inner, F32), shape_of(LANES, F32), shape_of(LANES, F32),
                   jax.ShapeDtypeStruct((seqs, blocks, n, inner), F32), shape_of(width, BF16), shape_of(inner, F32),
                   shape_of(inner, F32), jax.ShapeDtypeStruct((n_chunks, CHUNK, width), BF16)],
        scratch_shapes=[
            vmem((seqs, length, inner), BF16), vmem((seqs, length, n2), BF16), vmem((seqs, length, inner), F32),
            vmem((seqs, length, LANES), F32), vmem((seqs, length, LANES), F32), vmem((seqs, blocks, n, inner), F32),
            vmem((ext, width), BF16), vmem((1, length, inner), F32), vmem((1, length, inner), F32),
            vmem((length // CHUNK, CHUNK, width), BF16), vmem((length, inner), BF16),
            vmem((ext, inner), F32), vmem((ext, n2), F32), vmem((n, inner), F32), vmem((8, LANES), F32),
            vmem((seqs, HALO, width), BF16), vmem((seqs, 8, length), F32), vmem((seqs, 4, 8, length), F32),
            dma((6, seqs)), dma((4,)), dma((seqs,)), dma((seqs,)), dma((seqs, 4)), dma((seqs, 4)),
        ] + Exchange.scratch(rounds, seqs, n, inner) + Rider.scratch(*plan, width),
        compiler_params=pltpu.CompilerParams(
            dimension_semantics=("arbitrary",), vmem_limit_bytes=62 * 1024 * 1024, collective_id=1, has_side_effects=True
        ),
        cost_estimate=pl.CostEstimate(flops=2 * flat * width * 4 * inner, bytes_accessed=10**8, transcendentals=0),
    )(tokens, tokens, cotangent, *fixed)
    plan = (plan[1], 2 * (seqs + rounds), n_chunks)
    gnormed, gate_grad, lend, rms, xg, cumg, stepg, bcg, mgg, skg, after, y = call(
        functools.partial(back_one, inner_all=inner_all, seqs=seqs, rounds=rounds, plan=plan), seqs + rounds, seqs,
        [xact, bcact, cum, gate, ssd, gn, sums, pre, gain, skip, wide]
        + [(v, rounds) for v in (xact, bcact, step, cum, lstart, entry, pre)],
        [big(inner, BF16), big(inner, BF16), ((seqs, blocks, n, inner), F32, 0), big(LANES, F32),
         big(inner, F32, lag=rounds), big(LANES, F32, lag=rounds), big(LANES, F32, lag=rounds), big(n2, F32, lag=rounds),
         ((8, inner), F32, None), ((8, inner), F32, None), ((seqs, n, inner), F32, None)],
        [vmem((T, inner), F32), vmem((n, inner), F32), vmem((n, inner), F32), vmem((seqs, length, inner), BF16),
         vmem((seqs, length, LANES), F32)]
        + Exchange.scratch(rounds, seqs, n, inner) + Rider.scratch(*plan, width),
        2 * flat * T * inner * 8, 3, y,
    )
    plan = (plan[0] + plan[1], 3 * seqs, n_chunks)
    xpg, xhalo, bpg, bhalo, raw, vkg, skgr, head_rows, out_weight_grad, gate_weight_grad, y = call(
        functools.partial(back_two, seqs=seqs, plan=plan), seqs, seqs,
        [xact, bcact, xext, bcext, step, cum, sraw, xg, cumg, stepg, bcg, lstart, entry, lend, after, pre,
         gnormed, cotangent, normed, gate_grad, value_kernel, vo, state_kernel, so, bias, rate, wide, tri],
        [big(inner, BF16), big(inner, BF16, HALO), big(n2, BF16), big(n2, BF16, HALO), big(LANES, BF16),
         ((8, inner), F32, None), ((8, n2), F32, None), ((8, LANES), F32, None),
         ((inner, width), BF16, None), ((width, inner), BF16, None)],
        [vmem((ext, inner), F32), vmem((ext, n2), F32), vmem((ext + HALO, inner), F32),
         vmem((ext + HALO, n2), F32), vmem((inner, width), F32), vmem((width, inner), F32)] + Rider.scratch(*plan, width),
        2 * flat * T * inner * 4, 5, y,
    )
    def flatten(v):
        return v.reshape(flat, v.shape[-1])

    normed_f, xpg_f, bpg_f, raw_f, gg_f = [flatten(v) for v in (normed, xpg, bpg, raw, gate_grad)]
    first = min(plan[0] + plan[1], n_chunks + 2 * LAG)
    plan = (first, max(n_chunks - first, 0) + 3 * LAG, n_chunks)

    def product_rows(v):
        return pl.BlockSpec((T, v.shape[1]), lambda i: (jnp.minimum(i, flat // T - 1), 0))

    def lagged(cols, lag):
        return pl.BlockSpec((CHUNK, cols), lambda i: (jnp.clip(i - lag, 0, n_chunks - 1), 0))

    late = (gate_weight, value_weight, state_weight, step_w, norm_gain, vkg, mgg, skg, head_rows, skgr, xhalo, bhalo)
    result, tokens_grad, small, wout, wgate, wvalue, wmixed = pl.pallas_call(
        functools.partial(finish, n=n_chunks, rounds=rounds, plan=plan, per_seq=blocks),
        grid=(n_chunks + 3 * LAG,),
        in_specs=[lagged(width, 3 * LAG)]
        + [product_rows(v) for v in (gg_f, xpg_f, bpg_f, raw_f)]
        + [lagged(width, 3 * LAG), lagged(width, 3 * LAG), lagged(LANES, 3 * LAG)]
        + [once(v) for v in late] + [product_rows(normed_f), product_rows(flatten(tokens))] + [anywhere] * 3,
        out_specs=[lagged(width, 3 * LAG), lagged(width, 3 * LAG), pl.BlockSpec((24, inner), lambda i: (0, 0)),
                   anywhere, anywhere, anywhere, anywhere],
        out_shape=[
            jax.ShapeDtypeStruct((flat, width), BF16), jax.ShapeDtypeStruct((flat, width), BF16),
            jax.ShapeDtypeStruct((24, inner), F32), *[jax.ShapeDtypeStruct((width, c), BF16) for c in (inner, inner, inner, n2 + LANES)],
        ],
        scratch_shapes=Chain.scratch(n_chunks, CHUNK, width) + Rider.scratch(*plan, width) + [
            vmem((24, inner), F32), vmem((rounds, 24, inner), F32), vmem((rounds, 24, inner), F32),
            pltpu.SemaphoreType.DMA((rounds,)), pltpu.SemaphoreType.DMA((rounds,)),

            vmem((3, width, inner), BF16), vmem((3, width, inner), BF16), vmem((width, n2 + LANES), BF16),
            vmem((width, n2 + LANES), BF16), vmem((4, width >> rounds, n2), BF16), vmem((width, inner), F32),
            vmem((width, n2 + LANES), F32), dma((4, GradSum.sem_count(rounds))), dma((3,)),
            vmem((16, inner), F32), vmem((4, 16, inner), F32), dma((8,)), vmem(xhalo.shape, BF16), vmem(bhalo.shape, BF16), dma((4,)),
            vmem((HALO, inner), F32), vmem((HALO, n2), F32),
        ],
        compiler_params=pltpu.CompilerParams(
            dimension_semantics=("arbitrary",), vmem_limit_bytes=62 * 1024 * 1024, collective_id=4, has_side_effects=True
        ),
        cost_estimate=pl.CostEstimate(flops=10**11, bytes_accessed=10**8, transcendentals=0),
    )(y.reshape(flat, width), gg_f, xpg_f, bpg_f, raw_f, flatten(tokens), flatten(cotangent), flatten(rms),
      *late, normed_f, flatten(tokens), out_weight_grad, gate_weight_grad, y)
    parts = 4

    def strip(rows, cols, at=0):
        return pl.BlockSpec((rows // parts, cols), lambda i: (i + at, 0))

    def entire(shape):
        return pl.BlockSpec(shape, lambda i: (0,) * len(shape))

    fine = [strip(inner, inner), strip(inner, inner, parts)]
    flat_out = [
        ((flat, width), BF16), ((flat, width), F32), ((width,), F32), ((width, inner), F32), ((width, inner), F32), ((width, n2), F32),
        ((heads, width), F32), ((taps, inner), F32), ((inner,), F32), ((taps, n2), F32), ((n2,), F32), ((heads,), F32), ((heads,), F32),
        ((heads,), F32), ((inner,), F32), ((inner, width), F32),
    ]
    cut = (0, 1, 3, 4, 5, 15)
    found = pl.pallas_call(
        functools.partial(unpack, taps=taps, heads=heads),
        grid=(parts,),
        in_specs=[strip(flat, width), strip(flat, width)] + fine + [strip(width, inner)] * 2 + [strip(width, n2 + LANES)]
        + [entire(wmixed.shape), entire(small.shape), entire(rate.shape), entire(wide.shape)],
        out_specs=[strip(*shape) if k in cut else entire(shape) for k, (shape, _) in enumerate(flat_out)],
        out_shape=[jax.ShapeDtypeStruct(shape, dtype) for shape, dtype in flat_out],
        compiler_params=pltpu.CompilerParams(dimension_semantics=("arbitrary",), vmem_limit_bytes=60 * 1024 * 1024),
    )(tokens_grad, result, wout, wout, wgate, wvalue, wmixed, wmixed, small, rate, wide)
    found = [found[0].reshape(tokens.shape), found[1].reshape(tokens.shape), *found[2:6], found[6].T, *found[7:]]
    return tuple(found)


def solution(mesh):
    rows, cols, vec = P(None, "seq", None), P(None, "head"), P("head")
    in_specs = (rows, P(), cols, cols, P(), cols, cols, vec, P(), P(), vec, vec, vec, vec, P("head", None), rows)
    out_specs = (rows, rows, P(), cols, cols, P(), cols, cols, vec, P(), P(), vec, vec, vec, vec, P("head", None))
    return jax.shard_map(shards, mesh=mesh, in_specs=in_specs, out_specs=out_specs, check_vma=False)
```
